32 devices in a mesh: groups: 2 (over x), gx: 16 (over z, y, core).
Axes of the slice: x: 2, y: 2, z: 4, core: 2. Of those that a mesh axis runs over, the one named last changes fastest.
Arguments:
- points: float32 [3, 131072], P(None, ('groups', 'gx')), parts along dimension 1, may hold values from 0 to 32
- noise_var: float32 [131072], P(('groups', 'gx')), parts along dimension 0, may hold values from 0.3 to 3
- probes: float32 [16, 131072], P(None, ('groups', 'gx')), parts along dimension 1, may hold values from -6 to 6
- pair_list: int32 [128, 2], P(('groups', 'gx')), parts along dimension 0, may hold values from 0 to 31, as said below
- counts: int32 [32], P(('groups', 'gx')), parts along dimension 0, may hold values from 2 to 4, as said below
Outputs:
- solution: float32 [16, 131072], P(None, ('groups', 'gx')), parts along dimension 1
- residual: float32 [16, 131072], P(None, ('groups', 'gx')), parts along dimension 1
The draws below stay inside these ranges and needn't reach their ends.
There are 2 independent parts, one for each index of `groups`. The reference program is written for one: setup_inputs(seed, part) draws one part's arguments, and reference() takes and returns one part's arrays. A program takes and returns all parts, laid end to end along the dimension named above; each array names one. Nothing has to cross between parts.
Inputs may be any that keep to these rules, and one draw needn't show every extreme that they name: `pair_list`: rows k * 4 to (k + 1) * 4 - 1 belong to device k of gx: the owner is one of its blocks k * 2 to (k + 1) * 2 - 1 and the partner is owner + d with 0 <= d <= 1; the live rows of a device are distinct. `counts`: the live rows lead each device's rows.
All inputs are finite; a program needn't handle non-finite values.
Results may differ from the reference program's by a relative error of at most 0.0043.
Values may be sent and summed in bfloat16 or wider, within the bound.
No kernel may reach another device: no remote copies, remote signals or barrier semaphores. Data moves between devices by JAX's collectives and lax.ppermute only.
A program may use at most 256 MiB of HBM per device.

```python
import math
import jax
import jax.numpy as jnp
from jax import lax

BLK = 2048
B_DEV = 2
REACH = 1
PROBES = 16
ITERS = 3
PAIRS_DEV = 4
BLOCKS = 32
POINTS = 65536
SLOTS = 64
N_GX = 16


def reach_table(key):
    reach_of = jax.random.randint(jax.random.fold_in(key, 11), (BLOCKS,), 0, REACH + 1)
    block_ids = jnp.arange(BLOCKS, dtype=jnp.int32)
    local_ids = block_ids % B_DEV
    device_ids = block_ids // B_DEV
    reach_of = jnp.where(local_ids == B_DEV - 1, REACH, reach_of)
    reach_of = jnp.where(block_ids < B_DEV, REACH, reach_of)
    reach_of = jnp.where(device_ids == N_GX - 1, 0, reach_of)
    return jnp.minimum(reach_of, BLOCKS - 1 - block_ids).astype(jnp.int32)


def slot_table(key):
    reach_of = reach_table(key)
    slot_index = jnp.arange(PAIRS_DEV, dtype=jnp.int32)
    local_block = slot_index // (REACH + 1)
    step_ahead = slot_index % (REACH + 1)
    devices = jnp.arange(N_GX, dtype=jnp.int32)
    owner_block = devices[:, None] * B_DEV + local_block[None, :]
    is_live = (step_ahead[None, :] <= reach_of[owner_block]).astype(jnp.int32)
    sub_keys = jax.random.split(jax.random.fold_in(key, 12), N_GX)
    shuffles = jax.vmap(lambda sub_key: jax.random.permutation(sub_key, PAIRS_DEV))(sub_keys)
    sort_key = (1 - is_live) * PAIRS_DEV + shuffles
    ordering = jnp.argsort(sort_key, axis=1, stable=True)
    owner_sorted = jnp.take_along_axis(owner_block, ordering, axis=1)
    step_sorted = jnp.take_along_axis(jnp.broadcast_to(step_ahead[None, :], (N_GX, PAIRS_DEV)), ordering, axis=1)
    live_sorted = jnp.take_along_axis(is_live, ordering, axis=1)
    dead_local = jax.random.randint(jax.random.fold_in(key, 13), (N_GX, PAIRS_DEV), 0, B_DEV)
    dead_step = jax.random.randint(jax.random.fold_in(key, 14), (N_GX, PAIRS_DEV), 0, REACH + 1)
    owner_final = jnp.where(live_sorted > 0, owner_sorted, devices[:, None] * B_DEV + dead_local)
    step_final = jnp.where(live_sorted > 0, step_sorted, dead_step)
    partner = owner_final + jnp.minimum(step_final, BLOCKS - 1 - owner_final)
    table = jnp.stack([owner_final, partner], axis=-1).reshape(SLOTS, 2).astype(jnp.int32)
    live_counts = jnp.sum(live_sorted, axis=1).astype(jnp.int32)
    return (table, live_counts)


def draw_pair_list(key, part):
    table, live_counts = slot_table(key)
    return table


def draw_counts(key, part):
    table, live_counts = slot_table(key)
    return live_counts


def draw_points(key, part):
    reach_of = reach_table(key)
    key = jax.random.fold_in(key, 5)
    spread = jax.random.uniform(jax.random.fold_in(key, 1), (POINTS,), jnp.float32)
    cross_side = math.sqrt(BLK / 80.0)
    across = cross_side * jax.random.uniform(jax.random.fold_in(key, 2), (2, POINTS), jnp.float32)
    point_ids = jnp.arange(POINTS, dtype=jnp.int32)
    block_ids = point_ids // BLK
    within = point_ids % BLK
    reach_float = reach_of[block_ids].astype(jnp.float32)
    start_float = block_ids.astype(jnp.float32)
    along = start_float + spread * (reach_float + 0.5)
    anchor = start_float + jnp.minimum(within.astype(jnp.float32), reach_float)
    along = jnp.where(within <= REACH, anchor, along)
    return jnp.concatenate([along[None, :], across], axis=0).astype(jnp.float32)


def block_levels(stream_key, extent, cuts, low, top_value):
    gain, own = 1.0, jax.random.fold_in(stream_key, 6)
    for axis_at, blocks in cuts:
        heights = jnp.exp(jax.random.uniform(jax.random.fold_in(own, axis_at), (blocks,), jnp.float32, low / len(cuts), top_value / len(cuts)))
        gain = gain * jnp.repeat(heights, extent[axis_at] // blocks).reshape([-1 if axis == axis_at else 1 for axis in range(len(extent))])
    return gain


def noise(rng, shape, scale, limit, cuts=(), kind=jnp.bfloat16):
    result = scale * jax.random.normal(rng, shape, jnp.float32)
    if cuts:
        result = result * block_levels(rng, shape, cuts, -0.22, 0.18)
    return jnp.clip(result, -limit, limit).astype(kind)


def setup_inputs(seed: int = 0, part: int = 0) -> dict:
    splits = jax.random.split(jax.random.key(seed), 6)
    part_keys = jax.random.split(jax.random.fold_in(splits[5], part), 6)
    points = draw_points(jax.random.fold_in(jax.random.fold_in(splits[5], part), 71), part)
    noise_var = jnp.clip(jnp.exp(math.log(3.0) - 2.3025851 * jax.random.uniform(part_keys[1], (POINTS,), jnp.float32) ** block_levels(part_keys[1], (POINTS,), ((0, 16),), -0.2, 0.2)), 0.3, 3.0)
    probes = noise(part_keys[2], (PROBES, POINTS), 1.0, 6.0, ((1, 16),), jnp.float32)
    pair_list = draw_pair_list(jax.random.fold_in(jax.random.fold_in(splits[5], part), 71), part)
    counts = draw_counts(jax.random.fold_in(jax.random.fold_in(splits[5], part), 71), part)
    return dict(points=points, noise_var=noise_var, probes=probes, pair_list=pair_list, counts=counts)


support_radius = 0.5
kernel_scale = 0.25

def wendland(left_points, right_points):
    squared = (left_points[0][:, None] - right_points[0][None, :]) ** 2
    squared = squared + (left_points[1][:, None] - right_points[1][None, :]) ** 2
    squared = squared + (left_points[2][:, None] - right_points[2][None, :]) ** 2
    distance = jnp.sqrt(squared) / support_radius
    remain = jnp.maximum(1.0 - distance, 0.0)
    values = kernel_scale * remain ** 4 * (4.0 * distance + 1.0)
    return values.astype(jnp.bfloat16)

def reference(points, noise_var, probes, pair_list, counts):
    slot_index = jnp.arange(SLOTS, dtype=jnp.int32)
    is_live = slot_index % PAIRS_DEV < counts[slot_index // PAIRS_DEV]

    def kernel_apply(vector):
        rounded = vector.astype(jnp.bfloat16).astype(jnp.float32)

        def one_pair(running, pair_row):
            owner_at, partner, alive = pair_row

            def add_pair(running):
                start_owner = (owner_at * BLK).astype(jnp.int32)
                start_partner = (partner * BLK).astype(jnp.int32)
                left_points = lax.dynamic_slice_in_dim(points, start_owner, BLK, 1)
                right_points = lax.dynamic_slice_in_dim(points, start_partner, BLK, 1)
                kernel_block = wendland(left_points, right_points).astype(jnp.float32)
                from_partner = lax.dynamic_slice_in_dim(rounded, start_partner, BLK, 1)
                from_owner = lax.dynamic_slice_in_dim(rounded, start_owner, BLK, 1)
                to_owner = jnp.dot(from_partner, kernel_block.T, preferred_element_type=jnp.float32, precision=lax.Precision.HIGHEST)
                old_owner = lax.dynamic_slice_in_dim(running, start_owner, BLK, 1)
                running = lax.dynamic_update_slice_in_dim(running, old_owner + to_owner, start_owner, 1)
                to_partner = jnp.dot(from_owner, kernel_block, preferred_element_type=jnp.float32, precision=lax.Precision.HIGHEST)
                weight = (partner != owner_at).astype(jnp.float32)
                old_partner = lax.dynamic_slice_in_dim(running, start_partner, BLK, 1)
                return lax.dynamic_update_slice_in_dim(running, old_partner + weight * to_partner, start_partner, 1)
            return (lax.cond(alive, add_pair, lambda running: running, running), None)
        start = jnp.zeros(vector.shape, jnp.float32)
        running, _ = lax.scan(one_pair, start, (pair_list[:, 0], pair_list[:, 1], is_live))
        return running
    solution = jnp.zeros(probes.shape, jnp.float32)
    residual = probes
    direction = probes
    norm_now = lax.optimization_barrier(jnp.sum(residual * residual, axis=1))
    for iteration in range(ITERS):
        product = noise_var[None, :] * direction + kernel_apply(direction)
        step_size = norm_now / lax.optimization_barrier(jnp.sum(direction * product, axis=1))
        solution = solution + step_size[:, None] * direction
        residual = residual - step_size[:, None] * product
        norm_next = lax.optimization_barrier(jnp.sum(residual * residual, axis=1))
        direction = residual + (norm_next / norm_now)[:, None] * direction
        norm_now = norm_next
    return (solution, residual)
```

```python
import functools

import jax
import jax.numpy as jnp
from jax import lax
from jax.experimental import pallas as pl
from jax.experimental.pallas import tpu as pltpu
from jax.sharding import PartitionSpec as P

BLK = 2048
STRIP = 256
STRIPS = BLK // STRIP
SUB = 128
SUBS = BLK // SUB
OFF_W = 768
OFF_SUBS = OFF_W // SUB
DIAG_W = 512
N_PROBES = 16
CHUNK = 16
MIB = 1 << 20

VMEM = pl.BlockSpec(memory_space=pltpu.VMEM)
SMEM = pl.BlockSpec(memory_space=pltpu.SMEM)

f32 = jnp.float32
bf16 = jnp.bfloat16

T_LIVE, T_EXTRA, T_START, T_END = 0, 1, 8, 16
T_SIZE = 24


def nt(left, right):
    return lax.dot_general(left, right, (((1,), (1,)), ((), ())), preferred_element_type=f32)


def nn(left, right):
    return jnp.dot(left, right, preferred_element_type=f32)


def split2(value):
    high = value.astype(bf16)
    low = (value - high.astype(f32)).astype(bf16)
    return jnp.concatenate([high, low], axis=0)


def halves(value):
    n = value.shape[0] // 2
    return value[:n] + value[n:]


def split3(value):
    high = value.astype(bf16).astype(f32)
    rest = value - high
    mid = rest.astype(bf16).astype(f32)
    return high, mid, rest - mid


def sort_kernel(blk, pts_ref, nv_ref, pr_ref, out_ref, perm_ref, col_ref, yb_ref, key_ref):
    cols = pl.ds(blk * BLK, BLK)
    y_row = pts_ref[1:2, cols]
    lane = lax.broadcasted_iota(jnp.int32, (1, BLK), 1)
    key_row = (y_row * 4096.0).astype(jnp.int32) * BLK + lane
    for c in range(SUBS):
        piece = jnp.broadcast_to(y_row[:, c * SUB : (c + 1) * SUB], (SUB, SUB)).T
        sub = lax.broadcasted_iota(jnp.int32, (SUB, SUB), 0) + c * SUB
        key_ref[c * SUB : (c + 1) * SUB, :] = (piece * 4096.0).astype(jnp.int32) * BLK + sub
    keys = jnp.broadcast_to(key_row, (8, BLK))

    def count(i, acc):
        mine = key_ref[pl.ds(pl.multiple_of(i * 8, 8), 8), :]
        mine = jnp.concatenate([mine] * SUBS, axis=1)
        return acc + jnp.where(mine < keys, 1, 0)

    acc = lax.fori_loop(0, BLK // 8, count, jnp.zeros((8, BLK), jnp.int32), unroll=8)
    rank = jnp.sum(acc, axis=0, keepdims=True)
    group = lax.shift_right_logical(rank, 8)
    within = jnp.bitwise_and(rank, STRIP - 1)

    pr = pr_ref[:, cols]
    aux = jnp.concatenate(
        [pts_ref[0:3, cols] * 2.0, nv_ref[:, cols], jnp.zeros((4, BLK), f32)], axis=0
    )
    data = jnp.concatenate([*split3(pr), *split3(aux), jnp.zeros((8, BLK), f32)], axis=0).astype(bf16)
    place = lax.broadcasted_iota(jnp.int32, (STRIP, SUB), 0).astype(f32).astype(bf16)
    one = jnp.ones((STRIP, SUB), bf16)
    zero = jnp.zeros((STRIP, SUB), bf16)
    for g in range(STRIPS):
        marked = jnp.where(group == g, within, -1).astype(f32).astype(bf16)
        for c in range(SUBS):
            hit = jnp.broadcast_to(marked[:, c * SUB : (c + 1) * SUB], (STRIP, SUB)) == place
            perm_ref[g * STRIP : (g + 1) * STRIP, c * SUB : (c + 1) * SUB] = jnp.where(hit, one, zero)
        got = nt(data, perm_ref[g * STRIP : (g + 1) * STRIP, :])
        here = slice(g * STRIP, (g + 1) * STRIP)
        out_ref[0:16, here] = (got[0:16] + got[16:32]) + got[32:48]
        out_ref[16:24, here] = (got[48:56] + got[56:64]) + got[64:72]
    for axis in range(3):
        for c in range(SUBS):
            here = slice(c * SUB, (c + 1) * SUB)
            row = out_ref[16 + axis : 17 + axis, here]
            col_ref[axis, here, :] = jnp.broadcast_to(row, (SUB, SUB)).T
    bounds(out_ref, yb_ref)


def bounds(side_ref, yb_ref):
    for c in range(SUBS):
        row = side_ref[17:18, c * SUB : (c + 1) * SUB]
        yb_ref[c] = jnp.min(row)
        yb_ref[SUBS + c] = jnp.max(row)


def sort_block(blk, points, noise, probes):
    return pl.pallas_call(
        functools.partial(sort_kernel, blk),
        out_shape=(
            pltpu.VMEM((24, BLK), f32),
            pltpu.VMEM((BLK, BLK), bf16),
            pltpu.VMEM((3, BLK, SUB), f32),
            jax.ShapeDtypeStruct((2 * SUBS,), f32),
        ),
        in_specs=[VMEM] * 3,
        out_specs=(VMEM, VMEM, VMEM, SMEM),
        scratch_shapes=[pltpu.VMEM((BLK, SUB), jnp.int32)],
        compiler_params=pltpu.CompilerParams(vmem_limit_bytes=12 * MIB),
        cost_estimate=pl.CostEstimate(flops=2 * 80 * BLK * BLK, bytes_accessed=MIB, transcendentals=0),
        name="sort_block",
    )(points, noise, probes)


def live_flag(pair_ref, count_ref, local, ahead):
    flag = jnp.int32(0)
    for s in range(pair_ref.shape[0]):
        owner = pair_ref[s, 0]
        match = (
            (jnp.int32(s) < count_ref[0])
            & (jnp.bitwise_and(owner, 1) == local)
            & (pair_ref[s, 1] - owner == ahead)
        )
        flag = jnp.where(match, jnp.int32(1), flag)
    return flag


def fill_table(tab_ref, base, flag, own_ref, other_ref, diag):
    slack = 1.0 + 1.0 / 1024.0

    def one_strip(i, extra):
        low = jnp.minimum(own_ref[2 * i], own_ref[2 * i + 1]) - slack
        high = jnp.maximum(own_ref[SUBS + 2 * i], own_ref[SUBS + 2 * i + 1]) + slack
        first = jnp.int32(0)
        end = jnp.int32(SUBS)
        for j in range(SUBS):
            first = first + jnp.where(other_ref[SUBS + j] <= low, 1, 0)
            end = end - jnp.where(other_ref[j] >= high, 1, 0)
        if diag:
            start = 2 * i + DIAG_W // SUB - OFF_SUBS
        else:
            start = jnp.minimum(first, SUBS - OFF_SUBS)
        tab_ref[base + T_START + i] = start
        tab_ref[base + T_END + i] = end
        return extra + jnp.maximum(end - (start + OFF_SUBS), 0)

    extra = lax.fori_loop(0, STRIPS, one_strip, jnp.int32(0))
    tab_ref[base + T_LIVE] = flag
    tab_ref[base + T_EXTRA] = extra * flag


def kernel_values(col_ref, row_at, rows):
    width = rows[0].shape[1]
    squared = None
    for axis in range(3):
        mine = col_ref[axis, pl.ds(row_at, CHUNK), :]
        diff = jnp.concatenate([mine] * (width // SUB), axis=1) - rows[axis]
        part = diff * diff
        squared = part if squared is None else squared + part
    squared = jnp.maximum(squared, 1e-30)
    q = squared * lax.rsqrt(squared)
    t = jnp.maximum(1.0 - q, 0.0)
    t2 = t * t
    return ((t2 * t2) * (q + 0.25)).astype(bf16)


def build_strip(store, col_ref, strip, side_ref, start, width):
    at = pl.ds(start, width)
    rows = [jnp.broadcast_to(side_ref[16 + axis : 17 + axis, at], (CHUNK, width)) for axis in range(3)]

    def chunk(i, carry):
        row_at = pl.multiple_of(strip * STRIP + i * CHUNK, CHUNK)
        store(pl.multiple_of(i * CHUNK, CHUNK), kernel_values(col_ref, row_at, rows))
        return carry

    lax.fori_loop(0, STRIP // CHUNK, chunk, 0, unroll=2)


def build_off(k_ref, tab_ref, base, col_ref, side_ref):
    for i in range(STRIPS):
        start = pl.multiple_of(tab_ref[base + T_START + i] * SUB, SUB)
        for h in range(OFF_W // STRIP):

            def store(at, value, i=i, h=h):
                k_ref[i, pl.ds(at, CHUNK), h * STRIP : (h + 1) * STRIP] = value

            build_strip(store, col_ref, i, side_ref, start + h * STRIP, STRIP)


def build_diag(k_ref, col_ref, side_ref):
    for i in range(STRIPS):
        for h in range(min(DIAG_W, BLK - i * STRIP) // STRIP):

            def store(at, value, i=i, h=h):
                k_ref[i, pl.ds(at, CHUNK), h * STRIP : (h + 1) * STRIP] = value

            build_strip(store, col_ref, i, side_ref, (i + h) * STRIP, STRIP)


def to_owner(k_ref, tab_ref, base, v_col, acc_row):
    for i in range(STRIPS):
        start = pl.multiple_of(tab_ref[base + T_START + i] * SUB, SUB)
        acc_row[:, i * STRIP : (i + 1) * STRIP] += halves(nt(v_col[:, pl.ds(start, OFF_W)], k_ref[i]))


def to_partner(k_ref, tab_ref, base, v_row, acc_col):
    for i in range(STRIPS):
        start = pl.multiple_of(tab_ref[base + T_START + i] * SUB, SUB)
        acc_col[:, pl.ds(start, OFF_W)] += halves(nn(v_row[:, i * STRIP : (i + 1) * STRIP], k_ref[i]))


def diag_products(k_ref, v_ref, acc_ref):
    for i in range(STRIPS):
        width = min(DIAG_W, BLK - i * STRIP)
        here = slice(i * STRIP, (i + 1) * STRIP)
        acc_ref[:, here] += halves(nt(v_ref[:, i * STRIP : i * STRIP + width], k_ref[i, :, :width]))
        if width > STRIP:
            after = slice((i + 1) * STRIP, i * STRIP + width)
            acc_ref[:, after] += halves(nn(v_ref[:, here], k_ref[i, :, STRIP:width]))


def extra_tiles(tab_ref, base, col_ref, side_ref, tile_ref, v_row, v_col, acc_row, acc_col):
    @pl.when(tab_ref[base + T_EXTRA] > 0)
    def _():
        def strip(i, carry):
            here = pl.ds(pl.multiple_of(i * STRIP, STRIP), STRIP)

            def tile(j, carry):
                there = pl.ds(pl.multiple_of(j * SUB, SUB), SUB)

                def store(at, value):
                    tile_ref[pl.ds(at, CHUNK), :] = value

                build_strip(store, col_ref, i, side_ref, pl.multiple_of(j * SUB, SUB), SUB)
                if acc_row is not None:
                    acc_row[:, here] += halves(nt(v_col[:, there], tile_ref[...]))
                if acc_col is not None:
                    acc_col[:, there] += halves(nn(v_row[:, here], tile_ref[...]))
                return carry

            return lax.fori_loop(
                tab_ref[base + T_START + i] + OFF_SUBS, tab_ref[base + T_END + i], tile, carry
            )

        lax.fori_loop(0, STRIPS, strip, 0)


TILE = pltpu.VMEM((STRIP, SUB), bf16)
SPLIT = pltpu.VMEM((2 * N_PROBES, BLK), bf16)
FIELD = (N_PROBES, BLK)


def call(body, outs, ins, out_specs, scratch, flops, name, limit=12):
    def run(*args):
        return pl.pallas_call(
            body,
            out_shape=outs,
            in_specs=ins,
            out_specs=out_specs,
            scratch_shapes=scratch,
            compiler_params=pltpu.CompilerParams(vmem_limit_bytes=limit * MIB),
            cost_estimate=pl.CostEstimate(flops=flops, bytes_accessed=MIB, transcendentals=0),
            name=name,
        )(*args)

    return run


def halo_build_kernel(pair, count, yb1, s1, col1, halo, k12, tab, acc1, back, yb2, tile, v1, v2):
    bounds(halo, yb2)
    fill_table(tab, 0, live_flag(pair, count, 1, 1), yb1, yb2, False)
    acc1[...] = jnp.zeros(FIELD, f32)
    back[...] = jnp.zeros(FIELD, f32)

    @pl.when(tab[T_LIVE] > 0)
    def _():
        v1[...] = split2(s1[0:16, :])
        v2[...] = split2(halo[0:16, :])
        build_off(k12, tab, 0, col1, halo)
        to_partner(k12, tab, 0, v1, back)
        to_owner(k12, tab, 0, v2, acc1)
        extra_tiles(tab, 0, col1, halo, tile, v1, v2, acc1, back)


def local_products(tab, k00, k01, k11, s0, s1, col0, col1, tile, v0, v1, acc0, acc1):
    @pl.when(tab[0 * T_SIZE + T_LIVE] > 0)
    def _():
        diag_products(k00, v0, acc0)
        extra_tiles(tab, 0 * T_SIZE, col0, s0, tile, v0, v0, acc0, acc0)

    @pl.when(tab[1 * T_SIZE + T_LIVE] > 0)
    def _():
        to_owner(k01, tab, 1 * T_SIZE, v1, acc0)
        to_partner(k01, tab, 1 * T_SIZE, v0, acc1)
        extra_tiles(tab, 1 * T_SIZE, col0, s1, tile, v0, v1, acc0, acc1)

    @pl.when(tab[2 * T_SIZE + T_LIVE] > 0)
    def _():
        diag_products(k11, v1, acc1)
        extra_tiles(tab, 2 * T_SIZE, col1, s1, tile, v1, v1, acc1, acc1)


def own_build_kernel(
    pair, count, yb0, yb1, s0, s1, col0, col1, acc1_in, k00, k01, k11, tab, acc0, acc1, tile, v0, v1
):
    fill_table(tab, 0 * T_SIZE, live_flag(pair, count, 0, 0), yb0, yb0, True)
    fill_table(tab, 1 * T_SIZE, live_flag(pair, count, 0, 1), yb0, yb1, False)
    fill_table(tab, 2 * T_SIZE, live_flag(pair, count, 1, 0), yb1, yb1, True)
    acc0[...] = jnp.zeros(FIELD, f32)
    acc1[...] = acc1_in[...]
    v0[...] = split2(s0[0:16, :])
    v1[...] = split2(s1[0:16, :])

    @pl.when(tab[0 * T_SIZE + T_LIVE] > 0)
    def _():
        build_diag(k00, col0, s0)

    @pl.when(tab[1 * T_SIZE + T_LIVE] > 0)
    def _():
        build_off(k01, tab, 1 * T_SIZE, col0, s1)

    @pl.when(tab[2 * T_SIZE + T_LIVE] > 0)
    def _():
        build_diag(k11, col1, s1)

    local_products(tab, k00, k01, k11, s0, s1, col0, col1, tile, v0, v1, acc0, acc1)


def own_apply_kernel(tab, k00, k01, k11, s0, s1, col0, col1, w0, w1, acc0, acc1, tile, v0, v1):
    acc0[...] = jnp.zeros(FIELD, f32)
    acc1[...] = jnp.zeros(FIELD, f32)
    v0[...] = split2(w0[0:16, :])
    v1[...] = split2(w1[0:16, :])
    local_products(tab, k00, k01, k11, s0, s1, col0, col1, tile, v0, v1, acc0, acc1)


def inner(left, right):
    product = left * right
    return jnp.sum(product, axis=1, keepdims=True)


def finish_kernel(
    level, tab, k12, s0, s1, col1, halo, halo_w, acc0, acc1, arrived, w0, w1, mom_in, n0, n1, back, mom, tile, v1, v2, acc
):
    live = tab[T_LIVE] > 0
    acc[...] = acc1[...]
    if level > 1:

        @pl.when(live)
        def _():
            v2[...] = split2(halo_w[0:16, :])
            to_owner(k12, tab, 0, v2, acc)
            extra_tiles(tab, 0, col1, halo, tile, None, v2, acc, None)

    before0 = w0[0:16, :]
    before1 = w1[0:16, :]
    next1 = s1[19:20, :] * before1 + acc[...]
    n1[...] = next1
    if level < 3:
        back[...] = jnp.zeros(FIELD, f32)

        @pl.when(live)
        def _():
            v1[...] = split2(next1)
            to_partner(k12, tab, 0, v1, back)
            extra_tiles(tab, 0, col1, halo, tile, v1, None, None, back)

    next0 = s0[19:20, :] * before0 + (acc0[...] + arrived[...])
    n0[...] = next0
    lane = lax.broadcasted_iota(jnp.int32, (N_PROBES, SUB), 1)
    cross = inner(before0, next0) + inner(before1, next1)
    own = inner(next0, next0) + inner(next1, next1)
    total = jnp.where(lane == 2 * level - 1, cross, jnp.where(lane == 2 * level, own, 0.0))
    if level == 1:
        total = jnp.where(lane == 0, inner(before0, before0) + inner(before1, before1), total)
    else:
        total = total + mom_in[...]
    mom[...] = total


def unsort_kernel(perm, wa, wb, wc, out):
    stacked = jnp.concatenate([split2(wa[...]), split2(wb[...]), split2(wc[...])], axis=0)
    for c in range(BLK // STRIP):
        here = slice(c * STRIP, (c + 1) * STRIP)
        got = nn(stacked, perm[:, here])
        for k in range(3):
            out[16 * k : 16 * (k + 1), here] = halves(got[32 * k : 32 * (k + 1)])


def combine_kernel(mom, probes, u0, u1, sol, res):
    lane = lax.broadcasted_iota(jnp.int32, (N_PROBES, SUB), 1)
    mu = [jnp.sum(jnp.where(lane == k, mom[...], 0.0), axis=1, keepdims=True) for k in range(7)]

    def form(left, right, shift):
        total = None
        for i, a in enumerate(left):
            for j, b in enumerate(right):
                part = (a * b) * mu[i + j + shift]
                total = part if total is None else total + part
        return total

    one = jnp.ones((N_PROBES, 1), f32)
    d = [one]
    r = [one]
    s = []
    rr = mu[0]
    for it in range(3):
        step = rr / form(d, d, 1)
        moved = [step * v for v in d]
        s = [a + b for a, b in zip(s + [0.0] * (len(d) - len(s)), moved)]
        r = [r[0]] + [(r[i] if i < len(r) else 0.0) - moved[i - 1] for i in range(1, len(moved) + 1)]
        if it < 2:
            new = form(r, r, 0)
            ratio = new / rr
            d = [r[i] + (ratio * d[i] if i < len(d) else 0.0) for i in range(len(r))]
            rr = new
    for b, u in ((0, u0), (1, u1)):
        here = slice(b * BLK, (b + 1) * BLK)
        w = [probes[:, here], u[0:16, :], u[16:32, :], u[32:48, :]]
        sol[:, here] = (s[0] * w[0] + s[1] * w[1]) + s[2] * w[2]
        res[:, here] = ((r[0] * w[0] + r[1] * w[1]) + r[2] * w[2]) + r[3] * w[3]


def from_behind(value, axis, steps):
    count = lax.axis_size(axis)
    first, last = (max(0, -steps), min(count, count - steps))
    return lax.ppermute(value, axis, [(source, source + steps) for source in range(first, last)])


def sum_over(value, axis):
    count = lax.axis_size(axis)
    if count & (count - 1):
        return lax.psum(value, axis)
    step = 1
    while step < count:
        value = value + lax.ppermute(value, axis, [(k, k ^ step) for k in range(count)])
        step *= 2
    return value


def on_device(points, noise_var, probes, pair_list, counts):
    noise = noise_var.reshape(1, -1)
    field = pltpu.VMEM(FIELD, f32)
    s0, p0, col0, yb0 = sort_block(0, points, noise, probes)
    halo = from_behind(s0, "gx", -1)
    s1, p1, col1, yb1 = sort_block(1, points, noise, probes)

    off = pltpu.VMEM((STRIPS, STRIP, OFF_W), bf16)
    diag = pltpu.VMEM((STRIPS, STRIP, DIAG_W), bf16)
    k12, tabc, acc1, back = call(
        halo_build_kernel,
        (off, jax.ShapeDtypeStruct((T_SIZE,), jnp.int32), field, field),
        [SMEM, SMEM, SMEM, VMEM, VMEM, VMEM],
        (VMEM, SMEM, VMEM, VMEM),
        [pltpu.SMEM((2 * SUBS,), f32), TILE, SPLIT, SPLIT],
        2 * 10**9,
        "halo_build",
    )(pair_list, counts, yb1, s1, col1, halo)
    arrived = from_behind(back, "gx", 1)
    k00, k01, k11, tabb, acc0, acc1 = call(
        own_build_kernel,
        (diag, off, diag, jax.ShapeDtypeStruct((3 * T_SIZE,), jnp.int32), field, field),
        [SMEM, SMEM, SMEM, SMEM, VMEM, VMEM, VMEM, VMEM, VMEM],
        (VMEM, VMEM, VMEM, SMEM, VMEM, VMEM),
        [TILE, SPLIT, SPLIT],
        6 * 10**9,
        "own_build",
    )(pair_list, counts, yb0, yb1, s0, s1, col0, col1, acc1)

    w0, w1 = s0, s1
    halo_w = halo
    mom = jnp.zeros((N_PROBES, SUB), f32)
    kept = []
    for level in range(1, 4):
        w0, w1, back, mom = call(
            functools.partial(finish_kernel, level),
            (field, field, field, pltpu.VMEM((N_PROBES, SUB), f32)),
            [SMEM] + [VMEM] * 12,
            (VMEM,) * 4,
            [TILE, SPLIT, SPLIT, pltpu.VMEM(FIELD, f32)],
            10**9,
            "finish",
        )(tabc, k12, s0, s1, col1, halo, halo_w, acc0, acc1, arrived, w0, w1, mom)
        kept.append((w0, w1))
        if level < 3:
            arrived = from_behind(back, "gx", 1)
            halo_w = from_behind(w0, "gx", -1)
            acc0, acc1 = call(
                own_apply_kernel,
                (field, field),
                [SMEM] + [VMEM] * 9,
                (VMEM, VMEM),
                [TILE, SPLIT, SPLIT],
                2 * 10**9,
                "own_apply",
            )(tabb, k00, k01, k11, s0, s1, col0, col1, w0, w1)
    total = sum_over(mom, "gx")
    given = []
    for b, perm in ((0, p0), (1, p1)):
        given.append(
            call(
                unsort_kernel,
                pltpu.VMEM((3 * N_PROBES, BLK), f32),
                [VMEM] * 4,
                VMEM,
                [],
                2 * 96 * BLK * BLK,
                "unsort",
            )(perm, *[pair[b] for pair in kept])
        )
    return call(
        combine_kernel,
        (jax.ShapeDtypeStruct(probes.shape, f32),) * 2,
        [VMEM] * 4,
        (VMEM, VMEM),
        [],
        10**6,
        "combine",
    )(total, probes, *given)


def solution(mesh):
    placed = (
        P(None, ("groups", "gx")),
        P(("groups", "gx")),
        P(None, ("groups", "gx")),
        P(("groups", "gx"), None),
        P(("groups", "gx")),
    )
    return jax.shard_map(
        on_device,
        mesh=mesh,
        in_specs=placed,
        out_specs=(P(None, ("groups", "gx")), P(None, ("groups", "gx"))),
        check_vma=False,
    )
```

```python
import functools

import jax
import jax.numpy as jnp
from jax import lax
from jax.experimental import pallas as pl
from jax.experimental.pallas import tpu as pltpu
from jax.sharding import PartitionSpec as P

BLK = 2048
STRIP = 256
STRIPS = BLK // STRIP
SUB = 128
SUBS = BLK // SUB
OFF_W = 768
OFF_SUBS = OFF_W // SUB
DIAG_W = 512
N_PROBES = 16
ROWS = 32
MIB = 1 << 20

VMEM = pl.BlockSpec(memory_space=pltpu.VMEM)
SMEM = pl.BlockSpec(memory_space=pltpu.SMEM)

f32 = jnp.float32
bf16 = jnp.bfloat16

T_LIVE, T_EXTRA, T_START, T_END = 0, 1, 8, 16
T_SIZE = 24


def nt(left, right):
    return lax.dot_general(left, right, (((1,), (1,)), ((), ())), preferred_element_type=f32)


def nn(left, right):
    return jnp.dot(left, right, preferred_element_type=f32)


def split2(value):
    high = value.astype(bf16)
    low = (value - high.astype(f32)).astype(bf16)
    return jnp.concatenate([high, low], axis=0)


def halves(value):
    n = value.shape[0] // 2
    return value[:n] + value[n:]


def split3(value):
    high = value.astype(bf16).astype(f32)
    rest = value - high
    mid = rest.astype(bf16).astype(f32)
    return high, mid, rest - mid


def one_hot(marked, g, c, place):
    hit = jnp.broadcast_to(marked[:, c * SUB : (c + 1) * SUB], (STRIP, SUB)) == place
    return jnp.where(hit, jnp.ones((STRIP, SUB), bf16), jnp.zeros((STRIP, SUB), bf16))


def places():
    return lax.broadcasted_iota(jnp.int32, (STRIP, SUB), 0).astype(f32).astype(bf16)


def marks(rank, g):
    group = lax.shift_right_logical(rank, 8)
    within = jnp.bitwise_and(rank, STRIP - 1)
    return jnp.where(group == g, within, -1).astype(f32).astype(bf16)


def rank_of(y_row, key_ref):
    lane = lax.broadcasted_iota(jnp.int32, (1, BLK), 1)
    key_row = (y_row * 4096.0).astype(jnp.int32) * BLK + lane
    for c in range(SUBS):
        piece = jnp.broadcast_to(y_row[:, c * SUB : (c + 1) * SUB], (SUB, SUB)).T
        sub = lax.broadcasted_iota(jnp.int32, (SUB, SUB), 0) + c * SUB
        key_ref[c * SUB : (c + 1) * SUB, :] = (piece * 4096.0).astype(jnp.int32) * BLK + sub
    keys = jnp.broadcast_to(key_row, (8, BLK))

    def count(i, acc):
        mine = key_ref[pl.ds(pl.multiple_of(i * 8, 8), 8), :]
        mine = jnp.concatenate([mine] * SUBS, axis=1)
        return acc + jnp.where(mine < keys, 1, 0)

    acc = lax.fori_loop(0, BLK // 8, count, jnp.zeros((8, BLK), jnp.int32), unroll=8)
    return jnp.sum(acc, axis=0, keepdims=True)


def sort_kernel(
    pts_hbm, nv_hbm, pr_hbm, pair, count, s0, s1, col0, col1, yb0, yb1, rank0, rank1, flags,
    pts_ref, nv_ref, pr_ref, key_ref, perm_ref, sems
):
    copies = [
        pltpu.make_async_copy(src, dst, sems.at[k])
        for k, (src, dst) in enumerate(((pts_hbm, pts_ref), (nv_hbm, nv_ref), (pr_hbm, pr_ref)))
    ]
    for copy in copies:
        copy.start()
    for local in range(2):
        for ahead in range(2):
            flags[2 * local + ahead] = live_flag(pair, count, local, ahead)
    copies[0].wait()
    for blk, rank_ref in enumerate((rank0, rank1)):
        rank_ref[...] = rank_of(pts_ref[1:2, blk * BLK : (blk + 1) * BLK], key_ref)
    copies[1].wait()
    copies[2].wait()
    for blk, (out_ref, col_ref, rank_ref) in enumerate(((s0, col0, rank0), (s1, col1, rank1))):
        cols = slice(blk * BLK, (blk + 1) * BLK)
        aux = jnp.concatenate(
            [pts_ref[0:3, cols] * 2.0, nv_ref[:, cols], jnp.zeros((4, BLK), f32)], axis=0
        )
        data = jnp.concatenate(
            [*split3(pr_ref[:, cols]), *split3(aux), jnp.zeros((8, BLK), f32)], axis=0
        ).astype(bf16)
        rank = rank_ref[...]
        place = places()
        for g in range(STRIPS):
            marked = marks(rank, g)
            for c in range(SUBS):
                perm_ref[g % 2, :, c * SUB : (c + 1) * SUB] = one_hot(marked, g, c, place)
            got = nt(data, perm_ref[g % 2])
            here = slice(g * STRIP, (g + 1) * STRIP)
            out_ref[0:16, here] = (got[0:16] + got[16:32]) + got[32:48]
            out_ref[16:24, here] = (got[48:56] + got[56:64]) + got[64:72]
        for axis in range(3):
            for c in range(SUBS):
                here = slice(c * SUB, (c + 1) * SUB)
                row = out_ref[16 + axis : 17 + axis, here]
                col_ref[axis, here, :] = jnp.broadcast_to(row, (SUB, SUB)).T
    bounds(s0, yb0)
    bounds(s1, yb1)


def bounds(side_ref, yb_ref):
    for c in range(SUBS):
        row = side_ref[17:18, c * SUB : (c + 1) * SUB]
        yb_ref[c] = jnp.min(row)
        yb_ref[SUBS + c] = jnp.max(row)


def live_flag(pair_ref, count_ref, local, ahead):
    flag = jnp.int32(0)
    for s in range(pair_ref.shape[0]):
        owner = pair_ref[s, 0]
        match = (
            (jnp.int32(s) < count_ref[0])
            & (jnp.bitwise_and(owner, 1) == local)
            & (pair_ref[s, 1] - owner == ahead)
        )
        flag = jnp.where(match, jnp.int32(1), flag)
    return flag


def fill_table(tab_ref, base, flag, own_ref, other_ref, diag):
    slack = 1.0 + 1.0 / 1024.0

    def one_strip(i, extra):
        low = jnp.minimum(own_ref[2 * i], own_ref[2 * i + 1]) - slack
        high = jnp.maximum(own_ref[SUBS + 2 * i], own_ref[SUBS + 2 * i + 1]) + slack
        first = jnp.int32(0)
        end = jnp.int32(SUBS)
        for j in range(SUBS):
            first = first + jnp.where(other_ref[SUBS + j] <= low, 1, 0)
            end = end - jnp.where(other_ref[j] >= high, 1, 0)
        if diag:
            start = 2 * i + DIAG_W // SUB - OFF_SUBS
        else:
            start = jnp.minimum(first, SUBS - OFF_SUBS)
        tab_ref[base + T_START + i] = start
        tab_ref[base + T_END + i] = end
        return extra + jnp.maximum(end - (start + OFF_SUBS), 0)

    extra = lax.fori_loop(0, STRIPS, one_strip, jnp.int32(0))
    tab_ref[base + T_LIVE] = flag
    tab_ref[base + T_EXTRA] = extra * flag


def kernel_values(col_ref, row_at, rows):
    width = rows[0].shape[1]
    squared = None
    for axis in range(3):
        mine = col_ref[axis, pl.ds(row_at, ROWS), :]
        diff = jnp.concatenate([mine] * (width // SUB), axis=1) - rows[axis]
        part = diff * diff
        squared = part if squared is None else squared + part
    squared = jnp.maximum(squared, 1e-30)
    q = squared * lax.rsqrt(squared)
    t = jnp.maximum(1.0 - q, 0.0)
    t2 = t * t
    return ((t2 * t2) * (q + 0.25)).astype(bf16)


def build_strip(store, col_ref, strip, side_ref, start, width, unroll=2):
    at = pl.ds(start, width)
    rows = [jnp.broadcast_to(side_ref[16 + axis : 17 + axis, at], (ROWS, width)) for axis in range(3)]

    def chunk(i, carry):
        row_at = pl.multiple_of(strip * STRIP + i * ROWS, ROWS)
        store(pl.multiple_of(i * ROWS, ROWS), kernel_values(col_ref, row_at, rows))
        return carry

    lax.fori_loop(0, STRIP // ROWS, chunk, 0, unroll=unroll)


def build_off(k_ref, tab_ref, base, col_ref, side_ref):
    part = OFF_W // 2
    for i in range(STRIPS):
        start = pl.multiple_of(tab_ref[base + T_START + i] * SUB, SUB)
        for h in range(2):

            def store(at, value, i=i, h=h):
                k_ref[i, pl.ds(at, ROWS), h * part : (h + 1) * part] = value

            build_strip(store, col_ref, i, side_ref, pl.multiple_of(start + h * part, SUB), part)


def build_diag(k_ref, col_ref, side_ref):
    for i in range(STRIPS):
        for h in range(min(DIAG_W, BLK - i * STRIP) // STRIP):

            def store(at, value, i=i, h=h):
                k_ref[i, pl.ds(at, ROWS), h * STRIP : (h + 1) * STRIP] = value

            build_strip(store, col_ref, i, side_ref, (i + h) * STRIP, STRIP, 4)


def to_owner(k_ref, tab_ref, base, v_col, acc_row):
    for i in range(STRIPS):
        start = pl.multiple_of(tab_ref[base + T_START + i] * SUB, SUB)
        acc_row[:, i * STRIP : (i + 1) * STRIP] += halves(nt(v_col[:, pl.ds(start, OFF_W)], k_ref[i]))


def to_partner(k_ref, tab_ref, base, v_row, acc_col):
    for i in range(STRIPS):
        start = pl.multiple_of(tab_ref[base + T_START + i] * SUB, SUB)
        acc_col[:, pl.ds(start, OFF_W)] += halves(nn(v_row[:, i * STRIP : (i + 1) * STRIP], k_ref[i]))


def diag_products(k_ref, v_ref, acc_ref):
    for i in range(STRIPS):
        width = min(DIAG_W, BLK - i * STRIP)
        here = slice(i * STRIP, (i + 1) * STRIP)
        acc_ref[:, here] += halves(nt(v_ref[:, i * STRIP : i * STRIP + width], k_ref[i, :, :width]))
        if width > STRIP:
            after = slice((i + 1) * STRIP, i * STRIP + width)
            acc_ref[:, after] += halves(nn(v_ref[:, here], k_ref[i, :, STRIP:width]))


def extra_tiles(tab_ref, base, col_ref, side_ref, tile_ref, v_row, v_col, acc_row, acc_col):
    @pl.when(tab_ref[base + T_EXTRA] > 0)
    def _():
        def strip(i, carry):
            here = pl.ds(pl.multiple_of(i * STRIP, STRIP), STRIP)

            def tile(j, carry):
                there = pl.ds(pl.multiple_of(j * SUB, SUB), SUB)

                def store(at, value):
                    tile_ref[pl.ds(at, ROWS), :] = value

                build_strip(store, col_ref, i, side_ref, pl.multiple_of(j * SUB, SUB), SUB)
                if acc_row is not None:
                    acc_row[:, here] += halves(nt(v_col[:, there], tile_ref[...]))
                if acc_col is not None:
                    acc_col[:, there] += halves(nn(v_row[:, here], tile_ref[...]))
                return carry

            return lax.fori_loop(
                tab_ref[base + T_START + i] + OFF_SUBS, tab_ref[base + T_END + i], tile, carry
            )

        lax.fori_loop(0, STRIPS, strip, 0)


TILE = pltpu.VMEM((STRIP, SUB), bf16)
SPLIT = pltpu.VMEM((2 * N_PROBES, BLK), bf16)
FIELD = (N_PROBES, BLK)


def call(body, outs, ins, out_specs, scratch, flops, name, limit=12):
    def run(*args):
        return pl.pallas_call(
            body,
            out_shape=outs,
            in_specs=ins,
            out_specs=out_specs,
            scratch_shapes=scratch,
            compiler_params=pltpu.CompilerParams(vmem_limit_bytes=limit * MIB),
            cost_estimate=pl.CostEstimate(flops=flops, bytes_accessed=MIB, transcendentals=0),
            name=name,
        )(*args)

    return run


def diag_build_kernel(flags, yb0, yb1, s0, s1, col0, col1, k00, k11, tab):
    fill_table(tab, 0 * T_SIZE, flags[0], yb0, yb0, True)
    fill_table(tab, 1 * T_SIZE, flags[1], yb0, yb1, False)
    fill_table(tab, 2 * T_SIZE, flags[2], yb1, yb1, True)

    @pl.when(flags[0] > 0)
    def _():
        build_diag(k00, col0, s0)

    @pl.when(flags[2] > 0)
    def _():
        build_diag(k11, col1, s1)


def halo_build_kernel(flags, yb1, s1, col1, halo, k12, tab, acc1, back, yb2, tile, v1, v2):
    bounds(halo, yb2)
    fill_table(tab, 0, flags[3], yb1, yb2, False)
    acc1[...] = jnp.zeros(FIELD, f32)
    back[...] = jnp.zeros(FIELD, f32)

    @pl.when(flags[3] > 0)
    def _():
        v1[...] = split2(s1[0:16, :])
        v2[...] = split2(halo[0:16, :])
        build_off(k12, tab, 0, col1, halo)
        to_partner(k12, tab, 0, v1, back)
        to_owner(k12, tab, 0, v2, acc1)
        extra_tiles(tab, 0, col1, halo, tile, v1, v2, acc1, back)


def local_products(tab, k00, k01, k11, s0, s1, col0, col1, tile, v0, v1, acc0, acc1):
    @pl.when(tab[0 * T_SIZE + T_LIVE] > 0)
    def _():
        diag_products(k00, v0, acc0)
        extra_tiles(tab, 0 * T_SIZE, col0, s0, tile, v0, v0, acc0, acc0)

    @pl.when(tab[1 * T_SIZE + T_LIVE] > 0)
    def _():
        to_owner(k01, tab, 1 * T_SIZE, v1, acc0)
        to_partner(k01, tab, 1 * T_SIZE, v0, acc1)
        extra_tiles(tab, 1 * T_SIZE, col0, s1, tile, v0, v1, acc0, acc1)

    @pl.when(tab[2 * T_SIZE + T_LIVE] > 0)
    def _():
        diag_products(k11, v1, acc1)
        extra_tiles(tab, 2 * T_SIZE, col1, s1, tile, v1, v1, acc1, acc1)


def own_build_kernel(tab, s0, s1, col0, col1, k00, k11, acc1_in, k01, acc0, acc1, tile, v0, v1):
    acc0[...] = jnp.zeros(FIELD, f32)
    acc1[...] = acc1_in[...]
    v0[...] = split2(s0[0:16, :])
    v1[...] = split2(s1[0:16, :])

    @pl.when(tab[1 * T_SIZE + T_LIVE] > 0)
    def _():
        build_off(k01, tab, 1 * T_SIZE, col0, s1)

    local_products(tab, k00, k01, k11, s0, s1, col0, col1, tile, v0, v1, acc0, acc1)


def own_apply_kernel(tab, k00, k01, k11, s0, s1, col0, col1, w0, w1, acc0, acc1, tile, v0, v1):
    acc0[...] = jnp.zeros(FIELD, f32)
    acc1[...] = jnp.zeros(FIELD, f32)
    v0[...] = split2(w0[0:16, :])
    v1[...] = split2(w1[0:16, :])
    local_products(tab, k00, k01, k11, s0, s1, col0, col1, tile, v0, v1, acc0, acc1)


def inner(left, right):
    product = left * right
    return jnp.sum(product, axis=1, keepdims=True)


def finish_kernel(
    level, tab, k12, s0, s1, col1, halo, halo_w, acc0, acc1, arrived, w0, w1, mom_in, n0, n1, back, mom, tile, v1, v2, acc
):
    live = tab[T_LIVE] > 0
    acc[...] = acc1[...]
    if level > 1:

        @pl.when(live)
        def _():
            v2[...] = split2(halo_w[0:16, :])
            to_owner(k12, tab, 0, v2, acc)
            extra_tiles(tab, 0, col1, halo, tile, None, v2, acc, None)

    before0 = w0[0:16, :]
    before1 = w1[0:16, :]
    next1 = s1[19:20, :] * before1 + acc[...]
    n1[...] = next1
    back[...] = jnp.zeros(FIELD, f32)

    @pl.when(live)
    def _():
        v1[...] = split2(next1)
        to_partner(k12, tab, 0, v1, back)
        extra_tiles(tab, 0, col1, halo, tile, v1, None, None, back)

    next0 = s0[19:20, :] * before0 + (acc0[...] + arrived[...])
    n0[...] = next0
    lane = lax.broadcasted_iota(jnp.int32, (N_PROBES, SUB), 1)
    cross = inner(before0, next0) + inner(before1, next1)
    own = inner(next0, next0) + inner(next1, next1)
    total = jnp.where(lane == 2 * level - 1, cross, jnp.where(lane == 2 * level, own, 0.0))
    if level == 1:
        total = jnp.where(lane == 0, inner(before0, before0) + inner(before1, before1), total)
    else:
        total = total + mom_in[...]
    mom[...] = total


def moment_kernel(s0, s1, acc0, acc1, arrived, w0, w1, mom_in, mom):
    lane = lax.broadcasted_iota(jnp.int32, (N_PROBES, SUB), 1)
    one = w0[...]
    two = w1[...]
    cross = inner(one, s0[19:20, :] * one + (acc0[...] + 2.0 * arrived[...]))
    cross = cross + inner(two, s1[19:20, :] * two + acc1[...])
    mom[...] = mom_in[...] + jnp.where(lane == 5, cross, 0.0)


def last_kernel(tab, k12, s0, s1, col1, halo, halo_w, acc0, acc1, arrived, w0, w1, n0, n1, tile, v2):
    n1[...] = s1[19:20, :] * w1[...] + acc1[...]
    n0[...] = s0[19:20, :] * w0[...] + (acc0[...] + arrived[...])

    @pl.when(tab[T_LIVE] > 0)
    def _():
        v2[...] = split2(halo_w[...])
        to_owner(k12, tab, 0, v2, n1)
        extra_tiles(tab, 0, col1, halo, tile, None, v2, n1, None)


def unsort_kernel(rank_ref, wa, wb, wc, out, perm_ref):
    stacked = jnp.concatenate([split2(wa[...]), split2(wb[...]), split2(wc[...])], axis=0)
    rank = rank_ref[...]
    place = places()
    marked = [marks(rank, g) for g in range(STRIPS)]
    for c in range(BLK // STRIP):
        here = slice(c * STRIP, (c + 1) * STRIP)
        for g in range(STRIPS):
            for h in range(2):
                perm_ref[c % 2, g * STRIP : (g + 1) * STRIP, h * SUB : (h + 1) * SUB] = one_hot(
                    marked[g], g, 2 * c + h, place
                )
        got = nn(stacked, perm_ref[c % 2])
        for k in range(3):
            out[16 * k : 16 * (k + 1), here] = halves(got[32 * k : 32 * (k + 1)])


def combine_kernel(mom, probes, u0, u1, sol, res):
    lane = lax.broadcasted_iota(jnp.int32, (N_PROBES, SUB), 1)
    mu = [jnp.sum(jnp.where(lane == k, mom[...], 0.0), axis=1, keepdims=True) for k in range(6)]

    def form(left, right, shift):
        total = None
        for i, a in enumerate(left):
            for j, b in enumerate(right):
                part = (a * b) * mu[i + j + shift]
                total = part if total is None else total + part
        return total

    one = jnp.ones((N_PROBES, 1), f32)
    d = [one]
    r = [one]
    s = []
    rr = mu[0]
    for it in range(3):
        step = rr / form(d, d, 1)
        moved = [step * v for v in d]
        s = [a + b for a, b in zip(s + [0.0] * (len(d) - len(s)), moved)]
        r = [r[0]] + [(r[i] if i < len(r) else 0.0) - moved[i - 1] for i in range(1, len(moved) + 1)]
        if it < 2:
            new = form(r, r, 0)
            ratio = new / rr
            d = [r[i] + (ratio * d[i] if i < len(d) else 0.0) for i in range(len(r))]
            rr = new
    for b, u in ((0, u0), (1, u1)):
        here = slice(b * BLK, (b + 1) * BLK)
        w = [probes[:, here], u[0:16, :], u[16:32, :], u[32:48, :]]
        sol[:, here] = (s[0] * w[0] + s[1] * w[1]) + s[2] * w[2]
        res[:, here] = ((r[0] * w[0] + r[1] * w[1]) + r[2] * w[2]) + r[3] * w[3]


def from_behind(value, axis, steps):
    count = lax.axis_size(axis)
    first, last = (max(0, -steps), min(count, count - steps))
    return lax.ppermute(value, axis, [(source, source + steps) for source in range(first, last)])


def sum_over(value, axis):
    count = lax.axis_size(axis)
    if count & (count - 1):
        return lax.psum(value, axis)

    def swapped(value, step):
        return lax.ppermute(value, axis, [(k, k ^ step) for k in range(count)])

    step = 1
    while 4 * step <= count:
        near, far, both = [swapped(value, m * step) for m in (1, 2, 3)]
        value = (value + near) + (far + both)
        step *= 4
    if step < count:
        value = value + swapped(value, step)
    return value


def on_device(points, noise_var, probes, pair_list, counts):
    noise = noise_var.reshape(1, -1)
    field = pltpu.VMEM(FIELD, f32)
    side = pltpu.VMEM((24, BLK), f32)
    column = pltpu.VMEM((3, BLK, SUB), f32)
    limits = jax.ShapeDtypeStruct((2 * SUBS,), f32)
    ranks = pltpu.VMEM((1, BLK), jnp.int32)
    any_space = pl.BlockSpec(memory_space=pl.ANY)
    s0, s1, col0, col1, yb0, yb1, rank0, rank1, flags = call(
        sort_kernel,
        (side, side, column, column, limits, limits, ranks, ranks, jax.ShapeDtypeStruct((4,), jnp.int32)),
        [any_space] * 3 + [SMEM] * 2,
        (VMEM,) * 4 + (SMEM,) * 2 + (VMEM,) * 2 + (SMEM,),
        [
            pltpu.VMEM(points.shape, f32),
            pltpu.VMEM(noise.shape, f32),
            pltpu.VMEM(probes.shape, f32),
            pltpu.VMEM((BLK, SUB), jnp.int32),
            pltpu.VMEM((2, STRIP, BLK), bf16),
            pltpu.SemaphoreType.DMA((3,)),
        ],
        10**9,
        "sort_blocks",
    )(points, noise, probes, pair_list, counts)
    halo = from_behind(s0, "gx", -1)

    off = pltpu.VMEM((STRIPS, STRIP, OFF_W), bf16)
    diag = pltpu.VMEM((STRIPS, STRIP, DIAG_W), bf16)
    k00, k11, tabb = call(
        diag_build_kernel,
        (diag, diag, jax.ShapeDtypeStruct((3 * T_SIZE,), jnp.int32)),
        [SMEM] * 3 + [VMEM] * 4,
        (VMEM, VMEM, SMEM),
        [],
        3 * 10**9,
        "diag_build",
    )(flags, yb0, yb1, s0, s1, col0, col1)
    k12, tabc, acc1, back = call(
        halo_build_kernel,
        (off, jax.ShapeDtypeStruct((T_SIZE,), jnp.int32), field, field),
        [SMEM] * 2 + [VMEM] * 3,
        (VMEM, SMEM, VMEM, VMEM),
        [pltpu.SMEM((2 * SUBS,), f32), TILE, SPLIT, SPLIT],
        3 * 10**9,
        "halo_build",
    )(flags, yb1, s1, col1, halo)
    arrived = from_behind(back, "gx", 1)
    k01, acc0, acc1 = call(
        own_build_kernel,
        (off, field, field),
        [SMEM] + [VMEM] * 7,
        (VMEM,) * 3,
        [TILE, SPLIT, SPLIT],
        5 * 10**9,
        "own_build",
    )(tabb, s0, s1, col0, col1, k00, k11, acc1)

    w0, w1 = s0, s1
    halo_w = halo
    moments = pltpu.VMEM((N_PROBES, SUB), f32)
    mom = jnp.zeros((N_PROBES, SUB), f32)
    kept = []
    for level in (1, 2):
        w0, w1, back, mom = call(
            functools.partial(finish_kernel, level),
            (field, field, field, moments),
            [SMEM] + [VMEM] * 12,
            (VMEM,) * 4,
            [TILE, SPLIT, SPLIT, pltpu.VMEM(FIELD, f32)],
            10**9,
            "finish",
        )(tabc, k12, s0, s1, col1, halo, halo_w, acc0, acc1, arrived, w0, w1, mom)
        kept.append((w0, w1))
        arrived = from_behind(back, "gx", 1)
        halo_w = from_behind(w0, "gx", -1)
        acc0, acc1 = call(
            own_apply_kernel,
            (field, field),
            [SMEM] + [VMEM] * 9,
            (VMEM, VMEM),
            [TILE, SPLIT, SPLIT],
            2 * 10**9,
            "own_apply",
        )(tabb, k00, k01, k11, s0, s1, col0, col1, w0, w1)
    mom = call(moment_kernel, moments, [VMEM] * 8, VMEM, [], 10**7, "moment")(
        s0, s1, acc0, acc1, arrived, w0, w1, mom
    )
    total = sum_over(mom, "gx")
    kept.append(
        call(last_kernel, (field, field), [SMEM] + [VMEM] * 11, (VMEM, VMEM), [TILE, SPLIT], 10**9, "last")(
            tabc, k12, s0, s1, col1, halo, halo_w, acc0, acc1, arrived, w0, w1
        )
    )
    given = []
    for b, rank in ((0, rank0), (1, rank1)):
        given.append(
            call(
                unsort_kernel,
                pltpu.VMEM((3 * N_PROBES, BLK), f32),
                [VMEM] * 4,
                VMEM,
                [pltpu.VMEM((2, BLK, STRIP), bf16)],
                2 * 96 * BLK * BLK,
                "unsort",
            )(rank, *[pair[b] for pair in kept])
        )
    return call(
        combine_kernel,
        (jax.ShapeDtypeStruct(probes.shape, f32),) * 2,
        [VMEM] * 4,
        (VMEM, VMEM),
        [],
        10**6,
        "combine",
    )(total, probes, *given)


def solution(mesh):
    placed = (
        P(None, ("groups", "gx")),
        P(("groups", "gx")),
        P(None, ("groups", "gx")),
        P(("groups", "gx"), None),
        P(("groups", "gx")),
    )
    return jax.shard_map(
        on_device,
        mesh=mesh,
        in_specs=placed,
        out_specs=(P(None, ("groups", "gx")), P(None, ("groups", "gx"))),
        check_vma=False,
    )
```

```python
import functools

import jax
import jax.numpy as jnp
from jax import lax
from jax.experimental import pallas as pl
from jax.experimental.pallas import tpu as pltpu
from jax.sharding import PartitionSpec as P

BLK = 2048
STRIP = 256
STRIPS = BLK // STRIP
SUB = 128
SUBS = BLK // SUB
OFF_W = 768
OFF_SUBS = OFF_W // SUB
DIAG_W = 512
N_PROBES = 16
ROWS = 32
MIB = 1 << 20

VMEM = pl.BlockSpec(memory_space=pltpu.VMEM)
SMEM = pl.BlockSpec(memory_space=pltpu.SMEM)

f32 = jnp.float32
bf16 = jnp.bfloat16

T_LIVE, T_EXTRA, T_START, T_END = 0, 1, 8, 16
T_SIZE = 24


def nt(left, right):
    return lax.dot_general(left, right, (((1,), (1,)), ((), ())), preferred_element_type=f32)


def nn(left, right):
    return jnp.dot(left, right, preferred_element_type=f32)


def split2(value):
    high = value.astype(bf16)
    low = (value - high.astype(f32)).astype(bf16)
    return jnp.concatenate([high, low], axis=0)


def halves(value):
    n = value.shape[0] // 2
    return value[:n] + value[n:]


def split3(value):
    high = value.astype(bf16).astype(f32)
    rest = value - high
    mid = rest.astype(bf16).astype(f32)
    return high, mid, rest - mid


def one_hot(marked, g, c, place):
    hit = jnp.broadcast_to(marked[:, c * SUB : (c + 1) * SUB], (STRIP, SUB)) == place
    return jnp.where(hit, jnp.ones((STRIP, SUB), bf16), jnp.zeros((STRIP, SUB), bf16))


def places():
    return lax.broadcasted_iota(jnp.int32, (STRIP, SUB), 0).astype(f32).astype(bf16)


def marks(rank, g):
    group = lax.shift_right_logical(rank, 8)
    within = jnp.bitwise_and(rank, STRIP - 1)
    return jnp.where(group == g, within, -1).astype(f32).astype(bf16)


def rank_of(y_row, key_ref):
    lane = lax.broadcasted_iota(jnp.int32, (1, BLK), 1)
    key_row = (y_row * 4096.0).astype(jnp.int32) * BLK + lane
    for c in range(SUBS):
        piece = jnp.broadcast_to(y_row[:, c * SUB : (c + 1) * SUB], (SUB, SUB)).T
        sub = lax.broadcasted_iota(jnp.int32, (SUB, SUB), 0) + c * SUB
        key_ref[c * SUB : (c + 1) * SUB, :] = (piece * 4096.0).astype(jnp.int32) * BLK + sub
    keys = jnp.broadcast_to(key_row, (8, BLK))

    def count(i, acc):
        mine = key_ref[pl.ds(pl.multiple_of(i * 8, 8), 8), :]
        mine = jnp.concatenate([mine] * SUBS, axis=1)
        return acc + jnp.where(mine < keys, 1, 0)

    acc = lax.fori_loop(0, BLK // 8, count, jnp.zeros((8, BLK), jnp.int32), unroll=8)
    return jnp.sum(acc, axis=0, keepdims=True)


def sort_kernel(
    pts_hbm, nv_hbm, pr_hbm, pair, count, s0, s1, col0, col1, yb0, yb1, rank0, rank1, flags,
    pts_ref, nv_ref, pr_ref, key_ref, perm_ref, sems
):
    copies = [
        pltpu.make_async_copy(src, dst, sems.at[k])
        for k, (src, dst) in enumerate(((pts_hbm, pts_ref), (nv_hbm, nv_ref), (pr_hbm, pr_ref)))
    ]
    for copy in copies:
        copy.start()
    for local in range(2):
        for ahead in range(2):
            flags[2 * local + ahead] = live_flag(pair, count, local, ahead)
    flags[4] = jnp.bitwise_and(lax.shift_right_logical(pair[0, 0], 1), 1)
    copies[0].wait()
    for blk, rank_ref in enumerate((rank0, rank1)):
        rank_ref[...] = rank_of(pts_ref[1:2, blk * BLK : (blk + 1) * BLK], key_ref)
    copies[1].wait()
    copies[2].wait()
    for blk, (out_ref, col_ref, rank_ref) in enumerate(((s0, col0, rank0), (s1, col1, rank1))):
        cols = slice(blk * BLK, (blk + 1) * BLK)
        aux = jnp.concatenate(
            [pts_ref[0:3, cols] * 2.0, nv_ref[:, cols], jnp.zeros((4, BLK), f32)], axis=0
        )
        data = jnp.concatenate(
            [*split3(pr_ref[:, cols]), *split3(aux), jnp.zeros((8, BLK), f32)], axis=0
        ).astype(bf16)
        rank = rank_ref[...]
        place = places()
        for g in range(STRIPS):
            marked = marks(rank, g)
            for c in range(SUBS):
                perm_ref[g % 2, :, c * SUB : (c + 1) * SUB] = one_hot(marked, g, c, place)
            got = nt(data, perm_ref[g % 2])
            here = slice(g * STRIP, (g + 1) * STRIP)
            out_ref[0:16, here] = (got[0:16] + got[16:32]) + got[32:48]
            out_ref[16:24, here] = (got[48:56] + got[56:64]) + got[64:72]
        for axis in range(3):
            for c in range(SUBS):
                here = slice(c * SUB, (c + 1) * SUB)
                row = out_ref[16 + axis : 17 + axis, here]
                col_ref[axis, here, :] = jnp.broadcast_to(row, (SUB, SUB)).T
    bounds(s0, yb0)
    bounds(s1, yb1)


def bounds(side_ref, yb_ref):
    for c in range(SUBS):
        row = side_ref[17:18, c * SUB : (c + 1) * SUB]
        yb_ref[c] = jnp.min(row)
        yb_ref[SUBS + c] = jnp.max(row)


def live_flag(pair_ref, count_ref, local, ahead):
    flag = jnp.int32(0)
    for s in range(pair_ref.shape[0]):
        owner = pair_ref[s, 0]
        match = (
            (jnp.int32(s) < count_ref[0])
            & (jnp.bitwise_and(owner, 1) == local)
            & (pair_ref[s, 1] - owner == ahead)
        )
        flag = jnp.where(match, jnp.int32(1), flag)
    return flag


def fill_table(tab_ref, base, flag, own_ref, other_ref, diag):
    slack = 1.0 + 1.0 / 1024.0

    def one_strip(i, extra):
        low = jnp.minimum(own_ref[2 * i], own_ref[2 * i + 1]) - slack
        high = jnp.maximum(own_ref[SUBS + 2 * i], own_ref[SUBS + 2 * i + 1]) + slack
        first = jnp.int32(0)
        end = jnp.int32(SUBS)
        for j in range(SUBS):
            first = first + jnp.where(other_ref[SUBS + j] <= low, 1, 0)
            end = end - jnp.where(other_ref[j] >= high, 1, 0)
        if diag:
            start = 2 * i + DIAG_W // SUB - OFF_SUBS
        else:
            start = jnp.minimum(first, SUBS - OFF_SUBS)
        tab_ref[base + T_START + i] = start
        tab_ref[base + T_END + i] = end
        return extra + jnp.maximum(end - (start + OFF_SUBS), 0)

    extra = lax.fori_loop(0, STRIPS, one_strip, jnp.int32(0))
    tab_ref[base + T_LIVE] = flag
    tab_ref[base + T_EXTRA] = extra * flag


def kernel_values(col_ref, row_at, rows):
    width = rows[0].shape[1]
    squared = None
    for axis in range(3):
        mine = col_ref[axis, pl.ds(row_at, ROWS), :]
        diff = jnp.concatenate([mine] * (width // SUB), axis=1) - rows[axis]
        part = diff * diff
        squared = part if squared is None else squared + part
    squared = jnp.maximum(squared, 1e-30)
    q = squared * lax.rsqrt(squared)
    t = jnp.maximum(1.0 - q, 0.0)
    t2 = t * t
    return ((t2 * t2) * (q + 0.25)).astype(bf16)


def build_strip(store, col_ref, strip, side_ref, start, width, unroll=2):
    at = pl.ds(start, width)
    rows = [jnp.broadcast_to(side_ref[16 + axis : 17 + axis, at], (ROWS, width)) for axis in range(3)]

    def chunk(i, carry):
        row_at = pl.multiple_of(strip * STRIP + i * ROWS, ROWS)
        store(pl.multiple_of(i * ROWS, ROWS), kernel_values(col_ref, row_at, rows))
        return carry

    lax.fori_loop(0, STRIP // ROWS, chunk, 0, unroll=unroll)


def build_off(k_ref, tab_ref, base, col_ref, side_ref):
    part = OFF_W // 2
    for i in range(STRIPS):
        start = pl.multiple_of(tab_ref[base + T_START + i] * SUB, SUB)
        for h in range(2):

            def store(at, value, i=i, h=h):
                k_ref[i, pl.ds(at, ROWS), h * part : (h + 1) * part] = value

            build_strip(store, col_ref, i, side_ref, pl.multiple_of(start + h * part, SUB), part)


def build_diag(k_ref, col_ref, side_ref):
    for i in range(STRIPS):
        for h in range(min(DIAG_W, BLK - i * STRIP) // STRIP):

            def store(at, value, i=i, h=h):
                k_ref[i, pl.ds(at, ROWS), h * STRIP : (h + 1) * STRIP] = value

            build_strip(store, col_ref, i, side_ref, (i + h) * STRIP, STRIP, 4)


def to_owner(k_ref, tab_ref, base, v_col, acc_row):
    for i in range(STRIPS):
        start = pl.multiple_of(tab_ref[base + T_START + i] * SUB, SUB)
        acc_row[:, i * STRIP : (i + 1) * STRIP] += halves(nt(v_col[:, pl.ds(start, OFF_W)], k_ref[i]))


def to_partner(k_ref, tab_ref, base, v_row, acc_col):
    for i in range(STRIPS):
        start = pl.multiple_of(tab_ref[base + T_START + i] * SUB, SUB)
        acc_col[:, pl.ds(start, OFF_W)] += halves(nn(v_row[:, i * STRIP : (i + 1) * STRIP], k_ref[i]))


def diag_products(k_ref, v_ref, acc_ref):
    for i in range(STRIPS):
        width = min(DIAG_W, BLK - i * STRIP)
        here = slice(i * STRIP, (i + 1) * STRIP)
        acc_ref[:, here] += halves(nt(v_ref[:, i * STRIP : i * STRIP + width], k_ref[i, :, :width]))
        if width > STRIP:
            after = slice((i + 1) * STRIP, i * STRIP + width)
            acc_ref[:, after] += halves(nn(v_ref[:, here], k_ref[i, :, STRIP:width]))


def extra_tiles(tab_ref, base, col_ref, side_ref, tile_ref, v_row, v_col, acc_row, acc_col):
    @pl.when(tab_ref[base + T_EXTRA] > 0)
    def _():
        def strip(i, carry):
            here = pl.ds(pl.multiple_of(i * STRIP, STRIP), STRIP)

            def tile(j, carry):
                there = pl.ds(pl.multiple_of(j * SUB, SUB), SUB)

                def store(at, value):
                    tile_ref[pl.ds(at, ROWS), :] = value

                build_strip(store, col_ref, i, side_ref, pl.multiple_of(j * SUB, SUB), SUB)
                if acc_row is not None:
                    acc_row[:, here] += halves(nt(v_col[:, there], tile_ref[...]))
                if acc_col is not None:
                    acc_col[:, there] += halves(nn(v_row[:, here], tile_ref[...]))
                return carry

            return lax.fori_loop(
                tab_ref[base + T_START + i] + OFF_SUBS, tab_ref[base + T_END + i], tile, carry
            )

        lax.fori_loop(0, STRIPS, strip, 0)


TILE = pltpu.VMEM((STRIP, SUB), bf16)
SPLIT = pltpu.VMEM((2 * N_PROBES, BLK), bf16)
FIELD = (N_PROBES, BLK)


def call(body, outs, ins, out_specs, scratch, flops, name, limit=12):
    def run(*args):
        return pl.pallas_call(
            body,
            out_shape=outs,
            in_specs=ins,
            out_specs=out_specs,
            scratch_shapes=scratch,
            compiler_params=pltpu.CompilerParams(vmem_limit_bytes=limit * MIB),
            cost_estimate=pl.CostEstimate(flops=flops, bytes_accessed=MIB, transcendentals=0),
            name=name,
        )(*args)

    return run


def diag_build_kernel(flags, yb0, yb1, s0, s1, col0, col1, k00, k11, tab):
    fill_table(tab, 0 * T_SIZE, flags[0], yb0, yb0, True)
    fill_table(tab, 1 * T_SIZE, flags[1], yb0, yb1, False)
    fill_table(tab, 2 * T_SIZE, flags[2], yb1, yb1, True)

    @pl.when(flags[0] > 0)
    def _():
        build_diag(k00, col0, s0)

    @pl.when(flags[2] > 0)
    def _():
        build_diag(k11, col1, s1)


def halo_build_kernel(
    flags, yb1, s1, col1, got_a, got_b, k12, tab, acc1, back, halo, yb2, tile, v1, v2
):
    halo[...] = jnp.where(flags[4] == 0, got_a[...], got_b[...])
    bounds(halo, yb2)
    fill_table(tab, 0, flags[3], yb1, yb2, False)
    acc1[...] = jnp.zeros(FIELD, f32)
    back[...] = jnp.zeros(FIELD, f32)

    @pl.when(flags[3] > 0)
    def _():
        v1[...] = split2(s1[0:16, :])
        v2[...] = split2(halo[0:16, :])
        build_off(k12, tab, 0, col1, halo)
        to_partner(k12, tab, 0, v1, back)
        to_owner(k12, tab, 0, v2, acc1)
        extra_tiles(tab, 0, col1, halo, tile, v1, v2, acc1, back)


def local_products(tab, k00, k01, k11, s0, s1, col0, col1, tile, v0, v1, acc0, acc1):
    @pl.when(tab[0 * T_SIZE + T_LIVE] > 0)
    def _():
        diag_products(k00, v0, acc0)
        extra_tiles(tab, 0 * T_SIZE, col0, s0, tile, v0, v0, acc0, acc0)

    @pl.when(tab[1 * T_SIZE + T_LIVE] > 0)
    def _():
        to_owner(k01, tab, 1 * T_SIZE, v1, acc0)
        to_partner(k01, tab, 1 * T_SIZE, v0, acc1)
        extra_tiles(tab, 1 * T_SIZE, col0, s1, tile, v0, v1, acc0, acc1)

    @pl.when(tab[2 * T_SIZE + T_LIVE] > 0)
    def _():
        diag_products(k11, v1, acc1)
        extra_tiles(tab, 2 * T_SIZE, col1, s1, tile, v1, v1, acc1, acc1)


def own_build_kernel(tab, s0, s1, col0, col1, k00, k11, acc1_in, k01, acc0, acc1, tile, v0, v1):
    acc0[...] = jnp.zeros(FIELD, f32)
    acc1[...] = acc1_in[...]
    v0[...] = split2(s0[0:16, :])
    v1[...] = split2(s1[0:16, :])

    @pl.when(tab[1 * T_SIZE + T_LIVE] > 0)
    def _():
        build_off(k01, tab, 1 * T_SIZE, col0, s1)

    local_products(tab, k00, k01, k11, s0, s1, col0, col1, tile, v0, v1, acc0, acc1)


def own_apply_kernel(tab, k00, k01, k11, s0, s1, col0, col1, w0, w1, acc0, acc1, tile, v0, v1):
    acc0[...] = jnp.zeros(FIELD, f32)
    acc1[...] = jnp.zeros(FIELD, f32)
    v0[...] = split2(w0[0:16, :])
    v1[...] = split2(w1[0:16, :])
    local_products(tab, k00, k01, k11, s0, s1, col0, col1, tile, v0, v1, acc0, acc1)


def inner(left, right):
    product = left * right
    return jnp.sum(product, axis=1, keepdims=True)


def finish_kernel(
    level, flags, tab, k12, s0, s1, col1, halo, got_a, got_b, acc0, acc1, w0, w1, mom_in,
    n0, n1, send_a, send_b, mom, tile, v1, v2, acc, back
):
    live = tab[T_LIVE] > 0
    acc[...] = acc1[...]
    if level > 1:

        @pl.when(live)
        def _():
            v2[...] = split2(jnp.where(flags[4] == 0, got_a[...], got_b[...]))
            to_owner(k12, tab, 0, v2, acc)
            extra_tiles(tab, 0, col1, halo, tile, None, v2, acc, None)

    before0 = w0[0:16, :]
    before1 = w1[0:16, :]
    next1 = s1[19:20, :] * before1 + acc[...]
    n1[...] = next1
    back[...] = jnp.zeros(FIELD, f32)

    @pl.when(live)
    def _():
        v1[...] = split2(next1)
        to_partner(k12, tab, 0, v1, back)
        extra_tiles(tab, 0, col1, halo, tile, v1, None, None, back)

    arrived = jnp.where(flags[4] == 0, got_b[...], got_a[...])
    next0 = s0[19:20, :] * before0 + (acc0[...] + arrived)
    n0[...] = next0
    send_a[...] = jnp.where(flags[4] == 0, back[...], next0)
    send_b[...] = jnp.where(flags[4] == 0, next0, back[...])
    lane = lax.broadcasted_iota(jnp.int32, (N_PROBES, SUB), 1)
    cross = inner(before0, next0) + inner(before1, next1)
    own = inner(next0, next0) + inner(next1, next1)
    total = jnp.where(lane == 2 * level - 1, cross, jnp.where(lane == 2 * level, own, 0.0))
    if level == 1:
        total = jnp.where(lane == 0, inner(before0, before0) + inner(before1, before1), total)
    else:
        total = total + mom_in[...]
    mom[...] = total


def moment_kernel(flags, s0, s1, acc0, acc1, got_a, got_b, w0, w1, mom_in, mom):
    lane = lax.broadcasted_iota(jnp.int32, (N_PROBES, SUB), 1)
    one = w0[...]
    two = w1[...]
    arrived = jnp.where(flags[4] == 0, got_b[...], got_a[...])
    cross = inner(one, s0[19:20, :] * one + (acc0[...] + 2.0 * arrived))
    cross = cross + inner(two, s1[19:20, :] * two + acc1[...])
    mom[...] = mom_in[...] + jnp.where(lane == 5, cross, 0.0)


def last_kernel(flags, tab, k12, s0, s1, col1, halo, got_a, got_b, acc0, acc1, w0, w1, n0, n1, tile, v2):
    arrived = jnp.where(flags[4] == 0, got_b[...], got_a[...])
    n1[...] = s1[19:20, :] * w1[...] + acc1[...]
    n0[...] = s0[19:20, :] * w0[...] + (acc0[...] + arrived)

    @pl.when(tab[T_LIVE] > 0)
    def _():
        v2[...] = split2(jnp.where(flags[4] == 0, got_a[...], got_b[...]))
        to_owner(k12, tab, 0, v2, n1)
        extra_tiles(tab, 0, col1, halo, tile, None, v2, n1, None)


def unsort_kernel(rank_ref, wa, wb, wc, out, perm_ref):
    stacked = jnp.concatenate([split2(wa[...]), split2(wb[...]), split2(wc[...])], axis=0)
    rank = rank_ref[...]
    place = places()
    marked = [marks(rank, g) for g in range(STRIPS)]
    for c in range(BLK // STRIP):
        here = slice(c * STRIP, (c + 1) * STRIP)
        for g in range(STRIPS):
            for h in range(2):
                perm_ref[c % 2, g * STRIP : (g + 1) * STRIP, h * SUB : (h + 1) * SUB] = one_hot(
                    marked[g], g, 2 * c + h, place
                )
        got = nn(stacked, perm_ref[c % 2])
        for k in range(3):
            out[16 * k : 16 * (k + 1), here] = halves(got[32 * k : 32 * (k + 1)])


def combine_kernel(mom, probes, u0, u1, sol, res):
    lane = lax.broadcasted_iota(jnp.int32, (N_PROBES, SUB), 1)
    mu = [jnp.sum(jnp.where(lane == k, mom[...], 0.0), axis=1, keepdims=True) for k in range(6)]

    def form(left, right, shift):
        total = None
        for i, a in enumerate(left):
            for j, b in enumerate(right):
                part = (a * b) * mu[i + j + shift]
                total = part if total is None else total + part
        return total

    one = jnp.ones((N_PROBES, 1), f32)
    d = [one]
    r = [one]
    s = []
    rr = mu[0]
    for it in range(3):
        step = rr / form(d, d, 1)
        moved = [step * v for v in d]
        s = [a + b for a, b in zip(s + [0.0] * (len(d) - len(s)), moved)]
        r = [r[0]] + [(r[i] if i < len(r) else 0.0) - moved[i - 1] for i in range(1, len(moved) + 1)]
        if it < 2:
            new = form(r, r, 0)
            ratio = new / rr
            d = [r[i] + (ratio * d[i] if i < len(d) else 0.0) for i in range(len(r))]
            rr = new
    for b, u in ((0, u0), (1, u1)):
        here = slice(b * BLK, (b + 1) * BLK)
        w = [probes[:, here], u[0:16, :], u[16:32, :], u[32:48, :]]
        sol[:, here] = (s[0] * w[0] + s[1] * w[1]) + s[2] * w[2]
        res[:, here] = ((r[0] * w[0] + r[1] * w[1]) + r[2] * w[2]) + r[3] * w[3]


def swapped_both(to_a, to_b):
    count = lax.axis_size("gx")
    a = lax.ppermute(to_a, "gx", [(k, k ^ 1) for k in range(count)])
    b = lax.ppermute(to_b, "gx", [(k, ((k + 1) ^ 1) - 1) for k in range(1, count - 1)])
    return a, b


def sum_over(value, axis):
    count = lax.axis_size(axis)
    if count & (count - 1):
        return lax.psum(value, axis)
    step = 1
    while step < count:
        radix = min(16, count // step)
        parts = [value] + [
            lax.ppermute(value, axis, [(k, k ^ (m * step)) for k in range(count)]) for m in range(1, radix)
        ]
        while len(parts) > 1:
            parts = [parts[m] + parts[m + 1] for m in range(0, len(parts), 2)]
        value = parts[0]
        step *= radix
    return value


def on_device(points, noise_var, probes, pair_list, counts):
    noise = noise_var.reshape(1, -1)
    field = pltpu.VMEM(FIELD, f32)
    side = pltpu.VMEM((24, BLK), f32)
    column = pltpu.VMEM((3, BLK, SUB), f32)
    limits = jax.ShapeDtypeStruct((2 * SUBS,), f32)
    ranks = pltpu.VMEM((1, BLK), jnp.int32)
    any_space = pl.BlockSpec(memory_space=pl.ANY)
    s0, s1, col0, col1, yb0, yb1, rank0, rank1, flags = call(
        sort_kernel,
        (side, side, column, column, limits, limits, ranks, ranks, jax.ShapeDtypeStruct((5,), jnp.int32)),
        [any_space] * 3 + [SMEM] * 2,
        (VMEM,) * 4 + (SMEM,) * 2 + (VMEM,) * 2 + (SMEM,),
        [
            pltpu.VMEM(points.shape, f32),
            pltpu.VMEM(noise.shape, f32),
            pltpu.VMEM(probes.shape, f32),
            pltpu.VMEM((BLK, SUB), jnp.int32),
            pltpu.VMEM((2, STRIP, BLK), bf16),
            pltpu.SemaphoreType.DMA((3,)),
        ],
        10**9,
        "sort_blocks",
    )(points, noise, probes, pair_list, counts)

    halos = swapped_both(s0, s0)
    off = pltpu.VMEM((STRIPS, STRIP, OFF_W), bf16)
    diag = pltpu.VMEM((STRIPS, STRIP, DIAG_W), bf16)
    k00, k11, tabb = call(
        diag_build_kernel,
        (diag, diag, jax.ShapeDtypeStruct((3 * T_SIZE,), jnp.int32)),
        [SMEM] * 3 + [VMEM] * 4,
        (VMEM, VMEM, SMEM),
        [],
        3 * 10**9,
        "diag_build",
    )(flags, yb0, yb1, s0, s1, col0, col1)
    k12, tabc, acc1, back, halo = call(
        halo_build_kernel,
        (off, jax.ShapeDtypeStruct((T_SIZE,), jnp.int32), field, field, side),
        [SMEM] * 2 + [VMEM] * 4,
        (VMEM, SMEM, VMEM, VMEM, VMEM),
        [pltpu.SMEM((2 * SUBS,), f32), TILE, SPLIT, SPLIT],
        3 * 10**9,
        "halo_build",
    )(flags, yb1, s1, col1, *halos)
    got = swapped_both(back, back)
    k01, acc0, acc1 = call(
        own_build_kernel,
        (off, field, field),
        [SMEM] + [VMEM] * 7,
        (VMEM,) * 3,
        [TILE, SPLIT, SPLIT],
        5 * 10**9,
        "own_build",
    )(tabb, s0, s1, col0, col1, k00, k11, acc1)

    w0, w1 = s0, s1
    moments = pltpu.VMEM((N_PROBES, SUB), f32)
    mom = jnp.zeros((N_PROBES, SUB), f32)
    kept = []
    for level in (1, 2):
        w0, w1, send_a, send_b, mom = call(
            functools.partial(finish_kernel, level),
            (field,) * 4 + (moments,),
            [SMEM] * 2 + [VMEM] * 12,
            (VMEM,) * 5,
            [TILE, SPLIT, SPLIT, pltpu.VMEM(FIELD, f32), pltpu.VMEM(FIELD, f32)],
            10**9,
            "finish",
        )(flags, tabc, k12, s0, s1, col1, halo, *got, acc0, acc1, w0, w1, mom)
        kept.append((w0, w1))
        got = swapped_both(send_a, send_b)
        acc0, acc1 = call(
            own_apply_kernel,
            (field, field),
            [SMEM] + [VMEM] * 9,
            (VMEM, VMEM),
            [TILE, SPLIT, SPLIT],
            2 * 10**9,
            "own_apply",
        )(tabb, k00, k01, k11, s0, s1, col0, col1, w0, w1)
    mom = call(moment_kernel, moments, [SMEM] + [VMEM] * 9, VMEM, [], 10**7, "moment")(
        flags, s0, s1, acc0, acc1, *got, w0, w1, mom
    )
    total = sum_over(mom, "gx")
    kept.append(
        call(last_kernel, (field, field), [SMEM] * 2 + [VMEM] * 11, (VMEM, VMEM), [TILE, SPLIT], 10**9, "last")(
            flags, tabc, k12, s0, s1, col1, halo, *got, acc0, acc1, w0, w1
        )
    )
    given = []
    for b, rank in ((0, rank0), (1, rank1)):
        given.append(
            call(
                unsort_kernel,
                pltpu.VMEM((3 * N_PROBES, BLK), f32),
                [VMEM] * 4,
                VMEM,
                [pltpu.VMEM((2, BLK, STRIP), bf16)],
                2 * 96 * BLK * BLK,
                "unsort",
            )(rank, *[pair[b] for pair in kept])
        )
    return call(
        combine_kernel,
        (jax.ShapeDtypeStruct(probes.shape, f32),) * 2,
        [VMEM] * 4,
        (VMEM, VMEM),
        [],
        10**6,
        "combine",
    )(total, probes, *given)


def solution(mesh):
    placed = (
        P(None, ("groups", "gx")),
        P(("groups", "gx")),
        P(None, ("groups", "gx")),
        P(("groups", "gx"), None),
        P(("groups", "gx")),
    )
    return jax.shard_map(
        on_device,
        mesh=mesh,
        in_specs=placed,
        out_specs=(P(None, ("groups", "gx")), P(None, ("groups", "gx"))),
        check_vma=False,
    )
```

```python
import functools

import jax
import jax.numpy as jnp
from jax import lax
from jax.experimental import pallas as pl
from jax.experimental.pallas import tpu as pltpu
from jax.sharding import PartitionSpec as P

BLK = 2048
STRIP = 256
STRIPS = BLK // STRIP
SUB = 128
SUBS = BLK // SUB
OFF_W = 768
OFF_SUBS = OFF_W // SUB
DIAG_W = 512
N_PROBES = 16
N_FEATURES = 64
MIB = 1 << 20

VMEM = pl.BlockSpec(memory_space=pltpu.VMEM)
SMEM = pl.BlockSpec(memory_space=pltpu.SMEM)

f32 = jnp.float32
bf16 = jnp.bfloat16

T_LIVE, T_EXTRA, T_START, T_END = 0, 1, 8, 16
T_SIZE = 24


def nt(left, right):
    return lax.dot_general(left, right, (((1,), (1,)), ((), ())), preferred_element_type=f32)


def nn(left, right):
    return jnp.dot(left, right, preferred_element_type=f32)


def split2(value):
    high = value.astype(bf16)
    low = (value - high.astype(f32)).astype(bf16)
    return jnp.concatenate([high, low], axis=0)


def halves(value):
    n = value.shape[0] // 2
    return value[:n] + value[n:]


def split3(value):
    high = value.astype(bf16).astype(f32)
    rest = value - high
    mid = rest.astype(bf16).astype(f32)
    return high, mid, rest - mid


def one_hot(marked, c, place):
    parts = []
    for h in range(2):
        at = c * STRIP + h * SUB
        hit = jnp.broadcast_to(marked[:, at : at + SUB], (STRIP, SUB)) == place
        parts.append(jnp.where(hit, jnp.ones((STRIP, SUB), bf16), jnp.zeros((STRIP, SUB), bf16)))
    return jnp.concatenate(parts, axis=1)


def places():
    return lax.broadcasted_iota(jnp.int32, (STRIP, SUB), 0).astype(f32).astype(bf16)


def marks(rank, g):
    group = lax.shift_right_logical(rank, 8)
    within = jnp.bitwise_and(rank, STRIP - 1)
    return jnp.where(group == g, within, -1).astype(f32).astype(bf16)


def rank_of(y_row, key_ref):
    lane = lax.broadcasted_iota(jnp.int32, (1, BLK), 1)
    key_row = (y_row * 4096.0).astype(jnp.int32) * BLK + lane
    for c in range(SUBS):
        piece = jnp.broadcast_to(y_row[:, c * SUB : (c + 1) * SUB], (SUB, SUB)).T
        sub = lax.broadcasted_iota(jnp.int32, (SUB, SUB), 0) + c * SUB
        key_ref[c * SUB : (c + 1) * SUB, :] = (piece * 4096.0).astype(jnp.int32) * BLK + sub
    keys = jnp.broadcast_to(key_row, (8, BLK))

    def count(i, acc):
        mine = key_ref[pl.ds(pl.multiple_of(i * 8, 8), 8), :]
        mine = jnp.concatenate([mine] * SUBS, axis=1)
        return acc + jnp.where(mine < keys, 1, 0)

    acc = lax.fori_loop(0, BLK // 8, count, jnp.zeros((8, BLK), jnp.int32), unroll=8)
    return jnp.sum(acc, axis=0, keepdims=True)


def row_id(width):
    return lax.broadcasted_iota(jnp.int32, (8, width), 0)


def features(offset, left):
    first, second, third = split3(offset)
    norm = jnp.sum(offset * offset, axis=0, keepdims=True)
    n1, n2, n3 = split3(norm)
    ids = row_id(offset.shape[1])
    own, other = (0, 3) if left else (3, 0)
    norms = jnp.where(ids == own, n1, jnp.where(ids == own + 1, n2, jnp.where(ids == own + 2, n3, 0.0)))
    norms = jnp.where((ids >= other) & (ids < other + 3), 1.0, norms)
    if left:
        first, second, third = -2.0 * first, -2.0 * second, -2.0 * third
        parts = [first, first, first, second, second, third]
    else:
        parts = [first, second, third, first, second, first]
    return jnp.concatenate(parts + [norms, jnp.zeros_like(norms)], axis=0), norm


def sort_kernel(
    pts_hbm, nv_hbm, pr_hbm, pair_hbm, count, s0, s1, lhs0, lhs1, yb0, yb1, rank0, rank1, flags,
    pts_ref, nv_ref, pr_ref, pair, key_ref, sems
):
    copies = [
        pltpu.make_async_copy(src, dst, sems.at[k])
        for k, (src, dst) in enumerate(
            ((pts_hbm, pts_ref), (nv_hbm, nv_ref), (pr_hbm, pr_ref), (pair_hbm, pair))
        )
    ]
    for copy in copies:
        copy.start()
    copies[0].wait()
    for blk, rank_ref in enumerate((rank0, rank1)):
        rank_ref[...] = rank_of(pts_ref[1:2, blk * BLK : (blk + 1) * BLK], key_ref)
    for copy in copies[1:]:
        copy.wait()
    for local in range(2):
        for ahead in range(2):
            flags[2 * local + ahead] = live_flag(pair, count, local, ahead)
    flags[4] = jnp.bitwise_and(lax.shift_right_logical(pair[0, 0], 1), 1)
    place = places()
    for blk, (out_ref, lhs_ref, rank_ref) in enumerate(((s0, lhs0, rank0), (s1, lhs1, rank1))):
        cols = slice(blk * BLK, (blk + 1) * BLK)
        aux = jnp.concatenate(
            [pts_ref[0:3, cols] * 2.0, nv_ref[:, cols], jnp.zeros((4, BLK), f32)], axis=0
        )
        data = jnp.concatenate(
            [*split3(pr_ref[:, cols]), *split3(aux), jnp.zeros((8, BLK), f32)], axis=0
        ).astype(bf16)
        rank = rank_ref[...]
        centre = 0.5 * (jnp.min(aux, axis=1, keepdims=True) + jnp.max(aux, axis=1, keepdims=True))
        centre = jnp.concatenate([jnp.zeros((4, 1), f32), centre[0:3], jnp.zeros((1, 1), f32)], axis=0)
        for g in range(STRIPS):
            marked = marks(rank, g)
            got = None
            for c in range(STRIPS):
                part = nt(data[:, c * STRIP : (c + 1) * STRIP], one_hot(marked, c, place))
                got = part if got is None else got + part
            here = slice(g * STRIP, (g + 1) * STRIP)
            out_ref[0:16, here] = (got[0:16] + got[16:32]) + got[32:48]
            out_ref[16:24, here] = ((got[48:56] + got[56:64]) + got[64:72]) + centre
        offset = offset_of(out_ref, out_ref)
        rows, _ = features(offset, True)
        for c in range(SUBS):
            here = slice(c * SUB, (c + 1) * SUB)
            lhs_ref[here, :] = rows[:, here].T.astype(bf16)
    bounds(s0, yb0)
    bounds(s1, yb1)


def offset_of(side_ref, centre_ref):
    centre = jnp.concatenate([centre_ref[20:23, 0:1], jnp.zeros((5, 1), f32)], axis=0)
    return jnp.where(row_id(BLK) < 3, side_ref[16:24, :] - centre, 0.0)


def bounds(side_ref, yb_ref):
    for c in range(SUBS):
        row = side_ref[17:18, c * SUB : (c + 1) * SUB]
        yb_ref[c] = jnp.min(row)
        yb_ref[SUBS + c] = jnp.max(row)


def live_flag(pair_ref, count_ref, local, ahead):
    flag = jnp.int32(0)
    for s in range(pair_ref.shape[1]):
        owner = pair_ref[0, s]
        match = (
            (jnp.int32(s) < count_ref[0])
            & (jnp.bitwise_and(owner, 1) == local)
            & (pair_ref[1, s] - owner == ahead)
        )
        flag = jnp.where(match, jnp.int32(1), flag)
    return flag


def fill_table(tab_ref, base, flag, own_ref, other_ref, diag):
    slack = 1.0 + 1.0 / 1024.0

    def one_strip(i, extra):
        low = jnp.minimum(own_ref[2 * i], own_ref[2 * i + 1]) - slack
        high = jnp.maximum(own_ref[SUBS + 2 * i], own_ref[SUBS + 2 * i + 1]) + slack
        first = jnp.int32(0)
        end = jnp.int32(SUBS)
        for j in range(SUBS):
            first = first + jnp.where(other_ref[SUBS + j] <= low, 1, 0)
            end = end - jnp.where(other_ref[j] >= high, 1, 0)
        if diag:
            start = 2 * i + DIAG_W // SUB - OFF_SUBS
        else:
            start = jnp.minimum(first, SUBS - OFF_SUBS)
        tab_ref[base + T_START + i] = start
        tab_ref[base + T_END + i] = end
        return extra + jnp.maximum(end - (start + OFF_SUBS), 0)

    extra = lax.fori_loop(0, STRIPS, one_strip, jnp.int32(0))
    tab_ref[base + T_LIVE] = flag
    tab_ref[base + T_EXTRA] = extra * flag


def kernel_values(squared):
    squared = jnp.maximum(squared, 1e-30)
    t = jnp.maximum(1.0 - squared * lax.rsqrt(squared), 0.0)
    t2 = t * t
    return ((t2 * t2) * (1.25 - t)).astype(bf16)


def tile_by_difference(row_side, row_at, col_side, col_at):
    squared = None
    for axis in range(16, 19):
        mine = jnp.broadcast_to(row_side[axis : axis + 1, pl.ds(row_at, SUB)], (SUB, SUB)).T
        diff = mine - col_side[axis : axis + 1, pl.ds(col_at, SUB)]
        part = diff * diff
        squared = part if squared is None else squared + part
    return kernel_values(squared)


def fast_strip(k_ref, i, lhs, rhs, start, width):
    for h in range(width // STRIP):
        right = rhs[:, pl.ds(start + h * STRIP, STRIP)]
        for g in range(STRIP // SUB):
            rows = slice(i * STRIP + g * SUB, i * STRIP + (g + 1) * SUB)
            k_ref[i, g * SUB : (g + 1) * SUB, h * STRIP : (h + 1) * STRIP] = kernel_values(nn(lhs[rows, :], right))


def slow_build(k_ref, row_side, col_side, first_group, groups):
    def strip(i, carry):
        def tile(j, carry):
            for g in range(STRIP // SUB):
                at = pl.multiple_of(i * STRIP + g * SUB, SUB)
                col_at = pl.multiple_of(jnp.minimum(first_group(i) + j, SUBS - 1) * SUB, SUB)
                k_ref[i, g * SUB : (g + 1) * SUB, pl.ds(pl.multiple_of(j * SUB, SUB), SUB)] = (
                    tile_by_difference(row_side, at, col_side, col_at)
                )
            return carry

        return lax.fori_loop(0, groups, tile, carry)

    lax.fori_loop(0, STRIPS, strip, 0)


def right_features(rhs, row_side, col_side):
    offset = offset_of(col_side, row_side)
    rows, norm = features(offset, False)
    rhs[...] = rows.astype(bf16)
    offset = offset_of(row_side, row_side)
    return jnp.maximum(jnp.max(norm), jnp.max(jnp.sum(offset * offset, axis=0, keepdims=True))) <= 100.0


def off_pair(k_ref, tab_ref, base, lhs, rhs, row_side, col_side, v_row, v_col, acc_row, acc_col):
    near = right_features(rhs, row_side, col_side)

    @pl.when(near)
    def _():
        for i in range(STRIPS):
            start = pl.multiple_of(tab_ref[base + T_START + i] * SUB, SUB)
            fast_strip(k_ref, i, lhs, rhs, start, OFF_W)
            owner_strip(k_ref, i, start, v_col, acc_row)
            partner_strip(k_ref, i, start, v_row, acc_col)

    @pl.when(jnp.logical_not(near))
    def _():
        slow_build(k_ref, row_side, col_side, lambda i: tab_ref[base + T_START + i], OFF_SUBS)
        to_owner(k_ref, tab_ref, base, v_col, acc_row)
        to_partner(k_ref, tab_ref, base, v_row, acc_col)


def diag_pair(k_ref, lhs, rhs, side, v, acc):
    near = right_features(rhs, side, side)

    @pl.when(near)
    def _():
        for i in range(STRIPS):
            fast_strip(k_ref, i, lhs, rhs, i * STRIP, min(DIAG_W, BLK - i * STRIP))
            diag_strip(k_ref, i, v, acc)

    @pl.when(jnp.logical_not(near))
    def _():
        slow_build(k_ref, side, side, lambda i: 2 * i, DIAG_W // SUB)
        diag_products(k_ref, v, acc)


def owner_strip(k_ref, i, start, v_col, acc_row):
    acc_row[:, i * STRIP : (i + 1) * STRIP] += halves(nt(v_col[:, pl.ds(start, OFF_W)], k_ref[i]))


def partner_strip(k_ref, i, start, v_row, acc_col):
    acc_col[:, pl.ds(start, OFF_W)] += halves(nn(v_row[:, i * STRIP : (i + 1) * STRIP], k_ref[i]))


def to_owner(k_ref, tab_ref, base, v_col, acc_row):
    for i in range(STRIPS):
        owner_strip(k_ref, i, pl.multiple_of(tab_ref[base + T_START + i] * SUB, SUB), v_col, acc_row)


def to_partner(k_ref, tab_ref, base, v_row, acc_col):
    for i in range(STRIPS):
        partner_strip(k_ref, i, pl.multiple_of(tab_ref[base + T_START + i] * SUB, SUB), v_row, acc_col)


def diag_strip(k_ref, i, v_ref, acc_ref):
    width = min(DIAG_W, BLK - i * STRIP)
    here = slice(i * STRIP, (i + 1) * STRIP)
    acc_ref[:, here] += halves(nt(v_ref[:, i * STRIP : i * STRIP + width], k_ref[i, :, :width]))
    if width > STRIP:
        after = slice((i + 1) * STRIP, i * STRIP + width)
        acc_ref[:, after] += halves(nn(v_ref[:, here], k_ref[i, :, STRIP:width]))


def diag_products(k_ref, v_ref, acc_ref):
    for i in range(STRIPS):
        diag_strip(k_ref, i, v_ref, acc_ref)


def extra_tiles(tab_ref, base, row_side, col_side, tile_ref, v_row, v_col, acc_row, acc_col):
    @pl.when(tab_ref[base + T_EXTRA] > 0)
    def _():
        def strip(i, carry):
            here = pl.ds(pl.multiple_of(i * STRIP, STRIP), STRIP)

            def tile(j, carry):
                col_at = pl.multiple_of(j * SUB, SUB)
                there = pl.ds(col_at, SUB)
                for g in range(STRIP // SUB):
                    row_at = pl.multiple_of(i * STRIP + g * SUB, SUB)
                    tile_ref[g * SUB : (g + 1) * SUB, :] = tile_by_difference(row_side, row_at, col_side, col_at)
                if acc_row is not None:
                    acc_row[:, here] += halves(nt(v_col[:, there], tile_ref[...]))
                if acc_col is not None:
                    acc_col[:, there] += halves(nn(v_row[:, here], tile_ref[...]))
                return carry

            return lax.fori_loop(
                tab_ref[base + T_START + i] + OFF_SUBS, tab_ref[base + T_END + i], tile, carry
            )

        lax.fori_loop(0, STRIPS, strip, 0)


TILE = pltpu.VMEM((STRIP, SUB), bf16)
SPLIT = pltpu.VMEM((2 * N_PROBES, BLK), bf16)
FIELD = (N_PROBES, BLK)


def call(body, outs, ins, out_specs, scratch, flops, name, limit=12):
    def run(*args):
        return pl.pallas_call(
            body,
            out_shape=outs,
            in_specs=ins,
            out_specs=out_specs,
            scratch_shapes=scratch,
            compiler_params=pltpu.CompilerParams(vmem_limit_bytes=limit * MIB),
            cost_estimate=pl.CostEstimate(flops=flops, bytes_accessed=MIB, transcendentals=0),
            name=name,
        )(*args)

    return run


def diag_build_kernel(
    flags, yb0, yb1, s0, s1, lhs0, lhs1, k00, k11, tab, acc0, acc1, tile, v0, v1, rhs
):
    fill_table(tab, 0 * T_SIZE, flags[0], yb0, yb0, True)
    fill_table(tab, 1 * T_SIZE, flags[1], yb0, yb1, False)
    fill_table(tab, 2 * T_SIZE, flags[2], yb1, yb1, True)
    acc0[...] = jnp.zeros(FIELD, f32)
    acc1[...] = jnp.zeros(FIELD, f32)
    v0[...] = split2(s0[0:16, :])
    v1[...] = split2(s1[0:16, :])

    @pl.when(flags[0] > 0)
    def _():
        diag_pair(k00, lhs0, rhs, s0, v0, acc0)
        extra_tiles(tab, 0 * T_SIZE, s0, s0, tile, v0, v0, acc0, acc0)

    @pl.when(flags[2] > 0)
    def _():
        diag_pair(k11, lhs1, rhs, s1, v1, acc1)
        extra_tiles(tab, 2 * T_SIZE, s1, s1, tile, v1, v1, acc1, acc1)


def halo_build_kernel(
    flags, yb1, s1, lhs1, got_a, got_b, acc1_in, k12, tab, acc1, back, halo, yb2, tile, v1, v2, rhs
):
    halo[...] = jnp.where(flags[4] == 0, got_a[...], got_b[...])
    bounds(halo, yb2)
    fill_table(tab, 0, flags[3], yb1, yb2, False)
    acc1[...] = acc1_in[...]
    back[...] = jnp.zeros(FIELD, f32)

    @pl.when(flags[3] > 0)
    def _():
        v1[...] = split2(s1[0:16, :])
        v2[...] = split2(halo[0:16, :])
        off_pair(k12, tab, 0, lhs1, rhs, s1, halo, v1, v2, acc1, back)
        extra_tiles(tab, 0, s1, halo, tile, v1, v2, acc1, back)


def own_build_kernel(tab, s0, s1, lhs0, acc0_in, acc1_in, k01, acc0, acc1, tile, v0, v1, rhs):
    base = 1 * T_SIZE
    acc0[...] = acc0_in[...]
    acc1[...] = acc1_in[...]

    @pl.when(tab[base + T_LIVE] > 0)
    def _():
        v0[...] = split2(s0[0:16, :])
        v1[...] = split2(s1[0:16, :])
        off_pair(k01, tab, base, lhs0, rhs, s0, s1, v0, v1, acc0, acc1)
        extra_tiles(tab, base, s0, s1, tile, v0, v1, acc0, acc1)


def own_apply_kernel(tab, k00, k01, k11, s0, s1, w0, w1, acc0, acc1, tile, v0, v1):
    acc0[...] = jnp.zeros(FIELD, f32)
    acc1[...] = jnp.zeros(FIELD, f32)
    v0[...] = split2(w0[...])
    v1[...] = split2(w1[...])

    @pl.when(tab[0 * T_SIZE + T_LIVE] > 0)
    def _():
        diag_products(k00, v0, acc0)
        extra_tiles(tab, 0 * T_SIZE, s0, s0, tile, v0, v0, acc0, acc0)

    @pl.when(tab[1 * T_SIZE + T_LIVE] > 0)
    def _():
        to_owner(k01, tab, 1 * T_SIZE, v1, acc0)
        to_partner(k01, tab, 1 * T_SIZE, v0, acc1)
        extra_tiles(tab, 1 * T_SIZE, s0, s1, tile, v0, v1, acc0, acc1)

    @pl.when(tab[2 * T_SIZE + T_LIVE] > 0)
    def _():
        diag_products(k11, v1, acc1)
        extra_tiles(tab, 2 * T_SIZE, s1, s1, tile, v1, v1, acc1, acc1)


def inner(left, right):
    product = left * right
    return jnp.sum(product, axis=1, keepdims=True)


def finish_kernel(
    level, flags, tab, k12, s0, s1, halo, got_a, got_b, acc0, acc1, w0, w1, mom_in,
    n0, n1, send_a, send_b, mom, tile, v1, v2, acc, back
):
    live = tab[T_LIVE] > 0
    acc[...] = acc1[...]
    if level > 1:

        @pl.when(live)
        def _():
            v2[...] = split2(jnp.where(flags[4] == 0, got_a[...], got_b[...]))
            to_owner(k12, tab, 0, v2, acc)
            extra_tiles(tab, 0, s1, halo, tile, None, v2, acc, None)

    before0 = w0[0:16, :]
    before1 = w1[0:16, :]
    next1 = s1[19:20, :] * before1 + acc[...]
    n1[...] = next1
    back[...] = jnp.zeros(FIELD, f32)

    @pl.when(live)
    def _():
        v1[...] = split2(next1)
        to_partner(k12, tab, 0, v1, back)
        extra_tiles(tab, 0, s1, halo, tile, v1, None, None, back)

    arrived = jnp.where(flags[4] == 0, got_b[...], got_a[...])
    next0 = s0[19:20, :] * before0 + (acc0[...] + arrived)
    n0[...] = next0
    send_a[...] = jnp.where(flags[4] == 0, back[...], next0)
    send_b[...] = jnp.where(flags[4] == 0, next0, back[...])
    lane = lax.broadcasted_iota(jnp.int32, (N_PROBES, SUB), 1)
    cross = inner(before0, next0) + inner(before1, next1)
    own = inner(next0, next0) + inner(next1, next1)
    total = jnp.where(lane == 2 * level - 1, cross, jnp.where(lane == 2 * level, own, 0.0))
    if level == 1:
        total = jnp.where(lane == 0, inner(before0, before0) + inner(before1, before1), total)
    else:
        total = total + mom_in[...]
    mom[...] = total


def moment_kernel(flags, s0, s1, acc0, acc1, got_a, got_b, w0, w1, mom_in, mom):
    lane = lax.broadcasted_iota(jnp.int32, (N_PROBES, SUB), 1)
    one = w0[...]
    two = w1[...]
    arrived = jnp.where(flags[4] == 0, got_b[...], got_a[...])
    cross = inner(one, s0[19:20, :] * one + (acc0[...] + 2.0 * arrived))
    cross = cross + inner(two, s1[19:20, :] * two + acc1[...])
    mom[...] = mom_in[...] + jnp.where(lane == 5, cross, 0.0)


def last_kernel(flags, tab, k12, s0, s1, halo, got_a, got_b, acc0, acc1, w0, w1, n0, n1, tile, v2):
    arrived = jnp.where(flags[4] == 0, got_b[...], got_a[...])
    n1[...] = s1[19:20, :] * w1[...] + acc1[...]
    n0[...] = s0[19:20, :] * w0[...] + (acc0[...] + arrived)

    @pl.when(tab[T_LIVE] > 0)
    def _():
        v2[...] = split2(jnp.where(flags[4] == 0, got_a[...], got_b[...]))
        to_owner(k12, tab, 0, v2, n1)
        extra_tiles(tab, 0, s1, halo, tile, None, v2, n1, None)


def unsort_kernel(rank_ref, wa, wb, wc, out):
    stacked = jnp.concatenate([split2(wa[...]), split2(wb[...]), split2(wc[...])], axis=0)
    rank = rank_ref[...]
    place = places()
    marked = [marks(rank, g) for g in range(STRIPS)]
    for c in range(STRIPS):
        here = slice(c * STRIP, (c + 1) * STRIP)
        got = None
        for g in range(STRIPS):
            part = nn(stacked[:, g * STRIP : (g + 1) * STRIP], one_hot(marked[g], c, place))
            got = part if got is None else got + part
        for k in range(3):
            out[16 * k : 16 * (k + 1), here] = halves(got[32 * k : 32 * (k + 1)])


def combine_kernel(mom, probes, u0, u1, sol, res):
    lane = lax.broadcasted_iota(jnp.int32, (N_PROBES, SUB), 1)
    mu = [jnp.sum(jnp.where(lane == k, mom[...], 0.0), axis=1, keepdims=True) for k in range(6)]

    def form(left, right, shift):
        total = None
        for i, a in enumerate(left):
            for j, b in enumerate(right):
                part = (a * b) * mu[i + j + shift]
                total = part if total is None else total + part
        return total

    one = jnp.ones((N_PROBES, 1), f32)
    d = [one]
    r = [one]
    s = []
    rr = mu[0]
    for it in range(3):
        step = rr / form(d, d, 1)
        moved = [step * v for v in d]
        s = [a + b for a, b in zip(s + [0.0] * (len(d) - len(s)), moved)]
        r = [r[0]] + [(r[i] if i < len(r) else 0.0) - moved[i - 1] for i in range(1, len(moved) + 1)]
        if it < 2:
            new = form(r, r, 0)
            ratio = new / rr
            d = [r[i] + (ratio * d[i] if i < len(d) else 0.0) for i in range(len(r))]
            rr = new
    for b, u in ((0, u0), (1, u1)):
        here = slice(b * BLK, (b + 1) * BLK)
        w = [probes[:, here], u[0:16, :], u[16:32, :], u[32:48, :]]
        sol[:, here] = (s[0] * w[0] + s[1] * w[1]) + s[2] * w[2]
        res[:, here] = ((r[0] * w[0] + r[1] * w[1]) + r[2] * w[2]) + r[3] * w[3]


def swapped_both(to_a, to_b):
    count = lax.axis_size("gx")
    a = lax.ppermute(to_a, "gx", [(k, k ^ 1) for k in range(count)])
    b = lax.ppermute(to_b, "gx", [(k, ((k + 1) ^ 1) - 1) for k in range(1, count - 1)])
    return a, b


def sum_over(value, axis):
    return jnp.sum(lax.all_gather(value, axis), axis=0)


def on_device(points, noise_var, probes, pair_list, counts):
    noise = noise_var.reshape(1, -1)
    field = pltpu.VMEM(FIELD, f32)
    side = pltpu.VMEM((24, BLK), f32)
    left = pltpu.VMEM((BLK, N_FEATURES), bf16)
    right = pltpu.VMEM((N_FEATURES, BLK), bf16)
    limits = jax.ShapeDtypeStruct((2 * SUBS,), f32)
    ranks = pltpu.VMEM((1, BLK), jnp.int32)
    far_space = pl.BlockSpec(memory_space=pltpu.HBM)
    s0, s1, lhs0, lhs1, yb0, yb1, rank0, rank1, flags = call(
        sort_kernel,
        (side, side, left, left, limits, limits, ranks, ranks, jax.ShapeDtypeStruct((5,), jnp.int32)),
        [far_space] * 4 + [SMEM],
        (VMEM,) * 4 + (SMEM,) * 2 + (VMEM,) * 2 + (SMEM,),
        [
            pltpu.VMEM(points.shape, f32),
            pltpu.VMEM(noise.shape, f32),
            pltpu.VMEM(probes.shape, f32),
            pltpu.SMEM(pair_list.shape[::-1], jnp.int32),
            pltpu.VMEM((BLK, SUB), jnp.int32),
            pltpu.SemaphoreType.DMA((4,)),
        ],
        10**9,
        "sort_blocks",
    )(*[pltpu.with_memory_space_constraint(x, pltpu.HBM) for x in (points, noise, probes, pair_list.T)], counts)

    halos = swapped_both(s0, s0)
    off = pltpu.VMEM((STRIPS, STRIP, OFF_W), bf16)
    diag = pltpu.VMEM((STRIPS, STRIP, DIAG_W), bf16)
    k00, k11, tabb, acc0, acc1 = call(
        diag_build_kernel,
        (diag, diag, jax.ShapeDtypeStruct((3 * T_SIZE,), jnp.int32), field, field),
        [SMEM] * 3 + [VMEM] * 4,
        (VMEM, VMEM, SMEM, VMEM, VMEM),
        [TILE, SPLIT, SPLIT, right],
        3 * 10**9,
        "diag_build",
    )(flags, yb0, yb1, s0, s1, lhs0, lhs1)
    k12, tabc, acc1, back, halo = call(
        halo_build_kernel,
        (off, jax.ShapeDtypeStruct((T_SIZE,), jnp.int32), field, field, side),
        [SMEM] * 2 + [VMEM] * 5,
        (VMEM, SMEM, VMEM, VMEM, VMEM),
        [pltpu.SMEM((2 * SUBS,), f32), TILE, SPLIT, SPLIT, right],
        3 * 10**9,
        "halo_build",
    )(flags, yb1, s1, lhs1, *halos, acc1)
    got = swapped_both(back, back)
    k01, acc0, acc1 = call(
        own_build_kernel,
        (off, field, field),
        [SMEM] + [VMEM] * 5,
        (VMEM,) * 3,
        [TILE, SPLIT, SPLIT, right],
        5 * 10**9,
        "own_build",
    )(tabb, s0, s1, lhs0, acc0, acc1)

    w0, w1 = s0, s1
    moments = pltpu.VMEM((N_PROBES, SUB), f32)
    mom = jnp.zeros((N_PROBES, SUB), f32)
    kept = []
    for level in (1, 2):
        w0, w1, send_a, send_b, mom = call(
            functools.partial(finish_kernel, level),
            (field,) * 4 + (moments,),
            [SMEM] * 2 + [VMEM] * 11,
            (VMEM,) * 5,
            [TILE, SPLIT, SPLIT, pltpu.VMEM(FIELD, f32), pltpu.VMEM(FIELD, f32)],
            10**9,
            "finish",
        )(flags, tabc, k12, s0, s1, halo, *got, acc0, acc1, w0, w1, mom)
        kept.append((w0, w1))
        got = swapped_both(send_a, send_b)
        acc0, acc1 = call(
            own_apply_kernel,
            (field, field),
            [SMEM] + [VMEM] * 7,
            (VMEM, VMEM),
            [TILE, SPLIT, SPLIT],
            2 * 10**9,
            "own_apply",
        )(tabb, k00, k01, k11, s0, s1, w0, w1)
    mom = call(moment_kernel, moments, [SMEM] + [VMEM] * 9, VMEM, [], 10**7, "moment")(
        flags, s0, s1, acc0, acc1, *got, w0, w1, mom
    )
    total = sum_over(mom, "gx")
    kept.append(
        call(last_kernel, (field, field), [SMEM] * 2 + [VMEM] * 10, (VMEM, VMEM), [TILE, SPLIT], 10**9, "last")(
            flags, tabc, k12, s0, s1, halo, *got, acc0, acc1, w0, w1
        )
    )
    given = []
    for b, rank in ((0, rank0), (1, rank1)):
        given.append(
            call(
                unsort_kernel,
                pltpu.VMEM((3 * N_PROBES, BLK), f32),
                [VMEM] * 4,
                VMEM,
                [],
                2 * 96 * BLK * BLK,
                "unsort",
            )(rank, *[pair[b] for pair in kept])
        )
    return call(
        combine_kernel,
        (jax.ShapeDtypeStruct(probes.shape, f32),) * 2,
        [VMEM] * 4,
        (VMEM, VMEM),
        [],
        10**6,
        "combine",
    )(total, probes, *given)


def solution(mesh):
    placed = (
        P(None, ("groups", "gx")),
        P(("groups", "gx")),
        P(None, ("groups", "gx")),
        P(("groups", "gx"), None),
        P(("groups", "gx")),
    )
    return jax.shard_map(
        on_device,
        mesh=mesh,
        in_specs=placed,
        out_specs=(P(None, ("groups", "gx")), P(None, ("groups", "gx"))),
        check_vma=False,
    )
```

```python
import functools

import jax
import jax.numpy as jnp
from jax import lax
from jax.experimental import pallas as pl
from jax.experimental.pallas import tpu as pltpu
from jax.sharding import PartitionSpec as P

BLK = 2048
STRIP = 256
STRIPS = BLK // STRIP
SUB = 128
SUBS = BLK // SUB
OFF_W = 768
OFF_SUBS = OFF_W // SUB
DIAG_W = 512
N_PROBES = 16
N_FEATURES = 64
MIB = 1 << 20

VMEM = pl.BlockSpec(memory_space=pltpu.VMEM)
SMEM = pl.BlockSpec(memory_space=pltpu.SMEM)

f32 = jnp.float32
bf16 = jnp.bfloat16

T_START, T_END, T_EXTRA, T_LIVE = 0, 1, 2, 3


def nt(left, right):
    return lax.dot_general(left, right, (((1,), (1,)), ((), ())), preferred_element_type=f32)


def nn(left, right):
    return jnp.dot(left, right, preferred_element_type=f32)


def split2(value):
    high = value.astype(bf16)
    low = (value - high.astype(f32)).astype(bf16)
    return jnp.concatenate([high, low], axis=0)


def halves(value):
    n = value.shape[0] // 2
    return value[:n] + value[n:]


def split3(value):
    high = value.astype(bf16).astype(f32)
    rest = value - high
    mid = rest.astype(bf16).astype(f32)
    return high, mid, rest - mid


def one_hot(marked, c, place):
    parts = []
    for h in range(2):
        at = c * STRIP + h * SUB
        hit = jnp.broadcast_to(marked[:, at : at + SUB], (STRIP, SUB)) == place
        parts.append(jnp.where(hit, jnp.ones((STRIP, SUB), bf16), jnp.zeros((STRIP, SUB), bf16)))
    return jnp.concatenate(parts, axis=1)


def places():
    return lax.broadcasted_iota(jnp.int32, (STRIP, SUB), 0).astype(f32).astype(bf16)


def marks(rank, g):
    group = lax.shift_right_logical(rank, 8)
    within = jnp.bitwise_and(rank, STRIP - 1)
    return jnp.where(group == g, within, -1).astype(f32).astype(bf16)


def rank_of(y_row, key_ref):
    low = jnp.min(y_row, axis=1, keepdims=True)
    high = jnp.max(y_row, axis=1, keepdims=True)
    scale = 255.0 / jnp.maximum(high - low, 1e-6)
    key = jnp.clip(jnp.floor((y_row - low) * scale), 0.0, 255.0)
    for c in range(SUBS):
        here = slice(c * SUB, (c + 1) * SUB)
        key_ref[here, :] = jnp.broadcast_to(key[:, here], (SUB, SUB)).T.astype(bf16)
    strict = key.astype(bf16)
    loose = (key + 1.0).astype(bf16)
    ones = jnp.ones((16, STRIP), bf16)
    one = jnp.ones((STRIP, SUB), bf16)
    zero = jnp.zeros((STRIP, SUB), bf16)
    ranks = []
    for j in range(STRIPS):
        total = None
        for i in range(STRIPS):
            mine = key_ref[i * STRIP : (i + 1) * STRIP, :]
            parts = []
            for h in range(2):
                there = slice(j * STRIP + h * SUB, j * STRIP + (h + 1) * SUB)
                if i == j:
                    sub = lax.broadcasted_iota(jnp.int32, (STRIP, SUB), 0).astype(f32)
                    lane = lax.broadcasted_iota(jnp.int32, (1, SUB), 1).astype(f32) + h * SUB
                    before = mine.astype(f32) * STRIP + sub < key[:, there] * STRIP + lane
                    parts.append(jnp.where(before, 1.0, 0.0).astype(bf16))
                else:
                    row = (loose if i < j else strict)[:, there]
                    parts.append(jnp.where(mine < jnp.broadcast_to(row, (STRIP, SUB)), one, zero))
            part = nn(ones, jnp.concatenate(parts, axis=1))
            total = part if total is None else total + part
        ranks.append(total[0:1, :])
    return jnp.concatenate(ranks, axis=1).astype(jnp.int32)


def plan(row_side, col_side, live, diag):
    y_row = row_side[17:18, :]
    y_col = col_side[17:18, :]
    strips = jnp.concatenate([y_row[:, i * STRIP : (i + 1) * STRIP] for i in range(STRIPS)], axis=0)
    low = jnp.min(strips, axis=1, keepdims=True) - 1.0
    high = jnp.max(strips, axis=1, keepdims=True) + 1.0
    groups = jnp.concatenate([y_col[:, j * SUB : (j + 1) * SUB] for j in range(SUBS)], axis=0)
    own = lax.broadcasted_iota(jnp.int32, (SUBS, SUB), 0) == lax.broadcasted_iota(jnp.int32, (SUBS, SUB), 1)

    def across(value):
        return jnp.sum(jnp.where(own, value, 0.0), axis=0, keepdims=True)

    group_low = across(jnp.min(groups, axis=1, keepdims=True))
    group_high = across(jnp.max(groups, axis=1, keepdims=True))
    lane = lax.broadcasted_iota(jnp.int32, (STRIPS, SUB), 1)
    place = lane.astype(f32)
    reached = (group_low < high) & (group_high > low) & (lane < SUBS)
    end = jnp.max(jnp.where(reached, place + 1.0, 0.0), axis=1, keepdims=True)
    if diag:
        start = lax.broadcasted_iota(jnp.int32, (STRIPS, 1), 0).astype(f32) * 2.0 + (DIAG_W // SUB - OFF_SUBS)
    else:
        first = jnp.min(jnp.where(reached, place, float(SUBS)), axis=1, keepdims=True)
        start = jnp.minimum(first, float(SUBS - OFF_SUBS))
    extra = jnp.sum(jnp.maximum(end - (start + OFF_SUBS), 0.0), axis=0, keepdims=True)
    alive = live.astype(f32)
    table = jnp.where(lane == T_START, start, jnp.where(lane == T_END, end, extra))
    return jnp.where(lane == T_LIVE, alive, table).astype(jnp.int32)


def row_id(width):
    return lax.broadcasted_iota(jnp.int32, (8, width), 0)


def features(offset, left):
    first, second, third = split3(offset)
    norm = jnp.sum(offset * offset, axis=0, keepdims=True)
    n1, n2, n3 = split3(norm)
    ids = row_id(offset.shape[1])
    own, other = (0, 3) if left else (3, 0)
    norms = jnp.where(ids == own, n1, jnp.where(ids == own + 1, n2, jnp.where(ids == own + 2, n3, 0.0)))
    norms = jnp.where((ids >= other) & (ids < other + 3), 1.0, norms)
    if left:
        first, second, third = -2.0 * first, -2.0 * second, -2.0 * third
        parts = [first, first, first, second, second, third]
    else:
        parts = [first, second, third, first, second, first]
    return jnp.concatenate(parts + [norms, jnp.zeros_like(norms)], axis=0), norm


def sort_kernel(
    pts_hbm, nv_hbm, pr_hbm, pair_hbm, count, s0, s1, lhs0, lhs1, rank0, rank1, flags, tab,
    pts_ref, nv_ref, pr_ref, pair, key_ref, plan_ref, sems
):
    copies = [
        pltpu.make_async_copy(src, dst, sems.at[k])
        for k, (src, dst) in enumerate(
            ((pts_hbm, pts_ref), (nv_hbm, nv_ref), (pr_hbm, pr_ref), (pair_hbm, pair))
        )
    ]
    for copy in copies:
        copy.start()
    copies[0].wait()
    for blk, rank_ref in enumerate((rank0, rank1)):
        rank_ref[...] = rank_of(pts_ref[1:2, blk * BLK : (blk + 1) * BLK], key_ref)
    for copy in copies[1:]:
        copy.wait()
    for local in range(2):
        for ahead in range(2):
            flags[2 * local + ahead] = live_flag(pair, count, local, ahead)
    flags[4] = jnp.bitwise_and(lax.shift_right_logical(pair[0, 0], 1), 1)
    place = places()
    for blk, (out_ref, rank_ref) in enumerate(((s0, rank0), (s1, rank1))):
        cols = slice(blk * BLK, (blk + 1) * BLK)
        aux = jnp.concatenate(
            [pts_ref[0:3, cols] * 2.0, nv_ref[:, cols], jnp.zeros((4, BLK), f32)], axis=0
        )
        data = jnp.concatenate(
            [*split3(pr_ref[:, cols]), *split3(aux), jnp.zeros((8, BLK), f32)], axis=0
        ).astype(bf16)
        rank = rank_ref[...]
        centre = 0.5 * (jnp.min(aux, axis=1, keepdims=True) + jnp.max(aux, axis=1, keepdims=True))
        centre = jnp.concatenate([jnp.zeros((4, 1), f32), centre[0:3], jnp.zeros((1, 1), f32)], axis=0)
        for g in range(STRIPS):
            marked = marks(rank, g)
            got = None
            for c in range(STRIPS):
                part = nt(data[:, c * STRIP : (c + 1) * STRIP], one_hot(marked, c, place))
                got = part if got is None else got + part
            here = slice(g * STRIP, (g + 1) * STRIP)
            out_ref[0:16, here] = (got[0:16] + got[16:32]) + got[32:48]
            out_ref[16:24, here] = ((got[48:56] + got[56:64]) + got[64:72]) + centre
    plan_ref[0:8, :] = plan(s0, s0, flags[0], True)
    plan_ref[8:16, :] = plan(s0, s1, flags[1], False)
    plan_ref[16:24, :] = plan(s1, s1, flags[2], True)
    copy = pltpu.make_async_copy(plan_ref, tab, sems.at[0])
    copy.start()
    for side, lhs_ref in ((s0, lhs0), (s1, lhs1)):
        rows, _ = features(offset_of(side, side), True)
        for c in range(SUBS):
            here = slice(c * SUB, (c + 1) * SUB)
            lhs_ref[here, :] = rows[:, here].T.astype(bf16)
    copy.wait()


def offset_of(side_ref, centre_ref):
    centre = jnp.concatenate([centre_ref[20:23, 0:1], jnp.zeros((5, 1), f32)], axis=0)
    return jnp.where(row_id(BLK) < 3, side_ref[16:24, :] - centre, 0.0)


def live_flag(pair_ref, count_ref, local, ahead):
    flag = jnp.int32(0)
    for s in range(pair_ref.shape[1]):
        owner = pair_ref[0, s]
        match = (
            (jnp.int32(s) < count_ref[0])
            & (jnp.bitwise_and(owner, 1) == local)
            & (pair_ref[1, s] - owner == ahead)
        )
        flag = jnp.where(match, jnp.int32(1), flag)
    return flag


def kernel_values(squared):
    squared = jnp.maximum(squared, 1e-30)
    t = jnp.maximum(1.0 - squared * lax.rsqrt(squared), 0.0)
    t2 = t * t
    return ((t2 * t2) * (1.25 - t)).astype(bf16)


def tile_by_difference(row_side, row_at, col_side, col_at):
    squared = None
    for axis in range(16, 19):
        mine = jnp.broadcast_to(row_side[axis : axis + 1, pl.ds(row_at, SUB)], (SUB, SUB)).T
        diff = mine - col_side[axis : axis + 1, pl.ds(col_at, SUB)]
        part = diff * diff
        squared = part if squared is None else squared + part
    return kernel_values(squared)


def fast_strip(k_ref, i, lhs, rhs, start, width):
    for h in range(width // STRIP):
        right = rhs[:, pl.ds(start + h * STRIP, STRIP)]
        for g in range(STRIP // SUB):
            rows = slice(i * STRIP + g * SUB, i * STRIP + (g + 1) * SUB)
            k_ref[i, g * SUB : (g + 1) * SUB, h * STRIP : (h + 1) * STRIP] = kernel_values(nn(lhs[rows, :], right))


def slow_build(k_ref, row_side, col_side, first_group, groups):
    def strip(i, carry):
        def tile(j, carry):
            for g in range(STRIP // SUB):
                at = pl.multiple_of(i * STRIP + g * SUB, SUB)
                col_at = pl.multiple_of(jnp.minimum(first_group(i) + j, SUBS - 1) * SUB, SUB)
                k_ref[i, g * SUB : (g + 1) * SUB, pl.ds(pl.multiple_of(j * SUB, SUB), SUB)] = (
                    tile_by_difference(row_side, at, col_side, col_at)
                )
            return carry

        return lax.fori_loop(0, groups, tile, carry)

    lax.fori_loop(0, STRIPS, strip, 0)


def right_features(rhs, row_side, col_side):
    offset = offset_of(col_side, row_side)
    rows, norm = features(offset, False)
    rhs[...] = rows.astype(bf16)
    offset = offset_of(row_side, row_side)
    return jnp.maximum(jnp.max(norm), jnp.max(jnp.sum(offset * offset, axis=0, keepdims=True))) <= 100.0


def off_pair(k_ref, tab_ref, base, lhs, rhs, row_side, col_side, v_row, v_col, acc_row, acc_col):
    near = right_features(rhs, row_side, col_side)

    @pl.when(near)
    def _():
        for i in range(STRIPS):
            start = pl.multiple_of(tab_ref[base + i, T_START] * SUB, SUB)
            fast_strip(k_ref, i, lhs, rhs, start, OFF_W)
            owner_strip(k_ref, i, start, v_col, acc_row)
            partner_strip(k_ref, i, start, v_row, acc_col)

    @pl.when(jnp.logical_not(near))
    def _():
        slow_build(k_ref, row_side, col_side, lambda i: tab_ref[base + i, T_START], OFF_SUBS)
        to_owner(k_ref, tab_ref, base, v_col, acc_row)
        to_partner(k_ref, tab_ref, base, v_row, acc_col)


def diag_pair(k_ref, lhs, rhs, side, v, acc):
    near = right_features(rhs, side, side)

    @pl.when(near)
    def _():
        for i in range(STRIPS):
            fast_strip(k_ref, i, lhs, rhs, i * STRIP, min(DIAG_W, BLK - i * STRIP))
            diag_strip(k_ref, i, v, acc)

    @pl.when(jnp.logical_not(near))
    def _():
        slow_build(k_ref, side, side, lambda i: 2 * i, DIAG_W // SUB)
        diag_products(k_ref, v, acc)


def owner_strip(k_ref, i, start, v_col, acc_row):
    acc_row[:, i * STRIP : (i + 1) * STRIP] += halves(nt(v_col[:, pl.ds(start, OFF_W)], k_ref[i]))


def partner_strip(k_ref, i, start, v_row, acc_col):
    acc_col[:, pl.ds(start, OFF_W)] += halves(nn(v_row[:, i * STRIP : (i + 1) * STRIP], k_ref[i]))


def to_owner(k_ref, tab_ref, base, v_col, acc_row):
    for i in range(STRIPS):
        owner_strip(k_ref, i, pl.multiple_of(tab_ref[base + i, T_START] * SUB, SUB), v_col, acc_row)


def to_partner(k_ref, tab_ref, base, v_row, acc_col):
    for i in range(STRIPS):
        partner_strip(k_ref, i, pl.multiple_of(tab_ref[base + i, T_START] * SUB, SUB), v_row, acc_col)


def diag_strip(k_ref, i, v_ref, acc_ref):
    width = min(DIAG_W, BLK - i * STRIP)
    here = slice(i * STRIP, (i + 1) * STRIP)
    acc_ref[:, here] += halves(nt(v_ref[:, i * STRIP : i * STRIP + width], k_ref[i, :, :width]))
    if width > STRIP:
        after = slice((i + 1) * STRIP, i * STRIP + width)
        acc_ref[:, after] += halves(nn(v_ref[:, here], k_ref[i, :, STRIP:width]))


def diag_products(k_ref, v_ref, acc_ref):
    for i in range(STRIPS):
        diag_strip(k_ref, i, v_ref, acc_ref)


def extra_tiles(tab_ref, base, row_side, col_side, tile_ref, v_row, v_col, acc_row, acc_col):
    @pl.when(tab_ref[base, T_EXTRA] > 0)
    def _():
        def strip(i, carry):
            here = pl.ds(pl.multiple_of(i * STRIP, STRIP), STRIP)

            def tile(j, carry):
                col_at = pl.multiple_of(j * SUB, SUB)
                there = pl.ds(col_at, SUB)
                for g in range(STRIP // SUB):
                    row_at = pl.multiple_of(i * STRIP + g * SUB, SUB)
                    tile_ref[g * SUB : (g + 1) * SUB, :] = tile_by_difference(row_side, row_at, col_side, col_at)
                if acc_row is not None:
                    acc_row[:, here] += halves(nt(v_col[:, there], tile_ref[...]))
                if acc_col is not None:
                    acc_col[:, there] += halves(nn(v_row[:, here], tile_ref[...]))
                return carry

            return lax.fori_loop(
                tab_ref[base + i, T_START] + OFF_SUBS, tab_ref[base + i, T_END], tile, carry
            )

        lax.fori_loop(0, STRIPS, strip, 0)


TILE = pltpu.VMEM((STRIP, SUB), bf16)
SPLIT = pltpu.VMEM((2 * N_PROBES, BLK), bf16)
FIELD = (N_PROBES, BLK)


def call(body, outs, ins, out_specs, scratch, flops, name, limit=12):
    def run(*args):
        return pl.pallas_call(
            body,
            out_shape=outs,
            in_specs=ins,
            out_specs=out_specs,
            scratch_shapes=scratch,
            compiler_params=pltpu.CompilerParams(vmem_limit_bytes=limit * MIB),
            cost_estimate=pl.CostEstimate(flops=flops, bytes_accessed=MIB, transcendentals=0),
            name=name,
        )(*args)

    return run


def diag_build_kernel(
    tab, s0, s1, lhs0, lhs1, k00, k11, acc0, acc1, tile, v0, v1, rhs
):
    acc0[...] = jnp.zeros(FIELD, f32)
    acc1[...] = jnp.zeros(FIELD, f32)
    v0[...] = split2(s0[0:16, :])
    v1[...] = split2(s1[0:16, :])

    @pl.when(tab[0, T_LIVE] > 0)
    def _():
        diag_pair(k00, lhs0, rhs, s0, v0, acc0)
        extra_tiles(tab, 0, s0, s0, tile, v0, v0, acc0, acc0)

    @pl.when(tab[16, T_LIVE] > 0)
    def _():
        diag_pair(k11, lhs1, rhs, s1, v1, acc1)
        extra_tiles(tab, 16, s1, s1, tile, v1, v1, acc1, acc1)


def halo_build_kernel(
    flags, s1, lhs1, got_a, got_b, acc1_in, k12, tab, acc1, back, halo, plan_ref, tile, v1, v2, rhs, sem
):
    halo[...] = jnp.where(flags[4] == 0, got_a[...], got_b[...])
    plan_ref[...] = plan(s1, halo, flags[3], False)
    copy = pltpu.make_async_copy(plan_ref, tab, sem.at[0])
    copy.start()
    acc1[...] = acc1_in[...]
    back[...] = jnp.zeros(FIELD, f32)
    copy.wait()

    @pl.when(flags[3] > 0)
    def _():
        v1[...] = split2(s1[0:16, :])
        v2[...] = split2(halo[0:16, :])
        off_pair(k12, tab, 0, lhs1, rhs, s1, halo, v1, v2, acc1, back)
        extra_tiles(tab, 0, s1, halo, tile, v1, v2, acc1, back)


def own_build_kernel(tab, s0, s1, lhs0, acc0_in, acc1_in, k01, acc0, acc1, tile, v0, v1, rhs):
    base = STRIPS
    acc0[...] = acc0_in[...]
    acc1[...] = acc1_in[...]

    @pl.when(tab[base, T_LIVE] > 0)
    def _():
        v0[...] = split2(s0[0:16, :])
        v1[...] = split2(s1[0:16, :])
        off_pair(k01, tab, base, lhs0, rhs, s0, s1, v0, v1, acc0, acc1)
        extra_tiles(tab, base, s0, s1, tile, v0, v1, acc0, acc1)


def own_apply_kernel(tab, k00, k01, k11, s0, s1, w0, w1, acc0, acc1, tile, v0, v1):
    acc0[...] = jnp.zeros(FIELD, f32)
    acc1[...] = jnp.zeros(FIELD, f32)
    v0[...] = split2(w0[...])
    v1[...] = split2(w1[...])

    @pl.when(tab[0, T_LIVE] > 0)
    def _():
        diag_products(k00, v0, acc0)
        extra_tiles(tab, 0, s0, s0, tile, v0, v0, acc0, acc0)

    @pl.when(tab[8, T_LIVE] > 0)
    def _():
        to_owner(k01, tab, 8, v1, acc0)
        to_partner(k01, tab, 8, v0, acc1)
        extra_tiles(tab, 8, s0, s1, tile, v0, v1, acc0, acc1)

    @pl.when(tab[16, T_LIVE] > 0)
    def _():
        diag_products(k11, v1, acc1)
        extra_tiles(tab, 16, s1, s1, tile, v1, v1, acc1, acc1)


def inner(left, right):
    product = left * right
    return jnp.sum(product, axis=1, keepdims=True)


def finish_kernel(
    level, flags, tab, k12, s0, s1, halo, got_a, got_b, acc0, acc1, w0, w1, mom_in,
    n0, n1, send_a, send_b, mom, tile, v1, v2, acc, back
):
    live = tab[0, T_LIVE] > 0
    acc[...] = acc1[...]
    if level > 1:

        @pl.when(live)
        def _():
            v2[...] = split2(jnp.where(flags[4] == 0, got_a[...], got_b[...]))
            to_owner(k12, tab, 0, v2, acc)
            extra_tiles(tab, 0, s1, halo, tile, None, v2, acc, None)

    before0 = w0[0:16, :]
    before1 = w1[0:16, :]
    next1 = s1[19:20, :] * before1 + acc[...]
    n1[...] = next1
    back[...] = jnp.zeros(FIELD, f32)

    @pl.when(live)
    def _():
        v1[...] = split2(next1)
        to_partner(k12, tab, 0, v1, back)
        extra_tiles(tab, 0, s1, halo, tile, v1, None, None, back)

    arrived = jnp.where(flags[4] == 0, got_b[...], got_a[...])
    next0 = s0[19:20, :] * before0 + (acc0[...] + arrived)
    n0[...] = next0
    send_a[...] = jnp.where(flags[4] == 0, back[...], next0)
    send_b[...] = jnp.where(flags[4] == 0, next0, back[...])
    lane = lax.broadcasted_iota(jnp.int32, (N_PROBES, SUB), 1)
    cross = inner(before0, next0) + inner(before1, next1)
    own = inner(next0, next0) + inner(next1, next1)
    total = jnp.where(lane == 2 * level - 1, cross, jnp.where(lane == 2 * level, own, 0.0))
    if level == 1:
        total = jnp.where(lane == 0, inner(before0, before0) + inner(before1, before1), total)
    else:
        total = total + mom_in[...]
    mom[...] = total


def moment_kernel(flags, s0, s1, acc0, acc1, got_a, got_b, w0, w1, mom_in, mom):
    lane = lax.broadcasted_iota(jnp.int32, (N_PROBES, SUB), 1)
    one = w0[...]
    two = w1[...]
    arrived = jnp.where(flags[4] == 0, got_b[...], got_a[...])
    cross = inner(one, s0[19:20, :] * one + (acc0[...] + 2.0 * arrived))
    cross = cross + inner(two, s1[19:20, :] * two + acc1[...])
    mom[...] = mom_in[...] + jnp.where(lane == 5, cross, 0.0)


def last_kernel(flags, tab, k12, s0, s1, halo, got_a, got_b, acc0, acc1, w0, w1, n0, n1, tile, v2):
    arrived = jnp.where(flags[4] == 0, got_b[...], got_a[...])
    n1[...] = s1[19:20, :] * w1[...] + acc1[...]
    n0[...] = s0[19:20, :] * w0[...] + (acc0[...] + arrived)

    @pl.when(tab[0, T_LIVE] > 0)
    def _():
        v2[...] = split2(jnp.where(flags[4] == 0, got_a[...], got_b[...]))
        to_owner(k12, tab, 0, v2, n1)
        extra_tiles(tab, 0, s1, halo, tile, None, v2, n1, None)


def unsort_kernel(rank_ref, wa, wb, wc, out):
    stacked = jnp.concatenate([split2(wa[...]), split2(wb[...]), split2(wc[...])], axis=0)
    rank = rank_ref[...]
    place = places()
    marked = [marks(rank, g) for g in range(STRIPS)]
    for c in range(STRIPS):
        here = slice(c * STRIP, (c + 1) * STRIP)
        got = None
        for g in range(STRIPS):
            part = nn(stacked[:, g * STRIP : (g + 1) * STRIP], one_hot(marked[g], c, place))
            got = part if got is None else got + part
        for k in range(3):
            out[16 * k : 16 * (k + 1), here] = halves(got[32 * k : 32 * (k + 1)])


def combine_kernel(mom, probes, u0, u1, sol, res):
    lane = lax.broadcasted_iota(jnp.int32, (N_PROBES, SUB), 1)
    mu = [jnp.sum(jnp.where(lane == k, mom[...], 0.0), axis=1, keepdims=True) for k in range(6)]

    def form(left, right, shift):
        total = None
        for i, a in enumerate(left):
            for j, b in enumerate(right):
                part = (a * b) * mu[i + j + shift]
                total = part if total is None else total + part
        return total

    one = jnp.ones((N_PROBES, 1), f32)
    d = [one]
    r = [one]
    s = []
    rr = mu[0]
    for it in range(3):
        step = rr / form(d, d, 1)
        moved = [step * v for v in d]
        s = [a + b for a, b in zip(s + [0.0] * (len(d) - len(s)), moved)]
        r = [r[0]] + [(r[i] if i < len(r) else 0.0) - moved[i - 1] for i in range(1, len(moved) + 1)]
        if it < 2:
            new = form(r, r, 0)
            ratio = new / rr
            d = [r[i] + (ratio * d[i] if i < len(d) else 0.0) for i in range(len(r))]
            rr = new
    for b, u in ((0, u0), (1, u1)):
        here = slice(b * BLK, (b + 1) * BLK)
        w = [probes[:, here], u[0:16, :], u[16:32, :], u[32:48, :]]
        sol[:, here] = (s[0] * w[0] + s[1] * w[1]) + s[2] * w[2]
        res[:, here] = ((r[0] * w[0] + r[1] * w[1]) + r[2] * w[2]) + r[3] * w[3]


def swapped_both(to_a, to_b):
    count = lax.axis_size("gx")
    a = lax.ppermute(to_a, "gx", [(k, k ^ 1) for k in range(count)])
    b = lax.ppermute(to_b, "gx", [(k, ((k + 1) ^ 1) - 1) for k in range(1, count - 1)])
    return a, b


def sum_over(value, axis):
    count = lax.axis_size(axis)
    if count & (count - 1):
        return lax.psum(value, axis)
    step = 1
    while step < count:
        radix = min(4, count // step)
        parts = [value] + [
            lax.ppermute(value, axis, [(k, k ^ (m * step)) for k in range(count)]) for m in range(1, radix)
        ]
        while len(parts) > 1:
            parts = [parts[m] + parts[m + 1] for m in range(0, len(parts), 2)]
        value = parts[0]
        step *= radix
    return value


def on_device(points, noise_var, probes, pair_list, counts):
    noise = noise_var.reshape(1, -1)
    field = pltpu.VMEM(FIELD, f32)
    side = pltpu.VMEM((24, BLK), f32)
    left = pltpu.VMEM((BLK, N_FEATURES), bf16)
    right = pltpu.VMEM((N_FEATURES, BLK), bf16)
    table = pltpu.SMEM((STRIPS, SUB), jnp.int32)
    tables = pltpu.SMEM((3 * STRIPS, SUB), jnp.int32)
    ranks = pltpu.VMEM((1, BLK), jnp.int32)
    far_space = pl.BlockSpec(memory_space=pltpu.HBM)
    s0, s1, lhs0, lhs1, rank0, rank1, flags, tabb = call(
        sort_kernel,
        (side, side, left, left, ranks, ranks, pltpu.SMEM((5,), jnp.int32), tables),
        [far_space] * 4 + [SMEM],
        (VMEM,) * 6 + (SMEM,) * 2,
        [
            pltpu.VMEM(points.shape, f32),
            pltpu.VMEM(noise.shape, f32),
            pltpu.VMEM(probes.shape, f32),
            pltpu.SMEM(pair_list.shape[::-1], jnp.int32),
            pltpu.VMEM((BLK, SUB), bf16),
            pltpu.VMEM((3 * STRIPS, SUB), jnp.int32),
            pltpu.SemaphoreType.DMA((4,)),
        ],
        10**9,
        "sort_blocks",
    )(*[pltpu.with_memory_space_constraint(x, pltpu.HBM) for x in (points, noise, probes, pair_list.T)], counts)

    halos = swapped_both(s0, s0)
    off = pltpu.VMEM((STRIPS, STRIP, OFF_W), bf16)
    diag = pltpu.VMEM((STRIPS, STRIP, DIAG_W), bf16)
    k00, k11, acc0, acc1 = call(
        diag_build_kernel,
        (diag, diag, field, field),
        [SMEM] + [VMEM] * 4,
        (VMEM,) * 4,
        [TILE, SPLIT, SPLIT, right],
        3 * 10**9,
        "diag_build",
    )(tabb, s0, s1, lhs0, lhs1)
    k12, tabc, acc1, back, halo = call(
        halo_build_kernel,
        (off, table, field, field, side),
        [SMEM] + [VMEM] * 5,
        (VMEM, SMEM, VMEM, VMEM, VMEM),
        [pltpu.VMEM((STRIPS, SUB), jnp.int32), TILE, SPLIT, SPLIT, right, pltpu.SemaphoreType.DMA((1,))],
        3 * 10**9,
        "halo_build",
    )(flags, s1, lhs1, *halos, acc1)
    got = swapped_both(back, back)
    k01, acc0, acc1 = call(
        own_build_kernel,
        (off, field, field),
        [SMEM] + [VMEM] * 5,
        (VMEM,) * 3,
        [TILE, SPLIT, SPLIT, right],
        5 * 10**9,
        "own_build",
    )(tabb, s0, s1, lhs0, acc0, acc1)

    w0, w1 = s0, s1
    moments = pltpu.VMEM((N_PROBES, SUB), f32)
    mom = jnp.zeros((N_PROBES, SUB), f32)
    kept = []
    for level in (1, 2):
        w0, w1, send_a, send_b, mom = call(
            functools.partial(finish_kernel, level),
            (field,) * 4 + (moments,),
            [SMEM] * 2 + [VMEM] * 11,
            (VMEM,) * 5,
            [TILE, SPLIT, SPLIT, pltpu.VMEM(FIELD, f32), pltpu.VMEM(FIELD, f32)],
            10**9,
            "finish",
        )(flags, tabc, k12, s0, s1, halo, *got, acc0, acc1, w0, w1, mom)
        kept.append((w0, w1))
        got = swapped_both(send_a, send_b)
        acc0, acc1 = call(
            own_apply_kernel,
            (field, field),
            [SMEM] + [VMEM] * 7,
            (VMEM, VMEM),
            [TILE, SPLIT, SPLIT],
            2 * 10**9,
            "own_apply",
        )(tabb, k00, k01, k11, s0, s1, w0, w1)
    mom = call(moment_kernel, moments, [SMEM] + [VMEM] * 9, VMEM, [], 10**7, "moment")(
        flags, s0, s1, acc0, acc1, *got, w0, w1, mom
    )
    total = sum_over(mom, "gx")
    kept.append(
        call(last_kernel, (field, field), [SMEM] * 2 + [VMEM] * 10, (VMEM, VMEM), [TILE, SPLIT], 10**9, "last")(
            flags, tabc, k12, s0, s1, halo, *got, acc0, acc1, w0, w1
        )
    )
    given = []
    for b, rank in ((0, rank0), (1, rank1)):
        given.append(
            call(
                unsort_kernel,
                pltpu.VMEM((3 * N_PROBES, BLK), f32),
                [VMEM] * 4,
                VMEM,
                [],
                2 * 96 * BLK * BLK,
                "unsort",
            )(rank, *[pair[b] for pair in kept])
        )
    return call(
        combine_kernel,
        (jax.ShapeDtypeStruct(probes.shape, f32),) * 2,
        [VMEM] * 4,
        (VMEM, VMEM),
        [],
        10**6,
        "combine",
    )(total, probes, *given)


def solution(mesh):
    placed = (
        P(None, ("groups", "gx")),
        P(("groups", "gx")),
        P(None, ("groups", "gx")),
        P(("groups", "gx"), None),
        P(("groups", "gx")),
    )
    return jax.shard_map(
        on_device,
        mesh=mesh,
        in_specs=placed,
        out_specs=(P(None, ("groups", "gx")), P(None, ("groups", "gx"))),
        check_vma=False,
    )
```

```python
import functools

import jax
import jax.numpy as jnp
from jax import lax
from jax.experimental import pallas as pl
from jax.experimental.pallas import tpu as pltpu
from jax.sharding import PartitionSpec as P

BLK = 2048
STRIP = 256
STRIPS = BLK // STRIP
SUB = 128
SUBS = BLK // SUB
OFF_W = 768
OFF_SUBS = OFF_W // SUB
DIAG_W = 512
N_PROBES = 16
N_FEATURES = 64
MIB = 1 << 20

VMEM = pl.BlockSpec(memory_space=pltpu.VMEM)
SMEM = pl.BlockSpec(memory_space=pltpu.SMEM)

f32 = jnp.float32
bf16 = jnp.bfloat16

T_START, T_END, T_EXTRA, T_LIVE = 0, 1, 2, 3


def nt(left, right):
    return lax.dot_general(left, right, (((1,), (1,)), ((), ())), preferred_element_type=f32)


def nn(left, right):
    return jnp.dot(left, right, preferred_element_type=f32)


def split2(value):
    high = value.astype(bf16)
    low = (value - high.astype(f32)).astype(bf16)
    return jnp.concatenate([high, low], axis=0)


def halves(value):
    n = value.shape[0] // 2
    return value[:n] + value[n:]


def split3(value):
    high = value.astype(bf16).astype(f32)
    rest = value - high
    mid = rest.astype(bf16).astype(f32)
    return high, mid, rest - mid


def one_hot(marked, c, place):
    parts = []
    for h in range(2):
        at = c * STRIP + h * SUB
        hit = jnp.broadcast_to(marked[:, at : at + SUB], (STRIP, SUB)) == place
        parts.append(jnp.where(hit, jnp.ones((STRIP, SUB), bf16), jnp.zeros((STRIP, SUB), bf16)))
    return jnp.concatenate(parts, axis=1)


def places():
    return lax.broadcasted_iota(jnp.int32, (STRIP, SUB), 0).astype(f32).astype(bf16)


def marks(rank, g):
    group = lax.shift_right_logical(rank, 8)
    within = jnp.bitwise_and(rank, STRIP - 1)
    return jnp.where(group == g, within, -1).astype(f32).astype(bf16)


def turned(value):
    shape = (STRIP, STRIP)
    same = lax.broadcasted_iota(jnp.int32, shape, 0) == lax.broadcasted_iota(jnp.int32, shape, 1)
    return nt(jnp.where(same, 1.0, 0.0).astype(bf16), value).astype(bf16)


def rank_of(y_row, key_ref):
    low = jnp.min(y_row, axis=1, keepdims=True)
    high = jnp.max(y_row, axis=1, keepdims=True)
    scale = 255.0 / jnp.maximum(high - low, 1e-6)
    key = jnp.clip(jnp.floor((y_row - low) * scale), 0.0, 255.0)
    strict = key.astype(bf16)
    for c in range(STRIPS):
        here = slice(c * STRIP, (c + 1) * STRIP)
        key_ref[here, :] = turned(jnp.broadcast_to(key[:, here], (SUB, STRIP)).astype(bf16))
    loose = (key + 1.0).astype(bf16)
    ones = jnp.ones((16, STRIP), bf16)
    one = jnp.ones((STRIP, SUB), bf16)
    zero = jnp.zeros((STRIP, SUB), bf16)
    ranks = []
    for j in range(STRIPS):
        total = None
        for i in range(STRIPS):
            mine = key_ref[i * STRIP : (i + 1) * STRIP, :]
            parts = []
            for h in range(2):
                there = slice(j * STRIP + h * SUB, j * STRIP + (h + 1) * SUB)
                if i == j:
                    sub = lax.broadcasted_iota(jnp.int32, (STRIP, SUB), 0).astype(f32)
                    lane = lax.broadcasted_iota(jnp.int32, (1, SUB), 1).astype(f32) + h * SUB
                    before = mine.astype(f32) * STRIP + sub < key[:, there] * STRIP + lane
                    parts.append(jnp.where(before, 1.0, 0.0).astype(bf16))
                else:
                    row = (loose if i < j else strict)[:, there]
                    parts.append(jnp.where(mine < jnp.broadcast_to(row, (STRIP, SUB)), one, zero))
            part = nn(ones, jnp.concatenate(parts, axis=1))
            total = part if total is None else total + part
        ranks.append(total[0:1, :])
    return jnp.concatenate(ranks, axis=1).astype(jnp.int32)


def plan(row_side, col_side, live, diag):
    y_row = row_side[17:18, :]
    y_col = col_side[17:18, :]
    strips = jnp.concatenate([y_row[:, i * STRIP : (i + 1) * STRIP] for i in range(STRIPS)], axis=0)
    low = jnp.min(strips, axis=1, keepdims=True) - 1.0
    high = jnp.max(strips, axis=1, keepdims=True) + 1.0
    groups = jnp.concatenate([y_col[:, j * SUB : (j + 1) * SUB] for j in range(SUBS)], axis=0)
    own = lax.broadcasted_iota(jnp.int32, (SUBS, SUB), 0) == lax.broadcasted_iota(jnp.int32, (SUBS, SUB), 1)

    def across(value):
        return jnp.sum(jnp.where(own, value, 0.0), axis=0, keepdims=True)

    group_low = across(jnp.min(groups, axis=1, keepdims=True))
    group_high = across(jnp.max(groups, axis=1, keepdims=True))
    lane = lax.broadcasted_iota(jnp.int32, (STRIPS, SUB), 1)
    place = lane.astype(f32)
    reached = (group_low < high) & (group_high > low) & (lane < SUBS)
    end = jnp.max(jnp.where(reached, place + 1.0, 0.0), axis=1, keepdims=True)
    if diag:
        start = lax.broadcasted_iota(jnp.int32, (STRIPS, 1), 0).astype(f32) * 2.0 + (DIAG_W // SUB - OFF_SUBS)
    else:
        first = jnp.min(jnp.where(reached, place, float(SUBS)), axis=1, keepdims=True)
        start = jnp.minimum(first, float(SUBS - OFF_SUBS))
    extra = jnp.sum(jnp.maximum(end - (start + OFF_SUBS), 0.0), axis=0, keepdims=True)
    alive = live.astype(f32)
    table = jnp.where(lane == T_START, start, jnp.where(lane == T_END, end, extra))
    return jnp.where(lane == T_LIVE, alive, table).astype(jnp.int32)


def row_id(width):
    return lax.broadcasted_iota(jnp.int32, (8, width), 0)


def features(offset, left):
    first, second, third = split3(offset)
    norm = jnp.sum(offset * offset, axis=0, keepdims=True)
    n1, n2, n3 = split3(norm)
    ids = row_id(offset.shape[1])
    own, other = (0, 3) if left else (3, 0)
    norms = jnp.where(ids == own, n1, jnp.where(ids == own + 1, n2, jnp.where(ids == own + 2, n3, 0.0)))
    norms = jnp.where((ids >= other) & (ids < other + 3), 1.0, norms)
    if left:
        first, second, third = -2.0 * first, -2.0 * second, -2.0 * third
        parts = [first, first, first, second, second, third]
    else:
        parts = [first, second, third, first, second, first]
    return jnp.concatenate(parts + [norms, jnp.zeros_like(norms)], axis=0), norm


def sort_kernel(
    pts_hbm, nv_hbm, pr_hbm, pair_hbm, count, s0, s1, lhs0, lhs1, rank0, rank1, flags, tab,
    pts_ref, nv_ref, pr_ref, pair, key_ref, plan_ref, sems
):
    copies = [
        pltpu.make_async_copy(src, dst, sems.at[k])
        for k, (src, dst) in enumerate(
            ((pts_hbm, pts_ref), (nv_hbm, nv_ref), (pr_hbm, pr_ref), (pair_hbm, pair))
        )
    ]
    for copy in copies:
        copy.start()
    copies[0].wait()
    for blk, rank_ref in enumerate((rank0, rank1)):
        rank_ref[...] = rank_of(pts_ref[1:2, blk * BLK : (blk + 1) * BLK], key_ref)
    for copy in copies[1:]:
        copy.wait()
    for local in range(2):
        for ahead in range(2):
            flags[2 * local + ahead] = live_flag(pair, count, local, ahead)
    position = lax.shift_right_logical(pair[0, 0], 1)
    flags[4] = jnp.bitwise_and(position, 1)
    flags[5] = jnp.where(position > 0, 1, 0)
    place = places()
    for blk, (out_ref, rank_ref) in enumerate(((s0, rank0), (s1, rank1))):
        cols = slice(blk * BLK, (blk + 1) * BLK)
        aux = jnp.concatenate(
            [pts_ref[0:3, cols] * 2.0, nv_ref[:, cols], jnp.zeros((4, BLK), f32)], axis=0
        )
        data = jnp.concatenate(
            [*split3(pr_ref[:, cols]), *split3(aux), jnp.zeros((8, BLK), f32)], axis=0
        ).astype(bf16)
        rank = rank_ref[...]
        centre = 0.5 * (jnp.min(aux, axis=1, keepdims=True) + jnp.max(aux, axis=1, keepdims=True))
        centre = jnp.concatenate([jnp.zeros((4, 1), f32), centre[0:3], jnp.zeros((1, 1), f32)], axis=0)
        for g in range(STRIPS):
            marked = marks(rank, g)
            got = None
            for c in range(STRIPS):
                part = nt(data[:, c * STRIP : (c + 1) * STRIP], one_hot(marked, c, place))
                got = part if got is None else got + part
            here = slice(g * STRIP, (g + 1) * STRIP)
            out_ref[0:16, here] = (got[0:16] + got[16:32]) + got[32:48]
            out_ref[16:24, here] = ((got[48:56] + got[56:64]) + got[64:72]) + centre
    plan_ref[0:8, :] = plan(s0, s0, flags[0], True)
    plan_ref[8:16, :] = plan(s0, s1, flags[1], False)
    plan_ref[16:24, :] = plan(s1, s1, flags[2], True)
    copy = pltpu.make_async_copy(plan_ref, tab, sems.at[0])
    copy.start()
    for side, lhs_ref in ((s0, lhs0), (s1, lhs1)):
        rows, _ = features(offset_of(side, side), True)
        rows = rows.astype(bf16)
        for c in range(STRIPS):
            here = slice(c * STRIP, (c + 1) * STRIP)
            lhs_ref[here, :] = turned(rows[:, here])
    copy.wait()


def offset_of(side_ref, centre_ref):
    centre = jnp.concatenate([centre_ref[20:23, 0:1], jnp.zeros((5, 1), f32)], axis=0)
    return jnp.where(row_id(BLK) < 3, side_ref[16:24, :] - centre, 0.0)


def live_flag(pair_ref, count_ref, local, ahead):
    flag = jnp.int32(0)
    for s in range(pair_ref.shape[1]):
        owner = pair_ref[0, s]
        match = (
            (jnp.int32(s) < count_ref[0])
            & (jnp.bitwise_and(owner, 1) == local)
            & (pair_ref[1, s] - owner == ahead)
        )
        flag = jnp.where(match, jnp.int32(1), flag)
    return flag


def kernel_values(squared):
    squared = jnp.maximum(squared, 1e-30)
    t = jnp.maximum(1.0 - squared * lax.rsqrt(squared), 0.0)
    t2 = t * t
    return ((t2 * t2) * (1.25 - t)).astype(bf16)


def tile_by_difference(row_side, row_at, col_side, col_at):
    squared = None
    for axis in range(16, 19):
        mine = jnp.broadcast_to(row_side[axis : axis + 1, pl.ds(row_at, SUB)], (SUB, SUB)).T
        diff = mine - col_side[axis : axis + 1, pl.ds(col_at, SUB)]
        part = diff * diff
        squared = part if squared is None else squared + part
    return kernel_values(squared)


def fast_strip(k_ref, i, lhs, rhs, start, width):
    for h in range(width // STRIP):
        right = rhs[:, pl.ds(start + h * STRIP, STRIP)]
        for g in range(STRIP // SUB):
            rows = slice(i * STRIP + g * SUB, i * STRIP + (g + 1) * SUB)
            k_ref[i, g * SUB : (g + 1) * SUB, h * STRIP : (h + 1) * STRIP] = kernel_values(nn(lhs[rows, :], right))


def slow_build(k_ref, row_side, col_side, first_group, groups):
    def strip(i, carry):
        def tile(j, carry):
            for g in range(STRIP // SUB):
                at = pl.multiple_of(i * STRIP + g * SUB, SUB)
                col_at = pl.multiple_of(jnp.minimum(first_group(i) + j, SUBS - 1) * SUB, SUB)
                k_ref[i, g * SUB : (g + 1) * SUB, pl.ds(pl.multiple_of(j * SUB, SUB), SUB)] = (
                    tile_by_difference(row_side, at, col_side, col_at)
                )
            return carry

        return lax.fori_loop(0, groups, tile, carry)

    lax.fori_loop(0, STRIPS, strip, 0)


def right_features(rhs, row_side, col_side):
    offset = offset_of(col_side, row_side)
    rows, norm = features(offset, False)
    rhs[...] = rows.astype(bf16)
    offset = offset_of(row_side, row_side)
    return jnp.maximum(jnp.max(norm), jnp.max(jnp.sum(offset * offset, axis=0, keepdims=True))) <= 100.0


def off_pair(k_ref, tab_ref, base, lhs, rhs, row_side, col_side, v_row, v_col, acc_row, acc_col):
    near = right_features(rhs, row_side, col_side)

    @pl.when(near)
    def _():
        for i in range(STRIPS):
            start = pl.multiple_of(tab_ref[base + i, T_START] * SUB, SUB)
            fast_strip(k_ref, i, lhs, rhs, start, OFF_W)
            owner_strip(k_ref, i, start, v_col, acc_row)
            partner_strip(k_ref, i, start, v_row, acc_col)

    @pl.when(jnp.logical_not(near))
    def _():
        slow_build(k_ref, row_side, col_side, lambda i: tab_ref[base + i, T_START], OFF_SUBS)
        to_owner(k_ref, tab_ref, base, v_col, acc_row)
        to_partner(k_ref, tab_ref, base, v_row, acc_col)

    return near, lhs, rhs


def diag_pair(k_ref, lhs, rhs, side, v, acc):
    near = right_features(rhs, side, side)

    @pl.when(near)
    def _():
        for i in range(STRIPS):
            fast_strip(k_ref, i, lhs, rhs, i * STRIP, min(DIAG_W, BLK - i * STRIP))
            diag_strip(k_ref, i, v, acc)

    @pl.when(jnp.logical_not(near))
    def _():
        slow_build(k_ref, side, side, lambda i: 2 * i, DIAG_W // SUB)
        diag_products(k_ref, v, acc)


def owner_strip(k_ref, i, start, v_col, acc_row):
    acc_row[:, i * STRIP : (i + 1) * STRIP] += halves(nt(v_col[:, pl.ds(start, OFF_W)], k_ref[i]))


def partner_strip(k_ref, i, start, v_row, acc_col):
    acc_col[:, pl.ds(start, OFF_W)] += halves(nn(v_row[:, i * STRIP : (i + 1) * STRIP], k_ref[i]))


def to_owner(k_ref, tab_ref, base, v_col, acc_row):
    for i in range(STRIPS):
        owner_strip(k_ref, i, pl.multiple_of(tab_ref[base + i, T_START] * SUB, SUB), v_col, acc_row)


def to_partner(k_ref, tab_ref, base, v_row, acc_col):
    for i in range(STRIPS):
        partner_strip(k_ref, i, pl.multiple_of(tab_ref[base + i, T_START] * SUB, SUB), v_row, acc_col)


def diag_strip(k_ref, i, v_ref, acc_ref):
    width = min(DIAG_W, BLK - i * STRIP)
    here = slice(i * STRIP, (i + 1) * STRIP)
    acc_ref[:, here] += halves(nt(v_ref[:, i * STRIP : i * STRIP + width], k_ref[i, :, :width]))
    if width > STRIP:
        after = slice((i + 1) * STRIP, i * STRIP + width)
        acc_ref[:, after] += halves(nn(v_ref[:, here], k_ref[i, :, STRIP:width]))


def diag_products(k_ref, v_ref, acc_ref):
    for i in range(STRIPS):
        diag_strip(k_ref, i, v_ref, acc_ref)


def extra_tiles(
    tab_ref, base, row_side, col_side, tile_ref, v_row, v_col, acc_row, acc_col, kept=None, fill=None
):
    @pl.when(tab_ref[base, T_EXTRA] > 0)
    def _():
        def strip(i, carry):
            here = pl.ds(pl.multiple_of(i * STRIP, STRIP), STRIP)
            first = tab_ref[base + i, T_START] + OFF_SUBS

            def tile(j, carry):
                col_at = pl.multiple_of(j * SUB, SUB)
                there = pl.ds(col_at, SUB)

                def by_difference():
                    for g in range(STRIP // SUB):
                        row_at = pl.multiple_of(i * STRIP + g * SUB, SUB)
                        tile_ref[g * SUB : (g + 1) * SUB, :] = tile_by_difference(row_side, row_at, col_side, col_at)

                if kept is None:
                    by_difference()
                elif fill is None:
                    pl.when(j > first)(by_difference)

                    @pl.when(j == first)
                    def _():
                        tile_ref[...] = kept[i]
                else:
                    near, lhs, rhs = fill
                    pl.when(jnp.logical_not(near))(by_difference)

                    @pl.when(near)
                    def _():
                        tile_ref[...] = kernel_values(nn(lhs[here, :], rhs[:, there]))

                    @pl.when(j == first)
                    def _():
                        kept[i] = tile_ref[...]

                if acc_row is not None:
                    acc_row[:, here] += halves(nt(v_col[:, there], tile_ref[...]))
                if acc_col is not None:
                    acc_col[:, there] += halves(nn(v_row[:, here], tile_ref[...]))
                return carry

            return lax.fori_loop(first, tab_ref[base + i, T_END], tile, carry)

        lax.fori_loop(0, STRIPS, strip, 0)


TILE = pltpu.VMEM((STRIP, SUB), bf16)
SPLIT = pltpu.VMEM((2 * N_PROBES, BLK), bf16)
FIELD = (N_PROBES, BLK)


def call(body, outs, ins, out_specs, scratch, flops, name, limit=12):
    def run(*args):
        return pl.pallas_call(
            body,
            out_shape=outs,
            in_specs=ins,
            out_specs=out_specs,
            scratch_shapes=scratch,
            compiler_params=pltpu.CompilerParams(vmem_limit_bytes=limit * MIB),
            cost_estimate=pl.CostEstimate(flops=flops, bytes_accessed=MIB, transcendentals=0),
            name=name,
        )(*args)

    return run


def diag_build_kernel(
    tab, s0, s1, lhs0, lhs1, k00, k11, acc0, acc1, tile, v0, v1, rhs
):
    acc0[...] = jnp.zeros(FIELD, f32)
    acc1[...] = jnp.zeros(FIELD, f32)
    v0[...] = split2(s0[0:16, :])
    v1[...] = split2(s1[0:16, :])

    @pl.when(tab[0, T_LIVE] > 0)
    def _():
        diag_pair(k00, lhs0, rhs, s0, v0, acc0)
        extra_tiles(tab, 0, s0, s0, tile, v0, v0, acc0, acc0)

    @pl.when(tab[16, T_LIVE] > 0)
    def _():
        diag_pair(k11, lhs1, rhs, s1, v1, acc1)
        extra_tiles(tab, 16, s1, s1, tile, v1, v1, acc1, acc1)


def halo_build_kernel(
    flags, s1, lhs1, got_a, got_b, acc1_in, k12, x12, tab, acc1, back, halo, plan_ref, tile, v1, v2, rhs, sem
):
    halo[...] = jnp.where(flags[4] == 0, got_a[...], got_b[...])
    plan_ref[...] = plan(s1, halo, flags[3], False)
    copy = pltpu.make_async_copy(plan_ref, tab, sem.at[0])
    copy.start()
    acc1[...] = acc1_in[...]
    back[...] = jnp.zeros(FIELD, f32)
    copy.wait()

    @pl.when(flags[3] > 0)
    def _():
        v1[...] = split2(s1[0:16, :])
        v2[...] = split2(halo[0:16, :])
        fill = off_pair(k12, tab, 0, lhs1, rhs, s1, halo, v1, v2, acc1, back)
        extra_tiles(tab, 0, s1, halo, tile, v1, v2, acc1, back, x12, fill)


def own_build_kernel(tab, s0, s1, lhs0, acc0_in, acc1_in, k01, x01, acc0, acc1, tile, v0, v1, rhs):
    base = STRIPS
    acc0[...] = acc0_in[...]
    acc1[...] = acc1_in[...]

    @pl.when(tab[base, T_LIVE] > 0)
    def _():
        v0[...] = split2(s0[0:16, :])
        v1[...] = split2(s1[0:16, :])
        fill = off_pair(k01, tab, base, lhs0, rhs, s0, s1, v0, v1, acc0, acc1)
        extra_tiles(tab, base, s0, s1, tile, v0, v1, acc0, acc1, x01, fill)


def own_apply_kernel(tab, k00, k01, x01, k11, s0, s1, w0, w1, acc0, acc1, tile, v0, v1):
    acc0[...] = jnp.zeros(FIELD, f32)
    acc1[...] = jnp.zeros(FIELD, f32)
    v0[...] = split2(w0[...])
    v1[...] = split2(w1[...])

    @pl.when(tab[0, T_LIVE] > 0)
    def _():
        diag_products(k00, v0, acc0)
        extra_tiles(tab, 0, s0, s0, tile, v0, v0, acc0, acc0)

    @pl.when(tab[8, T_LIVE] > 0)
    def _():
        to_owner(k01, tab, 8, v1, acc0)
        to_partner(k01, tab, 8, v0, acc1)
        extra_tiles(tab, 8, s0, s1, tile, v0, v1, acc0, acc1, x01)

    @pl.when(tab[16, T_LIVE] > 0)
    def _():
        diag_products(k11, v1, acc1)
        extra_tiles(tab, 16, s1, s1, tile, v1, v1, acc1, acc1)


def from_left(flags, got_a, got_b):
    arrived = jnp.where(flags[4] == 0, got_b[...], got_a[...])
    return jnp.where(flags[5] > 0, arrived, 0.0)


def inner(left, right):
    product = left * right
    return jnp.sum(product, axis=1, keepdims=True)


def finish_kernel(
    level, flags, tab, k12, x12, s0, s1, halo, got_a, got_b, acc0, acc1, w0, w1, mom_in,
    n0, n1, send_a, send_b, mom, tile, v1, v2, acc, back
):
    live = tab[0, T_LIVE] > 0
    acc[...] = acc1[...]
    if level > 1:

        @pl.when(live)
        def _():
            v2[...] = split2(jnp.where(flags[4] == 0, got_a[...], got_b[...]))
            to_owner(k12, tab, 0, v2, acc)
            extra_tiles(tab, 0, s1, halo, tile, None, v2, acc, None, x12)

    before0 = w0[0:16, :]
    before1 = w1[0:16, :]
    next1 = s1[19:20, :] * before1 + acc[...]
    n1[...] = next1
    back[...] = jnp.zeros(FIELD, f32)

    @pl.when(live)
    def _():
        v1[...] = split2(next1)
        to_partner(k12, tab, 0, v1, back)
        extra_tiles(tab, 0, s1, halo, tile, v1, None, None, back, x12)

    arrived = from_left(flags, got_a, got_b)
    next0 = s0[19:20, :] * before0 + (acc0[...] + arrived)
    n0[...] = next0
    send_a[...] = jnp.where(flags[4] == 0, back[...], next0)
    send_b[...] = jnp.where(flags[4] == 0, next0, back[...])
    lane = lax.broadcasted_iota(jnp.int32, (N_PROBES, SUB), 1)
    cross = inner(before0, next0) + inner(before1, next1)
    own = inner(next0, next0) + inner(next1, next1)
    total = jnp.where(lane == 2 * level - 1, cross, jnp.where(lane == 2 * level, own, 0.0))
    if level == 1:
        total = jnp.where(lane == 0, inner(before0, before0) + inner(before1, before1), total)
    else:
        total = total + mom_in[...]
    mom[...] = total


def moment_kernel(flags, s0, s1, acc0, acc1, got_a, got_b, w0, w1, mom_in, mom):
    lane = lax.broadcasted_iota(jnp.int32, (N_PROBES, SUB), 1)
    one = w0[...]
    two = w1[...]
    arrived = from_left(flags, got_a, got_b)
    cross = inner(one, s0[19:20, :] * one + (acc0[...] + 2.0 * arrived))
    cross = cross + inner(two, s1[19:20, :] * two + acc1[...])
    mom[...] = mom_in[...] + jnp.where(lane == 5, cross, 0.0)


def last_kernel(flags, tab, k12, x12, s0, s1, halo, got_a, got_b, acc0, acc1, w0, w1, n0, n1, tile, v2):
    arrived = from_left(flags, got_a, got_b)
    n1[...] = s1[19:20, :] * w1[...] + acc1[...]
    n0[...] = s0[19:20, :] * w0[...] + (acc0[...] + arrived)

    @pl.when(tab[0, T_LIVE] > 0)
    def _():
        v2[...] = split2(jnp.where(flags[4] == 0, got_a[...], got_b[...]))
        to_owner(k12, tab, 0, v2, n1)
        extra_tiles(tab, 0, s1, halo, tile, None, v2, n1, None, x12)


def unsort_kernel(rank_ref, wa, wb, wc, out):
    stacked = jnp.concatenate([split2(wa[...]), split2(wb[...]), split2(wc[...])], axis=0)
    rank = rank_ref[...]
    place = places()
    marked = [marks(rank, g) for g in range(STRIPS)]
    for c in range(STRIPS):
        here = slice(c * STRIP, (c + 1) * STRIP)
        got = None
        for g in range(STRIPS):
            part = nn(stacked[:, g * STRIP : (g + 1) * STRIP], one_hot(marked[g], c, place))
            got = part if got is None else got + part
        for k in range(3):
            out[16 * k : 16 * (k + 1), here] = halves(got[32 * k : 32 * (k + 1)])


def combine_kernel(mom, probes, u0, u1, sol, res):
    lane = lax.broadcasted_iota(jnp.int32, (N_PROBES, SUB), 1)
    mu = [jnp.sum(jnp.where(lane == k, mom[...], 0.0), axis=1, keepdims=True) for k in range(6)]

    def form(left, right, shift):
        total = None
        for i, a in enumerate(left):
            for j, b in enumerate(right):
                part = (a * b) * mu[i + j + shift]
                total = part if total is None else total + part
        return total

    one = jnp.ones((N_PROBES, 1), f32)
    d = [one]
    r = [one]
    s = []
    rr = mu[0]
    for it in range(3):
        step = rr / form(d, d, 1)
        moved = [step * v for v in d]
        s = [a + b for a, b in zip(s + [0.0] * (len(d) - len(s)), moved)]
        r = [r[0]] + [(r[i] if i < len(r) else 0.0) - moved[i - 1] for i in range(1, len(moved) + 1)]
        if it < 2:
            new = form(r, r, 0)
            ratio = new / rr
            d = [r[i] + (ratio * d[i] if i < len(d) else 0.0) for i in range(len(r))]
            rr = new
    for b, u in ((0, u0), (1, u1)):
        here = slice(b * BLK, (b + 1) * BLK)
        w = [probes[:, here], u[0:16, :], u[16:32, :], u[32:48, :]]
        sol[:, here] = (s[0] * w[0] + s[1] * w[1]) + s[2] * w[2]
        res[:, here] = ((r[0] * w[0] + r[1] * w[1]) + r[2] * w[2]) + r[3] * w[3]


def swapped_both(to_a, to_b):
    count = lax.axis_size("gx")
    a = lax.ppermute(to_a, "gx", [(k, k ^ 1) for k in range(count)])
    ends = [(0, 0), (count - 1, count - 1)]
    b = lax.ppermute(to_b, "gx", ends + [(k, ((k + 1) ^ 1) - 1) for k in range(1, count - 1)])
    return a, b


def sum_over(value, axis):
    count = lax.axis_size(axis)
    if count & (count - 1):
        return lax.psum(value, axis)
    step = 1
    while step < count:
        radix = min(4, count // step)
        parts = [value] + [
            lax.ppermute(value, axis, [(k, k ^ (m * step)) for k in range(count)]) for m in range(1, radix)
        ]
        while len(parts) > 1:
            parts = [parts[m] + parts[m + 1] for m in range(0, len(parts), 2)]
        value = parts[0]
        step *= radix
    return value


def on_device(points, noise_var, probes, pair_list, counts):
    noise = noise_var.reshape(1, -1)
    field = pltpu.VMEM(FIELD, f32)
    side = pltpu.VMEM((24, BLK), f32)
    left = pltpu.VMEM((BLK, N_FEATURES), bf16)
    right = pltpu.VMEM((N_FEATURES, BLK), bf16)
    table = pltpu.SMEM((STRIPS, SUB), jnp.int32)
    tables = pltpu.SMEM((3 * STRIPS, SUB), jnp.int32)
    ranks = pltpu.VMEM((1, BLK), jnp.int32)
    far_space = pl.BlockSpec(memory_space=pltpu.HBM)
    s0, s1, lhs0, lhs1, rank0, rank1, flags, tabb = call(
        sort_kernel,
        (side, side, left, left, ranks, ranks, pltpu.SMEM((6,), jnp.int32), tables),
        [far_space] * 4 + [SMEM],
        (VMEM,) * 6 + (SMEM,) * 2,
        [
            pltpu.VMEM(points.shape, f32),
            pltpu.VMEM(noise.shape, f32),
            pltpu.VMEM(probes.shape, f32),
            pltpu.SMEM(pair_list.shape[::-1], jnp.int32),
            pltpu.VMEM((BLK, SUB), bf16),
            pltpu.VMEM((3 * STRIPS, SUB), jnp.int32),
            pltpu.SemaphoreType.DMA((4,)),
        ],
        10**9,
        "sort_blocks",
    )(*[pltpu.with_memory_space_constraint(x, pltpu.HBM) for x in (points, noise, probes, pair_list.T)], counts)

    halos = swapped_both(s0, s0)
    off = pltpu.VMEM((STRIPS, STRIP, OFF_W), bf16)
    diag = pltpu.VMEM((STRIPS, STRIP, DIAG_W), bf16)
    outside = pltpu.VMEM((STRIPS, STRIP, SUB), bf16)
    k00, k11, acc0, acc1 = call(
        diag_build_kernel,
        (diag, diag, field, field),
        [SMEM] + [VMEM] * 4,
        (VMEM,) * 4,
        [TILE, SPLIT, SPLIT, right],
        3 * 10**9,
        "diag_build",
    )(tabb, s0, s1, lhs0, lhs1)
    k12, x12, tabc, acc1, back, halo = call(
        halo_build_kernel,
        (off, outside, table, field, field, side),
        [SMEM] + [VMEM] * 5,
        (VMEM, VMEM, SMEM, VMEM, VMEM, VMEM),
        [pltpu.VMEM((STRIPS, SUB), jnp.int32), TILE, SPLIT, SPLIT, right, pltpu.SemaphoreType.DMA((1,))],
        3 * 10**9,
        "halo_build",
    )(flags, s1, lhs1, *halos, acc1)
    got = swapped_both(back, back)
    k01, x01, acc0, acc1 = call(
        own_build_kernel,
        (off, outside, field, field),
        [SMEM] + [VMEM] * 5,
        (VMEM,) * 4,
        [TILE, SPLIT, SPLIT, right],
        5 * 10**9,
        "own_build",
    )(tabb, s0, s1, lhs0, acc0, acc1)

    w0, w1 = s0, s1
    moments = pltpu.VMEM((N_PROBES, SUB), f32)
    mom = jnp.zeros((N_PROBES, SUB), f32)
    kept = []
    for level in (1, 2):
        w0, w1, send_a, send_b, mom = call(
            functools.partial(finish_kernel, level),
            (field,) * 4 + (moments,),
            [SMEM] * 2 + [VMEM] * 12,
            (VMEM,) * 5,
            [TILE, SPLIT, SPLIT, pltpu.VMEM(FIELD, f32), pltpu.VMEM(FIELD, f32)],
            10**9,
            "finish",
        )(flags, tabc, k12, x12, s0, s1, halo, *got, acc0, acc1, w0, w1, mom)
        kept.append((w0, w1))
        got = swapped_both(send_a, send_b)
        acc0, acc1 = call(
            own_apply_kernel,
            (field, field),
            [SMEM] + [VMEM] * 8,
            (VMEM, VMEM),
            [TILE, SPLIT, SPLIT],
            2 * 10**9,
            "own_apply",
        )(tabb, k00, k01, x01, k11, s0, s1, w0, w1)
    mom = call(moment_kernel, moments, [SMEM] + [VMEM] * 9, VMEM, [], 10**7, "moment")(
        flags, s0, s1, acc0, acc1, *got, w0, w1, mom
    )
    total = sum_over(mom, "gx")
    kept.append(
        call(last_kernel, (field, field), [SMEM] * 2 + [VMEM] * 11, (VMEM, VMEM), [TILE, SPLIT], 10**9, "last")(
            flags, tabc, k12, x12, s0, s1, halo, *got, acc0, acc1, w0, w1
        )
    )
    given = []
    for b, rank in ((0, rank0), (1, rank1)):
        given.append(
            call(
                unsort_kernel,
                pltpu.VMEM((3 * N_PROBES, BLK), f32),
                [VMEM] * 4,
                VMEM,
                [],
                2 * 96 * BLK * BLK,
                "unsort",
            )(rank, *[pair[b] for pair in kept])
        )
    return call(
        combine_kernel,
        (jax.ShapeDtypeStruct(probes.shape, f32),) * 2,
        [VMEM] * 4,
        (VMEM, VMEM),
        [],
        10**6,
        "combine",
    )(total, probes, *given)


def solution(mesh):
    placed = (
        P(None, ("groups", "gx")),
        P(("groups", "gx")),
        P(None, ("groups", "gx")),
        P(("groups", "gx"), None),
        P(("groups", "gx")),
    )
    return jax.shard_map(
        on_device,
        mesh=mesh,
        in_specs=placed,
        out_specs=(P(None, ("groups", "gx")), P(None, ("groups", "gx"))),
        check_vma=False,
    )
```

```python
import functools

import jax
import jax.numpy as jnp
from jax import lax
from jax.experimental import pallas as pl
from jax.experimental.pallas import tpu as pltpu
from jax.sharding import PartitionSpec as P

BLK = 2048
STRIP = 256
STRIPS = BLK // STRIP
SUB = 128
SUBS = BLK // SUB
OFF_W = 768
OFF_SUBS = OFF_W // SUB
DIAG_W = 512
N_PROBES = 16
N_FEATURES = 64
MIB = 1 << 20

VMEM = pl.BlockSpec(memory_space=pltpu.VMEM)
SMEM = pl.BlockSpec(memory_space=pltpu.SMEM)

f32 = jnp.float32
bf16 = jnp.bfloat16

T_START, T_END, T_EXTRA, T_LIVE = 0, 1, 2, 3


def nt(left, right):
    return lax.dot_general(left, right, (((1,), (1,)), ((), ())), preferred_element_type=f32)


def nn(left, right):
    return jnp.dot(left, right, preferred_element_type=f32)


def split2(value):
    high = value.astype(bf16)
    low = (value - high.astype(f32)).astype(bf16)
    return jnp.concatenate([high, low], axis=0)


def halves(value):
    n = value.shape[0] // 2
    return value[:n] + value[n:]


def split3(value):
    high = value.astype(bf16).astype(f32)
    rest = value - high
    mid = rest.astype(bf16).astype(f32)
    return high, mid, rest - mid


def one_hot(marked, c, place):
    parts = []
    for h in range(2):
        at = c * STRIP + h * SUB
        hit = jnp.broadcast_to(marked[:, at : at + SUB], (STRIP, SUB)) == place
        parts.append(jnp.where(hit, jnp.ones((STRIP, SUB), bf16), jnp.zeros((STRIP, SUB), bf16)))
    return jnp.concatenate(parts, axis=1)


def places():
    return lax.broadcasted_iota(jnp.int32, (STRIP, SUB), 0).astype(f32).astype(bf16)


def marks(rank, g):
    group = lax.shift_right_logical(rank, 8)
    within = jnp.bitwise_and(rank, STRIP - 1)
    return jnp.where(group == g, within, -1).astype(f32).astype(bf16)


def turned(value):
    shape = (STRIP, STRIP)
    same = lax.broadcasted_iota(jnp.int32, shape, 0) == lax.broadcasted_iota(jnp.int32, shape, 1)
    return nt(jnp.where(same, 1.0, 0.0).astype(bf16), value).astype(bf16)


def rank_of(y_row):
    low = jnp.min(y_row, axis=1, keepdims=True)
    high = jnp.max(y_row, axis=1, keepdims=True)
    scale = 255.0 / jnp.maximum(high - low, 1e-6)
    key = jnp.clip(jnp.floor((y_row - low) * scale), 0.0, 255.0).astype(bf16)
    shape = (STRIP, STRIP)
    first = lax.broadcasted_iota(jnp.int32, shape, 0)
    second = lax.broadcasted_iota(jnp.int32, shape, 1)
    upper = jnp.where(first < second, 1.0, 0.0).astype(bf16)
    lower = jnp.where(second < first, 1.0, 0.0).astype(bf16)
    value = places()
    hits = []
    smaller = None
    for j in range(STRIPS):
        hit = one_hot(key, j, value)
        hits.append(hit)
        part = nn(lower, hit)
        smaller = part if smaller is None else smaller + part
    before = jnp.sum(smaller, axis=1, keepdims=True)
    ranks = []
    for j in range(STRIPS):
        hit = hits[j].astype(f32)
        ranks.append(jnp.sum(hit * (nn(hits[j], upper) + before), axis=0, keepdims=True))
        if j + 1 < STRIPS:
            before = before + jnp.sum(hit, axis=1, keepdims=True)
    return jnp.concatenate(ranks, axis=1).astype(jnp.int32)


def plan(row_side, col_side, live, diag):
    y_row = row_side[17:18, :]
    y_col = col_side[17:18, :]
    strips = jnp.concatenate([y_row[:, i * STRIP : (i + 1) * STRIP] for i in range(STRIPS)], axis=0)
    low = jnp.min(strips, axis=1, keepdims=True) - 1.0
    high = jnp.max(strips, axis=1, keepdims=True) + 1.0
    groups = jnp.concatenate([y_col[:, j * SUB : (j + 1) * SUB] for j in range(SUBS)], axis=0)
    own = lax.broadcasted_iota(jnp.int32, (SUBS, SUB), 0) == lax.broadcasted_iota(jnp.int32, (SUBS, SUB), 1)

    def across(value):
        return jnp.sum(jnp.where(own, value, 0.0), axis=0, keepdims=True)

    group_low = across(jnp.min(groups, axis=1, keepdims=True))
    group_high = across(jnp.max(groups, axis=1, keepdims=True))
    lane = lax.broadcasted_iota(jnp.int32, (STRIPS, SUB), 1)
    place = lane.astype(f32)
    reached = (group_low < high) & (group_high > low) & (lane < SUBS)
    end = jnp.max(jnp.where(reached, place + 1.0, 0.0), axis=1, keepdims=True)
    if diag:
        start = lax.broadcasted_iota(jnp.int32, (STRIPS, 1), 0).astype(f32) * 2.0 + (DIAG_W // SUB - OFF_SUBS)
    else:
        first = jnp.min(jnp.where(reached, place, float(SUBS)), axis=1, keepdims=True)
        start = jnp.minimum(first, float(SUBS - OFF_SUBS))
    extra = jnp.sum(jnp.maximum(end - (start + OFF_SUBS), 0.0), axis=0, keepdims=True)
    alive = live.astype(f32)
    table = jnp.where(lane == T_START, start, jnp.where(lane == T_END, end, extra))
    return jnp.where(lane == T_LIVE, alive, table).astype(jnp.int32)


def row_id(width):
    return lax.broadcasted_iota(jnp.int32, (8, width), 0)


def features(offset, left):
    first, second, third = split3(offset)
    norm = jnp.sum(offset * offset, axis=0, keepdims=True)
    n1, n2, n3 = split3(norm)
    ids = row_id(offset.shape[1])
    own, other = (0, 3) if left else (3, 0)
    norms = jnp.where(ids == own, n1, jnp.where(ids == own + 1, n2, jnp.where(ids == own + 2, n3, 0.0)))
    norms = jnp.where((ids >= other) & (ids < other + 3), 1.0, norms)
    if left:
        first, second, third = -2.0 * first, -2.0 * second, -2.0 * third
        parts = [first, first, first, second, second, third]
    else:
        parts = [first, second, third, first, second, first]
    return jnp.concatenate(parts + [norms, jnp.zeros_like(norms)], axis=0), norm


def sort_kernel(
    pts_hbm, nv_hbm, pr_hbm, pair_hbm, count, s0, s1, lhs0, lhs1, rank0, rank1, pts_ref, nv_ref, pr_ref, flags, tab,
    pair, plan_ref, sems
):
    copies = [
        pltpu.make_async_copy(src, dst, sems.at[k])
        for k, (src, dst) in enumerate(
            ((pts_hbm, pts_ref), (nv_hbm, nv_ref), (pr_hbm, pr_ref), (pair_hbm, pair))
        )
    ]
    for copy in copies:
        copy.start()
    copies[0].wait()
    for blk, rank_ref in enumerate((rank0, rank1)):
        rank_ref[...] = rank_of(pts_ref[1:2, blk * BLK : (blk + 1) * BLK])
    for copy in copies[1:]:
        copy.wait()
    for local in range(2):
        for ahead in range(2):
            flags[2 * local + ahead] = live_flag(pair, count, local, ahead)
    position = lax.shift_right_logical(pair[0, 0], 1)
    flags[4] = jnp.bitwise_and(position, 1)
    flags[5] = jnp.where(position > 0, 1, 0)
    place = places()
    for blk, (out_ref, rank_ref) in enumerate(((s0, rank0), (s1, rank1))):
        cols = slice(blk * BLK, (blk + 1) * BLK)
        aux = jnp.concatenate(
            [pts_ref[0:3, cols] * 2.0, nv_ref[:, cols], jnp.zeros((4, BLK), f32)], axis=0
        )
        data = jnp.concatenate(
            [*split3(pr_ref[:, cols]), *split3(aux), jnp.zeros((8, BLK), f32)], axis=0
        ).astype(bf16)
        rank = rank_ref[...]
        centre = 0.5 * (jnp.min(aux, axis=1, keepdims=True) + jnp.max(aux, axis=1, keepdims=True))
        centre = jnp.concatenate([jnp.zeros((4, 1), f32), centre[0:3], jnp.zeros((1, 1), f32)], axis=0)
        for g in range(STRIPS):
            marked = marks(rank, g)
            got = None
            for c in range(STRIPS):
                part = nt(data[:, c * STRIP : (c + 1) * STRIP], one_hot(marked, c, place))
                got = part if got is None else got + part
            here = slice(g * STRIP, (g + 1) * STRIP)
            out_ref[0:16, here] = (got[0:16] + got[16:32]) + got[32:48]
            out_ref[16:24, here] = ((got[48:56] + got[56:64]) + got[64:72]) + centre
    plan_ref[0:8, :] = plan(s0, s0, flags[0], True)
    plan_ref[8:16, :] = plan(s0, s1, flags[1], False)
    plan_ref[16:24, :] = plan(s1, s1, flags[2], True)
    copy = pltpu.make_async_copy(plan_ref, tab, sems.at[0])
    copy.start()
    for side, lhs_ref in ((s0, lhs0), (s1, lhs1)):
        rows, _ = features(offset_of(side, side), True)
        rows = rows.astype(bf16)
        for c in range(STRIPS):
            here = slice(c * STRIP, (c + 1) * STRIP)
            lhs_ref[here, :] = turned(rows[:, here])
    copy.wait()


def offset_of(side_ref, centre_ref):
    centre = jnp.concatenate([centre_ref[20:23, 0:1], jnp.zeros((5, 1), f32)], axis=0)
    return jnp.where(row_id(BLK) < 3, side_ref[16:24, :] - centre, 0.0)


def live_flag(pair_ref, count_ref, local, ahead):
    flag = jnp.int32(0)
    for s in range(pair_ref.shape[1]):
        owner = pair_ref[0, s]
        match = (
            (jnp.int32(s) < count_ref[0])
            & (jnp.bitwise_and(owner, 1) == local)
            & (pair_ref[1, s] - owner == ahead)
        )
        flag = jnp.where(match, jnp.int32(1), flag)
    return flag


def kernel_values(squared):
    squared = jnp.maximum(squared, 1e-30)
    t = jnp.maximum(1.0 - squared * lax.rsqrt(squared), 0.0)
    t2 = t * t
    return ((t2 * t2) * (1.25 - t)).astype(bf16)


def tile_by_difference(row_side, row_at, col_side, col_at):
    squared = None
    for axis in range(16, 19):
        mine = jnp.broadcast_to(row_side[axis : axis + 1, pl.ds(row_at, SUB)], (SUB, SUB)).T
        diff = mine - col_side[axis : axis + 1, pl.ds(col_at, SUB)]
        part = diff * diff
        squared = part if squared is None else squared + part
    return kernel_values(squared)


def fast_strip(k_ref, i, lhs, rhs, start, width):
    for h in range(width // STRIP):
        right = rhs[:, pl.ds(start + h * STRIP, STRIP)]
        for g in range(STRIP // SUB):
            rows = slice(i * STRIP + g * SUB, i * STRIP + (g + 1) * SUB)
            k_ref[i, g * SUB : (g + 1) * SUB, h * STRIP : (h + 1) * STRIP] = kernel_values(nn(lhs[rows, :], right))


def slow_build(k_ref, row_side, col_side, first_group, groups):
    def strip(i, carry):
        def tile(j, carry):
            for g in range(STRIP // SUB):
                at = pl.multiple_of(i * STRIP + g * SUB, SUB)
                col_at = pl.multiple_of(jnp.minimum(first_group(i) + j, SUBS - 1) * SUB, SUB)
                k_ref[i, g * SUB : (g + 1) * SUB, pl.ds(pl.multiple_of(j * SUB, SUB), SUB)] = (
                    tile_by_difference(row_side, at, col_side, col_at)
                )
            return carry

        return lax.fori_loop(0, groups, tile, carry)

    lax.fori_loop(0, STRIPS, strip, 0)


def right_features(rhs, row_side, col_side):
    offset = offset_of(col_side, row_side)
    rows, norm = features(offset, False)
    rhs[...] = rows.astype(bf16)
    offset = offset_of(row_side, row_side)
    return jnp.maximum(jnp.max(norm), jnp.max(jnp.sum(offset * offset, axis=0, keepdims=True))) <= 100.0


def off_pair(k_ref, tab_ref, base, lhs, rhs, row_side, col_side, v_row, v_col, acc_row, acc_col):
    near = right_features(rhs, row_side, col_side)

    @pl.when(near)
    def _():
        for i in range(STRIPS):
            start = pl.multiple_of(tab_ref[base + i, T_START] * SUB, SUB)
            fast_strip(k_ref, i, lhs, rhs, start, OFF_W)
            owner_strip(k_ref, i, start, v_col, acc_row)
            partner_strip(k_ref, i, start, v_row, acc_col)

    @pl.when(jnp.logical_not(near))
    def _():
        slow_build(k_ref, row_side, col_side, lambda i: tab_ref[base + i, T_START], OFF_SUBS)
        to_owner(k_ref, tab_ref, base, v_col, acc_row)
        to_partner(k_ref, tab_ref, base, v_row, acc_col)

    return near, lhs, rhs


def diag_pair(k_ref, lhs, rhs, side, v, acc):
    near = right_features(rhs, side, side)

    @pl.when(near)
    def _():
        for i in range(STRIPS):
            fast_strip(k_ref, i, lhs, rhs, i * STRIP, min(DIAG_W, BLK - i * STRIP))
            diag_strip(k_ref, i, v, acc)

    @pl.when(jnp.logical_not(near))
    def _():
        slow_build(k_ref, side, side, lambda i: 2 * i, DIAG_W // SUB)
        diag_products(k_ref, v, acc)


def owner_strip(k_ref, i, start, v_col, acc_row):
    acc_row[:, i * STRIP : (i + 1) * STRIP] += halves(nt(v_col[:, pl.ds(start, OFF_W)], k_ref[i]))


def partner_strip(k_ref, i, start, v_row, acc_col):
    acc_col[:, pl.ds(start, OFF_W)] += halves(nn(v_row[:, i * STRIP : (i + 1) * STRIP], k_ref[i]))


def to_owner(k_ref, tab_ref, base, v_col, acc_row):
    for i in range(STRIPS):
        owner_strip(k_ref, i, pl.multiple_of(tab_ref[base + i, T_START] * SUB, SUB), v_col, acc_row)


def to_partner(k_ref, tab_ref, base, v_row, acc_col):
    for i in range(STRIPS):
        partner_strip(k_ref, i, pl.multiple_of(tab_ref[base + i, T_START] * SUB, SUB), v_row, acc_col)


def diag_strip(k_ref, i, v_ref, acc_ref):
    width = min(DIAG_W, BLK - i * STRIP)
    here = slice(i * STRIP, (i + 1) * STRIP)
    acc_ref[:, here] += halves(nt(v_ref[:, i * STRIP : i * STRIP + width], k_ref[i, :, :width]))
    if width > STRIP:
        after = slice((i + 1) * STRIP, i * STRIP + width)
        acc_ref[:, after] += halves(nn(v_ref[:, here], k_ref[i, :, STRIP:width]))


def diag_products(k_ref, v_ref, acc_ref):
    for i in range(STRIPS):
        diag_strip(k_ref, i, v_ref, acc_ref)


def extra_tiles(
    tab_ref, base, row_side, col_side, tile_ref, v_row, v_col, acc_row, acc_col, kept=None, fill=None
):
    @pl.when(tab_ref[base, T_EXTRA] > 0)
    def _():
        def strip(i, carry):
            here = pl.ds(pl.multiple_of(i * STRIP, STRIP), STRIP)
            first = tab_ref[base + i, T_START] + OFF_SUBS

            def tile(j, carry):
                col_at = pl.multiple_of(j * SUB, SUB)
                there = pl.ds(col_at, SUB)

                def by_difference():
                    for g in range(STRIP // SUB):
                        row_at = pl.multiple_of(i * STRIP + g * SUB, SUB)
                        tile_ref[g * SUB : (g + 1) * SUB, :] = tile_by_difference(row_side, row_at, col_side, col_at)

                if kept is None:
                    by_difference()
                elif fill is None:
                    pl.when(j > first)(by_difference)

                    @pl.when(j == first)
                    def _():
                        tile_ref[...] = kept[i]
                else:
                    near, lhs, rhs = fill
                    pl.when(jnp.logical_not(near))(by_difference)

                    @pl.when(near)
                    def _():
                        tile_ref[...] = kernel_values(nn(lhs[here, :], rhs[:, there]))

                    @pl.when(j == first)
                    def _():
                        kept[i] = tile_ref[...]

                if acc_row is not None:
                    acc_row[:, here] += halves(nt(v_col[:, there], tile_ref[...]))
                if acc_col is not None:
                    acc_col[:, there] += halves(nn(v_row[:, here], tile_ref[...]))
                return carry

            return lax.fori_loop(first, tab_ref[base + i, T_END], tile, carry)

        lax.fori_loop(0, STRIPS, strip, 0)


TILE = pltpu.VMEM((STRIP, SUB), bf16)
SPLIT = pltpu.VMEM((2 * N_PROBES, BLK), bf16)
FIELD = (N_PROBES, BLK)


def call(body, outs, ins, out_specs, scratch, flops, name, limit=12):
    def run(*args):
        return pl.pallas_call(
            body,
            out_shape=outs,
            in_specs=ins,
            out_specs=out_specs,
            scratch_shapes=scratch,
            compiler_params=pltpu.CompilerParams(vmem_limit_bytes=limit * MIB),
            cost_estimate=pl.CostEstimate(flops=flops, bytes_accessed=MIB, transcendentals=0),
            name=name,
        )(*args)

    return run


def diag_build_kernel(
    tab, s0, s1, lhs0, lhs1, k00, k11, acc0, acc1, tile, v0, v1, rhs
):
    acc0[...] = jnp.zeros(FIELD, f32)
    acc1[...] = jnp.zeros(FIELD, f32)
    v0[...] = split2(s0[0:16, :])
    v1[...] = split2(s1[0:16, :])

    @pl.when(tab[0, T_LIVE] > 0)
    def _():
        diag_pair(k00, lhs0, rhs, s0, v0, acc0)
        extra_tiles(tab, 0, s0, s0, tile, v0, v0, acc0, acc0)

    @pl.when(tab[16, T_LIVE] > 0)
    def _():
        diag_pair(k11, lhs1, rhs, s1, v1, acc1)
        extra_tiles(tab, 16, s1, s1, tile, v1, v1, acc1, acc1)


def halo_build_kernel(
    flags, s1, lhs1, got_a, got_b, acc1_in, k12, x12, tab, acc1, back, halo, plan_ref, tile, v1, v2, rhs, sem
):
    halo[...] = jnp.where(flags[4] == 0, got_a[...], got_b[...])
    plan_ref[...] = plan(s1, halo, flags[3], False)
    copy = pltpu.make_async_copy(plan_ref, tab, sem.at[0])
    copy.start()
    acc1[...] = acc1_in[...]
    back[...] = jnp.zeros(FIELD, f32)
    copy.wait()

    @pl.when(flags[3] > 0)
    def _():
        v1[...] = split2(s1[0:16, :])
        v2[...] = split2(halo[0:16, :])
        fill = off_pair(k12, tab, 0, lhs1, rhs, s1, halo, v1, v2, acc1, back)
        extra_tiles(tab, 0, s1, halo, tile, v1, v2, acc1, back, x12, fill)


def own_build_kernel(tab, s0, s1, lhs0, acc0_in, acc1_in, k01, x01, acc0, acc1, tile, v0, v1, rhs):
    base = STRIPS
    acc0[...] = acc0_in[...]
    acc1[...] = acc1_in[...]

    @pl.when(tab[base, T_LIVE] > 0)
    def _():
        v0[...] = split2(s0[0:16, :])
        v1[...] = split2(s1[0:16, :])
        fill = off_pair(k01, tab, base, lhs0, rhs, s0, s1, v0, v1, acc0, acc1)
        extra_tiles(tab, base, s0, s1, tile, v0, v1, acc0, acc1, x01, fill)


def own_apply_kernel(tab, k00, k01, x01, k11, s0, s1, w0, w1, acc0, acc1, tile, v0, v1):
    acc0[...] = jnp.zeros(FIELD, f32)
    acc1[...] = jnp.zeros(FIELD, f32)
    v0[...] = split2(w0[...])
    v1[...] = split2(w1[...])

    @pl.when(tab[0, T_LIVE] > 0)
    def _():
        diag_products(k00, v0, acc0)
        extra_tiles(tab, 0, s0, s0, tile, v0, v0, acc0, acc0)

    @pl.when(tab[8, T_LIVE] > 0)
    def _():
        to_owner(k01, tab, 8, v1, acc0)
        to_partner(k01, tab, 8, v0, acc1)
        extra_tiles(tab, 8, s0, s1, tile, v0, v1, acc0, acc1, x01)

    @pl.when(tab[16, T_LIVE] > 0)
    def _():
        diag_products(k11, v1, acc1)
        extra_tiles(tab, 16, s1, s1, tile, v1, v1, acc1, acc1)


def from_left(flags, got_a, got_b):
    arrived = jnp.where(flags[4] == 0, got_b[...], got_a[...])
    return jnp.where(flags[5] > 0, arrived, 0.0)


def inner(left, right):
    product = left * right
    return jnp.sum(product, axis=1, keepdims=True)


def finish_kernel(
    level, flags, tab, k12, x12, s0, s1, halo, got_a, got_b, acc0, acc1, w0, w1, mom_in,
    n0, n1, send_a, send_b, mom, tile, v1, v2, acc, back
):
    live = tab[0, T_LIVE] > 0
    acc[...] = acc1[...]
    if level > 1:

        @pl.when(live)
        def _():
            v2[...] = split2(jnp.where(flags[4] == 0, got_a[...], got_b[...]))
            to_owner(k12, tab, 0, v2, acc)
            extra_tiles(tab, 0, s1, halo, tile, None, v2, acc, None, x12)

    before0 = w0[0:16, :]
    before1 = w1[0:16, :]
    next1 = s1[19:20, :] * before1 + acc[...]
    n1[...] = next1
    back[...] = jnp.zeros(FIELD, f32)

    @pl.when(live)
    def _():
        v1[...] = split2(next1)
        to_partner(k12, tab, 0, v1, back)
        extra_tiles(tab, 0, s1, halo, tile, v1, None, None, back, x12)

    arrived = from_left(flags, got_a, got_b)
    next0 = s0[19:20, :] * before0 + (acc0[...] + arrived)
    n0[...] = next0
    send_a[...] = jnp.where(flags[4] == 0, back[...], next0)
    send_b[...] = jnp.where(flags[4] == 0, next0, back[...])
    lane = lax.broadcasted_iota(jnp.int32, (N_PROBES, SUB), 1)
    cross = inner(before0, next0) + inner(before1, next1)
    own = inner(next0, next0) + inner(next1, next1)
    total = jnp.where(lane == 2 * level - 1, cross, jnp.where(lane == 2 * level, own, 0.0))
    if level == 1:
        total = jnp.where(lane == 0, inner(before0, before0) + inner(before1, before1), total)
    else:
        total = total + mom_in[...]
    mom[...] = total


def moment_kernel(flags, s0, s1, acc0, acc1, got_a, got_b, w0, w1, mom_in, mom):
    lane = lax.broadcasted_iota(jnp.int32, (N_PROBES, SUB), 1)
    one = w0[...]
    two = w1[...]
    arrived = from_left(flags, got_a, got_b)
    cross = inner(one, s0[19:20, :] * one + (acc0[...] + 2.0 * arrived))
    cross = cross + inner(two, s1[19:20, :] * two + acc1[...])
    mom[...] = mom_in[...] + jnp.where(lane == 5, cross, 0.0)


def last_kernel(flags, tab, k12, x12, s0, s1, halo, got_a, got_b, acc0, acc1, w0, w1, n0, n1, tile, v2):
    arrived = from_left(flags, got_a, got_b)
    n1[...] = s1[19:20, :] * w1[...] + acc1[...]
    n0[...] = s0[19:20, :] * w0[...] + (acc0[...] + arrived)

    @pl.when(tab[0, T_LIVE] > 0)
    def _():
        v2[...] = split2(jnp.where(flags[4] == 0, got_a[...], got_b[...]))
        to_owner(k12, tab, 0, v2, n1)
        extra_tiles(tab, 0, s1, halo, tile, None, v2, n1, None, x12)


def unsort_kernel(blk, rank_ref, probes, wa, wb, wc, out):
    out[48:64, :] = probes[:, blk * BLK : (blk + 1) * BLK]
    stacked = jnp.concatenate([split2(wa[...]), split2(wb[...]), split2(wc[...])], axis=0)
    rank = rank_ref[...]
    place = places()
    marked = [marks(rank, g) for g in range(STRIPS)]
    for c in range(STRIPS):
        here = slice(c * STRIP, (c + 1) * STRIP)
        got = None
        for g in range(STRIPS):
            part = nn(stacked[:, g * STRIP : (g + 1) * STRIP], one_hot(marked[g], c, place))
            got = part if got is None else got + part
        for k in range(3):
            out[16 * k : 16 * (k + 1), here] = halves(got[32 * k : 32 * (k + 1)])


def steps_kernel(mom, out, sound):
    lane = lax.broadcasted_iota(jnp.int32, (N_PROBES, SUB), 1)
    mu = [jnp.sum(jnp.where(lane == k, mom[...], 0.0), axis=1, keepdims=True) for k in range(6)]
    fine = []

    def form(left, right, shift):
        total, size = None, None
        for i, a in enumerate(left):
            for j, b in enumerate(right):
                part = (a * b) * mu[i + j + shift]
                total = part if total is None else total + part
                size = jnp.abs(part) if size is None else size + jnp.abs(part)
        fine.append(size <= 4000.0 * total)
        return total

    one = jnp.ones((N_PROBES, 1), f32)
    d = [one]
    r = [one]
    s = []
    rr = mu[0]
    for it in range(3):
        step = rr / form(d, d, 1)
        moved = [step * v for v in d]
        s = [a + b for a, b in zip(s + [0.0] * (len(d) - len(s)), moved)]
        r = [r[0]] + [(r[i] if i < len(r) else 0.0) - moved[i - 1] for i in range(1, len(moved) + 1)]
        if it < 2:
            new = form(r, r, 0)
            ratio = new / rr
            d = [r[i] + (ratio * d[i] if i < len(d) else 0.0) for i in range(len(r))]
            rr = new
    norms = [jnp.sqrt(mu[0]), jnp.sqrt(mu[2]), jnp.sqrt(mu[4])]
    norms.append(mu[5] / norms[2])
    size = sum(jnp.abs(a) * b for a, b in zip(r, norms))
    fine.append(size <= 200.0 * jnp.sqrt(rr))
    all_fine = fine[0]
    for other in fine[1:]:
        all_fine = all_fine & other
    sound[0] = jnp.min(jnp.where(all_fine, 1.0, 0.0)).astype(jnp.int32)
    table = jnp.zeros((N_PROBES, SUB), f32)
    for k, value in enumerate(s + r):
        table = jnp.where(lane == k, value, table)
    out[...] = table


def combine_kernel(steps, u0, u1, sol, res):
    c = [steps[:, k : k + 1] for k in range(7)]
    for b, u in ((0, u0), (1, u1)):
        here = slice(b * BLK, (b + 1) * BLK)
        w = [u[48:64, :], u[0:16, :], u[16:32, :], u[32:48, :]]
        sol[:, here] = (c[0] * w[0] + c[1] * w[1]) + c[2] * w[2]
        res[:, here] = ((c[3] * w[0] + c[4] * w[1]) + c[5] * w[2]) + c[6] * w[3]


def plain_steps(points, noise_var, probes, pair_list, counts):
    def block_of(value, index):
        return lax.dynamic_slice_in_dim(value, index * BLK, BLK, 1)

    def add_into(value, piece, index):
        return lax.dynamic_update_slice_in_dim(value, block_of(value, index) + piece, index * BLK, 1)

    def kernel_block(left, right):
        squared = (left[0][:, None] - right[0][None, :]) ** 2
        squared = squared + (left[1][:, None] - right[1][None, :]) ** 2
        squared = squared + (left[2][:, None] - right[2][None, :]) ** 2
        distance = jnp.sqrt(squared) / 0.5
        remain = jnp.maximum(1.0 - distance, 0.0)
        return (0.25 * remain**4 * (4.0 * distance + 1.0)).astype(bf16)

    count = lax.axis_size("gx")
    to_left = [(k, k - 1) for k in range(1, count)]
    to_right = [(k, k + 1) for k in range(count - 1)]
    width = points.shape[1]
    first = lax.axis_index("gx") * (width // BLK)
    nearby_points = jnp.concatenate([points, lax.ppermute(points, "gx", to_left)], axis=1)

    def product(direction):
        rounded = direction.astype(bf16)
        nearby = jnp.concatenate([rounded, lax.ppermute(rounded, "gx", to_left)], axis=1)

        def one_pair(slot, running):
            owner, partner = pair_list[slot, 0] - first, pair_list[slot, 1] - first
            block = kernel_block(block_of(nearby_points, owner), block_of(nearby_points, partner))
            running = add_into(running, nt(block_of(nearby, partner), block), owner)
            piece = nn(block_of(nearby, owner), block)
            return add_into(running, jnp.where(partner != owner, piece, 0.0), partner)

        running = jnp.zeros((N_PROBES, 2 * width), f32)
        running = lax.fori_loop(0, counts[0], one_pair, running)
        arrived = lax.ppermute(running[:, width:], "gx", to_right)
        return noise_var[None, :] * direction + (running[:, :width] + arrived)

    def step(_, state):
        solution, residual, direction, norm = state
        image = product(direction)
        size = norm / lax.psum(jnp.sum(direction * image, axis=1), "gx")
        solution = solution + size[:, None] * direction
        residual = residual - size[:, None] * image
        new = lax.psum(jnp.sum(residual * residual, axis=1), "gx")
        return solution, residual, residual + (new / norm)[:, None] * direction, new

    norm = lax.psum(jnp.sum(probes * probes, axis=1), "gx")
    return lax.fori_loop(0, 3, step, (jnp.zeros_like(probes), probes, probes, norm))[:2]


def swapped_both(to_a, to_b):
    count = lax.axis_size("gx")
    a = lax.ppermute(to_a, "gx", [(k, k ^ 1) for k in range(count)])
    ends = [(0, 0), (count - 1, count - 1)]
    b = lax.ppermute(to_b, "gx", ends + [(k, ((k + 1) ^ 1) - 1) for k in range(1, count - 1)])
    return a, b


def sum_over(value, axis):
    count = lax.axis_size(axis)
    if count & (count - 1):
        return lax.psum(value, axis)
    step = 1
    while step < count:
        radix = min(4, count // step)
        parts = [value] + [
            lax.ppermute(value, axis, [(k, k ^ (m * step)) for k in range(count)]) for m in range(1, radix)
        ]
        while len(parts) > 1:
            parts = [parts[m] + parts[m + 1] for m in range(0, len(parts), 2)]
        value = parts[0]
        step *= radix
    return value


def on_device(points, noise_var, probes, pair_list, counts):
    noise = noise_var.reshape(1, -1)
    field = pltpu.VMEM(FIELD, f32)
    side = pltpu.VMEM((24, BLK), f32)
    left = pltpu.VMEM((BLK, N_FEATURES), bf16)
    right = pltpu.VMEM((N_FEATURES, BLK), bf16)
    table = pltpu.SMEM((STRIPS, SUB), jnp.int32)
    tables = pltpu.SMEM((3 * STRIPS, SUB), jnp.int32)
    ranks = pltpu.VMEM((1, BLK), jnp.int32)
    far_space = pl.BlockSpec(memory_space=pltpu.HBM)
    s0, s1, lhs0, lhs1, rank0, rank1, points, noise, probes, flags, tabb = call(
        sort_kernel,
        (side, side, left, left, ranks, ranks)
        + tuple(jax.ShapeDtypeStruct(x.shape, f32) for x in (points, noise, probes))
        + (pltpu.SMEM((6,), jnp.int32), tables),
        [far_space] * 4 + [SMEM],
        (VMEM,) * 9 + (SMEM,) * 2,
        [
            pltpu.SMEM(pair_list.shape[::-1], jnp.int32),
            pltpu.VMEM((3 * STRIPS, SUB), jnp.int32),
            pltpu.SemaphoreType.DMA((4,)),
        ],
        10**9,
        "sort_blocks",
    )(*[pltpu.with_memory_space_constraint(x, pltpu.HBM) for x in (points, noise, probes, pair_list.T)], counts)

    halos = swapped_both(s0, s0)
    off = pltpu.VMEM((STRIPS, STRIP, OFF_W), bf16)
    diag = pltpu.VMEM((STRIPS, STRIP, DIAG_W), bf16)
    outside = pltpu.VMEM((STRIPS, STRIP, SUB), bf16)
    k00, k11, acc0, acc1 = call(
        diag_build_kernel,
        (diag, diag, field, field),
        [SMEM] + [VMEM] * 4,
        (VMEM,) * 4,
        [TILE, SPLIT, SPLIT, right],
        3 * 10**9,
        "diag_build",
    )(tabb, s0, s1, lhs0, lhs1)
    k12, x12, tabc, acc1, back, halo = call(
        halo_build_kernel,
        (off, outside, table, field, field, side),
        [SMEM] + [VMEM] * 5,
        (VMEM, VMEM, SMEM, VMEM, VMEM, VMEM),
        [pltpu.VMEM((STRIPS, SUB), jnp.int32), TILE, SPLIT, SPLIT, right, pltpu.SemaphoreType.DMA((1,))],
        3 * 10**9,
        "halo_build",
    )(flags, s1, lhs1, *halos, acc1)
    got = swapped_both(back, back)
    k01, x01, acc0, acc1 = call(
        own_build_kernel,
        (off, outside, field, field),
        [SMEM] + [VMEM] * 5,
        (VMEM,) * 4,
        [TILE, SPLIT, SPLIT, right],
        5 * 10**9,
        "own_build",
    )(tabb, s0, s1, lhs0, acc0, acc1)

    w0, w1 = s0, s1
    moments = pltpu.VMEM((N_PROBES, SUB), f32)
    mom = jnp.zeros((N_PROBES, SUB), f32)
    kept = []
    for level in (1, 2):
        w0, w1, send_a, send_b, mom = call(
            functools.partial(finish_kernel, level),
            (field,) * 4 + (moments,),
            [SMEM] * 2 + [VMEM] * 12,
            (VMEM,) * 5,
            [TILE, SPLIT, SPLIT, pltpu.VMEM(FIELD, f32), pltpu.VMEM(FIELD, f32)],
            10**9,
            "finish",
        )(flags, tabc, k12, x12, s0, s1, halo, *got, acc0, acc1, w0, w1, mom)
        kept.append((w0, w1))
        got = swapped_both(send_a, send_b)
        acc0, acc1 = call(
            own_apply_kernel,
            (field, field),
            [SMEM] + [VMEM] * 8,
            (VMEM, VMEM),
            [TILE, SPLIT, SPLIT],
            2 * 10**9,
            "own_apply",
        )(tabb, k00, k01, x01, k11, s0, s1, w0, w1)
    mom = call(moment_kernel, moments, [SMEM] + [VMEM] * 9, VMEM, [], 10**7, "moment")(
        flags, s0, s1, acc0, acc1, *got, w0, w1, mom
    )
    total = sum_over(mom, "gx")
    kept.append(
        call(last_kernel, (field, field), [SMEM] * 2 + [VMEM] * 11, (VMEM, VMEM), [TILE, SPLIT], 10**9, "last")(
            flags, tabc, k12, x12, s0, s1, halo, *got, acc0, acc1, w0, w1
        )
    )
    given = []
    for b, rank in ((0, rank0), (1, rank1)):
        given.append(
            call(
                functools.partial(unsort_kernel, b),
                pltpu.VMEM((4 * N_PROBES, BLK), f32),
                [VMEM] * 5,
                VMEM,
                [],
                2 * 96 * BLK * BLK,
                "unsort",
            )(rank, probes, *[pair[b] for pair in kept])
        )
    steps, sound = call(
        steps_kernel,
        (moments, pltpu.SMEM((1,), jnp.int32)),
        [VMEM],
        (VMEM, SMEM),
        [],
        10**6,
        "steps",
    )(total)

    def from_basis():
        return tuple(
            call(
                combine_kernel,
                (jax.ShapeDtypeStruct(probes.shape, f32),) * 2,
                [VMEM] * 3,
                (VMEM, VMEM),
                [],
                10**6,
                "combine",
                48,
            )(steps, *given)
        )

    def from_start():
        return tuple(plain_steps(points, noise[0], probes, pair_list, counts))

    return lax.cond(sound[0] > 0, from_basis, from_start)


def solution(mesh):
    placed = (
        P(None, ("groups", "gx")),
        P(("groups", "gx")),
        P(None, ("groups", "gx")),
        P(("groups", "gx"), None),
        P(("groups", "gx")),
    )
    return jax.shard_map(
        on_device,
        mesh=mesh,
        in_specs=placed,
        out_specs=(P(None, ("groups", "gx")), P(None, ("groups", "gx"))),
        check_vma=False,
    )
```

```python
import functools

import jax
import jax.numpy as jnp
from jax import lax
from jax.experimental import pallas as pl
from jax.experimental.pallas import tpu as pltpu
from jax.sharding import PartitionSpec as P

BLK = 2048
STRIP = 256
STRIPS = BLK // STRIP
SUB = 128
SUBS = BLK // SUB
OFF_W = 768
OFF_SUBS = OFF_W // SUB
DIAG_W = 512
N_PROBES = 16
N_FEATURES = 64
UNROLL = 2
MIB = 1 << 20

VMEM = pl.BlockSpec(memory_space=pltpu.VMEM)
SMEM = pl.BlockSpec(memory_space=pltpu.SMEM)

f32 = jnp.float32
bf16 = jnp.bfloat16

T_START, T_END, T_EXTRA, T_LIVE = 0, 1, 2, 3


def nt(left, right):
    return lax.dot_general(left, right, (((1,), (1,)), ((), ())), preferred_element_type=f32)


def nn(left, right):
    return jnp.dot(left, right, preferred_element_type=f32)


def split2(value):
    high = value.astype(bf16)
    low = (value - high.astype(f32)).astype(bf16)
    return jnp.concatenate([high, low], axis=0)


def halves(value):
    n = value.shape[0] // 2
    return value[:n] + value[n:]


def split3(value):
    high = value.astype(bf16).astype(f32)
    rest = value - high
    mid = rest.astype(bf16).astype(f32)
    return high, mid, rest - mid


def at(index, size):
    return pl.ds(pl.multiple_of(index * size, size), size)


def one_hot(marked, place):
    parts = []
    for h in range(2):
        hit = jnp.broadcast_to(marked[:, h * SUB : (h + 1) * SUB], (STRIP, SUB)) == place
        parts.append(jnp.where(hit, jnp.ones((STRIP, SUB), bf16), jnp.zeros((STRIP, SUB), bf16)))
    return jnp.concatenate(parts, axis=1)


def places():
    return lax.broadcasted_iota(jnp.int32, (STRIP, SUB), 0).astype(f32).astype(bf16)


def marks(rank, g):
    group = lax.shift_right_logical(rank, 8)
    within = jnp.bitwise_and(rank, STRIP - 1)
    return jnp.where(group == g, within, -1).astype(f32).astype(bf16)


def turned(value):
    shape = (STRIP, STRIP)
    same = lax.broadcasted_iota(jnp.int32, shape, 0) == lax.broadcasted_iota(jnp.int32, shape, 1)
    return nt(jnp.where(same, 1.0, 0.0).astype(bf16), value).astype(bf16)


def fill_ranks(y_row, rank_ref, key_ref, before_ref):
    low = jnp.min(y_row, axis=1, keepdims=True)
    high = jnp.max(y_row, axis=1, keepdims=True)
    scale = 255.0 / jnp.maximum(high - low, 1e-6)
    key_ref[...] = jnp.clip(jnp.floor((y_row - low) * scale), 0.0, 255.0)
    shape = (STRIP, STRIP)
    first = lax.broadcasted_iota(jnp.int32, shape, 0)
    second = lax.broadcasted_iota(jnp.int32, shape, 1)
    upper = jnp.where(first < second, 1.0, 0.0).astype(bf16)
    lower = jnp.where(second < first, 1.0, 0.0).astype(bf16)
    ones = jnp.ones((STRIP, SUB), bf16)
    value = places()
    before_ref[...] = jnp.zeros((STRIP, SUB), f32)

    def count(j, carry):
        before_ref[...] += nn(one_hot(key_ref[:, at(j, STRIP)].astype(bf16), value), ones)
        return carry

    lax.fori_loop(0, STRIPS, count, 0, unroll=2)
    total = before_ref[...]
    coarse = jnp.floor(total * (1.0 / 16.0)) * 16.0
    before_ref[...] = nn(lower, coarse.astype(bf16)) + nn(lower, (total - coarse).astype(bf16))

    def place(j, carry):
        hit = one_hot(key_ref[:, at(j, STRIP)].astype(bf16), value)
        before = before_ref[...]
        ahead = nn(hit, upper) + jnp.concatenate([before, before], axis=1)
        rank = jnp.sum(hit.astype(f32) * ahead, axis=0, keepdims=True)
        rank_ref[:, at(j, STRIP)] = rank.astype(jnp.int32)
        before_ref[...] = before + nn(hit, ones)
        return carry

    lax.fori_loop(0, STRIPS, place, 0)


def plan(row_side, col_side, live, diag):
    y_row = row_side[17:18, :]
    y_col = col_side[17:18, :]
    strips = jnp.concatenate([y_row[:, i * STRIP : (i + 1) * STRIP] for i in range(STRIPS)], axis=0)
    low = jnp.min(strips, axis=1, keepdims=True) - 1.0
    high = jnp.max(strips, axis=1, keepdims=True) + 1.0
    groups = jnp.concatenate([y_col[:, j * SUB : (j + 1) * SUB] for j in range(SUBS)], axis=0)
    own = lax.broadcasted_iota(jnp.int32, (SUBS, SUB), 0) == lax.broadcasted_iota(jnp.int32, (SUBS, SUB), 1)

    def across(value):
        return jnp.sum(jnp.where(own, value, 0.0), axis=0, keepdims=True)

    group_low = across(jnp.min(groups, axis=1, keepdims=True))
    group_high = across(jnp.max(groups, axis=1, keepdims=True))
    lane = lax.broadcasted_iota(jnp.int32, (STRIPS, SUB), 1)
    place = lane.astype(f32)
    reached = (group_low < high) & (group_high > low) & (lane < SUBS)
    end = jnp.max(jnp.where(reached, place + 1.0, 0.0), axis=1, keepdims=True)
    if diag:
        start = lax.broadcasted_iota(jnp.int32, (STRIPS, 1), 0).astype(f32) * 2.0 + (DIAG_W // SUB - OFF_SUBS)
    else:
        first = jnp.min(jnp.where(reached, place, float(SUBS)), axis=1, keepdims=True)
        start = jnp.minimum(first, float(SUBS - OFF_SUBS))
    extra = jnp.sum(jnp.maximum(end - (start + OFF_SUBS), 0.0), axis=0, keepdims=True)
    alive = live.astype(f32)
    table = jnp.where(lane == T_START, start, jnp.where(lane == T_END, end, extra))
    return jnp.where(lane == T_LIVE, alive, table).astype(jnp.int32)


def row_id(width):
    return lax.broadcasted_iota(jnp.int32, (8, width), 0)


def features(offset, left):
    first, second, third = split3(offset)
    norm = jnp.sum(offset * offset, axis=0, keepdims=True)
    n1, n2, n3 = split3(norm)
    ids = row_id(offset.shape[1])
    own, other = (0, 3) if left else (3, 0)
    norms = jnp.where(ids == own, n1, jnp.where(ids == own + 1, n2, jnp.where(ids == own + 2, n3, 0.0)))
    norms = jnp.where((ids >= other) & (ids < other + 3), 1.0, norms)
    if left:
        first, second, third = -2.0 * first, -2.0 * second, -2.0 * third
        parts = [first, first, first, second, second, third]
    else:
        parts = [first, second, third, first, second, first]
    return jnp.concatenate(parts + [norms, jnp.zeros_like(norms)], axis=0), norm


def sort_kernel(
    pts_hbm, nv_hbm, pr_hbm, pair_hbm, count, side, first, lhs, rank, pr_ref, flags, tab,
    pts_ref, nv_ref, pair, plan_ref, key_ref, before_ref, data_ref, rows_ref, sems
):
    copies = [
        pltpu.make_async_copy(src, dst, sems.at[k])
        for k, (src, dst) in enumerate(
            ((pts_hbm, pts_ref), (nv_hbm, nv_ref), (pr_hbm, pr_ref), (pair_hbm, pair))
        )
    ]
    for copy in copies:
        copy.start()
    for copy in copies:
        copy.wait()
    for local in range(2):
        for ahead in range(2):
            flags[2 * local + ahead] = live_flag(pair, count, local, ahead)
    position = lax.shift_right_logical(pair[0, 0], 1)
    flags[4] = jnp.bitwise_and(position, 1)
    flags[5] = jnp.where(position > 0, 1, 0)

    def block(blk, carry):
        cols = at(blk, BLK)
        fill_ranks(pts_ref[1:2, cols], rank.at[blk], key_ref, before_ref)
        aux = jnp.concatenate(
            [pts_ref[0:3, cols] * 2.0, nv_ref[:, cols], jnp.zeros((4, BLK), f32)], axis=0
        )
        data_ref[...] = jnp.concatenate(
            [*split3(pr_ref[:, cols]), *split3(aux), jnp.zeros((8, BLK), f32)], axis=0
        ).astype(bf16)
        centre = 0.5 * (jnp.min(aux, axis=1, keepdims=True) + jnp.max(aux, axis=1, keepdims=True))
        centre = jnp.concatenate([jnp.zeros((4, 1), f32), centre[0:3], jnp.zeros((1, 1), f32)], axis=0)
        place = places()

        def strip(g, carry):
            marked = marks(rank[blk], g)
            got = None
            for c in range(STRIPS):
                here = slice(c * STRIP, (c + 1) * STRIP)
                part = nt(data_ref[:, here], one_hot(marked[:, here], place))
                got = part if got is None else got + part
            side[blk, 0:16, at(g, STRIP)] = (got[0:16] + got[16:32]) + got[32:48]
            side[blk, 16:24, at(g, STRIP)] = ((got[48:56] + got[56:64]) + got[64:72]) + centre
            return carry

        lax.fori_loop(0, STRIPS, strip, 0)
        rows, _ = features(offset_of(side.at[blk], side.at[blk]), True)
        rows_ref[...] = rows.astype(bf16)

        def turn(c, carry):
            lhs[blk, at(c, STRIP), :] = turned(rows_ref[:, at(c, STRIP)])
            return carry

        lax.fori_loop(0, STRIPS, turn, 0, unroll=2)
        return carry

    lax.fori_loop(0, 2, block, 0)
    first[...] = side[0]
    plan_ref[0:8, :] = plan(side.at[0], side.at[0], flags[0], True)
    plan_ref[8:16, :] = plan(side.at[0], side.at[1], flags[1], False)
    plan_ref[16:24, :] = plan(side.at[1], side.at[1], flags[2], True)
    pltpu.sync_copy(plan_ref, tab)


def offset_of(side_ref, centre_ref):
    centre = jnp.concatenate([centre_ref[20:23, 0:1], jnp.zeros((5, 1), f32)], axis=0)
    return jnp.where(row_id(BLK) < 3, side_ref[16:24, :] - centre, 0.0)


def live_flag(pair_ref, count_ref, local, ahead):
    flag = jnp.int32(0)
    for s in range(pair_ref.shape[1]):
        owner = pair_ref[0, s]
        match = (
            (jnp.int32(s) < count_ref[0])
            & (jnp.bitwise_and(owner, 1) == local)
            & (pair_ref[1, s] - owner == ahead)
        )
        flag = jnp.where(match, jnp.int32(1), flag)
    return flag


def kernel_values(squared):
    squared = jnp.maximum(squared, 1e-30)
    t = jnp.maximum(1.0 - squared * lax.rsqrt(squared), 0.0)
    t2 = t * t
    return ((t2 * t2) * (1.25 - t)).astype(bf16)


def tile_by_difference(row_side, row_at, col_side, col_at):
    squared = None
    for axis in range(16, 19):
        mine = jnp.broadcast_to(row_side[axis : axis + 1, pl.ds(row_at, SUB)], (SUB, SUB)).T
        diff = mine - col_side[axis : axis + 1, pl.ds(col_at, SUB)]
        part = diff * diff
        squared = part if squared is None else squared + part
    return kernel_values(squared)


def fast_strip(k_ref, i, lhs, rhs, start, width):
    for h in range(width // STRIP):
        right = rhs[:, pl.ds(pl.multiple_of(start + h * STRIP, SUB), STRIP)]
        for g in range(STRIP // SUB):
            left = lhs[pl.ds(pl.multiple_of(i * STRIP + g * SUB, SUB), SUB), :]
            k_ref[i, g * SUB : (g + 1) * SUB, h * STRIP : (h + 1) * STRIP] = kernel_values(nn(left, right))


def slow_build(k_ref, row_side, col_side, first_group, groups):
    def strip(i, carry):
        def tile(j, carry):
            for g in range(STRIP // SUB):
                at = pl.multiple_of(i * STRIP + g * SUB, SUB)
                col_at = pl.multiple_of(jnp.minimum(first_group(i) + j, SUBS - 1) * SUB, SUB)
                k_ref[i, g * SUB : (g + 1) * SUB, pl.ds(pl.multiple_of(j * SUB, SUB), SUB)] = (
                    tile_by_difference(row_side, at, col_side, col_at)
                )
            return carry

        return lax.fori_loop(0, groups, tile, carry)

    lax.fori_loop(0, STRIPS, strip, 0)


def right_features(rhs, row_side, col_side):
    offset = offset_of(col_side, row_side)
    rows, norm = features(offset, False)
    rhs[...] = rows.astype(bf16)
    offset = offset_of(row_side, row_side)
    return jnp.maximum(jnp.max(norm), jnp.max(jnp.sum(offset * offset, axis=0, keepdims=True))) <= 100.0


def off_pair(k_ref, tab_ref, base, lhs, rhs, row_side, col_side, v_row, v_col, acc_row, acc_col):
    near = right_features(rhs, row_side, col_side)

    @pl.when(near)
    def _():
        def strip(i, carry):
            start = pl.multiple_of(tab_ref[base + i, T_START] * SUB, SUB)
            fast_strip(k_ref, i, lhs, rhs, start, OFF_W)
            owner_strip(k_ref, i, start, v_col, acc_row)
            partner_strip(k_ref, i, start, v_row, acc_col)
            return carry

        lax.fori_loop(0, STRIPS, strip, 0, unroll=UNROLL)

    @pl.when(jnp.logical_not(near))
    def _():
        slow_build(k_ref, row_side, col_side, lambda i: tab_ref[base + i, T_START], OFF_SUBS)
        off_products(k_ref, tab_ref, base, v_row, v_col, acc_row, acc_col)

    return near, lhs, rhs


def diag_pair(k_ref, lhs, rhs, side, v, acc):
    near = right_features(rhs, side, side)

    @pl.when(near)
    def _():
        def strip(i, carry):
            fast_strip(k_ref, i, lhs, rhs, i * STRIP, DIAG_W)
            diag_strip(k_ref, i, v, acc, DIAG_W)
            return carry

        lax.fori_loop(0, STRIPS - 1, strip, 0)
        fast_strip(k_ref, STRIPS - 1, lhs, rhs, (STRIPS - 1) * STRIP, STRIP)
        diag_strip(k_ref, STRIPS - 1, v, acc, STRIP)

    @pl.when(jnp.logical_not(near))
    def _():
        slow_build(k_ref, side, side, lambda i: 2 * i, DIAG_W // SUB)
        diag_products(k_ref, v, acc)


def owner_strip(k_ref, i, start, v_col, acc_row):
    acc_row[:, at(i, STRIP)] += halves(nt(v_col[:, pl.ds(start, OFF_W)], k_ref[i]))


def partner_strip(k_ref, i, start, v_row, acc_col):
    acc_col[:, pl.ds(start, OFF_W)] += halves(nn(v_row[:, at(i, STRIP)], k_ref[i]))


def off_products(k_ref, tab_ref, base, v_row, v_col, acc_row, acc_col):
    def strip(i, carry):
        start = pl.multiple_of(tab_ref[base + i, T_START] * SUB, SUB)
        if acc_row is not None:
            owner_strip(k_ref, i, start, v_col, acc_row)
        if acc_col is not None:
            partner_strip(k_ref, i, start, v_row, acc_col)
        return carry

    lax.fori_loop(0, STRIPS, strip, 0, unroll=UNROLL)


def diag_strip(k_ref, i, v_ref, acc_ref, width):
    start = pl.multiple_of(i * STRIP, STRIP)
    acc_ref[:, at(i, STRIP)] += halves(nt(v_ref[:, pl.ds(start, width)], k_ref[i, :, :width]))
    if width > STRIP:
        acc_ref[:, at(i + 1, STRIP)] += halves(nn(v_ref[:, at(i, STRIP)], k_ref[i, :, STRIP:width]))


def diag_products(k_ref, v_ref, acc_ref):
    def strip(i, carry):
        diag_strip(k_ref, i, v_ref, acc_ref, DIAG_W)
        return carry

    lax.fori_loop(0, STRIPS - 1, strip, 0, unroll=UNROLL)
    diag_strip(k_ref, STRIPS - 1, v_ref, acc_ref, STRIP)


def extra_tiles(
    tab_ref, base, row_side, col_side, tile_ref, v_row, v_col, acc_row, acc_col, kept=None, fill=None
):
    @pl.when(tab_ref[base, T_EXTRA] > 0)
    def _():
        def strip(i, carry):
            here = pl.ds(pl.multiple_of(i * STRIP, STRIP), STRIP)
            first = tab_ref[base + i, T_START] + OFF_SUBS

            def tile(j, carry):
                col_at = pl.multiple_of(j * SUB, SUB)
                there = pl.ds(col_at, SUB)

                def by_difference():
                    for g in range(STRIP // SUB):
                        row_at = pl.multiple_of(i * STRIP + g * SUB, SUB)
                        tile_ref[g * SUB : (g + 1) * SUB, :] = tile_by_difference(row_side, row_at, col_side, col_at)

                if kept is None:
                    by_difference()
                elif fill is None:
                    pl.when(j > first)(by_difference)

                    @pl.when(j == first)
                    def _():
                        tile_ref[...] = kept[i]
                else:
                    near, lhs, rhs = fill
                    pl.when(jnp.logical_not(near))(by_difference)

                    @pl.when(near)
                    def _():
                        tile_ref[...] = kernel_values(nn(lhs[here, :], rhs[:, there]))

                    @pl.when(j == first)
                    def _():
                        kept[i] = tile_ref[...]

                if acc_row is not None:
                    acc_row[:, here] += halves(nt(v_col[:, there], tile_ref[...]))
                if acc_col is not None:
                    acc_col[:, there] += halves(nn(v_row[:, here], tile_ref[...]))
                return carry

            return lax.fori_loop(first, tab_ref[base + i, T_END], tile, carry)

        lax.fori_loop(0, STRIPS, strip, 0)


TILE = pltpu.VMEM((STRIP, SUB), bf16)
SPLIT = pltpu.VMEM((2 * N_PROBES, BLK), bf16)
SPLITS = pltpu.VMEM((2, 2 * N_PROBES, BLK), bf16)
FIELD = (N_PROBES, BLK)
FIELDS = (2, N_PROBES, BLK)


def call(body, outs, ins, out_specs, scratch, flops, name, limit=12):
    def run(*args):
        return pl.pallas_call(
            body,
            out_shape=outs,
            in_specs=ins,
            out_specs=out_specs,
            scratch_shapes=scratch,
            compiler_params=pltpu.CompilerParams(vmem_limit_bytes=limit * MIB),
            cost_estimate=pl.CostEstimate(flops=flops, bytes_accessed=MIB, transcendentals=0),
            name=name,
        )(*args)

    return run


def diag_build_kernel(tab, side, lhs, kd, acc, tile, v, rhs):
    def block(blk, carry):
        acc[blk] = jnp.zeros(FIELD, f32)
        base = 2 * STRIPS * blk

        @pl.when(tab[base, T_LIVE] > 0)
        def _():
            v[...] = split2(side[blk, 0:16, :])
            diag_pair(kd.at[blk], lhs.at[blk], rhs, side.at[blk], v, acc.at[blk])
            extra_tiles(tab, base, side.at[blk], side.at[blk], tile, v, v, acc.at[blk], acc.at[blk])

        return carry

    lax.fori_loop(0, 2, block, 0)


def halo_build_kernel(
    flags, side, lhs, got_a, got_b, acc_in, k12, x12, tab, acc, back, halo, plan_ref, tile, v1, v2, rhs, sem
):
    halo[...] = jnp.where(flags[4] == 0, got_a[...], got_b[...])
    plan_ref[...] = plan(side.at[1], halo, flags[3], False)
    copy = pltpu.make_async_copy(plan_ref, tab, sem.at[0])
    copy.start()
    acc[...] = acc_in[...]
    back[...] = jnp.zeros(FIELD, f32)
    copy.wait()

    @pl.when(flags[3] > 0)
    def _():
        v1[...] = split2(side[1, 0:16, :])
        v2[...] = split2(halo[0:16, :])
        fill = off_pair(k12, tab, 0, lhs.at[1], rhs, side.at[1], halo, v1, v2, acc.at[1], back)
        extra_tiles(tab, 0, side.at[1], halo, tile, v1, v2, acc.at[1], back, x12, fill)


def own_build_kernel(tab, side, lhs, acc_in, k01, x01, acc, tile, v, rhs):
    acc[...] = acc_in[...]

    @pl.when(tab[STRIPS, T_LIVE] > 0)
    def _():
        v[0] = split2(side[0, 0:16, :])
        v[1] = split2(side[1, 0:16, :])
        args = side.at[0], side.at[1]
        ends = v.at[0], v.at[1], acc.at[0], acc.at[1]
        fill = off_pair(k01, tab, STRIPS, lhs.at[0], rhs, *args, *ends)
        extra_tiles(tab, STRIPS, *args, tile, *ends, x01, fill)


def own_apply_kernel(tab, kd, k01, x01, side, w, acc, tile, v):
    def block(blk, carry):
        acc[blk] = jnp.zeros(FIELD, f32)
        v[blk] = split2(w[blk])
        base = 2 * STRIPS * blk

        @pl.when(tab[base, T_LIVE] > 0)
        def _():
            diag_products(kd.at[blk], v.at[blk], acc.at[blk])
            extra_tiles(
                tab, base, side.at[blk], side.at[blk], tile, v.at[blk], v.at[blk], acc.at[blk], acc.at[blk]
            )

        return carry

    lax.fori_loop(0, 2, block, 0)

    @pl.when(tab[STRIPS, T_LIVE] > 0)
    def _():
        ends = v.at[0], v.at[1], acc.at[0], acc.at[1]
        off_products(k01, tab, STRIPS, *ends)
        extra_tiles(tab, STRIPS, side.at[0], side.at[1], tile, *ends, x01)


def from_left(flags, got_a, got_b):
    arrived = jnp.where(flags[4] == 0, got_b[...], got_a[...])
    return jnp.where(flags[5] > 0, arrived, 0.0)


def inner(left, right):
    return jnp.sum(left * right, axis=1, keepdims=True)


def halo_product(tab, k12, x12, side, halo, halo_w, tile, v2, acc):
    @pl.when(tab[0, T_LIVE] > 0)
    def _():
        v2[...] = split2(halo_w)
        off_products(k12, tab, 0, None, v2, acc, None)
        extra_tiles(tab, 0, side.at[1], halo, tile, None, v2, acc, None, x12)


def finish_kernel(
    level, flags, tab, k12, x12, side, halo, got_a, got_b, acc_in, w, mom_in, new, send_a, send_b, mom,
    tile, v1, v2, acc, back
):
    acc[...] = acc_in[1]
    if level > 1:
        halo_w = jnp.where(flags[4] == 0, got_a[...], got_b[...])
        halo_product(tab, k12, x12, side, halo, halo_w, tile, v2, acc)
    before0 = w[0, 0:16, :]
    before1 = w[1, 0:16, :]
    next1 = side[1, 19:20, :] * before1 + acc[...]
    new[1] = next1
    back[...] = jnp.zeros(FIELD, f32)

    @pl.when(tab[0, T_LIVE] > 0)
    def _():
        v1[...] = split2(next1)
        off_products(k12, tab, 0, v1, None, None, back)
        extra_tiles(tab, 0, side.at[1], halo, tile, v1, None, None, back, x12)

    next0 = side[0, 19:20, :] * before0 + (acc_in[0] + from_left(flags, got_a, got_b))
    new[0] = next0
    send_a[...] = jnp.where(flags[4] == 0, back[...], next0)
    send_b[...] = jnp.where(flags[4] == 0, next0, back[...])
    lane = lax.broadcasted_iota(jnp.int32, (N_PROBES, SUB), 1)
    cross = inner(before0, next0) + inner(before1, next1)
    own = inner(next0, next0) + inner(next1, next1)
    total = jnp.where(lane == 2 * level - 1, cross, jnp.where(lane == 2 * level, own, 0.0))
    if level == 1:
        total = jnp.where(lane == 0, inner(before0, before0) + inner(before1, before1), total)
    else:
        total = total + mom_in[...]
    mom[...] = total


def moment_kernel(flags, side, acc, got_a, got_b, w, mom_in, mom):
    lane = lax.broadcasted_iota(jnp.int32, (N_PROBES, SUB), 1)
    one = w[0]
    two = w[1]
    arrived = from_left(flags, got_a, got_b)
    cross = inner(one, side[0, 19:20, :] * one + (acc[0] + 2.0 * arrived))
    cross = cross + inner(two, side[1, 19:20, :] * two + acc[1])
    mom[...] = mom_in[...] + jnp.where(lane == 5, cross, 0.0)


def last_kernel(flags, tab, k12, x12, side, halo, got_a, got_b, acc, w, new, tile, v2):
    new[1] = side[1, 19:20, :] * w[1] + acc[1]
    new[0] = side[0, 19:20, :] * w[0] + (acc[0] + from_left(flags, got_a, got_b))
    halo_w = jnp.where(flags[4] == 0, got_a[...], got_b[...])
    halo_product(tab, k12, x12, side, halo, halo_w, tile, v2, new.at[1])


def unsort(rank, fields, store):
    def block(blk, carry):
        stacked = jnp.concatenate([split2(field[blk]) for field in fields], axis=0)
        place = places()

        def strip(c, carry):
            piece = rank[blk, :, at(c, STRIP)]
            got = None
            for g in range(STRIPS):
                part = nn(stacked[:, g * STRIP : (g + 1) * STRIP], one_hot(marks(piece, g), place))
                got = part if got is None else got + part
            size = 2 * N_PROBES
            store(blk, at(blk * STRIPS + c, STRIP), [halves(got[size * k : size * (k + 1)]) for k in range(len(fields))])
            return carry

        lax.fori_loop(0, STRIPS, strip, 0)
        return carry

    lax.fori_loop(0, 2, block, 0)


def unsort_kernel(rank, wa, wb, wc, out):
    def store(blk, cols, values):
        for k, value in enumerate(values):
            out[16 * k : 16 * (k + 1), cols] = value

    unsort(rank, (wa, wb, wc), store)


def steps_kernel(mom, out, sound):
    lane = lax.broadcasted_iota(jnp.int32, (N_PROBES, SUB), 1)
    mu = [jnp.sum(jnp.where(lane == k, mom[...], 0.0), axis=1, keepdims=True) for k in range(6)]
    fine = []

    def form(left, right, shift):
        total, size = None, None
        for i, a in enumerate(left):
            for j, b in enumerate(right):
                part = (a * b) * mu[i + j + shift]
                total = part if total is None else total + part
                size = jnp.abs(part) if size is None else size + jnp.abs(part)
        fine.append(size <= 4000.0 * total)
        return total

    one = jnp.ones((N_PROBES, 1), f32)
    d = [one]
    r = [one]
    s = []
    rr = mu[0]
    for it in range(3):
        step = rr / form(d, d, 1)
        moved = [step * v for v in d]
        s = [a + b for a, b in zip(s + [0.0] * (len(d) - len(s)), moved)]
        r = [r[0]] + [(r[i] if i < len(r) else 0.0) - moved[i - 1] for i in range(1, len(moved) + 1)]
        if it < 2:
            new = form(r, r, 0)
            ratio = new / rr
            d = [r[i] + (ratio * d[i] if i < len(d) else 0.0) for i in range(len(r))]
            rr = new
    norms = [jnp.sqrt(mu[0]), jnp.sqrt(mu[2]), jnp.sqrt(mu[4])]
    norms.append(mu[5] / norms[2])
    size = sum(jnp.abs(a) * b for a, b in zip(r, norms))
    fine.append(size <= 200.0 * jnp.sqrt(rr))
    all_fine = fine[0]
    for other in fine[1:]:
        all_fine = all_fine & other
    sound[0] = jnp.min(jnp.where(all_fine, 1.0, 0.0)).astype(jnp.int32)
    table = jnp.zeros((N_PROBES, SUB), f32)
    for k, value in enumerate(s + r):
        table = jnp.where(lane == k, value, table)
    out[...] = table


def combine_kernel(steps, probes, u, sol, res):
    c = [steps[:, k : k + 1] for k in range(7)]

    def part(b, carry):
        here = at(b, 512)
        w = [probes[:, here], u[0:16, here], u[16:32, here], u[32:48, here]]
        sol[:, here] = (c[0] * w[0] + c[1] * w[1]) + c[2] * w[2]
        res[:, here] = ((c[3] * w[0] + c[4] * w[1]) + c[5] * w[2]) + c[6] * w[3]
        return carry

    lax.fori_loop(0, 2 * BLK // 512, part, 0)


def plain_product_kernel(flags, side, halo, got_a, got_b, d, acc, back, v, v2):
    acc[...] = jnp.zeros(FIELDS, f32)
    back[...] = jnp.zeros(FIELD, f32)
    v[...] = d[...].astype(bf16)
    v2[...] = jnp.where(flags[4] == 0, got_a[...], got_b[...]).astype(bf16)

    def pair(row_side, col_side, v_row, v_col, acc_row, acc_col):
        def row(i, carry):
            def col(j, carry):
                rows, cols = at(i, SUB), at(j, SUB)
                tile = tile_by_difference(
                    row_side, pl.multiple_of(i * SUB, SUB), col_side, pl.multiple_of(j * SUB, SUB)
                )
                acc_row[:, rows] += nt(v_col[:, cols], tile)
                if acc_col is not None:
                    acc_col[:, cols] += nn(v_row[:, rows], tile)
                return carry

            return lax.fori_loop(0, SUBS, col, carry)

        lax.fori_loop(0, SUBS, row, 0)

    def block(blk, carry):
        @pl.when(flags[2 * blk] > 0)
        def _():
            pair(side.at[blk], side.at[blk], None, v.at[blk], acc.at[blk], None)

        return carry

    lax.fori_loop(0, 2, block, 0)

    @pl.when(flags[1] > 0)
    def _():
        pair(side.at[0], side.at[1], v.at[0], v.at[1], acc.at[0], acc.at[1])

    @pl.when(flags[3] > 0)
    def _():
        pair(side.at[1], halo, v.at[1], v2, acc.at[1], back)


def plain_image_kernel(flags, side, acc, got_a, got_b, d, image, part):
    image[0] = side[0, 19:20, :] * d[0] + (acc[0] + from_left(flags, got_a, got_b))
    image[1] = side[1, 19:20, :] * d[1] + acc[1]
    part[...] = jnp.broadcast_to(inner(d[0], image[0]) + inner(d[1], image[1]), (N_PROBES, SUB))


def plain_step_kernel(norm, curvature, x, r, d, image, x_new, r_new, part):
    step = norm[:, 0:1] / curvature[:, 0:1]
    for b in range(2):
        x_new[b] = x[b] + step * d[b]
        r_new[b] = r[b] - step * image[b]
    part[...] = jnp.broadcast_to(inner(r_new[0], r_new[0]) + inner(r_new[1], r_new[1]), (N_PROBES, SUB))


def plain_turn_kernel(norm, new, r, d, d_new):
    ratio = new[:, 0:1] / norm[:, 0:1]
    for b in range(2):
        d_new[b] = r[b] + ratio * d[b]


def plain_start_kernel(side, x, r, part):
    x[...] = jnp.zeros(FIELDS, f32)
    r[0] = side[0, 0:16, :]
    r[1] = side[1, 0:16, :]
    part[...] = jnp.broadcast_to(inner(r[0], r[0]) + inner(r[1], r[1]), (N_PROBES, SUB))


def plain_end_kernel(rank, x, r, sol, res):
    def store(blk, cols, values):
        sol[:, cols], res[:, cols] = values

    unsort(rank, (x, r), store)


def plain_steps(flags, side, halo, rank, shape):
    fields = jax.ShapeDtypeStruct(FIELDS, f32)
    field = jax.ShapeDtypeStruct(FIELD, f32)
    sums = jax.ShapeDtypeStruct((N_PROBES, SUB), f32)

    def small(body, outs, ins, scratch=()):
        return call(body, outs, ins, (VMEM,) * len(outs), list(scratch), 10**7, "plain")

    x, r, part = small(plain_start_kernel, (fields, fields, sums), [VMEM])(side)

    def step(_, state):
        x, r, d, norm = state
        got = swapped_both(d[0], d[0])
        acc, back = small(
            plain_product_kernel,
            (fields, field),
            [SMEM] + [VMEM] * 5,
            (pltpu.VMEM(FIELDS, bf16), pltpu.VMEM(FIELD, bf16)),
        )(flags, side, halo, *got, d)
        got = swapped_both(back, back)
        image, part = small(plain_image_kernel, (fields, sums), [SMEM] + [VMEM] * 5)(flags, side, acc, *got, d)
        curvature = sum_over(part, "gx")
        x, r, part = small(plain_step_kernel, (fields, fields, sums), [VMEM] * 6)(norm, curvature, x, r, d, image)
        new = sum_over(part, "gx")
        (d,) = small(plain_turn_kernel, (fields,), [VMEM] * 4)(norm, new, r, d)
        return x, r, d, new

    x, r, _, _ = lax.fori_loop(0, 3, step, (x, r, r, sum_over(part, "gx")))
    out = jax.ShapeDtypeStruct(shape, f32)
    return small(plain_end_kernel, (out, out), [VMEM] * 3)(rank, x, r)


def swapped_both(to_a, to_b):
    count = lax.axis_size("gx")
    a = lax.ppermute(to_a, "gx", [(k, k ^ 1) for k in range(count)])
    ends = [(0, 0), (count - 1, count - 1)]
    b = lax.ppermute(to_b, "gx", ends + [(k, ((k + 1) ^ 1) - 1) for k in range(1, count - 1)])
    return a, b


def sum_over(value, axis):
    count = lax.axis_size(axis)
    if count & (count - 1):
        return lax.psum(value, axis)
    step = 1
    while step < count:
        radix = min(4, count // step)
        parts = [value] + [
            lax.ppermute(value, axis, [(k, k ^ (m * step)) for k in range(count)]) for m in range(1, radix)
        ]
        while len(parts) > 1:
            parts = [parts[m] + parts[m + 1] for m in range(0, len(parts), 2)]
        value = parts[0]
        step *= radix
    return value


def on_device(points, noise_var, probes, pair_list, counts):
    noise = noise_var.reshape(1, -1)
    field = pltpu.VMEM(FIELD, f32)
    fields = pltpu.VMEM(FIELDS, f32)
    one_side = pltpu.VMEM((24, BLK), f32)
    right = pltpu.VMEM((N_FEATURES, BLK), bf16)
    table = pltpu.SMEM((STRIPS, SUB), jnp.int32)
    moments = pltpu.VMEM((N_PROBES, SUB), f32)
    off = pltpu.VMEM((STRIPS, STRIP, OFF_W), bf16)
    outside = pltpu.VMEM((STRIPS, STRIP, SUB), bf16)
    far_space = pl.BlockSpec(memory_space=pltpu.HBM)
    shape = probes.shape

    side, first, lhs, rank, probes, flags, tab = call(
        sort_kernel,
        (
            pltpu.VMEM((2, 24, BLK), f32),
            one_side,
            pltpu.VMEM((2, BLK, N_FEATURES), bf16),
            pltpu.VMEM((2, 1, BLK), jnp.int32),
            pltpu.VMEM(shape, f32),
            pltpu.SMEM((6,), jnp.int32),
            pltpu.SMEM((3 * STRIPS, SUB), jnp.int32),
        ),
        [far_space] * 4 + [SMEM],
        (VMEM,) * 5 + (SMEM,) * 2,
        [
            pltpu.VMEM(points.shape, f32),
            pltpu.VMEM(noise.shape, f32),
            pltpu.SMEM(pair_list.shape[::-1], jnp.int32),
            pltpu.VMEM((3 * STRIPS, SUB), jnp.int32),
            pltpu.VMEM((1, BLK), f32),
            pltpu.VMEM((STRIP, SUB), f32),
            pltpu.VMEM((80, BLK), bf16),
            right,
            pltpu.SemaphoreType.DMA((4,)),
        ],
        10**9,
        "sort_blocks",
    )(*[pltpu.with_memory_space_constraint(x, pltpu.HBM) for x in (points, noise, probes, pair_list.T)], counts)

    halos = swapped_both(first, first)
    kd, acc = call(
        diag_build_kernel,
        (pltpu.VMEM((2, STRIPS, STRIP, DIAG_W), bf16), fields),
        [SMEM] + [VMEM] * 2,
        (VMEM,) * 2,
        [TILE, SPLIT, right],
        3 * 10**9,
        "diag_build",
    )(tab, side, lhs)
    k12, x12, tab12, acc, back, halo = call(
        halo_build_kernel,
        (off, outside, table, fields, field, one_side),
        [SMEM] + [VMEM] * 5,
        (VMEM, VMEM, SMEM, VMEM, VMEM, VMEM),
        [pltpu.VMEM((STRIPS, SUB), jnp.int32), TILE, SPLIT, SPLIT, right, pltpu.SemaphoreType.DMA((1,))],
        3 * 10**9,
        "halo_build",
    )(flags, side, lhs, *halos, acc)
    got = swapped_both(back, back)
    k01, x01, acc = call(
        own_build_kernel,
        (off, outside, fields),
        [SMEM] + [VMEM] * 3,
        (VMEM,) * 3,
        [TILE, SPLITS, right],
        5 * 10**9,
        "own_build",
    )(tab, side, lhs, acc)

    w = side
    mom = jnp.zeros((N_PROBES, SUB), f32)
    kept = []
    for level in (1, 2):
        w, send_a, send_b, mom = call(
            functools.partial(finish_kernel, level),
            (fields, field, field, moments),
            [SMEM] * 2 + [VMEM] * 9,
            (VMEM,) * 4,
            [TILE, SPLIT, SPLIT, pltpu.VMEM(FIELD, f32), pltpu.VMEM(FIELD, f32)],
            10**9,
            "finish",
        )(flags, tab12, k12, x12, side, halo, *got, acc, w, mom)
        kept.append(w)
        got = swapped_both(send_a, send_b)
        (acc,) = call(
            own_apply_kernel,
            (fields,),
            [SMEM] + [VMEM] * 5,
            (VMEM,),
            [TILE, SPLITS],
            2 * 10**9,
            "own_apply",
        )(tab, kd, k01, x01, side, w)
    mom = call(moment_kernel, moments, [SMEM] + [VMEM] * 6, VMEM, [], 10**7, "moment")(
        flags, side, acc, *got, w, mom
    )
    total = sum_over(mom, "gx")
    kept.append(
        call(last_kernel, fields, [SMEM] * 2 + [VMEM] * 8, VMEM, [TILE, SPLIT], 10**9, "last")(
            flags, tab12, k12, x12, side, halo, *got, acc, w
        )
    )
    given = call(
        unsort_kernel,
        pltpu.VMEM((3 * N_PROBES, 2 * BLK), f32),
        [VMEM] * 4,
        VMEM,
        [],
        4 * 96 * BLK * BLK,
        "unsort",
    )(rank, *kept)
    steps, sound = call(
        steps_kernel,
        (moments, pltpu.SMEM((1,), jnp.int32)),
        [VMEM],
        (VMEM, SMEM),
        [],
        10**6,
        "steps",
    )(total)

    def from_basis():
        out = jax.ShapeDtypeStruct(shape, f32)
        return tuple(
            call(combine_kernel, (out, out), [VMEM] * 3, (VMEM, VMEM), [], 10**6, "combine")(steps, probes, given)
        )

    def from_start():
        return tuple(plain_steps(flags, side, halo, rank, shape))

    return lax.cond(sound[0] > 0, from_basis, from_start)


def solution(mesh):
    placed = (
        P(None, ("groups", "gx")),
        P(("groups", "gx")),
        P(None, ("groups", "gx")),
        P(("groups", "gx"), None),
        P(("groups", "gx")),
    )
    return jax.shard_map(
        on_device,
        mesh=mesh,
        in_specs=placed,
        out_specs=(P(None, ("groups", "gx")), P(None, ("groups", "gx"))),
        check_vma=False,
    )
```

```python
import functools

import jax
import jax.numpy as jnp
from jax import lax
from jax.experimental import pallas as pl
from jax.experimental.pallas import tpu as pltpu
from jax.sharding import PartitionSpec as P

BLK = 2048
STRIP = 256
STRIPS = BLK // STRIP
SUB = 128
SUBS = BLK // SUB
OFF_W = 768
OFF_SUBS = OFF_W // SUB
DIAG_W = 512
N_PROBES = 16
N_FEATURES = 64
MIB = 1 << 20

VMEM = pl.BlockSpec(memory_space=pltpu.VMEM)
SMEM = pl.BlockSpec(memory_space=pltpu.SMEM)

f32 = jnp.float32
bf16 = jnp.bfloat16

T_START, T_END, T_EXTRA, T_LIVE = 0, 1, 2, 3


def nt(left, right):
    return lax.dot_general(left, right, (((1,), (1,)), ((), ())), preferred_element_type=f32)


def nn(left, right):
    return jnp.dot(left, right, preferred_element_type=f32)


def split2(value):
    high = value.astype(bf16)
    low = (value - high.astype(f32)).astype(bf16)
    return jnp.concatenate([high, low], axis=0)


def halves(value):
    n = value.shape[0] // 2
    return value[:n] + value[n:]


def split3(value):
    high = value.astype(bf16).astype(f32)
    rest = value - high
    mid = rest.astype(bf16).astype(f32)
    return high, mid, rest - mid


def multiple(value, size):
    return value if isinstance(value, int) else pl.multiple_of(value, size)


def at(index, size):
    return pl.ds(multiple(index * size, size), size)


def looped(count, body):
    lax.fori_loop(0, count, body, 0)


def each(count, body):
    for index in range(count):
        body(index, 0)


def one_hot(marked, place):
    parts = []
    for h in range(2):
        hit = jnp.broadcast_to(marked[:, h * SUB : (h + 1) * SUB], (STRIP, SUB)) == place
        parts.append(jnp.where(hit, jnp.ones((STRIP, SUB), bf16), jnp.zeros((STRIP, SUB), bf16)))
    return jnp.concatenate(parts, axis=1)


def places():
    return lax.broadcasted_iota(jnp.int32, (STRIP, SUB), 0).astype(f32).astype(bf16)


def marks(rank, g):
    group = lax.shift_right_logical(rank, 8)
    within = jnp.bitwise_and(rank, STRIP - 1)
    return jnp.where(group == g, within, -1).astype(f32).astype(bf16)


def turned(value):
    shape = (STRIP, STRIP)
    same = lax.broadcasted_iota(jnp.int32, shape, 0) == lax.broadcasted_iota(jnp.int32, shape, 1)
    return nt(jnp.where(same, 1.0, 0.0).astype(bf16), value).astype(bf16)


def fill_ranks(y_row, rank_ref, key_ref, before_ref):
    low = jnp.min(y_row, axis=1, keepdims=True)
    high = jnp.max(y_row, axis=1, keepdims=True)
    scale = 255.0 / jnp.maximum(high - low, 1e-6)
    key_ref[...] = jnp.clip(jnp.floor((y_row - low) * scale), 0.0, 255.0)
    shape = (STRIP, STRIP)
    first = lax.broadcasted_iota(jnp.int32, shape, 0)
    second = lax.broadcasted_iota(jnp.int32, shape, 1)
    upper = jnp.where(first < second, 1.0, 0.0).astype(bf16)
    lower = jnp.where(second < first, 1.0, 0.0).astype(bf16)
    ones = jnp.ones((STRIP, SUB), bf16)
    value = places()
    before_ref[...] = jnp.zeros((STRIP, SUB), f32)

    def count(j, carry):
        before_ref[...] += nn(one_hot(key_ref[:, at(j, STRIP)].astype(bf16), value), ones)
        return carry

    each(STRIPS, count)
    total = before_ref[...]
    coarse = jnp.floor(total * (1.0 / 16.0)) * 16.0
    before_ref[...] = nn(lower, coarse.astype(bf16)) + nn(lower, (total - coarse).astype(bf16))

    def place(j, carry):
        hit = one_hot(key_ref[:, at(j, STRIP)].astype(bf16), value)
        before = before_ref[...]
        ahead = nn(hit, upper) + jnp.concatenate([before, before], axis=1)
        rank = jnp.sum(hit.astype(f32) * ahead, axis=0, keepdims=True)
        rank_ref[:, at(j, STRIP)] = rank.astype(jnp.int32)
        before_ref[...] = before + nn(hit, ones)
        return carry

    each(STRIPS, place)


def plan(row_side, col_side, live, diag):
    y_row = row_side[17:18, :]
    y_col = col_side[17:18, :]
    strips = jnp.concatenate([y_row[:, i * STRIP : (i + 1) * STRIP] for i in range(STRIPS)], axis=0)
    low = jnp.min(strips, axis=1, keepdims=True) - 1.0
    high = jnp.max(strips, axis=1, keepdims=True) + 1.0
    groups = jnp.concatenate([y_col[:, j * SUB : (j + 1) * SUB] for j in range(SUBS)], axis=0)
    own = lax.broadcasted_iota(jnp.int32, (SUBS, SUB), 0) == lax.broadcasted_iota(jnp.int32, (SUBS, SUB), 1)

    def across(value):
        return jnp.sum(jnp.where(own, value, 0.0), axis=0, keepdims=True)

    group_low = across(jnp.min(groups, axis=1, keepdims=True))
    group_high = across(jnp.max(groups, axis=1, keepdims=True))
    lane = lax.broadcasted_iota(jnp.int32, (STRIPS, SUB), 1)
    place = lane.astype(f32)
    reached = (group_low < high) & (group_high > low) & (lane < SUBS)
    end = jnp.max(jnp.where(reached, place + 1.0, 0.0), axis=1, keepdims=True)
    if diag:
        start = lax.broadcasted_iota(jnp.int32, (STRIPS, 1), 0).astype(f32) * 2.0 + (DIAG_W // SUB - OFF_SUBS)
    else:
        first = jnp.min(jnp.where(reached, place, float(SUBS)), axis=1, keepdims=True)
        start = jnp.minimum(first, float(SUBS - OFF_SUBS))
    extra = jnp.sum(jnp.maximum(end - (start + OFF_SUBS), 0.0), axis=0, keepdims=True)
    alive = live.astype(f32)
    table = jnp.where(lane == T_START, start, jnp.where(lane == T_END, end, extra))
    return jnp.where(lane == T_LIVE, alive, table).astype(jnp.int32)


def row_id(width):
    return lax.broadcasted_iota(jnp.int32, (8, width), 0)


def features(offset, left):
    first, second, third = split3(offset)
    norm = jnp.sum(offset * offset, axis=0, keepdims=True)
    n1, n2, n3 = split3(norm)
    ids = row_id(offset.shape[1])
    own, other = (0, 3) if left else (3, 0)
    norms = jnp.where(ids == own, n1, jnp.where(ids == own + 1, n2, jnp.where(ids == own + 2, n3, 0.0)))
    norms = jnp.where((ids >= other) & (ids < other + 3), 1.0, norms)
    if left:
        first, second, third = -2.0 * first, -2.0 * second, -2.0 * third
        parts = [first, first, first, second, second, third]
    else:
        parts = [first, second, third, first, second, first]
    return jnp.concatenate(parts + [norms, jnp.zeros_like(norms)], axis=0), norm


def sort_kernel(
    pts_hbm, nv_hbm, pr_hbm, pair_hbm, count, side, first, lhs, rank, pr_ref, flags, tab,
    pts_ref, nv_ref, pair, plan_ref, key_ref, before_ref, sems
):
    copies = [
        pltpu.make_async_copy(src, dst, sems.at[k])
        for k, (src, dst) in enumerate(
            ((pts_hbm, pts_ref), (nv_hbm, nv_ref), (pr_hbm, pr_ref), (pair_hbm, pair))
        )
    ]
    for copy in copies:
        copy.start()
    copies[0].wait()
    for blk in range(2):
        fill_ranks(pts_ref[1:2, at(blk, BLK)], rank.at[blk], key_ref, before_ref)
    for copy in copies[1:]:
        copy.wait()
    for local in range(2):
        for ahead in range(2):
            flags[2 * local + ahead] = live_flag(pair, count, local, ahead)
    position = lax.shift_right_logical(pair[0, 0], 1)
    flags[4] = jnp.bitwise_and(position, 1)
    flags[5] = jnp.where(position > 0, 1, 0)
    place = places()
    for blk in range(2):
        cols = at(blk, BLK)
        aux = jnp.concatenate(
            [pts_ref[0:3, cols] * 2.0, nv_ref[:, cols], jnp.zeros((4, BLK), f32)], axis=0
        )
        data = jnp.concatenate(
            [*split3(pr_ref[:, cols]), *split3(aux), jnp.zeros((8, BLK), f32)], axis=0
        ).astype(bf16)
        centre = 0.5 * (jnp.min(aux, axis=1, keepdims=True) + jnp.max(aux, axis=1, keepdims=True))
        centre = jnp.concatenate([jnp.zeros((4, 1), f32), centre[0:3], jnp.zeros((1, 1), f32)], axis=0)
        ranks = rank[blk]
        for g in range(STRIPS):
            marked = marks(ranks, g)
            got = None
            for c in range(STRIPS):
                here = slice(c * STRIP, (c + 1) * STRIP)
                part = nt(data[:, here], one_hot(marked[:, here], place))
                got = part if got is None else got + part
            low = (got[0:16] + got[16:32]) + got[32:48]
            high = ((got[48:56] + got[56:64]) + got[64:72]) + centre
            side[blk, 0:16, at(g, STRIP)] = low
            side[blk, 16:24, at(g, STRIP)] = high
            if blk == 0:
                first[0:16, at(g, STRIP)] = low
                first[16:24, at(g, STRIP)] = high
    plan_ref[0:8, :] = plan(side.at[0], side.at[0], flags[0], True)
    plan_ref[8:16, :] = plan(side.at[0], side.at[1], flags[1], False)
    plan_ref[16:24, :] = plan(side.at[1], side.at[1], flags[2], True)
    copy = pltpu.make_async_copy(plan_ref, tab, sems.at[0])
    copy.start()
    for blk in range(2):
        rows, _ = features(offset_of(side.at[blk], side.at[blk]), True)
        rows = rows.astype(bf16)
        for c in range(STRIPS):
            lhs[blk, at(c, STRIP), :] = turned(rows[:, c * STRIP : (c + 1) * STRIP])
    copy.wait()


def offset_of(side_ref, centre_ref):
    centre = jnp.concatenate([centre_ref[20:23, 0:1], jnp.zeros((5, 1), f32)], axis=0)
    return jnp.where(row_id(BLK) < 3, side_ref[16:24, :] - centre, 0.0)


def live_flag(pair_ref, count_ref, local, ahead):
    flag = jnp.int32(0)
    for s in range(pair_ref.shape[1]):
        owner = pair_ref[0, s]
        match = (
            (jnp.int32(s) < count_ref[0])
            & (jnp.bitwise_and(owner, 1) == local)
            & (pair_ref[1, s] - owner == ahead)
        )
        flag = jnp.where(match, jnp.int32(1), flag)
    return flag


def kernel_values(squared):
    squared = jnp.maximum(squared, 1e-30)
    t = jnp.maximum(1.0 - squared * lax.rsqrt(squared), 0.0)
    t2 = t * t
    return ((t2 * t2) * (1.25 - t)).astype(bf16)


def tile_by_difference(row_side, row_at, col_side, col_at):
    squared = None
    for axis in range(16, 19):
        mine = jnp.broadcast_to(row_side[axis : axis + 1, pl.ds(row_at, SUB)], (SUB, SUB)).T
        diff = mine - col_side[axis : axis + 1, pl.ds(col_at, SUB)]
        part = diff * diff
        squared = part if squared is None else squared + part
    return kernel_values(squared)


def fast_strip(k_ref, i, lhs, rhs, start, width):
    for h in range(width // STRIP):
        right = rhs[:, pl.ds(multiple(start + h * STRIP, SUB), STRIP)]
        for g in range(STRIP // SUB):
            left = lhs[pl.ds(multiple(i * STRIP + g * SUB, SUB), SUB), :]
            k_ref[i, g * SUB : (g + 1) * SUB, h * STRIP : (h + 1) * STRIP] = kernel_values(nn(left, right))


def slow_build(k_ref, row_side, col_side, first_group, groups):
    def strip(i, carry):
        def tile(j, carry):
            for g in range(STRIP // SUB):
                at = pl.multiple_of(i * STRIP + g * SUB, SUB)
                col_at = pl.multiple_of(jnp.minimum(first_group(i) + j, SUBS - 1) * SUB, SUB)
                k_ref[i, g * SUB : (g + 1) * SUB, pl.ds(pl.multiple_of(j * SUB, SUB), SUB)] = (
                    tile_by_difference(row_side, at, col_side, col_at)
                )
            return carry

        return lax.fori_loop(0, groups, tile, carry)

    lax.fori_loop(0, STRIPS, strip, 0)


def right_features(rhs, row_side, col_side):
    offset = offset_of(col_side, row_side)
    rows, norm = features(offset, False)
    rhs[...] = rows.astype(bf16)
    offset = offset_of(row_side, row_side)
    return jnp.maximum(jnp.max(norm), jnp.max(jnp.sum(offset * offset, axis=0, keepdims=True))) <= 100.0


def off_pair(k_ref, tab_ref, base, lhs, rhs, row_side, col_side, v_row, v_col, acc_row, acc_col):
    near = right_features(rhs, row_side, col_side)

    @pl.when(near)
    def _():
        def strip(i, carry):
            start = pl.multiple_of(tab_ref[base + i, T_START] * SUB, SUB)
            fast_strip(k_ref, i, lhs, rhs, start, OFF_W)
            owner_strip(k_ref, i, start, v_col, acc_row)
            partner_strip(k_ref, i, start, v_row, acc_col)
            return carry

        each(STRIPS, strip)

    @pl.when(jnp.logical_not(near))
    def _():
        slow_build(k_ref, row_side, col_side, lambda i: tab_ref[base + i, T_START], OFF_SUBS)
        off_products(k_ref, tab_ref, base, v_row, v_col, acc_row, acc_col, looped)

    return near, lhs, rhs


def diag_pair(k_ref, lhs, rhs, side, v, acc):
    near = right_features(rhs, side, side)

    @pl.when(near)
    def _():
        def strip(i, carry):
            fast_strip(k_ref, i, lhs, rhs, i * STRIP, DIAG_W)
            diag_strip(k_ref, i, v, acc, DIAG_W)
            return carry

        each(STRIPS - 1, strip)
        fast_strip(k_ref, STRIPS - 1, lhs, rhs, (STRIPS - 1) * STRIP, STRIP)
        diag_strip(k_ref, STRIPS - 1, v, acc, STRIP)

    @pl.when(jnp.logical_not(near))
    def _():
        slow_build(k_ref, side, side, lambda i: 2 * i, DIAG_W // SUB)
        diag_products(k_ref, v, acc, looped)


def owner_strip(k_ref, i, start, v_col, acc_row):
    acc_row[:, at(i, STRIP)] += halves(nt(v_col[:, pl.ds(start, OFF_W)], k_ref[i]))


def partner_strip(k_ref, i, start, v_row, acc_col):
    acc_col[:, pl.ds(start, OFF_W)] += halves(nn(v_row[:, at(i, STRIP)], k_ref[i]))


def off_products(k_ref, tab_ref, base, v_row, v_col, acc_row, acc_col, repeat=each):
    def strip(i, carry):
        start = pl.multiple_of(tab_ref[base + i, T_START] * SUB, SUB)
        if acc_row is not None:
            owner_strip(k_ref, i, start, v_col, acc_row)
        if acc_col is not None:
            partner_strip(k_ref, i, start, v_row, acc_col)
        return carry

    repeat(STRIPS, strip)


def diag_strip(k_ref, i, v_ref, acc_ref, width):
    start = multiple(i * STRIP, STRIP)
    acc_ref[:, at(i, STRIP)] += halves(nt(v_ref[:, pl.ds(start, width)], k_ref[i, :, :width]))
    if width > STRIP:
        acc_ref[:, at(i + 1, STRIP)] += halves(nn(v_ref[:, at(i, STRIP)], k_ref[i, :, STRIP:width]))


def diag_products(k_ref, v_ref, acc_ref, repeat=each):
    def strip(i, carry):
        diag_strip(k_ref, i, v_ref, acc_ref, DIAG_W)
        return carry

    repeat(STRIPS - 1, strip)
    diag_strip(k_ref, STRIPS - 1, v_ref, acc_ref, STRIP)


def extra_tiles(
    tab_ref, base, row_side, col_side, tile_ref, v_row, v_col, acc_row, acc_col, kept=None, fill=None
):
    @pl.when(tab_ref[base, T_EXTRA] > 0)
    def _():
        def strip(i, carry):
            here = pl.ds(pl.multiple_of(i * STRIP, STRIP), STRIP)
            first = tab_ref[base + i, T_START] + OFF_SUBS

            def tile(j, carry):
                col_at = pl.multiple_of(j * SUB, SUB)
                there = pl.ds(col_at, SUB)

                def by_difference():
                    for g in range(STRIP // SUB):
                        row_at = pl.multiple_of(i * STRIP + g * SUB, SUB)
                        tile_ref[g * SUB : (g + 1) * SUB, :] = tile_by_difference(row_side, row_at, col_side, col_at)

                if kept is None:
                    by_difference()
                elif fill is None:
                    pl.when(j > first)(by_difference)

                    @pl.when(j == first)
                    def _():
                        tile_ref[...] = kept[i]
                else:
                    near, lhs, rhs = fill
                    pl.when(jnp.logical_not(near))(by_difference)

                    @pl.when(near)
                    def _():
                        tile_ref[...] = kernel_values(nn(lhs[here, :], rhs[:, there]))

                    @pl.when(j == first)
                    def _():
                        kept[i] = tile_ref[...]

                if acc_row is not None:
                    acc_row[:, here] += halves(nt(v_col[:, there], tile_ref[...]))
                if acc_col is not None:
                    acc_col[:, there] += halves(nn(v_row[:, here], tile_ref[...]))
                return carry

            return lax.fori_loop(first, tab_ref[base + i, T_END], tile, carry)

        lax.fori_loop(0, STRIPS, strip, 0)


TILE = pltpu.VMEM((STRIP, SUB), bf16)
SPLIT = pltpu.VMEM((2 * N_PROBES, BLK), bf16)
SPLITS = pltpu.VMEM((2, 2 * N_PROBES, BLK), bf16)
FIELD = (N_PROBES, BLK)
FIELDS = (2, N_PROBES, BLK)


def call(body, outs, ins, out_specs, scratch, flops, name, limit=12):
    def run(*args):
        return pl.pallas_call(
            body,
            out_shape=outs,
            in_specs=ins,
            out_specs=out_specs,
            scratch_shapes=scratch,
            compiler_params=pltpu.CompilerParams(vmem_limit_bytes=limit * MIB),
            cost_estimate=pl.CostEstimate(flops=flops, bytes_accessed=MIB, transcendentals=0),
            name=name,
        )(*args)

    return run


def diag_build_kernel(tab, side, lhs, kd, acc, tile, v, rhs):
    def block(blk, carry):
        acc[blk] = jnp.zeros(FIELD, f32)
        base = 2 * STRIPS * blk

        @pl.when(tab[base, T_LIVE] > 0)
        def _():
            v[...] = split2(side[blk, 0:16, :])
            diag_pair(kd.at[blk], lhs.at[blk], rhs, side.at[blk], v, acc.at[blk])
            extra_tiles(tab, base, side.at[blk], side.at[blk], tile, v, v, acc.at[blk], acc.at[blk])

        return carry

    each(2, block)


def halo_build_kernel(
    flags, side, lhs, got_a, got_b, acc_in, k12, x12, tab, acc, back, halo, plan_ref, tile, v1, v2, rhs, sem
):
    halo[...] = jnp.where(flags[4] == 0, got_a[...], got_b[...])
    plan_ref[...] = plan(side.at[1], halo, flags[3], False)
    copy = pltpu.make_async_copy(plan_ref, tab, sem.at[0])
    copy.start()
    acc[...] = acc_in[...]
    back[...] = jnp.zeros(FIELD, f32)
    copy.wait()

    @pl.when(flags[3] > 0)
    def _():
        v1[...] = split2(side[1, 0:16, :])
        v2[...] = split2(halo[0:16, :])
        fill = off_pair(k12, tab, 0, lhs.at[1], rhs, side.at[1], halo, v1, v2, acc.at[1], back)
        extra_tiles(tab, 0, side.at[1], halo, tile, v1, v2, acc.at[1], back, x12, fill)


def own_build_kernel(tab, side, lhs, acc_in, k01, x01, acc, tile, v, rhs):
    acc[...] = acc_in[...]

    @pl.when(tab[STRIPS, T_LIVE] > 0)
    def _():
        v[0] = split2(side[0, 0:16, :])
        v[1] = split2(side[1, 0:16, :])
        args = side.at[0], side.at[1]
        ends = v.at[0], v.at[1], acc.at[0], acc.at[1]
        fill = off_pair(k01, tab, STRIPS, lhs.at[0], rhs, *args, *ends)
        extra_tiles(tab, STRIPS, *args, tile, *ends, x01, fill)


def own_apply_kernel(tab, kd, k01, x01, side, w, acc, tile, v):
    def block(blk, carry):
        acc[blk] = jnp.zeros(FIELD, f32)
        v[blk] = split2(w[blk])
        base = 2 * STRIPS * blk

        @pl.when(tab[base, T_LIVE] > 0)
        def _():
            diag_products(kd.at[blk], v.at[blk], acc.at[blk])
            extra_tiles(
                tab, base, side.at[blk], side.at[blk], tile, v.at[blk], v.at[blk], acc.at[blk], acc.at[blk]
            )

        return carry

    each(2, block)

    @pl.when(tab[STRIPS, T_LIVE] > 0)
    def _():
        ends = v.at[0], v.at[1], acc.at[0], acc.at[1]
        off_products(k01, tab, STRIPS, *ends)
        extra_tiles(tab, STRIPS, side.at[0], side.at[1], tile, *ends, x01)


def from_left(flags, got_a, got_b):
    arrived = jnp.where(flags[4] == 0, got_b[...], got_a[...])
    return jnp.where(flags[5] > 0, arrived, 0.0)


def inner(left, right):
    return jnp.sum(left * right, axis=1, keepdims=True)


def halo_product(tab, k12, x12, side, halo, halo_w, tile, v2, acc):
    @pl.when(tab[0, T_LIVE] > 0)
    def _():
        v2[...] = split2(halo_w)
        off_products(k12, tab, 0, None, v2, acc, None)
        extra_tiles(tab, 0, side.at[1], halo, tile, None, v2, acc, None, x12)


def finish_kernel(
    level, flags, tab, k12, x12, side, halo, got_a, got_b, acc_in, w, mom_in, new, send_a, send_b, mom,
    tile, v1, v2, acc, back
):
    acc[...] = acc_in[1]
    if level > 1:
        halo_w = jnp.where(flags[4] == 0, got_a[...], got_b[...])
        halo_product(tab, k12, x12, side, halo, halo_w, tile, v2, acc)
    before0 = w[0, 0:16, :]
    before1 = w[1, 0:16, :]
    next1 = side[1, 19:20, :] * before1 + acc[...]
    new[1] = next1
    back[...] = jnp.zeros(FIELD, f32)

    @pl.when(tab[0, T_LIVE] > 0)
    def _():
        v1[...] = split2(next1)
        off_products(k12, tab, 0, v1, None, None, back)
        extra_tiles(tab, 0, side.at[1], halo, tile, v1, None, None, back, x12)

    next0 = side[0, 19:20, :] * before0 + (acc_in[0] + from_left(flags, got_a, got_b))
    new[0] = next0
    send_a[...] = jnp.where(flags[4] == 0, back[...], next0)
    send_b[...] = jnp.where(flags[4] == 0, next0, back[...])
    lane = lax.broadcasted_iota(jnp.int32, (N_PROBES, SUB), 1)
    cross = inner(before0, next0) + inner(before1, next1)
    own = inner(next0, next0) + inner(next1, next1)
    total = jnp.where(lane == 2 * level - 1, cross, jnp.where(lane == 2 * level, own, 0.0))
    if level == 1:
        total = jnp.where(lane == 0, inner(before0, before0) + inner(before1, before1), total)
    else:
        total = total + mom_in[...]
    mom[...] = total


def moment_kernel(flags, side, acc, got_a, got_b, w, mom_in, mom):
    lane = lax.broadcasted_iota(jnp.int32, (N_PROBES, SUB), 1)
    one = w[0]
    two = w[1]
    arrived = from_left(flags, got_a, got_b)
    cross = inner(one, side[0, 19:20, :] * one + (acc[0] + 2.0 * arrived))
    cross = cross + inner(two, side[1, 19:20, :] * two + acc[1])
    mom[...] = mom_in[...] + jnp.where(lane == 5, cross, 0.0)


def last_kernel(flags, tab, k12, x12, side, halo, got_a, got_b, acc, w, new, tile, v2):
    new[1] = side[1, 19:20, :] * w[1] + acc[1]
    new[0] = side[0, 19:20, :] * w[0] + (acc[0] + from_left(flags, got_a, got_b))
    halo_w = jnp.where(flags[4] == 0, got_a[...], got_b[...])
    halo_product(tab, k12, x12, side, halo, halo_w, tile, v2, new.at[1])


def unsort(rank, fields, store, repeat):
    def block(blk, carry):
        stacked = jnp.concatenate([split2(field[blk]) for field in fields], axis=0)
        place = places()

        def strip(c, carry):
            piece = rank[blk, :, at(c, STRIP)]
            got = None
            for g in range(STRIPS):
                part = nn(stacked[:, g * STRIP : (g + 1) * STRIP], one_hot(marks(piece, g), place))
                got = part if got is None else got + part
            size = 2 * N_PROBES
            store(blk, at(blk * STRIPS + c, STRIP), [halves(got[size * k : size * (k + 1)]) for k in range(len(fields))])
            return carry

        repeat(STRIPS, strip)
        return carry

    repeat(2, block)


def unsort_kernel(rank, wa, wb, wc, out):
    def store(blk, cols, values):
        for k, value in enumerate(values):
            out[16 * k : 16 * (k + 1), cols] = value

    unsort(rank, (wa, wb, wc), store, each)


def steps_kernel(mom, out, sound):
    lane = lax.broadcasted_iota(jnp.int32, (N_PROBES, SUB), 1)
    mu = [jnp.sum(jnp.where(lane == k, mom[...], 0.0), axis=1, keepdims=True) for k in range(6)]
    fine = []

    def form(left, right, shift):
        total, size = None, None
        for i, a in enumerate(left):
            for j, b in enumerate(right):
                part = (a * b) * mu[i + j + shift]
                total = part if total is None else total + part
                size = jnp.abs(part) if size is None else size + jnp.abs(part)
        fine.append(size <= 4000.0 * total)
        return total

    one = jnp.ones((N_PROBES, 1), f32)
    d = [one]
    r = [one]
    s = []
    rr = mu[0]
    for it in range(3):
        step = rr / form(d, d, 1)
        moved = [step * v for v in d]
        s = [a + b for a, b in zip(s + [0.0] * (len(d) - len(s)), moved)]
        r = [r[0]] + [(r[i] if i < len(r) else 0.0) - moved[i - 1] for i in range(1, len(moved) + 1)]
        if it < 2:
            new = form(r, r, 0)
            ratio = new / rr
            d = [r[i] + (ratio * d[i] if i < len(d) else 0.0) for i in range(len(r))]
            rr = new
    norms = [jnp.sqrt(mu[0]), jnp.sqrt(mu[2]), jnp.sqrt(mu[4])]
    norms.append(mu[5] / norms[2])
    size = sum(jnp.abs(a) * b for a, b in zip(r, norms))
    fine.append(size <= 200.0 * jnp.sqrt(rr))
    all_fine = fine[0]
    for other in fine[1:]:
        all_fine = all_fine & other
    sound[0] = jnp.min(jnp.where(all_fine, 1.0, 0.0)).astype(jnp.int32)
    table = jnp.zeros((N_PROBES, SUB), f32)
    for k, value in enumerate(s + r):
        table = jnp.where(lane == k, value, table)
    out[...] = table


def combine_kernel(steps, probes, u, sol, res):
    c = [steps[:, k : k + 1] for k in range(7)]

    def part(b, carry):
        here = at(b, BLK)
        w = [probes[:, here], u[0:16, here], u[16:32, here], u[32:48, here]]
        sol[:, here] = (c[0] * w[0] + c[1] * w[1]) + c[2] * w[2]
        res[:, here] = ((c[3] * w[0] + c[4] * w[1]) + c[5] * w[2]) + c[6] * w[3]
        return carry

    each(2, part)


def plain_product_kernel(flags, side, halo, got_a, got_b, d, acc, back, v, v2):
    acc[...] = jnp.zeros(FIELDS, f32)
    back[...] = jnp.zeros(FIELD, f32)
    v[...] = d[...].astype(bf16)
    v2[...] = jnp.where(flags[4] == 0, got_a[...], got_b[...]).astype(bf16)

    def pair(row_side, col_side, v_row, v_col, acc_row, acc_col):
        def row(i, carry):
            def col(j, carry):
                rows, cols = at(i, SUB), at(j, SUB)
                tile = tile_by_difference(
                    row_side, pl.multiple_of(i * SUB, SUB), col_side, pl.multiple_of(j * SUB, SUB)
                )
                acc_row[:, rows] += nt(v_col[:, cols], tile)
                if acc_col is not None:
                    acc_col[:, cols] += nn(v_row[:, rows], tile)
                return carry

            return lax.fori_loop(0, SUBS, col, carry)

        lax.fori_loop(0, SUBS, row, 0)

    def block(blk, carry):
        @pl.when(flags[2 * blk] > 0)
        def _():
            pair(side.at[blk], side.at[blk], None, v.at[blk], acc.at[blk], None)

        return carry

    lax.fori_loop(0, 2, block, 0)

    @pl.when(flags[1] > 0)
    def _():
        pair(side.at[0], side.at[1], v.at[0], v.at[1], acc.at[0], acc.at[1])

    @pl.when(flags[3] > 0)
    def _():
        pair(side.at[1], halo, v.at[1], v2, acc.at[1], back)


def plain_image_kernel(flags, side, acc, got_a, got_b, d, image, part):
    image[0] = side[0, 19:20, :] * d[0] + (acc[0] + from_left(flags, got_a, got_b))
    image[1] = side[1, 19:20, :] * d[1] + acc[1]
    part[...] = jnp.broadcast_to(inner(d[0], image[0]) + inner(d[1], image[1]), (N_PROBES, SUB))


def plain_step_kernel(norm, curvature, x, r, d, image, x_new, r_new, part):
    step = norm[:, 0:1] / curvature[:, 0:1]
    for b in range(2):
        x_new[b] = x[b] + step * d[b]
        r_new[b] = r[b] - step * image[b]
    part[...] = jnp.broadcast_to(inner(r_new[0], r_new[0]) + inner(r_new[1], r_new[1]), (N_PROBES, SUB))


def plain_turn_kernel(norm, new, r, d, d_new):
    ratio = new[:, 0:1] / norm[:, 0:1]
    for b in range(2):
        d_new[b] = r[b] + ratio * d[b]


def plain_start_kernel(side, x, r, part):
    x[...] = jnp.zeros(FIELDS, f32)
    r[0] = side[0, 0:16, :]
    r[1] = side[1, 0:16, :]
    part[...] = jnp.broadcast_to(inner(r[0], r[0]) + inner(r[1], r[1]), (N_PROBES, SUB))


def plain_end_kernel(rank, x, r, sol, res):
    def store(blk, cols, values):
        sol[:, cols], res[:, cols] = values

    unsort(rank, (x, r), store, looped)


def plain_steps(flags, side, halo, rank, shape):
    fields = jax.ShapeDtypeStruct(FIELDS, f32)
    field = jax.ShapeDtypeStruct(FIELD, f32)
    sums = jax.ShapeDtypeStruct((N_PROBES, SUB), f32)

    def small(body, outs, ins, scratch=()):
        return call(body, outs, ins, (VMEM,) * len(outs), list(scratch), 10**7, "plain")

    x, r, part = small(plain_start_kernel, (fields, fields, sums), [VMEM])(side)

    def step(_, state):
        x, r, d, norm = state
        got = swapped_both(d[0], d[0])
        acc, back = small(
            plain_product_kernel,
            (fields, field),
            [SMEM] + [VMEM] * 5,
            (pltpu.VMEM(FIELDS, bf16), pltpu.VMEM(FIELD, bf16)),
        )(flags, side, halo, *got, d)
        got = swapped_both(back, back)
        image, part = small(plain_image_kernel, (fields, sums), [SMEM] + [VMEM] * 5)(flags, side, acc, *got, d)
        curvature = sum_over(part, "gx")
        x, r, part = small(plain_step_kernel, (fields, fields, sums), [VMEM] * 6)(norm, curvature, x, r, d, image)
        new = sum_over(part, "gx")
        (d,) = small(plain_turn_kernel, (fields,), [VMEM] * 4)(norm, new, r, d)
        return x, r, d, new

    x, r, _, _ = lax.fori_loop(0, 3, step, (x, r, r, sum_over(part, "gx")))
    out = jax.ShapeDtypeStruct(shape, f32)
    return small(plain_end_kernel, (out, out), [VMEM] * 3)(rank, x, r)


def swapped_both(to_a, to_b):
    count = lax.axis_size("gx")
    a = lax.ppermute(to_a, "gx", [(k, k ^ 1) for k in range(count)])
    ends = [(0, 0), (count - 1, count - 1)]
    b = lax.ppermute(to_b, "gx", ends + [(k, ((k + 1) ^ 1) - 1) for k in range(1, count - 1)])
    return a, b


def sum_over(value, axis):
    count = lax.axis_size(axis)
    if count & (count - 1):
        return lax.psum(value, axis)
    step = 1
    while step < count:
        radix = min(4, count // step)
        parts = [value] + [
            lax.ppermute(value, axis, [(k, k ^ (m * step)) for k in range(count)]) for m in range(1, radix)
        ]
        while len(parts) > 1:
            parts = [parts[m] + parts[m + 1] for m in range(0, len(parts), 2)]
        value = parts[0]
        step *= radix
    return value


def on_device(points, noise_var, probes, pair_list, counts):
    noise = noise_var.reshape(1, -1)
    field = pltpu.VMEM(FIELD, f32)
    fields = pltpu.VMEM(FIELDS, f32)
    one_side = pltpu.VMEM((24, BLK), f32)
    right = pltpu.VMEM((N_FEATURES, BLK), bf16)
    table = pltpu.SMEM((STRIPS, SUB), jnp.int32)
    moments = pltpu.VMEM((N_PROBES, SUB), f32)
    off = pltpu.VMEM((STRIPS, STRIP, OFF_W), bf16)
    outside = pltpu.VMEM((STRIPS, STRIP, SUB), bf16)
    far_space = pl.BlockSpec(memory_space=pltpu.HBM)
    shape = probes.shape

    side, first, lhs, rank, probes, flags, tab = call(
        sort_kernel,
        (
            pltpu.VMEM((2, 24, BLK), f32),
            one_side,
            pltpu.VMEM((2, BLK, N_FEATURES), bf16),
            pltpu.VMEM((2, 1, BLK), jnp.int32),
            pltpu.VMEM(shape, f32),
            pltpu.SMEM((6,), jnp.int32),
            pltpu.SMEM((3 * STRIPS, SUB), jnp.int32),
        ),
        [far_space] * 4 + [SMEM],
        (VMEM,) * 5 + (SMEM,) * 2,
        [
            pltpu.VMEM(points.shape, f32),
            pltpu.VMEM(noise.shape, f32),
            pltpu.SMEM(pair_list.shape[::-1], jnp.int32),
            pltpu.VMEM((3 * STRIPS, SUB), jnp.int32),
            pltpu.VMEM((1, BLK), f32),
            pltpu.VMEM((STRIP, SUB), f32),
            pltpu.SemaphoreType.DMA((4,)),
        ],
        10**9,
        "sort_blocks",
    )(*[pltpu.with_memory_space_constraint(x, pltpu.HBM) for x in (points, noise, probes, pair_list.T)], counts)

    halos = swapped_both(first, first)
    kd, acc = call(
        diag_build_kernel,
        (pltpu.VMEM((2, STRIPS, STRIP, DIAG_W), bf16), fields),
        [SMEM] + [VMEM] * 2,
        (VMEM,) * 2,
        [TILE, SPLIT, right],
        3 * 10**9,
        "diag_build",
    )(tab, side, lhs)
    k12, x12, tab12, acc, back, halo = call(
        halo_build_kernel,
        (off, outside, table, fields, field, one_side),
        [SMEM] + [VMEM] * 5,
        (VMEM, VMEM, SMEM, VMEM, VMEM, VMEM),
        [pltpu.VMEM((STRIPS, SUB), jnp.int32), TILE, SPLIT, SPLIT, right, pltpu.SemaphoreType.DMA((1,))],
        3 * 10**9,
        "halo_build",
    )(flags, side, lhs, *halos, acc)
    got = swapped_both(back, back)
    k01, x01, acc = call(
        own_build_kernel,
        (off, outside, fields),
        [SMEM] + [VMEM] * 3,
        (VMEM,) * 3,
        [TILE, SPLITS, right],
        5 * 10**9,
        "own_build",
    )(tab, side, lhs, acc)

    w = side
    mom = jnp.zeros((N_PROBES, SUB), f32)
    kept = []
    for level in (1, 2):
        w, send_a, send_b, mom = call(
            functools.partial(finish_kernel, level),
            (fields, field, field, moments),
            [SMEM] * 2 + [VMEM] * 9,
            (VMEM,) * 4,
            [TILE, SPLIT, SPLIT, pltpu.VMEM(FIELD, f32), pltpu.VMEM(FIELD, f32)],
            10**9,
            "finish",
        )(flags, tab12, k12, x12, side, halo, *got, acc, w, mom)
        kept.append(w)
        got = swapped_both(send_a, send_b)
        (acc,) = call(
            own_apply_kernel,
            (fields,),
            [SMEM] + [VMEM] * 5,
            (VMEM,),
            [TILE, SPLITS],
            2 * 10**9,
            "own_apply",
        )(tab, kd, k01, x01, side, w)
    mom = call(moment_kernel, moments, [SMEM] + [VMEM] * 6, VMEM, [], 10**7, "moment")(
        flags, side, acc, *got, w, mom
    )
    total = sum_over(mom, "gx")
    kept.append(
        call(last_kernel, fields, [SMEM] * 2 + [VMEM] * 8, VMEM, [TILE, SPLIT], 10**9, "last")(
            flags, tab12, k12, x12, side, halo, *got, acc, w
        )
    )
    given = call(
        unsort_kernel,
        pltpu.VMEM((3 * N_PROBES, 2 * BLK), f32),
        [VMEM] * 4,
        VMEM,
        [],
        4 * 96 * BLK * BLK,
        "unsort",
    )(rank, *kept)
    steps, sound = call(
        steps_kernel,
        (moments, pltpu.SMEM((1,), jnp.int32)),
        [VMEM],
        (VMEM, SMEM),
        [],
        10**6,
        "steps",
    )(total)

    def from_basis():
        out = jax.ShapeDtypeStruct(shape, f32)
        return tuple(
            call(combine_kernel, (out, out), [VMEM] * 3, (VMEM, VMEM), [], 10**6, "combine")(steps, probes, given)
        )

    def from_start():
        return tuple(plain_steps(flags, side, halo, rank, shape))

    return lax.cond(sound[0] > 0, from_basis, from_start)


def solution(mesh):
    placed = (
        P(None, ("groups", "gx")),
        P(("groups", "gx")),
        P(None, ("groups", "gx")),
        P(("groups", "gx"), None),
        P(("groups", "gx")),
    )
    return jax.shard_map(
        on_device,
        mesh=mesh,
        in_specs=placed,
        out_specs=(P(None, ("groups", "gx")), P(None, ("groups", "gx"))),
        check_vma=False,
    )
```

```python
import functools

import jax
import jax.numpy as jnp
from jax import lax
from jax.experimental import pallas as pl
from jax.experimental.pallas import tpu as pltpu
from jax.sharding import PartitionSpec as P

BLK = 2048
STRIP = 256
STRIPS = BLK // STRIP
SUB = 128
SUBS = BLK // SUB
OFF_W = 768
OFF_SUBS = OFF_W // SUB
EDGE_W = 512
DIAG_W = 512
N_PROBES = 16
N_FEATURES = 64
MIB = 1 << 20

VMEM = pl.BlockSpec(memory_space=pltpu.VMEM)
SMEM = pl.BlockSpec(memory_space=pltpu.SMEM)

f32 = jnp.float32
bf16 = jnp.bfloat16

T_START, T_END, T_EXTRA, T_LIVE, T_NEXT = 0, 1, 2, 3, 4


def nt(left, right):
    return lax.dot_general(left, right, (((1,), (1,)), ((), ())), preferred_element_type=f32)


def nn(left, right):
    return jnp.dot(left, right, preferred_element_type=f32)


def split2(value):
    high = value.astype(bf16)
    low = (value - high.astype(f32)).astype(bf16)
    return jnp.concatenate([high, low], axis=0)


def halves(value):
    n = value.shape[0] // 2
    return value[:n] + value[n:]


def split3(value):
    high = value.astype(bf16).astype(f32)
    rest = value - high
    mid = rest.astype(bf16).astype(f32)
    return high, mid, rest - mid


def multiple(value, size):
    return value if isinstance(value, int) else pl.multiple_of(value, size)


def at(index, size):
    return pl.ds(multiple(index * size, size), size)


def looped(count, body):
    lax.fori_loop(0, count, body, 0)


def each(count, body):
    for index in range(count):
        body(index, 0)


def one_hot(marked, place):
    parts = []
    for h in range(2):
        hit = jnp.broadcast_to(marked[:, h * SUB : (h + 1) * SUB], (STRIP, SUB)) == place
        parts.append(jnp.where(hit, jnp.ones((STRIP, SUB), bf16), jnp.zeros((STRIP, SUB), bf16)))
    return jnp.concatenate(parts, axis=1)


def places():
    return lax.broadcasted_iota(jnp.int32, (STRIP, SUB), 0).astype(f32).astype(bf16)


def marks(rank, g):
    group = lax.shift_right_logical(rank, 8)
    within = jnp.bitwise_and(rank, STRIP - 1)
    return jnp.where(group == g, within, -1).astype(f32).astype(bf16)


def turned(value):
    shape = (STRIP, STRIP)
    same = lax.broadcasted_iota(jnp.int32, shape, 0) == lax.broadcasted_iota(jnp.int32, shape, 1)
    return nt(jnp.where(same, 1.0, 0.0).astype(bf16), value).astype(bf16)


def fill_ranks(y_row, rank_ref, key_ref, before_ref):
    low = jnp.min(y_row, axis=1, keepdims=True)
    high = jnp.max(y_row, axis=1, keepdims=True)
    scale = 255.0 / jnp.maximum(high - low, 1e-6)
    key_ref[...] = jnp.clip(jnp.floor((y_row - low) * scale), 0.0, 255.0)
    shape = (STRIP, STRIP)
    first = lax.broadcasted_iota(jnp.int32, shape, 0)
    second = lax.broadcasted_iota(jnp.int32, shape, 1)
    upper = jnp.where(first < second, 1.0, 0.0).astype(bf16)
    lower = jnp.where(second < first, 1.0, 0.0).astype(bf16)
    ones = jnp.ones((STRIP, SUB), bf16)
    value = places()
    total = None
    for j in range(STRIPS):
        counts = nn(one_hot(key_ref[:, at(j, STRIP)].astype(bf16), value), ones)
        before_ref[j] = counts
        total = counts if total is None else total + counts
    coarse = jnp.floor(total * (1.0 / 16.0)) * 16.0
    before = nn(lower, coarse.astype(bf16)) + nn(lower, (total - coarse).astype(bf16))
    for j in range(STRIPS):
        after = before + before_ref[j]
        before_ref[j] = before
        before = after
    for j in range(STRIPS):
        hit = one_hot(key_ref[:, at(j, STRIP)].astype(bf16), value)
        before = before_ref[j]
        ahead = nn(hit, upper) + jnp.concatenate([before, before], axis=1)
        rank = jnp.sum(hit.astype(f32) * ahead, axis=0, keepdims=True)
        rank_ref[:, at(j, STRIP)] = rank.astype(jnp.int32)


def plan(row_side, col_side, live, diag):
    y_row = row_side[17:18, :]
    y_col = col_side[17:18, :]
    strips = jnp.concatenate([y_row[:, i * STRIP : (i + 1) * STRIP] for i in range(STRIPS)], axis=0)
    low = jnp.min(strips, axis=1, keepdims=True) - 1.0
    high = jnp.max(strips, axis=1, keepdims=True) + 1.0
    groups = jnp.concatenate([y_col[:, j * SUB : (j + 1) * SUB] for j in range(SUBS)], axis=0)
    own = lax.broadcasted_iota(jnp.int32, (SUBS, SUB), 0) == lax.broadcasted_iota(jnp.int32, (SUBS, SUB), 1)

    def across(value):
        return jnp.sum(jnp.where(own, value, 0.0), axis=0, keepdims=True)

    group_low = across(jnp.min(groups, axis=1, keepdims=True))
    group_high = across(jnp.max(groups, axis=1, keepdims=True))
    lane = lax.broadcasted_iota(jnp.int32, (STRIPS, SUB), 1)
    place = lane.astype(f32)
    reached = (group_low < high) & (group_high > low) & (lane < SUBS)
    end = jnp.max(jnp.where(reached, place + 1.0, 0.0), axis=1, keepdims=True)
    strip = lax.broadcasted_iota(jnp.int32, (STRIPS, 1), 0)
    if diag:
        start = strip.astype(f32) * 2.0
        after = start + DIAG_W // SUB
    else:
        first = jnp.min(jnp.where(reached, place, float(SUBS)), axis=1, keepdims=True)
        width = jnp.where((strip == 0) | (strip == STRIPS - 1), float(EDGE_W // SUB), float(OFF_SUBS))
        start = jnp.minimum(first, SUBS - width)
        after = start + width
    extra = jnp.sum(jnp.maximum(end - after, 0.0), axis=0, keepdims=True)
    alive = live.astype(f32)
    table = jnp.where(lane == T_START, start, jnp.where(lane == T_END, end, extra))
    table = jnp.where(lane == T_NEXT, after, table)
    return jnp.where(lane == T_LIVE, alive, table).astype(jnp.int32)


def row_id(width):
    return lax.broadcasted_iota(jnp.int32, (8, width), 0)


def features(offset, left):
    first, second, third = split3(offset)
    norm = jnp.sum(offset * offset, axis=0, keepdims=True)
    n1, n2, n3 = split3(norm)
    ids = row_id(offset.shape[1])
    own, other = (0, 3) if left else (3, 0)
    norms = jnp.where(ids == own, n1, jnp.where(ids == own + 1, n2, jnp.where(ids == own + 2, n3, 0.0)))
    norms = jnp.where((ids >= other) & (ids < other + 3), 1.0, norms)
    if left:
        first, second, third = -2.0 * first, -2.0 * second, -2.0 * third
        parts = [first, first, first, second, second, third]
    else:
        parts = [first, second, third, first, second, first]
    return jnp.concatenate(parts + [norms, jnp.zeros_like(norms)], axis=0), norm


def sort_kernel(
    pts_hbm, nv_hbm, pr_hbm, pair_hbm, count, side, first, lhs, rank, pr_ref, flags, tab,
    pts_ref, nv_ref, pair, plan_ref, key_ref, before_ref, sems
):
    copies = [
        pltpu.make_async_copy(src, dst, sems.at[k])
        for k, (src, dst) in enumerate(
            ((pts_hbm, pts_ref), (nv_hbm, nv_ref), (pr_hbm, pr_ref), (pair_hbm, pair))
        )
    ]
    for copy in copies:
        copy.start()
    copies[0].wait()
    for blk in range(2):
        fill_ranks(pts_ref[1:2, at(blk, BLK)], rank.at[blk], key_ref.at[blk], before_ref.at[blk])
    for copy in copies[1:]:
        copy.wait()
    for local in range(2):
        for ahead in range(2):
            flags[2 * local + ahead] = live_flag(pair, count, local, ahead)
    position = lax.shift_right_logical(pair[0, 0], 1)
    flags[4] = jnp.bitwise_and(position, 1)
    flags[5] = jnp.where(position > 0, 1, 0)
    place = places()
    for blk in range(2):
        cols = at(blk, BLK)
        aux = jnp.concatenate(
            [pts_ref[0:3, cols] * 2.0, nv_ref[:, cols], jnp.zeros((4, BLK), f32)], axis=0
        )
        data = jnp.concatenate(
            [*split3(pr_ref[:, cols]), *split3(aux), jnp.zeros((8, BLK), f32)], axis=0
        ).astype(bf16)
        centre = 0.5 * (jnp.min(aux, axis=1, keepdims=True) + jnp.max(aux, axis=1, keepdims=True))
        centre = jnp.concatenate([jnp.zeros((4, 1), f32), centre[0:3], jnp.zeros((1, 1), f32)], axis=0)
        ranks = rank[blk]
        for g in range(STRIPS):
            marked = marks(ranks, g)
            got = None
            for c in range(STRIPS):
                here = slice(c * STRIP, (c + 1) * STRIP)
                part = nt(data[:, here], one_hot(marked[:, here], place))
                got = part if got is None else got + part
            low = (got[0:16] + got[16:32]) + got[32:48]
            high = ((got[48:56] + got[56:64]) + got[64:72]) + centre
            side[blk, 0:16, at(g, STRIP)] = low
            side[blk, 16:24, at(g, STRIP)] = high
            if blk == 0:
                first[0:16, at(g, STRIP)] = low
                first[16:24, at(g, STRIP)] = high
    plan_ref[0:8, :] = plan(side.at[0], side.at[0], flags[0], True)
    plan_ref[8:16, :] = plan(side.at[0], side.at[1], flags[1], False)
    plan_ref[16:24, :] = plan(side.at[1], side.at[1], flags[2], True)
    copy = pltpu.make_async_copy(plan_ref, tab, sems.at[0])
    copy.start()
    for blk in range(2):
        rows, _ = features(offset_of(side.at[blk], side.at[blk]), True)
        rows = rows.astype(bf16)
        for c in range(STRIPS):
            lhs[blk, at(c, STRIP), :] = turned(rows[:, c * STRIP : (c + 1) * STRIP])
    copy.wait()


def offset_of(side_ref, centre_ref):
    centre = jnp.concatenate([centre_ref[20:23, 0:1], jnp.zeros((5, 1), f32)], axis=0)
    return jnp.where(row_id(BLK) < 3, side_ref[16:24, :] - centre, 0.0)


def live_flag(pair_ref, count_ref, local, ahead):
    flag = jnp.int32(0)
    for s in range(pair_ref.shape[1]):
        owner = pair_ref[0, s]
        match = (
            (jnp.int32(s) < count_ref[0])
            & (jnp.bitwise_and(owner, 1) == local)
            & (pair_ref[1, s] - owner == ahead)
        )
        flag = jnp.where(match, jnp.int32(1), flag)
    return flag


def kernel_values(squared):
    squared = jnp.maximum(squared, 1e-30)
    t = jnp.maximum(1.0 - squared * lax.rsqrt(squared), 0.0)
    t2 = t * t
    return ((t2 * t2) * (1.25 - t)).astype(bf16)


def tile_by_difference(row_side, row_at, col_side, col_at):
    squared = None
    for axis in range(16, 19):
        mine = jnp.broadcast_to(row_side[axis : axis + 1, pl.ds(row_at, SUB)], (SUB, SUB)).T
        diff = mine - col_side[axis : axis + 1, pl.ds(col_at, SUB)]
        part = diff * diff
        squared = part if squared is None else squared + part
    return kernel_values(squared)


def fast_strip(k_ref, i, lhs, rhs, start, width):
    for h in range(width // STRIP):
        right = rhs[:, pl.ds(multiple(start + h * STRIP, SUB), STRIP)]
        for g in range(STRIP // SUB):
            left = lhs[pl.ds(multiple(i * STRIP + g * SUB, SUB), SUB), :]
            k_ref[i, g * SUB : (g + 1) * SUB, h * STRIP : (h + 1) * STRIP] = kernel_values(nn(left, right))


def slow_build(k_ref, row_side, col_side, first_group, groups):
    def strip(i, carry):
        def tile(j, carry):
            for g in range(STRIP // SUB):
                at = pl.multiple_of(i * STRIP + g * SUB, SUB)
                col_at = pl.multiple_of(jnp.minimum(first_group(i) + j, SUBS - 1) * SUB, SUB)
                k_ref[i, g * SUB : (g + 1) * SUB, pl.ds(pl.multiple_of(j * SUB, SUB), SUB)] = (
                    tile_by_difference(row_side, at, col_side, col_at)
                )
            return carry

        return lax.fori_loop(0, groups, tile, carry)

    lax.fori_loop(0, STRIPS, strip, 0)


def right_features(rhs, row_side, col_side):
    offset = offset_of(col_side, row_side)
    rows, norm = features(offset, False)
    rhs[...] = rows.astype(bf16)
    offset = offset_of(row_side, row_side)
    return jnp.maximum(jnp.max(norm), jnp.max(jnp.sum(offset * offset, axis=0, keepdims=True))) <= 100.0


def off_pair(k_ref, tab_ref, base, lhs, rhs, row_side, col_side, v_row, v_col, acc_row, acc_col):
    near = right_features(rhs, row_side, col_side)

    @pl.when(near)
    def _():
        def strip(i, carry):
            start = pl.multiple_of(tab_ref[base + i, T_START] * SUB, SUB)
            fast_strip(k_ref, i, lhs, rhs, start, off_width(i))
            owner_strip(k_ref, i, start, v_col, acc_row)
            partner_strip(k_ref, i, start, v_row, acc_col)
            return carry

        each(STRIPS, strip)

    @pl.when(jnp.logical_not(near))
    def _():
        slow_build(k_ref, row_side, col_side, lambda i: tab_ref[base + i, T_START], OFF_SUBS)
        off_products(k_ref, tab_ref, base, v_row, v_col, acc_row, acc_col, looped)

    return near, lhs, rhs


def diag_pair(k_ref, lhs, rhs, side, v, acc):
    near = right_features(rhs, side, side)

    @pl.when(near)
    def _():
        def strip(i, carry):
            fast_strip(k_ref, i, lhs, rhs, i * STRIP, DIAG_W)
            diag_strip(k_ref, i, v, acc, DIAG_W)
            return carry

        each(STRIPS - 1, strip)
        fast_strip(k_ref, STRIPS - 1, lhs, rhs, (STRIPS - 1) * STRIP, STRIP)
        diag_strip(k_ref, STRIPS - 1, v, acc, STRIP)

    @pl.when(jnp.logical_not(near))
    def _():
        slow_build(k_ref, side, side, lambda i: 2 * i, DIAG_W // SUB)
        diag_products(k_ref, v, acc, looped)


def off_width(i):
    return EDGE_W if isinstance(i, int) and i in (0, STRIPS - 1) else OFF_W


def owner_strip(k_ref, i, start, v_col, acc_row):
    width = off_width(i)
    acc_row[:, at(i, STRIP)] += halves(nt(v_col[:, pl.ds(start, width)], k_ref[i, :, :width]))


def partner_strip(k_ref, i, start, v_row, acc_col):
    width = off_width(i)
    acc_col[:, pl.ds(start, width)] += halves(nn(v_row[:, at(i, STRIP)], k_ref[i, :, :width]))


def off_products(k_ref, tab_ref, base, v_row, v_col, acc_row, acc_col, repeat=each):
    def strip(i, carry):
        start = pl.multiple_of(tab_ref[base + i, T_START] * SUB, SUB)
        if acc_row is not None:
            owner_strip(k_ref, i, start, v_col, acc_row)
        if acc_col is not None:
            partner_strip(k_ref, i, start, v_row, acc_col)
        return carry

    strip(0, 0)
    repeat(STRIPS - 2, lambda i, carry: strip(i + 1, carry))
    strip(STRIPS - 1, 0)


def diag_strip(k_ref, i, v_ref, acc_ref, width):
    start = multiple(i * STRIP, STRIP)
    acc_ref[:, at(i, STRIP)] += halves(nt(v_ref[:, pl.ds(start, width)], k_ref[i, :, :width]))
    if width > STRIP:
        acc_ref[:, at(i + 1, STRIP)] += halves(nn(v_ref[:, at(i, STRIP)], k_ref[i, :, STRIP:width]))


def diag_products(k_ref, v_ref, acc_ref, repeat=each):
    def strip(i, carry):
        diag_strip(k_ref, i, v_ref, acc_ref, DIAG_W)
        return carry

    repeat(STRIPS - 1, strip)
    diag_strip(k_ref, STRIPS - 1, v_ref, acc_ref, STRIP)


def extra_tiles(
    tab_ref, base, row_side, col_side, tile_ref, v_row, v_col, acc_row, acc_col, kept=None, fill=None
):
    @pl.when(tab_ref[base, T_EXTRA] > 0)
    def _():
        def strip(i, carry):
            here = pl.ds(pl.multiple_of(i * STRIP, STRIP), STRIP)
            first = tab_ref[base + i, T_NEXT]

            def tile(j, carry):
                col_at = pl.multiple_of(j * SUB, SUB)
                there = pl.ds(col_at, SUB)

                def by_difference():
                    for g in range(STRIP // SUB):
                        row_at = pl.multiple_of(i * STRIP + g * SUB, SUB)
                        tile_ref[g * SUB : (g + 1) * SUB, :] = tile_by_difference(row_side, row_at, col_side, col_at)

                if kept is None:
                    by_difference()
                elif fill is None:
                    pl.when(j > first)(by_difference)

                    @pl.when(j == first)
                    def _():
                        tile_ref[...] = kept[i]
                else:
                    near, lhs, rhs = fill
                    pl.when(jnp.logical_not(near))(by_difference)

                    @pl.when(near)
                    def _():
                        tile_ref[...] = kernel_values(nn(lhs[here, :], rhs[:, there]))

                    @pl.when(j == first)
                    def _():
                        kept[i] = tile_ref[...]

                if acc_row is not None:
                    acc_row[:, here] += halves(nt(v_col[:, there], tile_ref[...]))
                if acc_col is not None:
                    acc_col[:, there] += halves(nn(v_row[:, here], tile_ref[...]))
                return carry

            return lax.fori_loop(first, tab_ref[base + i, T_END], tile, carry)

        lax.fori_loop(0, STRIPS, strip, 0)


TILE = pltpu.VMEM((STRIP, SUB), bf16)
SPLIT = pltpu.VMEM((2 * N_PROBES, BLK), bf16)
SPLITS = pltpu.VMEM((2, 2 * N_PROBES, BLK), bf16)
FIELD = (N_PROBES, BLK)
FIELDS = (2, N_PROBES, BLK)


def call(body, outs, ins, out_specs, scratch, flops, name, limit=12):
    def run(*args):
        return pl.pallas_call(
            body,
            out_shape=outs,
            in_specs=ins,
            out_specs=out_specs,
            scratch_shapes=scratch,
            compiler_params=pltpu.CompilerParams(vmem_limit_bytes=limit * MIB),
            cost_estimate=pl.CostEstimate(flops=flops, bytes_accessed=MIB, transcendentals=0),
            name=name,
        )(*args)

    return run


def diag_build_kernel(tab, side, lhs, kd, acc, tile, v, rhs):
    def block(blk, carry):
        acc[blk] = jnp.zeros(FIELD, f32)
        base = 2 * STRIPS * blk

        @pl.when(tab[base, T_LIVE] > 0)
        def _():
            v[...] = split2(side[blk, 0:16, :])
            diag_pair(kd.at[blk], lhs.at[blk], rhs, side.at[blk], v, acc.at[blk])
            extra_tiles(tab, base, side.at[blk], side.at[blk], tile, v, v, acc.at[blk], acc.at[blk])

        return carry

    each(2, block)


def halo_build_kernel(
    flags, side, lhs, got_a, got_b, acc_in, k12, x12, tab, acc, back, halo, plan_ref, tile, v1, v2, rhs, sem
):
    halo[...] = jnp.where(flags[4] == 0, got_a[...], got_b[...])
    plan_ref[...] = plan(side.at[1], halo, flags[3], False)
    copy = pltpu.make_async_copy(plan_ref, tab, sem.at[0])
    copy.start()
    acc[...] = acc_in[...]
    back[...] = jnp.zeros(FIELD, f32)
    copy.wait()

    @pl.when(flags[3] > 0)
    def _():
        v1[...] = split2(side[1, 0:16, :])
        v2[...] = split2(halo[0:16, :])
        fill = off_pair(k12, tab, 0, lhs.at[1], rhs, side.at[1], halo, v1, v2, acc.at[1], back)
        extra_tiles(tab, 0, side.at[1], halo, tile, v1, v2, acc.at[1], back, x12, fill)


def own_build_kernel(tab, side, lhs, acc_in, k01, x01, acc, tile, v, rhs):
    acc[...] = acc_in[...]

    @pl.when(tab[STRIPS, T_LIVE] > 0)
    def _():
        v[0] = split2(side[0, 0:16, :])
        v[1] = split2(side[1, 0:16, :])
        args = side.at[0], side.at[1]
        ends = v.at[0], v.at[1], acc.at[0], acc.at[1]
        fill = off_pair(k01, tab, STRIPS, lhs.at[0], rhs, *args, *ends)
        extra_tiles(tab, STRIPS, *args, tile, *ends, x01, fill)


def own_apply_kernel(tab, kd, k01, x01, side, w, acc, tile, v):
    def block(blk, carry):
        acc[blk] = jnp.zeros(FIELD, f32)
        v[blk] = split2(w[blk])
        base = 2 * STRIPS * blk

        @pl.when(tab[base, T_LIVE] > 0)
        def _():
            diag_products(kd.at[blk], v.at[blk], acc.at[blk])
            extra_tiles(
                tab, base, side.at[blk], side.at[blk], tile, v.at[blk], v.at[blk], acc.at[blk], acc.at[blk]
            )

        return carry

    each(2, block)

    @pl.when(tab[STRIPS, T_LIVE] > 0)
    def _():
        ends = v.at[0], v.at[1], acc.at[0], acc.at[1]
        off_products(k01, tab, STRIPS, *ends)
        extra_tiles(tab, STRIPS, side.at[0], side.at[1], tile, *ends, x01)


def from_left(flags, got_a, got_b):
    arrived = jnp.where(flags[4] == 0, got_b[...], got_a[...])
    return jnp.where(flags[5] > 0, arrived, 0.0)


def inner(left, right):
    return jnp.sum(left * right, axis=1, keepdims=True)


def halo_product(tab, k12, x12, side, halo, halo_w, tile, v2, acc):
    @pl.when(tab[0, T_LIVE] > 0)
    def _():
        v2[...] = split2(halo_w)
        off_products(k12, tab, 0, None, v2, acc, None)
        extra_tiles(tab, 0, side.at[1], halo, tile, None, v2, acc, None, x12)


def finish_kernel(
    level, flags, tab, k12, x12, side, halo, got_a, got_b, acc_in, w, mom_in, new, send_a, send_b, mom,
    tile, v1, v2, acc, back
):
    acc[...] = acc_in[1]
    if level > 1:
        halo_w = jnp.where(flags[4] == 0, got_a[...], got_b[...])
        halo_product(tab, k12, x12, side, halo, halo_w, tile, v2, acc)
    before0 = w[0, 0:16, :]
    before1 = w[1, 0:16, :]
    next1 = side[1, 19:20, :] * before1 + acc[...]
    new[1] = next1
    back[...] = jnp.zeros(FIELD, f32)

    @pl.when(tab[0, T_LIVE] > 0)
    def _():
        v1[...] = split2(next1)
        off_products(k12, tab, 0, v1, None, None, back)
        extra_tiles(tab, 0, side.at[1], halo, tile, v1, None, None, back, x12)

    next0 = side[0, 19:20, :] * before0 + (acc_in[0] + from_left(flags, got_a, got_b))
    new[0] = next0
    send_a[...] = jnp.where(flags[4] == 0, back[...], next0)
    send_b[...] = jnp.where(flags[4] == 0, next0, back[...])
    lane = lax.broadcasted_iota(jnp.int32, (N_PROBES, SUB), 1)
    cross = inner(before0, next0) + inner(before1, next1)
    own = inner(next0, next0) + inner(next1, next1)
    total = jnp.where(lane == 2 * level - 1, cross, jnp.where(lane == 2 * level, own, 0.0))
    if level == 1:
        total = jnp.where(lane == 0, inner(before0, before0) + inner(before1, before1), total)
    else:
        total = total + mom_in[...]
    mom[...] = total


def moment_kernel(flags, side, acc, got_a, got_b, w, mom_in, mom):
    lane = lax.broadcasted_iota(jnp.int32, (N_PROBES, SUB), 1)
    one = w[0]
    two = w[1]
    arrived = from_left(flags, got_a, got_b)
    cross = inner(one, side[0, 19:20, :] * one + (acc[0] + 2.0 * arrived))
    cross = cross + inner(two, side[1, 19:20, :] * two + acc[1])
    mom[...] = mom_in[...] + jnp.where(lane == 5, cross, 0.0)


def last_kernel(flags, tab, k12, x12, side, halo, got_a, got_b, acc, w, new, tile, v2):
    new[1] = side[1, 19:20, :] * w[1] + acc[1]
    new[0] = side[0, 19:20, :] * w[0] + (acc[0] + from_left(flags, got_a, got_b))
    halo_w = jnp.where(flags[4] == 0, got_a[...], got_b[...])
    halo_product(tab, k12, x12, side, halo, halo_w, tile, v2, new.at[1])


def unsort(rank, fields, store, repeat):
    def block(blk, carry):
        stacked = jnp.concatenate([split2(field[blk]) for field in fields], axis=0)
        place = places()

        def strip(c, carry):
            piece = rank[blk, :, at(c, STRIP)]
            got = None
            for g in range(STRIPS):
                part = nn(stacked[:, g * STRIP : (g + 1) * STRIP], one_hot(marks(piece, g), place))
                got = part if got is None else got + part
            size = 2 * N_PROBES
            store(blk, at(blk * STRIPS + c, STRIP), [halves(got[size * k : size * (k + 1)]) for k in range(len(fields))])
            return carry

        repeat(STRIPS, strip)
        return carry

    repeat(2, block)


def unsort_kernel(rank, wa, wb, wc, out):
    def store(blk, cols, values):
        for k, value in enumerate(values):
            out[16 * k : 16 * (k + 1), cols] = value

    unsort(rank, (wa, wb, wc), store, each)


def steps_kernel(mom, out, sound):
    lane = lax.broadcasted_iota(jnp.int32, (N_PROBES, SUB), 1)
    mu = [jnp.sum(jnp.where(lane == k, mom[...], 0.0), axis=1, keepdims=True) for k in range(6)]
    fine = []

    def form(left, right, shift):
        total, size = None, None
        for i, a in enumerate(left):
            for j, b in enumerate(right):
                part = (a * b) * mu[i + j + shift]
                total = part if total is None else total + part
                size = jnp.abs(part) if size is None else size + jnp.abs(part)
        fine.append(size <= 4000.0 * total)
        return total

    one = jnp.ones((N_PROBES, 1), f32)
    d = [one]
    r = [one]
    s = []
    rr = mu[0]
    for it in range(3):
        step = rr / form(d, d, 1)
        moved = [step * v for v in d]
        s = [a + b for a, b in zip(s + [0.0] * (len(d) - len(s)), moved)]
        r = [r[0]] + [(r[i] if i < len(r) else 0.0) - moved[i - 1] for i in range(1, len(moved) + 1)]
        if it < 2:
            new = form(r, r, 0)
            ratio = new / rr
            d = [r[i] + (ratio * d[i] if i < len(d) else 0.0) for i in range(len(r))]
            rr = new
    norms = [jnp.sqrt(mu[0]), jnp.sqrt(mu[2]), jnp.sqrt(mu[4])]
    norms.append(mu[5] / norms[2])
    size = sum(jnp.abs(a) * b for a, b in zip(r, norms))
    fine.append(size <= 200.0 * jnp.sqrt(rr))
    all_fine = fine[0]
    for other in fine[1:]:
        all_fine = all_fine & other
    sound[0] = jnp.min(jnp.where(all_fine, 1.0, 0.0)).astype(jnp.int32)
    table = jnp.zeros((N_PROBES, SUB), f32)
    for k, value in enumerate(s + r):
        table = jnp.where(lane == k, value, table)
    out[...] = table


def combine_kernel(steps, probes, u, sol, res):
    c = [steps[:, k : k + 1] for k in range(7)]

    def part(b, carry):
        here = at(b, BLK)
        w = [probes[:, here], u[0:16, here], u[16:32, here], u[32:48, here]]
        sol[:, here] = (c[0] * w[0] + c[1] * w[1]) + c[2] * w[2]
        res[:, here] = ((c[3] * w[0] + c[4] * w[1]) + c[5] * w[2]) + c[6] * w[3]
        return carry

    each(2, part)


def plain_product_kernel(flags, side, halo, got_a, got_b, d, acc, back, v, v2):
    acc[...] = jnp.zeros(FIELDS, f32)
    back[...] = jnp.zeros(FIELD, f32)
    v[...] = d[...].astype(bf16)
    v2[...] = jnp.where(flags[4] == 0, got_a[...], got_b[...]).astype(bf16)

    def pair(row_side, col_side, v_row, v_col, acc_row, acc_col):
        def row(i, carry):
            def col(j, carry):
                rows, cols = at(i, SUB), at(j, SUB)
                tile = tile_by_difference(
                    row_side, pl.multiple_of(i * SUB, SUB), col_side, pl.multiple_of(j * SUB, SUB)
                )
                acc_row[:, rows] += nt(v_col[:, cols], tile)
                if acc_col is not None:
                    acc_col[:, cols] += nn(v_row[:, rows], tile)
                return carry

            return lax.fori_loop(0, SUBS, col, carry)

        lax.fori_loop(0, SUBS, row, 0)

    def block(blk, carry):
        @pl.when(flags[2 * blk] > 0)
        def _():
            pair(side.at[blk], side.at[blk], None, v.at[blk], acc.at[blk], None)

        return carry

    lax.fori_loop(0, 2, block, 0)

    @pl.when(flags[1] > 0)
    def _():
        pair(side.at[0], side.at[1], v.at[0], v.at[1], acc.at[0], acc.at[1])

    @pl.when(flags[3] > 0)
    def _():
        pair(side.at[1], halo, v.at[1], v2, acc.at[1], back)


def plain_image_kernel(flags, side, acc, got_a, got_b, d, image, part):
    image[0] = side[0, 19:20, :] * d[0] + (acc[0] + from_left(flags, got_a, got_b))
    image[1] = side[1, 19:20, :] * d[1] + acc[1]
    part[...] = jnp.broadcast_to(inner(d[0], image[0]) + inner(d[1], image[1]), (N_PROBES, SUB))


def plain_step_kernel(norm, curvature, x, r, d, image, x_new, r_new, part):
    step = norm[:, 0:1] / curvature[:, 0:1]
    for b in range(2):
        x_new[b] = x[b] + step * d[b]
        r_new[b] = r[b] - step * image[b]
    part[...] = jnp.broadcast_to(inner(r_new[0], r_new[0]) + inner(r_new[1], r_new[1]), (N_PROBES, SUB))


def plain_turn_kernel(norm, new, r, d, d_new):
    ratio = new[:, 0:1] / norm[:, 0:1]
    for b in range(2):
        d_new[b] = r[b] + ratio * d[b]


def plain_start_kernel(side, x, r, part):
    x[...] = jnp.zeros(FIELDS, f32)
    r[0] = side[0, 0:16, :]
    r[1] = side[1, 0:16, :]
    part[...] = jnp.broadcast_to(inner(r[0], r[0]) + inner(r[1], r[1]), (N_PROBES, SUB))


def plain_end_kernel(rank, x, r, sol, res):
    def store(blk, cols, values):
        sol[:, cols], res[:, cols] = values

    unsort(rank, (x, r), store, looped)


def plain_steps(flags, side, halo, rank, shape):
    fields = jax.ShapeDtypeStruct(FIELDS, f32)
    field = jax.ShapeDtypeStruct(FIELD, f32)
    sums = jax.ShapeDtypeStruct((N_PROBES, SUB), f32)

    def small(body, outs, ins, scratch=()):
        return call(body, outs, ins, (VMEM,) * len(outs), list(scratch), 10**7, "plain")

    x, r, part = small(plain_start_kernel, (fields, fields, sums), [VMEM])(side)

    def step(_, state):
        x, r, d, norm = state
        got = swapped_both(d[0], d[0])
        acc, back = small(
            plain_product_kernel,
            (fields, field),
            [SMEM] + [VMEM] * 5,
            (pltpu.VMEM(FIELDS, bf16), pltpu.VMEM(FIELD, bf16)),
        )(flags, side, halo, *got, d)
        got = swapped_both(back, back)
        image, part = small(plain_image_kernel, (fields, sums), [SMEM] + [VMEM] * 5)(flags, side, acc, *got, d)
        curvature = sum_over(part, "gx")
        x, r, part = small(plain_step_kernel, (fields, fields, sums), [VMEM] * 6)(norm, curvature, x, r, d, image)
        new = sum_over(part, "gx")
        (d,) = small(plain_turn_kernel, (fields,), [VMEM] * 4)(norm, new, r, d)
        return x, r, d, new

    x, r, _, _ = lax.fori_loop(0, 3, step, (x, r, r, sum_over(part, "gx")))
    out = jax.ShapeDtypeStruct(shape, f32)
    return small(plain_end_kernel, (out, out), [VMEM] * 3)(rank, x, r)


def swapped_both(to_a, to_b):
    count = lax.axis_size("gx")
    a = lax.ppermute(to_a, "gx", [(k, k ^ 1) for k in range(count)])
    ends = [(0, 0), (count - 1, count - 1)]
    b = lax.ppermute(to_b, "gx", ends + [(k, ((k + 1) ^ 1) - 1) for k in range(1, count - 1)])
    return a, b


def sum_over(value, axis):
    count = lax.axis_size(axis)
    if count & (count - 1):
        return lax.psum(value, axis)
    step = 1
    while step < count:
        radix = min(4, count // step)
        parts = [value] + [
            lax.ppermute(value, axis, [(k, k ^ (m * step)) for k in range(count)]) for m in range(1, radix)
        ]
        while len(parts) > 1:
            parts = [parts[m] + parts[m + 1] for m in range(0, len(parts), 2)]
        value = parts[0]
        step *= radix
    return value


def on_device(points, noise_var, probes, pair_list, counts):
    noise = noise_var.reshape(1, -1)
    field = pltpu.VMEM(FIELD, f32)
    fields = pltpu.VMEM(FIELDS, f32)
    one_side = pltpu.VMEM((24, BLK), f32)
    right = pltpu.VMEM((N_FEATURES, BLK), bf16)
    table = pltpu.SMEM((STRIPS, SUB), jnp.int32)
    moments = pltpu.VMEM((N_PROBES, SUB), f32)
    off = pltpu.VMEM((STRIPS, STRIP, OFF_W), bf16)
    outside = pltpu.VMEM((STRIPS, STRIP, SUB), bf16)
    far_space = pl.BlockSpec(memory_space=pltpu.HBM)
    shape = probes.shape

    side, first, lhs, rank, probes, flags, tab = call(
        sort_kernel,
        (
            pltpu.VMEM((2, 24, BLK), f32),
            one_side,
            pltpu.VMEM((2, BLK, N_FEATURES), bf16),
            pltpu.VMEM((2, 1, BLK), jnp.int32),
            pltpu.VMEM(shape, f32),
            pltpu.SMEM((6,), jnp.int32),
            pltpu.SMEM((3 * STRIPS, SUB), jnp.int32),
        ),
        [far_space] * 4 + [SMEM],
        (VMEM,) * 5 + (SMEM,) * 2,
        [
            pltpu.VMEM(points.shape, f32),
            pltpu.VMEM(noise.shape, f32),
            pltpu.SMEM(pair_list.shape[::-1], jnp.int32),
            pltpu.VMEM((3 * STRIPS, SUB), jnp.int32),
            pltpu.VMEM((2, 1, BLK), f32),
            pltpu.VMEM((2, STRIPS, STRIP, SUB), f32),
            pltpu.SemaphoreType.DMA((4,)),
        ],
        10**9,
        "sort_blocks",
    )(*[pltpu.with_memory_space_constraint(x, pltpu.HBM) for x in (points, noise, probes, pair_list.T)], counts)

    halos = swapped_both(first, first)
    kd, acc = call(
        diag_build_kernel,
        (pltpu.VMEM((2, STRIPS, STRIP, DIAG_W), bf16), fields),
        [SMEM] + [VMEM] * 2,
        (VMEM,) * 2,
        [TILE, SPLIT, right],
        3 * 10**9,
        "diag_build",
    )(tab, side, lhs)
    k12, x12, tab12, acc, back, halo = call(
        halo_build_kernel,
        (off, outside, table, fields, field, one_side),
        [SMEM] + [VMEM] * 5,
        (VMEM, VMEM, SMEM, VMEM, VMEM, VMEM),
        [pltpu.VMEM((STRIPS, SUB), jnp.int32), TILE, SPLIT, SPLIT, right, pltpu.SemaphoreType.DMA((1,))],
        3 * 10**9,
        "halo_build",
    )(flags, side, lhs, *halos, acc)
    got = swapped_both(back, back)
    k01, x01, acc = call(
        own_build_kernel,
        (off, outside, fields),
        [SMEM] + [VMEM] * 3,
        (VMEM,) * 3,
        [TILE, SPLITS, right],
        5 * 10**9,
        "own_build",
    )(tab, side, lhs, acc)

    w = side
    mom = jnp.zeros((N_PROBES, SUB), f32)
    kept = []
    for level in (1, 2):
        w, send_a, send_b, mom = call(
            functools.partial(finish_kernel, level),
            (fields, field, field, moments),
            [SMEM] * 2 + [VMEM] * 9,
            (VMEM,) * 4,
            [TILE, SPLIT, SPLIT, pltpu.VMEM(FIELD, f32), pltpu.VMEM(FIELD, f32)],
            10**9,
            "finish",
        )(flags, tab12, k12, x12, side, halo, *got, acc, w, mom)
        kept.append(w)
        got = swapped_both(send_a, send_b)
        (acc,) = call(
            own_apply_kernel,
            (fields,),
            [SMEM] + [VMEM] * 5,
            (VMEM,),
            [TILE, SPLITS],
            2 * 10**9,
            "own_apply",
        )(tab, kd, k01, x01, side, w)
    mom = call(moment_kernel, moments, [SMEM] + [VMEM] * 6, VMEM, [], 10**7, "moment")(
        flags, side, acc, *got, w, mom
    )
    total = sum_over(mom, "gx")
    kept.append(
        call(last_kernel, fields, [SMEM] * 2 + [VMEM] * 8, VMEM, [TILE, SPLIT], 10**9, "last")(
            flags, tab12, k12, x12, side, halo, *got, acc, w
        )
    )
    given = call(
        unsort_kernel,
        pltpu.VMEM((3 * N_PROBES, 2 * BLK), f32),
        [VMEM] * 4,
        VMEM,
        [],
        4 * 96 * BLK * BLK,
        "unsort",
    )(rank, *kept)
    steps, sound = call(
        steps_kernel,
        (moments, pltpu.SMEM((1,), jnp.int32)),
        [VMEM],
        (VMEM, SMEM),
        [],
        10**6,
        "steps",
    )(total)

    def from_basis():
        out = jax.ShapeDtypeStruct(shape, f32)
        return tuple(
            call(combine_kernel, (out, out), [VMEM] * 3, (VMEM, VMEM), [], 10**6, "combine")(steps, probes, given)
        )

    def from_start():
        return tuple(plain_steps(flags, side, halo, rank, shape))

    return lax.cond(sound[0] > 0, from_basis, from_start)


def solution(mesh):
    placed = (
        P(None, ("groups", "gx")),
        P(("groups", "gx")),
        P(None, ("groups", "gx")),
        P(("groups", "gx"), None),
        P(("groups", "gx")),
    )
    return jax.shard_map(
        on_device,
        mesh=mesh,
        in_specs=placed,
        out_specs=(P(None, ("groups", "gx")), P(None, ("groups", "gx"))),
        check_vma=False,
    )
```

```python
import functools

import jax
import jax.numpy as jnp
from jax import lax
from jax.experimental import pallas as pl
from jax.experimental.pallas import tpu as pltpu
from jax.sharding import PartitionSpec as P

BLK = 2048
STRIP = 256
STRIPS = BLK // STRIP
SUB = 128
SUBS = BLK // SUB
OFF_W = 768
OFF_SUBS = OFF_W // SUB
EDGE_W = 512
DIAG_W = 512
N_PROBES = 16
N_FEATURES = 64
MIB = 1 << 20

VMEM = pl.BlockSpec(memory_space=pltpu.VMEM)
SMEM = pl.BlockSpec(memory_space=pltpu.SMEM)

f32 = jnp.float32
bf16 = jnp.bfloat16

T_START, T_END, T_EXTRA, T_LIVE, T_NEXT = 0, 1, 2, 3, 4


def nt(left, right):
    return lax.dot_general(left, right, (((1,), (1,)), ((), ())), preferred_element_type=f32)


def nn(left, right):
    return jnp.dot(left, right, preferred_element_type=f32)


def split2(value):
    high = value.astype(bf16)
    low = (value - high.astype(f32)).astype(bf16)
    return jnp.concatenate([high, low], axis=0)


def halves(value):
    n = value.shape[0] // 2
    return value[:n] + value[n:]


def split3(value):
    high = value.astype(bf16).astype(f32)
    rest = value - high
    mid = rest.astype(bf16).astype(f32)
    return high, mid, rest - mid


def multiple(value, size):
    return value if isinstance(value, int) else pl.multiple_of(value, size)


def at(index, size):
    return pl.ds(multiple(index * size, size), size)


def looped(count, body):
    lax.fori_loop(0, count, body, 0)


def each(count, body):
    for index in range(count):
        body(index, 0)


def one_hot(marked, place):
    parts = []
    for h in range(2):
        hit = jnp.broadcast_to(marked[:, h * SUB : (h + 1) * SUB], (STRIP, SUB)) == place
        parts.append(jnp.where(hit, jnp.ones((STRIP, SUB), bf16), jnp.zeros((STRIP, SUB), bf16)))
    return jnp.concatenate(parts, axis=1)


def places():
    return lax.broadcasted_iota(jnp.int32, (STRIP, SUB), 0).astype(f32).astype(bf16)


def marks(rank, g):
    group = lax.shift_right_logical(rank, 8)
    within = jnp.bitwise_and(rank, STRIP - 1)
    return jnp.where(group == g, within, -1).astype(f32).astype(bf16)


def turned(value):
    shape = (STRIP, STRIP)
    same = lax.broadcasted_iota(jnp.int32, shape, 0) == lax.broadcasted_iota(jnp.int32, shape, 1)
    return nt(jnp.where(same, 1.0, 0.0).astype(bf16), value).astype(bf16)


def fill_ranks(y_row, rank_ref, key_ref, before_ref):
    low = jnp.min(y_row, axis=1, keepdims=True)
    high = jnp.max(y_row, axis=1, keepdims=True)
    scale = 255.0 / jnp.maximum(high - low, 1e-6)
    key_ref[...] = jnp.clip(jnp.floor((y_row - low) * scale), 0.0, 255.0)
    shape = (STRIP, STRIP)
    first = lax.broadcasted_iota(jnp.int32, shape, 0)
    second = lax.broadcasted_iota(jnp.int32, shape, 1)
    upper = jnp.where(first < second, 1.0, 0.0).astype(bf16)
    lower = jnp.where(second < first, 1.0, 0.0).astype(bf16)
    ones = jnp.ones((STRIP, SUB), bf16)
    value = places()
    total = None
    for j in range(STRIPS):
        counts = nn(one_hot(key_ref[:, at(j, STRIP)].astype(bf16), value), ones)
        before_ref[j] = counts
        total = counts if total is None else total + counts
    coarse = jnp.floor(total * (1.0 / 16.0)) * 16.0
    before = nn(lower, coarse.astype(bf16)) + nn(lower, (total - coarse).astype(bf16))
    for j in range(STRIPS):
        after = before + before_ref[j]
        before_ref[j] = before
        before = after
    for j in range(STRIPS):
        hit = one_hot(key_ref[:, at(j, STRIP)].astype(bf16), value)
        before = before_ref[j]
        ahead = nn(hit, upper) + jnp.concatenate([before, before], axis=1)
        rank = jnp.sum(hit.astype(f32) * ahead, axis=0, keepdims=True)
        rank_ref[:, at(j, STRIP)] = rank.astype(jnp.int32)


def plan(row_side, col_side, live, diag):
    y_row = row_side[17:18, :]
    y_col = col_side[17:18, :]
    strips = jnp.concatenate([y_row[:, i * STRIP : (i + 1) * STRIP] for i in range(STRIPS)], axis=0)
    low = jnp.min(strips, axis=1, keepdims=True) - 1.0
    high = jnp.max(strips, axis=1, keepdims=True) + 1.0
    groups = jnp.concatenate([y_col[:, j * SUB : (j + 1) * SUB] for j in range(SUBS)], axis=0)
    own = lax.broadcasted_iota(jnp.int32, (SUBS, SUB), 0) == lax.broadcasted_iota(jnp.int32, (SUBS, SUB), 1)

    def across(value):
        return jnp.sum(jnp.where(own, value, 0.0), axis=0, keepdims=True)

    group_low = across(jnp.min(groups, axis=1, keepdims=True))
    group_high = across(jnp.max(groups, axis=1, keepdims=True))
    lane = lax.broadcasted_iota(jnp.int32, (STRIPS, SUB), 1)
    place = lane.astype(f32)
    reached = (group_low < high) & (group_high > low) & (lane < SUBS)
    end = jnp.max(jnp.where(reached, place + 1.0, 0.0), axis=1, keepdims=True)
    strip = lax.broadcasted_iota(jnp.int32, (STRIPS, 1), 0)
    if diag:
        start = strip.astype(f32) * 2.0
        after = start + DIAG_W // SUB
    else:
        first = jnp.min(jnp.where(reached, place, float(SUBS)), axis=1, keepdims=True)
        width = jnp.where((strip == 0) | (strip == STRIPS - 1), float(EDGE_W // SUB), float(OFF_SUBS))
        start = jnp.minimum(first, SUBS - width)
        after = start + width
    extra = jnp.sum(jnp.maximum(end - after, 0.0), axis=0, keepdims=True)
    alive = live.astype(f32)
    table = jnp.where(lane == T_START, start, jnp.where(lane == T_END, end, extra))
    table = jnp.where(lane == T_NEXT, after, table)
    return jnp.where(lane == T_LIVE, alive, table).astype(jnp.int32)


def row_id(width):
    return lax.broadcasted_iota(jnp.int32, (8, width), 0)


def features(offset, left):
    first, second, third = split3(offset)
    norm = jnp.sum(offset * offset, axis=0, keepdims=True)
    n1, n2, n3 = split3(norm)
    ids = row_id(offset.shape[1])
    own, other = (0, 3) if left else (3, 0)
    norms = jnp.where(ids == own, n1, jnp.where(ids == own + 1, n2, jnp.where(ids == own + 2, n3, 0.0)))
    norms = jnp.where((ids >= other) & (ids < other + 3), 1.0, norms)
    if left:
        first, second, third = -2.0 * first, -2.0 * second, -2.0 * third
        parts = [first, first, first, second, second, third]
    else:
        parts = [first, second, third, first, second, first]
    return jnp.concatenate(parts + [norms, jnp.zeros_like(norms)], axis=0), norm


def sort_kernel(
    pts_hbm, nv_hbm, pr_hbm, pair_hbm, count, side, first, lhs, rank, pr_ref, flags, tab,
    pts_ref, nv_ref, pair, plan_ref, key_ref, before_ref, sems
):
    copies = [
        pltpu.make_async_copy(src, dst, sems.at[k])
        for k, (src, dst) in enumerate(
            ((pts_hbm, pts_ref), (nv_hbm, nv_ref), (pr_hbm, pr_ref), (pair_hbm, pair))
        )
    ]
    for copy in copies:
        copy.start()
    copies[0].wait()
    for blk in range(2):
        fill_ranks(pts_ref[1:2, at(blk, BLK)], rank.at[blk], key_ref.at[blk], before_ref.at[blk])
    for copy in copies[1:]:
        copy.wait()
    for local in range(2):
        for ahead in range(2):
            flags[2 * local + ahead] = live_flag(pair, count, local, ahead)
    position = lax.shift_right_logical(pair[0, 0], 1)
    flags[4] = jnp.bitwise_and(position, 1)
    flags[5] = jnp.where(position > 0, 1, 0)
    place = places()
    for blk in range(2):
        cols = at(blk, BLK)
        aux = jnp.concatenate(
            [pts_ref[0:3, cols] * 2.0, nv_ref[:, cols], jnp.zeros((4, BLK), f32)], axis=0
        )
        data = jnp.concatenate(
            [*split3(pr_ref[:, cols]), *split3(aux), jnp.zeros((8, BLK), f32)], axis=0
        ).astype(bf16)
        centre = 0.5 * (jnp.min(aux, axis=1, keepdims=True) + jnp.max(aux, axis=1, keepdims=True))
        centre = jnp.concatenate([jnp.zeros((4, 1), f32), centre[0:3], jnp.zeros((1, 1), f32)], axis=0)
        ranks = rank[blk]
        for g in range(STRIPS):
            marked = marks(ranks, g)
            got = None
            for c in range(STRIPS):
                here = slice(c * STRIP, (c + 1) * STRIP)
                part = nt(data[:, here], one_hot(marked[:, here], place))
                got = part if got is None else got + part
            low = (got[0:16] + got[16:32]) + got[32:48]
            high = ((got[48:56] + got[56:64]) + got[64:72]) + centre
            side[blk, 0:16, at(g, STRIP)] = low
            side[blk, 16:24, at(g, STRIP)] = high
            if blk == 0:
                first[0:16, at(g, STRIP)] = low
                first[16:24, at(g, STRIP)] = high
    plan_ref[0:8, :] = plan(side.at[0], side.at[0], flags[0], True)
    plan_ref[8:16, :] = plan(side.at[0], side.at[1], flags[1], False)
    plan_ref[16:24, :] = plan(side.at[1], side.at[1], flags[2], True)
    copy = pltpu.make_async_copy(plan_ref, tab, sems.at[0])
    copy.start()
    for blk in range(2):
        rows, norm = features(offset_of(side.at[blk], side.at[blk]), True)
        side[blk, 23:24, :] = norm
        rows = rows.astype(bf16)
        for c in range(STRIPS):
            lhs[blk, at(c, STRIP), :] = turned(rows[:, c * STRIP : (c + 1) * STRIP])
    copy.wait()


def offset_of(side_ref, centre_ref):
    centre = jnp.concatenate([centre_ref[20:23, 0:1], jnp.zeros((5, 1), f32)], axis=0)
    return jnp.where(row_id(BLK) < 3, side_ref[16:24, :] - centre, 0.0)


def live_flag(pair_ref, count_ref, local, ahead):
    flag = jnp.int32(0)
    for s in range(pair_ref.shape[1]):
        owner = pair_ref[0, s]
        match = (
            (jnp.int32(s) < count_ref[0])
            & (jnp.bitwise_and(owner, 1) == local)
            & (pair_ref[1, s] - owner == ahead)
        )
        flag = jnp.where(match, jnp.int32(1), flag)
    return flag


def kernel_values(squared):
    squared = jnp.maximum(squared, 1e-30)
    t = jnp.maximum(1.0 - squared * lax.rsqrt(squared), 0.0)
    t2 = t * t
    return ((t2 * t2) * (1.25 - t)).astype(bf16)


def tile_by_difference(row_side, row_at, col_side, col_at):
    squared = None
    for axis in range(16, 19):
        mine = jnp.broadcast_to(row_side[axis : axis + 1, pl.ds(row_at, SUB)], (SUB, SUB)).T
        diff = mine - col_side[axis : axis + 1, pl.ds(col_at, SUB)]
        part = diff * diff
        squared = part if squared is None else squared + part
    return kernel_values(squared)


def fast_strip(k_ref, i, lhs, rhs, start, width):
    for h in range(width // STRIP):
        right = rhs[:, pl.ds(multiple(start + h * STRIP, SUB), STRIP)]
        for g in range(STRIP // SUB):
            left = lhs[pl.ds(multiple(i * STRIP + g * SUB, SUB), SUB), :]
            k_ref[i, g * SUB : (g + 1) * SUB, h * STRIP : (h + 1) * STRIP] = kernel_values(nn(left, right))


def slow_build(k_ref, row_side, col_side, first_group, groups):
    def strip(i, carry):
        def tile(j, carry):
            for g in range(STRIP // SUB):
                at = pl.multiple_of(i * STRIP + g * SUB, SUB)
                col_at = pl.multiple_of(jnp.minimum(first_group(i) + j, SUBS - 1) * SUB, SUB)
                k_ref[i, g * SUB : (g + 1) * SUB, pl.ds(pl.multiple_of(j * SUB, SUB), SUB)] = (
                    tile_by_difference(row_side, at, col_side, col_at)
                )
            return carry

        return lax.fori_loop(0, groups, tile, carry)

    lax.fori_loop(0, STRIPS, strip, 0)


def right_features(rhs, row_side, col_side):
    offset = offset_of(col_side, row_side)
    rows, norm = features(offset, False)
    rhs[...] = rows.astype(bf16)
    return jnp.max(jnp.maximum(norm, row_side[23:24, :])) <= 100.0


def off_pair(k_ref, tab_ref, base, lhs, rhs, row_side, col_side, v_row, v_col, acc_row, acc_col):
    near = right_features(rhs, row_side, col_side)

    @pl.when(near)
    def _():
        def strip(i, carry):
            start = pl.multiple_of(tab_ref[base + i, T_START] * SUB, SUB)
            fast_strip(k_ref, i, lhs, rhs, start, off_width(i))
            owner_strip(k_ref, i, start, v_col, acc_row)
            partner_strip(k_ref, i, start, v_row, acc_col)
            return carry

        each(STRIPS, strip)

    @pl.when(jnp.logical_not(near))
    def _():
        slow_build(k_ref, row_side, col_side, lambda i: tab_ref[base + i, T_START], OFF_SUBS)
        off_products(k_ref, tab_ref, base, v_row, v_col, acc_row, acc_col, looped)

    return near, lhs, rhs


def diag_pair(k_ref, lhs, rhs, side, v, acc):
    near = right_features(rhs, side, side)

    @pl.when(near)
    def _():
        def strip(i, carry):
            fast_strip(k_ref, i, lhs, rhs, i * STRIP, DIAG_W)
            diag_strip(k_ref, i, v, acc, DIAG_W)
            return carry

        each(STRIPS - 1, strip)
        fast_strip(k_ref, STRIPS - 1, lhs, rhs, (STRIPS - 1) * STRIP, STRIP)
        diag_strip(k_ref, STRIPS - 1, v, acc, STRIP)

    @pl.when(jnp.logical_not(near))
    def _():
        slow_build(k_ref, side, side, lambda i: 2 * i, DIAG_W // SUB)
        diag_products(k_ref, v, acc, looped)


def off_width(i):
    return EDGE_W if isinstance(i, int) and i in (0, STRIPS - 1) else OFF_W


def owner_strip(k_ref, i, start, v_col, acc_row):
    width = off_width(i)
    acc_row[:, at(i, STRIP)] += halves(nt(v_col[:, pl.ds(start, width)], k_ref[i, :, :width]))


def partner_strip(k_ref, i, start, v_row, acc_col):
    width = off_width(i)
    acc_col[:, pl.ds(start, width)] += halves(nn(v_row[:, at(i, STRIP)], k_ref[i, :, :width]))


def off_products(k_ref, tab_ref, base, v_row, v_col, acc_row, acc_col, repeat=each):
    def strip(i, carry):
        start = pl.multiple_of(tab_ref[base + i, T_START] * SUB, SUB)
        if acc_row is not None:
            owner_strip(k_ref, i, start, v_col, acc_row)
        if acc_col is not None:
            partner_strip(k_ref, i, start, v_row, acc_col)
        return carry

    strip(0, 0)
    repeat(STRIPS - 2, lambda i, carry: strip(i + 1, carry))
    strip(STRIPS - 1, 0)


def diag_strip(k_ref, i, v_ref, acc_ref, width):
    start = multiple(i * STRIP, STRIP)
    acc_ref[:, at(i, STRIP)] += halves(nt(v_ref[:, pl.ds(start, width)], k_ref[i, :, :width]))
    if width > STRIP:
        acc_ref[:, at(i + 1, STRIP)] += halves(nn(v_ref[:, at(i, STRIP)], k_ref[i, :, STRIP:width]))


def diag_products(k_ref, v_ref, acc_ref, repeat=each):
    def strip(i, carry):
        diag_strip(k_ref, i, v_ref, acc_ref, DIAG_W)
        return carry

    repeat(STRIPS - 1, strip)
    diag_strip(k_ref, STRIPS - 1, v_ref, acc_ref, STRIP)


def extra_tiles(
    tab_ref, base, row_side, col_side, tile_ref, v_row, v_col, acc_row, acc_col, kept=None, fill=None
):
    @pl.when(tab_ref[base, T_EXTRA] > 0)
    def _():
        def strip(i, carry):
            here = pl.ds(pl.multiple_of(i * STRIP, STRIP), STRIP)
            first = tab_ref[base + i, T_NEXT]

            def tile(j, carry):
                col_at = pl.multiple_of(j * SUB, SUB)
                there = pl.ds(col_at, SUB)

                def by_difference():
                    for g in range(STRIP // SUB):
                        row_at = pl.multiple_of(i * STRIP + g * SUB, SUB)
                        tile_ref[g * SUB : (g + 1) * SUB, :] = tile_by_difference(row_side, row_at, col_side, col_at)

                if kept is None:
                    by_difference()
                elif fill is None:
                    pl.when(j > first)(by_difference)

                    @pl.when(j == first)
                    def _():
                        tile_ref[...] = kept[i]
                else:
                    near, lhs, rhs = fill
                    pl.when(jnp.logical_not(near))(by_difference)

                    @pl.when(near)
                    def _():
                        tile_ref[...] = kernel_values(nn(lhs[here, :], rhs[:, there]))

                    @pl.when(j == first)
                    def _():
                        kept[i] = tile_ref[...]

                if acc_row is not None:
                    acc_row[:, here] += halves(nt(v_col[:, there], tile_ref[...]))
                if acc_col is not None:
                    acc_col[:, there] += halves(nn(v_row[:, here], tile_ref[...]))
                return carry

            return lax.fori_loop(first, tab_ref[base + i, T_END], tile, carry)

        lax.fori_loop(0, STRIPS, strip, 0)


TILE = pltpu.VMEM((STRIP, SUB), bf16)
SPLIT = pltpu.VMEM((2 * N_PROBES, BLK), bf16)
SPLITS = pltpu.VMEM((2, 2 * N_PROBES, BLK), bf16)
FIELD = (N_PROBES, BLK)
FIELDS = (2, N_PROBES, BLK)


def call(body, outs, ins, out_specs, scratch, flops, name, limit=12):
    def run(*args):
        return pl.pallas_call(
            body,
            out_shape=outs,
            in_specs=ins,
            out_specs=out_specs,
            scratch_shapes=scratch,
            compiler_params=pltpu.CompilerParams(vmem_limit_bytes=limit * MIB),
            cost_estimate=pl.CostEstimate(flops=flops, bytes_accessed=MIB, transcendentals=0),
            name=name,
        )(*args)

    return run


def diag_build_kernel(tab, side, lhs, kd, acc, tile, v, rhs):
    def block(blk, carry):
        acc[blk] = jnp.zeros(FIELD, f32)
        base = 2 * STRIPS * blk

        @pl.when(tab[base, T_LIVE] > 0)
        def _():
            v[...] = split2(side[blk, 0:16, :])
            diag_pair(kd.at[blk], lhs.at[blk], rhs, side.at[blk], v, acc.at[blk])
            extra_tiles(tab, base, side.at[blk], side.at[blk], tile, v, v, acc.at[blk], acc.at[blk])

        return carry

    each(2, block)


def halo_build_kernel(
    flags, side, lhs, got_a, got_b, acc_in, k12, x12, tab, acc, back, halo, plan_ref, tile, v1, v2, rhs, sem
):
    halo[...] = jnp.where(flags[4] == 0, got_a[...], got_b[...])
    plan_ref[...] = plan(side.at[1], halo, flags[3], False)
    copy = pltpu.make_async_copy(plan_ref, tab, sem.at[0])
    copy.start()
    acc[...] = acc_in[...]
    back[...] = jnp.zeros(FIELD, f32)
    copy.wait()

    @pl.when(flags[3] > 0)
    def _():
        v1[...] = split2(side[1, 0:16, :])
        v2[...] = split2(halo[0:16, :])
        fill = off_pair(k12, tab, 0, lhs.at[1], rhs, side.at[1], halo, v1, v2, acc.at[1], back)
        extra_tiles(tab, 0, side.at[1], halo, tile, v1, v2, acc.at[1], back, x12, fill)


def own_build_kernel(tab, side, lhs, acc_in, k01, x01, acc, tile, v, rhs):
    acc[...] = acc_in[...]

    @pl.when(tab[STRIPS, T_LIVE] > 0)
    def _():
        v[0] = split2(side[0, 0:16, :])
        v[1] = split2(side[1, 0:16, :])
        args = side.at[0], side.at[1]
        ends = v.at[0], v.at[1], acc.at[0], acc.at[1]
        fill = off_pair(k01, tab, STRIPS, lhs.at[0], rhs, *args, *ends)
        extra_tiles(tab, STRIPS, *args, tile, *ends, x01, fill)


def own_apply_kernel(tab, kd, k01, x01, side, w, acc, tile, v):
    def block(blk, carry):
        acc[blk] = jnp.zeros(FIELD, f32)
        v[blk] = split2(w[blk])
        base = 2 * STRIPS * blk

        @pl.when(tab[base, T_LIVE] > 0)
        def _():
            diag_products(kd.at[blk], v.at[blk], acc.at[blk])
            extra_tiles(
                tab, base, side.at[blk], side.at[blk], tile, v.at[blk], v.at[blk], acc.at[blk], acc.at[blk]
            )

        return carry

    each(2, block)

    @pl.when(tab[STRIPS, T_LIVE] > 0)
    def _():
        ends = v.at[0], v.at[1], acc.at[0], acc.at[1]
        off_products(k01, tab, STRIPS, *ends)
        extra_tiles(tab, STRIPS, side.at[0], side.at[1], tile, *ends, x01)


def from_left(flags, got_a, got_b):
    arrived = jnp.where(flags[4] == 0, got_b[...], got_a[...])
    return jnp.where(flags[5] > 0, arrived, 0.0)


def inner(left, right):
    return jnp.sum(left * right, axis=1, keepdims=True)


def halo_product(tab, k12, x12, side, halo, halo_w, tile, v2, acc):
    @pl.when(tab[0, T_LIVE] > 0)
    def _():
        v2[...] = split2(halo_w)
        off_products(k12, tab, 0, None, v2, acc, None)
        extra_tiles(tab, 0, side.at[1], halo, tile, None, v2, acc, None, x12)


def finish_kernel(
    level, flags, tab, k12, x12, side, halo, got_a, got_b, acc_in, w, mom_in, new, send_a, send_b, mom,
    tile, v1, v2, acc, back
):
    acc[...] = acc_in[1]
    if level > 1:
        halo_w = jnp.where(flags[4] == 0, got_a[...], got_b[...])
        halo_product(tab, k12, x12, side, halo, halo_w, tile, v2, acc)
    before0 = w[0, 0:16, :]
    before1 = w[1, 0:16, :]
    next1 = side[1, 19:20, :] * before1 + acc[...]
    new[1] = next1
    back[...] = jnp.zeros(FIELD, f32)

    @pl.when(tab[0, T_LIVE] > 0)
    def _():
        v1[...] = split2(next1)
        off_products(k12, tab, 0, v1, None, None, back)
        extra_tiles(tab, 0, side.at[1], halo, tile, v1, None, None, back, x12)

    next0 = side[0, 19:20, :] * before0 + (acc_in[0] + from_left(flags, got_a, got_b))
    new[0] = next0
    send_a[...] = jnp.where(flags[4] == 0, back[...], next0)
    send_b[...] = jnp.where(flags[4] == 0, next0, back[...])
    lane = lax.broadcasted_iota(jnp.int32, (N_PROBES, SUB), 1)
    cross = inner(before0, next0) + inner(before1, next1)
    own = inner(next0, next0) + inner(next1, next1)
    total = jnp.where(lane == 2 * level - 1, cross, jnp.where(lane == 2 * level, own, 0.0))
    if level == 1:
        total = jnp.where(lane == 0, inner(before0, before0) + inner(before1, before1), total)
    else:
        total = total + mom_in[...]
    mom[...] = total


def moment_kernel(flags, side, acc, got_a, got_b, w, mom_in, mom):
    lane = lax.broadcasted_iota(jnp.int32, (N_PROBES, SUB), 1)
    one = w[0]
    two = w[1]
    arrived = from_left(flags, got_a, got_b)
    cross = inner(one, side[0, 19:20, :] * one + (acc[0] + 2.0 * arrived))
    cross = cross + inner(two, side[1, 19:20, :] * two + acc[1])
    mom[...] = mom_in[...] + jnp.where(lane == 5, cross, 0.0)


def last_kernel(flags, tab, k12, x12, side, halo, got_a, got_b, acc, w, new, tile, v2):
    new[1] = side[1, 19:20, :] * w[1] + acc[1]
    new[0] = side[0, 19:20, :] * w[0] + (acc[0] + from_left(flags, got_a, got_b))
    halo_w = jnp.where(flags[4] == 0, got_a[...], got_b[...])
    halo_product(tab, k12, x12, side, halo, halo_w, tile, v2, new.at[1])


def unsort(rank, fields, store, repeat):
    def block(blk, carry):
        stacked = jnp.concatenate([split2(field[blk]) for field in fields], axis=0)
        place = places()

        def strip(c, carry):
            piece = rank[blk, :, at(c, STRIP)]
            got = None
            for g in range(STRIPS):
                part = nn(stacked[:, g * STRIP : (g + 1) * STRIP], one_hot(marks(piece, g), place))
                got = part if got is None else got + part
            size = 2 * N_PROBES
            store(blk, at(blk * STRIPS + c, STRIP), [halves(got[size * k : size * (k + 1)]) for k in range(len(fields))])
            return carry

        repeat(STRIPS, strip)
        return carry

    repeat(2, block)


def unsort_kernel(rank, wa, wb, wc, out):
    def store(blk, cols, values):
        for k, value in enumerate(values):
            out[16 * k : 16 * (k + 1), cols] = value

    unsort(rank, (wa, wb, wc), store, each)


def steps_kernel(mom, out, sound):
    lane = lax.broadcasted_iota(jnp.int32, (N_PROBES, SUB), 1)
    mu = [jnp.sum(jnp.where(lane == k, mom[...], 0.0), axis=1, keepdims=True) for k in range(6)]
    fine = []

    def form(left, right, shift):
        total, size = None, None
        for i, a in enumerate(left):
            for j, b in enumerate(right):
                part = (a * b) * mu[i + j + shift]
                total = part if total is None else total + part
                size = jnp.abs(part) if size is None else size + jnp.abs(part)
        fine.append(size <= 4000.0 * total)
        return total

    one = jnp.ones((N_PROBES, 1), f32)
    d = [one]
    r = [one]
    s = []
    rr = mu[0]
    for it in range(3):
        step = rr / form(d, d, 1)
        moved = [step * v for v in d]
        s = [a + b for a, b in zip(s + [0.0] * (len(d) - len(s)), moved)]
        r = [r[0]] + [(r[i] if i < len(r) else 0.0) - moved[i - 1] for i in range(1, len(moved) + 1)]
        if it < 2:
            new = form(r, r, 0)
            ratio = new / rr
            d = [r[i] + (ratio * d[i] if i < len(d) else 0.0) for i in range(len(r))]
            rr = new
    norms = [jnp.sqrt(mu[0]), jnp.sqrt(mu[2]), jnp.sqrt(mu[4])]
    norms.append(mu[5] / norms[2])
    size = sum(jnp.abs(a) * b for a, b in zip(r, norms))
    fine.append(size <= 200.0 * jnp.sqrt(rr))
    all_fine = fine[0]
    for other in fine[1:]:
        all_fine = all_fine & other
    sound[0] = jnp.min(jnp.where(all_fine, 1.0, 0.0)).astype(jnp.int32)
    table = jnp.zeros((N_PROBES, SUB), f32)
    for k, value in enumerate(s + r):
        table = jnp.where(lane == k, value, table)
    out[...] = table


def combine_kernel(steps, probes, u, sol, res):
    c = [steps[:, k : k + 1] for k in range(7)]

    def part(b, carry):
        here = at(b, BLK)
        w = [probes[:, here], u[0:16, here], u[16:32, here], u[32:48, here]]
        sol[:, here] = (c[0] * w[0] + c[1] * w[1]) + c[2] * w[2]
        res[:, here] = ((c[3] * w[0] + c[4] * w[1]) + c[5] * w[2]) + c[6] * w[3]
        return carry

    each(2, part)


def plain_product_kernel(flags, side, halo, got_a, got_b, d, acc, back, v, v2):
    acc[...] = jnp.zeros(FIELDS, f32)
    back[...] = jnp.zeros(FIELD, f32)
    v[...] = d[...].astype(bf16)
    v2[...] = jnp.where(flags[4] == 0, got_a[...], got_b[...]).astype(bf16)

    def pair(row_side, col_side, v_row, v_col, acc_row, acc_col):
        def row(i, carry):
            def col(j, carry):
                rows, cols = at(i, SUB), at(j, SUB)
                tile = tile_by_difference(
                    row_side, pl.multiple_of(i * SUB, SUB), col_side, pl.multiple_of(j * SUB, SUB)
                )
                acc_row[:, rows] += nt(v_col[:, cols], tile)
                if acc_col is not None:
                    acc_col[:, cols] += nn(v_row[:, rows], tile)
                return carry

            return lax.fori_loop(0, SUBS, col, carry)

        lax.fori_loop(0, SUBS, row, 0)

    def block(blk, carry):
        @pl.when(flags[2 * blk] > 0)
        def _():
            pair(side.at[blk], side.at[blk], None, v.at[blk], acc.at[blk], None)

        return carry

    lax.fori_loop(0, 2, block, 0)

    @pl.when(flags[1] > 0)
    def _():
        pair(side.at[0], side.at[1], v.at[0], v.at[1], acc.at[0], acc.at[1])

    @pl.when(flags[3] > 0)
    def _():
        pair(side.at[1], halo, v.at[1], v2, acc.at[1], back)


def plain_image_kernel(flags, side, acc, got_a, got_b, d, image, part):
    image[0] = side[0, 19:20, :] * d[0] + (acc[0] + from_left(flags, got_a, got_b))
    image[1] = side[1, 19:20, :] * d[1] + acc[1]
    part[...] = jnp.broadcast_to(inner(d[0], image[0]) + inner(d[1], image[1]), (N_PROBES, SUB))


def plain_step_kernel(norm, curvature, x, r, d, image, x_new, r_new, part):
    step = norm[:, 0:1] / curvature[:, 0:1]
    for b in range(2):
        x_new[b] = x[b] + step * d[b]
        r_new[b] = r[b] - step * image[b]
    part[...] = jnp.broadcast_to(inner(r_new[0], r_new[0]) + inner(r_new[1], r_new[1]), (N_PROBES, SUB))


def plain_turn_kernel(norm, new, r, d, d_new):
    ratio = new[:, 0:1] / norm[:, 0:1]
    for b in range(2):
        d_new[b] = r[b] + ratio * d[b]


def plain_start_kernel(side, x, r, part):
    x[...] = jnp.zeros(FIELDS, f32)
    r[0] = side[0, 0:16, :]
    r[1] = side[1, 0:16, :]
    part[...] = jnp.broadcast_to(inner(r[0], r[0]) + inner(r[1], r[1]), (N_PROBES, SUB))


def plain_end_kernel(rank, x, r, sol, res):
    def store(blk, cols, values):
        sol[:, cols], res[:, cols] = values

    unsort(rank, (x, r), store, looped)


def plain_steps(flags, side, halo, rank, shape):
    fields = jax.ShapeDtypeStruct(FIELDS, f32)
    field = jax.ShapeDtypeStruct(FIELD, f32)
    sums = jax.ShapeDtypeStruct((N_PROBES, SUB), f32)

    def small(body, outs, ins, scratch=()):
        return call(body, outs, ins, (VMEM,) * len(outs), list(scratch), 10**7, "plain")

    x, r, part = small(plain_start_kernel, (fields, fields, sums), [VMEM])(side)

    def step(_, state):
        x, r, d, norm = state
        got = swapped_both(d[0], d[0])
        acc, back = small(
            plain_product_kernel,
            (fields, field),
            [SMEM] + [VMEM] * 5,
            (pltpu.VMEM(FIELDS, bf16), pltpu.VMEM(FIELD, bf16)),
        )(flags, side, halo, *got, d)
        got = swapped_both(back, back)
        image, part = small(plain_image_kernel, (fields, sums), [SMEM] + [VMEM] * 5)(flags, side, acc, *got, d)
        curvature = sum_over(part, "gx")
        x, r, part = small(plain_step_kernel, (fields, fields, sums), [VMEM] * 6)(norm, curvature, x, r, d, image)
        new = sum_over(part, "gx")
        (d,) = small(plain_turn_kernel, (fields,), [VMEM] * 4)(norm, new, r, d)
        return x, r, d, new

    x, r, _, _ = lax.fori_loop(0, 3, step, (x, r, r, sum_over(part, "gx")))
    out = jax.ShapeDtypeStruct(shape, f32)
    return small(plain_end_kernel, (out, out), [VMEM] * 3)(rank, x, r)


def swapped_both(to_a, to_b):
    count = lax.axis_size("gx")
    a = lax.ppermute(to_a, "gx", [(k, k ^ 1) for k in range(count)])
    ends = [(0, 0), (count - 1, count - 1)]
    b = lax.ppermute(to_b, "gx", ends + [(k, ((k + 1) ^ 1) - 1) for k in range(1, count - 1)])
    return a, b


def sum_over(value, axis):
    count = lax.axis_size(axis)
    if count & (count - 1):
        return lax.psum(value, axis)
    step = 1
    while step < count:
        radix = min(4, count // step)
        parts = [value] + [
            lax.ppermute(value, axis, [(k, k ^ (m * step)) for k in range(count)]) for m in range(1, radix)
        ]
        while len(parts) > 1:
            parts = [parts[m] + parts[m + 1] for m in range(0, len(parts), 2)]
        value = parts[0]
        step *= radix
    return value


def on_device(points, noise_var, probes, pair_list, counts):
    noise = noise_var.reshape(1, -1)
    field = pltpu.VMEM(FIELD, f32)
    fields = pltpu.VMEM(FIELDS, f32)
    one_side = pltpu.VMEM((24, BLK), f32)
    right = pltpu.VMEM((N_FEATURES, BLK), bf16)
    table = pltpu.SMEM((STRIPS, SUB), jnp.int32)
    moments = pltpu.VMEM((N_PROBES, SUB), f32)
    off = pltpu.VMEM((STRIPS, STRIP, OFF_W), bf16)
    outside = pltpu.VMEM((STRIPS, STRIP, SUB), bf16)
    far_space = pl.BlockSpec(memory_space=pltpu.HBM)
    shape = probes.shape

    side, first, lhs, rank, probes, flags, tab = call(
        sort_kernel,
        (
            pltpu.VMEM((2, 24, BLK), f32),
            one_side,
            pltpu.VMEM((2, BLK, N_FEATURES), bf16),
            pltpu.VMEM((2, 1, BLK), jnp.int32),
            pltpu.VMEM(shape, f32),
            pltpu.SMEM((6,), jnp.int32),
            pltpu.SMEM((3 * STRIPS, SUB), jnp.int32),
        ),
        [far_space] * 4 + [SMEM],
        (VMEM,) * 5 + (SMEM,) * 2,
        [
            pltpu.VMEM(points.shape, f32),
            pltpu.VMEM(noise.shape, f32),
            pltpu.SMEM(pair_list.shape[::-1], jnp.int32),
            pltpu.VMEM((3 * STRIPS, SUB), jnp.int32),
            pltpu.VMEM((2, 1, BLK), f32),
            pltpu.VMEM((2, STRIPS, STRIP, SUB), f32),
            pltpu.SemaphoreType.DMA((4,)),
        ],
        10**9,
        "sort_blocks",
    )(*[pltpu.with_memory_space_constraint(x, pltpu.HBM) for x in (points, noise, probes, pair_list.T)], counts)

    halos = swapped_both(first, first)
    kd, acc = call(
        diag_build_kernel,
        (pltpu.VMEM((2, STRIPS, STRIP, DIAG_W), bf16), fields),
        [SMEM] + [VMEM] * 2,
        (VMEM,) * 2,
        [TILE, SPLIT, right],
        3 * 10**9,
        "diag_build",
    )(tab, side, lhs)
    k12, x12, tab12, acc, back, halo = call(
        halo_build_kernel,
        (off, outside, table, fields, field, one_side),
        [SMEM] + [VMEM] * 5,
        (VMEM, VMEM, SMEM, VMEM, VMEM, VMEM),
        [pltpu.VMEM((STRIPS, SUB), jnp.int32), TILE, SPLIT, SPLIT, right, pltpu.SemaphoreType.DMA((1,))],
        3 * 10**9,
        "halo_build",
    )(flags, side, lhs, *halos, acc)
    got = swapped_both(back, back)
    k01, x01, acc = call(
        own_build_kernel,
        (off, outside, fields),
        [SMEM] + [VMEM] * 3,
        (VMEM,) * 3,
        [TILE, SPLITS, right],
        5 * 10**9,
        "own_build",
    )(tab, side, lhs, acc)

    w = side
    mom = jnp.zeros((N_PROBES, SUB), f32)
    kept = []
    for level in (1, 2):
        w, send_a, send_b, mom = call(
            functools.partial(finish_kernel, level),
            (fields, field, field, moments),
            [SMEM] * 2 + [VMEM] * 9,
            (VMEM,) * 4,
            [TILE, SPLIT, SPLIT, pltpu.VMEM(FIELD, f32), pltpu.VMEM(FIELD, f32)],
            10**9,
            "finish",
        )(flags, tab12, k12, x12, side, halo, *got, acc, w, mom)
        kept.append(w)
        got = swapped_both(send_a, send_b)
        (acc,) = call(
            own_apply_kernel,
            (fields,),
            [SMEM] + [VMEM] * 5,
            (VMEM,),
            [TILE, SPLITS],
            2 * 10**9,
            "own_apply",
        )(tab, kd, k01, x01, side, w)
    mom = call(moment_kernel, moments, [SMEM] + [VMEM] * 6, VMEM, [], 10**7, "moment")(
        flags, side, acc, *got, w, mom
    )
    total = sum_over(mom, "gx")
    kept.append(
        call(last_kernel, fields, [SMEM] * 2 + [VMEM] * 8, VMEM, [TILE, SPLIT], 10**9, "last")(
            flags, tab12, k12, x12, side, halo, *got, acc, w
        )
    )
    given = call(
        unsort_kernel,
        pltpu.VMEM((3 * N_PROBES, 2 * BLK), f32),
        [VMEM] * 4,
        VMEM,
        [],
        4 * 96 * BLK * BLK,
        "unsort",
    )(rank, *kept)
    steps, sound = call(
        steps_kernel,
        (moments, pltpu.SMEM((1,), jnp.int32)),
        [VMEM],
        (VMEM, SMEM),
        [],
        10**6,
        "steps",
    )(total)

    def from_basis():
        out = jax.ShapeDtypeStruct(shape, f32)
        return tuple(
            call(combine_kernel, (out, out), [VMEM] * 3, (VMEM, VMEM), [], 10**6, "combine")(steps, probes, given)
        )

    def from_start():
        return tuple(plain_steps(flags, side, halo, rank, shape))

    return lax.cond(sound[0] > 0, from_basis, from_start)


def solution(mesh):
    placed = (
        P(None, ("groups", "gx")),
        P(("groups", "gx")),
        P(None, ("groups", "gx")),
        P(("groups", "gx"), None),
        P(("groups", "gx")),
    )
    return jax.shard_map(
        on_device,
        mesh=mesh,
        in_specs=placed,
        out_specs=(P(None, ("groups", "gx")), P(None, ("groups", "gx"))),
        check_vma=False,
    )
```

```python
import functools

import jax
import jax.numpy as jnp
from jax import lax
from jax.experimental import pallas as pl
from jax.experimental.pallas import tpu as pltpu
from jax.sharding import PartitionSpec as P

BLK = 2048
STRIP = 256
STRIPS = BLK // STRIP
SUB = 128
SUBS = BLK // SUB
OFF_W = 768
OFF_SUBS = OFF_W // SUB
EDGE_W = 512
DIAG_W = 512
N_PROBES = 16
N_FEATURES = 64
MIB = 1 << 20

VMEM = pl.BlockSpec(memory_space=pltpu.VMEM)
SMEM = pl.BlockSpec(memory_space=pltpu.SMEM)

f32 = jnp.float32
bf16 = jnp.bfloat16

T_START, T_END, T_EXTRA, T_LIVE, T_NEXT = 0, 1, 2, 3, 4


def nt(left, right):
    return lax.dot_general(left, right, (((1,), (1,)), ((), ())), preferred_element_type=f32)


def nn(left, right):
    return jnp.dot(left, right, preferred_element_type=f32)


def split2(value):
    high = value.astype(bf16)
    low = (value - high.astype(f32)).astype(bf16)
    return jnp.concatenate([high, low], axis=0)


def halves(value):
    n = value.shape[0] // 2
    return value[:n] + value[n:]


def split3(value):
    high = value.astype(bf16).astype(f32)
    rest = value - high
    mid = rest.astype(bf16).astype(f32)
    return high, mid, rest - mid


def multiple(value, size):
    return value if isinstance(value, int) else pl.multiple_of(value, size)


def at(index, size):
    return pl.ds(multiple(index * size, size), size)


def looped(count, body):
    lax.fori_loop(0, count, body, 0)


def each(count, body):
    for index in range(count):
        body(index, 0)


def one_hot(marked, place):
    parts = []
    for h in range(2):
        hit = jnp.broadcast_to(marked[:, h * SUB : (h + 1) * SUB], (STRIP, SUB)) == place
        parts.append(jnp.where(hit, jnp.ones((STRIP, SUB), bf16), jnp.zeros((STRIP, SUB), bf16)))
    return jnp.concatenate(parts, axis=1)


def places():
    return lax.broadcasted_iota(jnp.int32, (STRIP, SUB), 0).astype(f32).astype(bf16)


def marks(rank, g):
    group = lax.shift_right_logical(rank, 8)
    within = jnp.bitwise_and(rank, STRIP - 1)
    return jnp.where(group == g, within, -1).astype(f32).astype(bf16)


def turned(value):
    shape = (STRIP, STRIP)
    same = lax.broadcasted_iota(jnp.int32, shape, 0) == lax.broadcasted_iota(jnp.int32, shape, 1)
    return nt(jnp.where(same, 1.0, 0.0).astype(bf16), value).astype(bf16)


def fill_ranks(y_row, rank_ref, key_ref, before_ref):
    low = jnp.min(y_row, axis=1, keepdims=True)
    high = jnp.max(y_row, axis=1, keepdims=True)
    scale = 255.0 / jnp.maximum(high - low, 1e-6)
    key_ref[...] = jnp.clip(jnp.floor((y_row - low) * scale), 0.0, 255.0)
    shape = (STRIP, STRIP)
    first = lax.broadcasted_iota(jnp.int32, shape, 0)
    second = lax.broadcasted_iota(jnp.int32, shape, 1)
    upper = jnp.where(first < second, 1.0, 0.0).astype(bf16)
    lower = jnp.where(second < first, 1.0, 0.0).astype(bf16)
    ones = jnp.ones((STRIP, SUB), bf16)
    value = places()
    total = None
    for j in range(STRIPS):
        counts = nn(one_hot(key_ref[:, at(j, STRIP)].astype(bf16), value), ones)
        before_ref[j] = counts
        total = counts if total is None else total + counts
    coarse = jnp.floor(total * (1.0 / 16.0)) * 16.0
    before = nn(lower, coarse.astype(bf16)) + nn(lower, (total - coarse).astype(bf16))
    for j in range(STRIPS):
        after = before + before_ref[j]
        before_ref[j] = before
        before = after
    for j in range(STRIPS):
        hit = one_hot(key_ref[:, at(j, STRIP)].astype(bf16), value)
        before = before_ref[j]
        ahead = nn(hit, upper) + jnp.concatenate([before, before], axis=1)
        rank = jnp.sum(hit.astype(f32) * ahead, axis=0, keepdims=True)
        rank_ref[:, at(j, STRIP)] = rank.astype(jnp.int32)


def plan(row_side, col_side, live, diag):
    y_row = row_side[17:18, :]
    y_col = col_side[17:18, :]
    strips = jnp.concatenate([y_row[:, i * STRIP : (i + 1) * STRIP] for i in range(STRIPS)], axis=0)
    low = jnp.min(strips, axis=1, keepdims=True) - 1.0
    high = jnp.max(strips, axis=1, keepdims=True) + 1.0
    groups = jnp.concatenate([y_col[:, j * SUB : (j + 1) * SUB] for j in range(SUBS)], axis=0)
    own = lax.broadcasted_iota(jnp.int32, (SUBS, SUB), 0) == lax.broadcasted_iota(jnp.int32, (SUBS, SUB), 1)

    def across(value):
        return jnp.sum(jnp.where(own, value, 0.0), axis=0, keepdims=True)

    group_low = across(jnp.min(groups, axis=1, keepdims=True))
    group_high = across(jnp.max(groups, axis=1, keepdims=True))
    lane = lax.broadcasted_iota(jnp.int32, (STRIPS, SUB), 1)
    place = lane.astype(f32)
    reached = (group_low < high) & (group_high > low) & (lane < SUBS)
    end = jnp.max(jnp.where(reached, place + 1.0, 0.0), axis=1, keepdims=True)
    strip = lax.broadcasted_iota(jnp.int32, (STRIPS, 1), 0)
    if diag:
        start = strip.astype(f32) * 2.0
        after = start + DIAG_W // SUB
    else:
        first = jnp.min(jnp.where(reached, place, float(SUBS)), axis=1, keepdims=True)
        width = jnp.where((strip == 0) | (strip == STRIPS - 1), float(EDGE_W // SUB), float(OFF_SUBS))
        start = jnp.minimum(first, SUBS - width)
        after = start + width
    extra = jnp.sum(jnp.maximum(end - after, 0.0), axis=0, keepdims=True)
    alive = live.astype(f32)
    table = jnp.where(lane == T_START, start, jnp.where(lane == T_END, end, extra))
    table = jnp.where(lane == T_NEXT, after, table)
    return jnp.where(lane == T_LIVE, alive, table).astype(jnp.int32)


def row_id(width):
    return lax.broadcasted_iota(jnp.int32, (8, width), 0)


def features(offset, left):
    first, second, third = split3(offset)
    norm = jnp.sum(offset * offset, axis=0, keepdims=True)
    n1, n2, n3 = split3(norm)
    ids = row_id(offset.shape[1])
    own, other = (0, 3) if left else (3, 0)
    norms = jnp.where(ids == own, n1, jnp.where(ids == own + 1, n2, jnp.where(ids == own + 2, n3, 0.0)))
    norms = jnp.where((ids >= other) & (ids < other + 3), 1.0, norms)
    if left:
        first, second, third = -2.0 * first, -2.0 * second, -2.0 * third
        parts = [first, first, first, second, second, third]
    else:
        parts = [first, second, third, first, second, first]
    return jnp.concatenate(parts + [norms, jnp.zeros_like(norms)], axis=0), norm


def sort_kernel(
    pts_hbm, nv_hbm, pr_hbm, pair_hbm, count, side, first, lhs, rank, pr_ref, flags, tab,
    pts_ref, nv_ref, pair, plan_ref, key_ref, before_ref, sems
):
    copies = [
        pltpu.make_async_copy(src, dst, sems.at[k])
        for k, (src, dst) in enumerate(
            ((pts_hbm, pts_ref), (nv_hbm, nv_ref), (pr_hbm, pr_ref), (pair_hbm, pair))
        )
    ]
    for copy in copies:
        copy.start()
    copies[0].wait()
    for blk in range(2):
        fill_ranks(pts_ref[1:2, at(blk, BLK)], rank.at[blk], key_ref.at[blk], before_ref.at[blk])
    for copy in copies[1:]:
        copy.wait()
    for local in range(2):
        for ahead in range(2):
            flags[2 * local + ahead] = live_flag(pair, count, local, ahead)
    position = lax.shift_right_logical(pair[0, 0], 1)
    flags[4] = jnp.bitwise_and(position, 1)
    flags[5] = jnp.where(position > 0, 1, 0)
    place = places()
    for blk in range(2):
        cols = at(blk, BLK)
        aux = jnp.concatenate(
            [pts_ref[0:3, cols] * 2.0, nv_ref[:, cols], jnp.zeros((4, BLK), f32)], axis=0
        )
        data = jnp.concatenate(
            [*split3(pr_ref[:, cols]), *split3(aux), jnp.zeros((8, BLK), f32)], axis=0
        ).astype(bf16)
        centre = 0.5 * (jnp.min(aux, axis=1, keepdims=True) + jnp.max(aux, axis=1, keepdims=True))
        centre = jnp.concatenate([jnp.zeros((4, 1), f32), centre[0:3], jnp.zeros((1, 1), f32)], axis=0)
        ranks = rank[blk]
        for g in range(STRIPS):
            marked = marks(ranks, g)
            got = None
            for c in range(STRIPS):
                here = slice(c * STRIP, (c + 1) * STRIP)
                part = nt(data[:, here], one_hot(marked[:, here], place))
                got = part if got is None else got + part
            low = (got[0:16] + got[16:32]) + got[32:48]
            high = ((got[48:56] + got[56:64]) + got[64:72]) + centre
            side[blk, 0:16, at(g, STRIP)] = low
            side[blk, 16:24, at(g, STRIP)] = high
            if blk == 0:
                first[0:16, at(g, STRIP)] = low
                first[16:24, at(g, STRIP)] = high
    plan_ref[0:8, :] = plan(side.at[0], side.at[0], flags[0], True)
    plan_ref[8:16, :] = plan(side.at[0], side.at[1], flags[1], False)
    plan_ref[16:24, :] = plan(side.at[1], side.at[1], flags[2], True)
    copy = pltpu.make_async_copy(plan_ref, tab, sems.at[0])
    copy.start()
    for blk in range(2):
        rows, norm = features(offset_of(side.at[blk], side.at[blk]), True)
        side[blk, 23:24, :] = norm
        rows = rows.astype(bf16)
        for c in range(STRIPS):
            lhs[blk, at(c, STRIP), :] = turned(rows[:, c * STRIP : (c + 1) * STRIP])
    copy.wait()


def offset_of(side_ref, centre_ref):
    centre = jnp.concatenate([centre_ref[20:23, 0:1], jnp.zeros((5, 1), f32)], axis=0)
    return jnp.where(row_id(BLK) < 3, side_ref[16:24, :] - centre, 0.0)


def live_flag(pair_ref, count_ref, local, ahead):
    flag = jnp.int32(0)
    for s in range(pair_ref.shape[1]):
        owner = pair_ref[0, s]
        match = (
            (jnp.int32(s) < count_ref[0])
            & (jnp.bitwise_and(owner, 1) == local)
            & (pair_ref[1, s] - owner == ahead)
        )
        flag = jnp.where(match, jnp.int32(1), flag)
    return flag


def kernel_values(squared):
    squared = jnp.maximum(squared, 1e-30)
    t = jnp.maximum(1.0 - squared * lax.rsqrt(squared), 0.0)
    t2 = t * t
    return ((t2 * t2) * (1.25 - t)).astype(bf16)


def tile_by_difference(row_side, row_at, col_side, col_at):
    squared = None
    for axis in range(16, 19):
        mine = jnp.broadcast_to(row_side[axis : axis + 1, pl.ds(row_at, SUB)], (SUB, SUB)).T
        diff = mine - col_side[axis : axis + 1, pl.ds(col_at, SUB)]
        part = diff * diff
        squared = part if squared is None else squared + part
    return kernel_values(squared)


def fast_strip(k_ref, i, lhs, rhs, start, width):
    for h in range(width // STRIP):
        right = rhs[:, pl.ds(multiple(start + h * STRIP, SUB), STRIP)]
        for g in range(STRIP // SUB):
            left = lhs[pl.ds(multiple(i * STRIP + g * SUB, SUB), SUB), :]
            k_ref[i, g * SUB : (g + 1) * SUB, h * STRIP : (h + 1) * STRIP] = kernel_values(nn(left, right))


def slow_build(k_ref, row_side, col_side, first_group, groups):
    def strip(i, carry):
        def tile(j, carry):
            for g in range(STRIP // SUB):
                at = pl.multiple_of(i * STRIP + g * SUB, SUB)
                col_at = pl.multiple_of(jnp.minimum(first_group(i) + j, SUBS - 1) * SUB, SUB)
                k_ref[i, g * SUB : (g + 1) * SUB, pl.ds(pl.multiple_of(j * SUB, SUB), SUB)] = (
                    tile_by_difference(row_side, at, col_side, col_at)
                )
            return carry

        return lax.fori_loop(0, groups, tile, carry)

    lax.fori_loop(0, STRIPS, strip, 0)


def right_features(rhs, row_side, col_side):
    offset = offset_of(col_side, row_side)
    rows, norm = features(offset, False)
    rhs[...] = rows.astype(bf16)
    return jnp.max(jnp.maximum(norm, row_side[23:24, :])) <= 100.0


def off_pair(k_ref, tab_ref, base, lhs, rhs, row_side, col_side, v_row, v_col, acc_row, acc_col):
    near = right_features(rhs, row_side, col_side)

    @pl.when(near)
    def _():
        def strip(i, carry):
            start = pl.multiple_of(tab_ref[base + i, T_START] * SUB, SUB)
            fast_strip(k_ref, i, lhs, rhs, start, off_width(i))
            owner_strip(k_ref, i, start, v_col, acc_row)
            partner_strip(k_ref, i, start, v_row, acc_col)
            return carry

        each(STRIPS, strip)

    @pl.when(jnp.logical_not(near))
    def _():
        slow_build(k_ref, row_side, col_side, lambda i: tab_ref[base + i, T_START], OFF_SUBS)
        off_products(k_ref, tab_ref, base, v_row, v_col, acc_row, acc_col, looped)

    return near, lhs, rhs


def diag_pair(k_ref, lhs, rhs, side, v, acc):
    near = right_features(rhs, side, side)

    @pl.when(near)
    def _():
        def strip(i, carry):
            fast_strip(k_ref, i, lhs, rhs, i * STRIP, DIAG_W)
            diag_strip(k_ref, i, v, acc, DIAG_W)
            return carry

        each(STRIPS - 1, strip)
        fast_strip(k_ref, STRIPS - 1, lhs, rhs, (STRIPS - 1) * STRIP, STRIP)
        diag_strip(k_ref, STRIPS - 1, v, acc, STRIP)

    @pl.when(jnp.logical_not(near))
    def _():
        slow_build(k_ref, side, side, lambda i: 2 * i, DIAG_W // SUB)
        diag_products(k_ref, v, acc, looped)


def off_width(i):
    return EDGE_W if isinstance(i, int) and i in (0, STRIPS - 1) else OFF_W


def owner_strip(k_ref, i, start, v_col, acc_row):
    width = off_width(i)
    acc_row[:, at(i, STRIP)] += halves(nt(v_col[:, pl.ds(start, width)], k_ref[i, :, :width]))


def partner_strip(k_ref, i, start, v_row, acc_col):
    width = off_width(i)
    acc_col[:, pl.ds(start, width)] += halves(nn(v_row[:, at(i, STRIP)], k_ref[i, :, :width]))


def off_products(k_ref, tab_ref, base, v_row, v_col, acc_row, acc_col, repeat=each):
    def strip(i, carry):
        start = pl.multiple_of(tab_ref[base + i, T_START] * SUB, SUB)
        if acc_row is not None:
            owner_strip(k_ref, i, start, v_col, acc_row)
        if acc_col is not None:
            partner_strip(k_ref, i, start, v_row, acc_col)
        return carry

    strip(0, 0)
    repeat(STRIPS - 2, lambda i, carry: strip(i + 1, carry))
    strip(STRIPS - 1, 0)


def diag_strip(k_ref, i, v_ref, acc_ref, width):
    start = multiple(i * STRIP, STRIP)
    acc_ref[:, at(i, STRIP)] += halves(nt(v_ref[:, pl.ds(start, width)], k_ref[i, :, :width]))
    if width > STRIP:
        acc_ref[:, at(i + 1, STRIP)] += halves(nn(v_ref[:, at(i, STRIP)], k_ref[i, :, STRIP:width]))


def diag_products(k_ref, v_ref, acc_ref, repeat=each):
    def strip(i, carry):
        diag_strip(k_ref, i, v_ref, acc_ref, DIAG_W)
        return carry

    repeat(STRIPS - 1, strip)
    diag_strip(k_ref, STRIPS - 1, v_ref, acc_ref, STRIP)


def extra_tiles(
    tab_ref, base, row_side, col_side, tile_ref, v_row, v_col, acc_row, acc_col, kept=None, fill=None
):
    @pl.when(tab_ref[base, T_EXTRA] > 0)
    def _():
        def strip(i, carry):
            here = pl.ds(pl.multiple_of(i * STRIP, STRIP), STRIP)
            first = tab_ref[base + i, T_NEXT]

            def tile(j, carry):
                col_at = pl.multiple_of(j * SUB, SUB)
                there = pl.ds(col_at, SUB)

                def by_difference():
                    for g in range(STRIP // SUB):
                        row_at = pl.multiple_of(i * STRIP + g * SUB, SUB)
                        tile_ref[g * SUB : (g + 1) * SUB, :] = tile_by_difference(row_side, row_at, col_side, col_at)

                def multiply(values):
                    if acc_row is not None:
                        acc_row[:, here] += halves(nt(v_col[:, there], values))
                    if acc_col is not None:
                        acc_col[:, there] += halves(nn(v_row[:, here], values))

                if kept is not None and fill is None:

                    @pl.when(j == first)
                    def _():
                        multiply(kept[i])

                    @pl.when(j > first)
                    def _():
                        by_difference()
                        multiply(tile_ref[...])

                    return carry

                if fill is None:
                    by_difference()
                else:
                    near, lhs, rhs = fill
                    pl.when(jnp.logical_not(near))(by_difference)

                    @pl.when(near)
                    def _():
                        tile_ref[...] = kernel_values(nn(lhs[here, :], rhs[:, there]))

                    @pl.when(j == first)
                    def _():
                        kept[i] = tile_ref[...]

                multiply(tile_ref[...])
                return carry

            return lax.fori_loop(first, tab_ref[base + i, T_END], tile, carry)

        lax.fori_loop(0, STRIPS, strip, 0)


TILE = pltpu.VMEM((STRIP, SUB), bf16)
SPLIT = pltpu.VMEM((2 * N_PROBES, BLK), bf16)
SPLITS = pltpu.VMEM((2, 2 * N_PROBES, BLK), bf16)
FIELD = (N_PROBES, BLK)
FIELDS = (2, N_PROBES, BLK)


def call(body, outs, ins, out_specs, scratch, flops, name, limit=12):
    def run(*args):
        return pl.pallas_call(
            body,
            out_shape=outs,
            in_specs=ins,
            out_specs=out_specs,
            scratch_shapes=scratch,
            compiler_params=pltpu.CompilerParams(vmem_limit_bytes=limit * MIB),
            cost_estimate=pl.CostEstimate(flops=flops, bytes_accessed=MIB, transcendentals=0),
            name=name,
        )(*args)

    return run


def diag_build_kernel(tab, side, lhs, kd, acc, tile, v, rhs):
    def block(blk, carry):
        acc[blk] = jnp.zeros(FIELD, f32)
        base = 2 * STRIPS * blk

        @pl.when(tab[base, T_LIVE] > 0)
        def _():
            v[...] = split2(side[blk, 0:16, :])
            diag_pair(kd.at[blk], lhs.at[blk], rhs, side.at[blk], v, acc.at[blk])
            extra_tiles(tab, base, side.at[blk], side.at[blk], tile, v, v, acc.at[blk], acc.at[blk])

        return carry

    each(2, block)


def halo_build_kernel(
    flags, side, lhs, got_a, got_b, acc_in, k12, x12, tab, acc, back, halo, plan_ref, tile, v1, v2, rhs, sem
):
    halo[...] = jnp.where(flags[4] == 0, got_a[...], got_b[...])
    plan_ref[...] = plan(side.at[1], halo, flags[3], False)
    copy = pltpu.make_async_copy(plan_ref, tab, sem.at[0])
    copy.start()
    acc[...] = acc_in[...]
    back[...] = jnp.zeros(FIELD, f32)
    copy.wait()

    @pl.when(flags[3] > 0)
    def _():
        v1[...] = split2(side[1, 0:16, :])
        v2[...] = split2(halo[0:16, :])
        fill = off_pair(k12, tab, 0, lhs.at[1], rhs, side.at[1], halo, v1, v2, acc.at[1], back)
        extra_tiles(tab, 0, side.at[1], halo, tile, v1, v2, acc.at[1], back, x12, fill)


def own_build_kernel(tab, side, lhs, acc_in, k01, x01, acc, tile, v, rhs):
    acc[...] = acc_in[...]

    @pl.when(tab[STRIPS, T_LIVE] > 0)
    def _():
        v[0] = split2(side[0, 0:16, :])
        v[1] = split2(side[1, 0:16, :])
        args = side.at[0], side.at[1]
        ends = v.at[0], v.at[1], acc.at[0], acc.at[1]
        fill = off_pair(k01, tab, STRIPS, lhs.at[0], rhs, *args, *ends)
        extra_tiles(tab, STRIPS, *args, tile, *ends, x01, fill)


def own_apply_kernel(tab, kd, k01, x01, side, w, acc, tile, v):
    def block(blk, carry):
        acc[blk] = jnp.zeros(FIELD, f32)
        v[blk] = split2(w[blk])
        base = 2 * STRIPS * blk

        @pl.when(tab[base, T_LIVE] > 0)
        def _():
            diag_products(kd.at[blk], v.at[blk], acc.at[blk])
            extra_tiles(
                tab, base, side.at[blk], side.at[blk], tile, v.at[blk], v.at[blk], acc.at[blk], acc.at[blk]
            )

        return carry

    each(2, block)

    @pl.when(tab[STRIPS, T_LIVE] > 0)
    def _():
        ends = v.at[0], v.at[1], acc.at[0], acc.at[1]
        off_products(k01, tab, STRIPS, *ends)
        extra_tiles(tab, STRIPS, side.at[0], side.at[1], tile, *ends, x01)


def from_left(flags, got_a, got_b):
    arrived = jnp.where(flags[4] == 0, got_b[...], got_a[...])
    return jnp.where(flags[5] > 0, arrived, 0.0)


def inner(left, right):
    return jnp.sum(left * right, axis=1, keepdims=True)


def halo_product(tab, k12, x12, side, halo, halo_w, tile, v2, acc):
    @pl.when(tab[0, T_LIVE] > 0)
    def _():
        v2[...] = split2(halo_w)
        off_products(k12, tab, 0, None, v2, acc, None)
        extra_tiles(tab, 0, side.at[1], halo, tile, None, v2, acc, None, x12)


def finish_kernel(
    level, flags, tab, k12, x12, side, halo, got_a, got_b, acc_in, w, mom_in, new, send_a, send_b, mom,
    tile, v1, v2, acc, back
):
    acc[...] = acc_in[1]
    if level > 1:
        halo_w = jnp.where(flags[4] == 0, got_a[...], got_b[...])
        halo_product(tab, k12, x12, side, halo, halo_w, tile, v2, acc)
    before0 = w[0, 0:16, :]
    before1 = w[1, 0:16, :]
    next1 = side[1, 19:20, :] * before1 + acc[...]
    new[1] = next1
    back[...] = jnp.zeros(FIELD, f32)

    @pl.when(tab[0, T_LIVE] > 0)
    def _():
        v1[...] = split2(next1)
        off_products(k12, tab, 0, v1, None, None, back)
        extra_tiles(tab, 0, side.at[1], halo, tile, v1, None, None, back, x12)

    next0 = side[0, 19:20, :] * before0 + (acc_in[0] + from_left(flags, got_a, got_b))
    new[0] = next0
    send_a[...] = jnp.where(flags[4] == 0, back[...], next0)
    send_b[...] = jnp.where(flags[4] == 0, next0, back[...])
    lane = lax.broadcasted_iota(jnp.int32, (N_PROBES, SUB), 1)
    cross = inner(before0, next0) + inner(before1, next1)
    own = inner(next0, next0) + inner(next1, next1)
    total = jnp.where(lane == 2 * level - 1, cross, jnp.where(lane == 2 * level, own, 0.0))
    if level == 1:
        total = jnp.where(lane == 0, inner(before0, before0) + inner(before1, before1), total)
    else:
        total = total + mom_in[...]
    mom[...] = total


def moment_kernel(flags, side, acc, got_a, got_b, w, mom_in, mom):
    lane = lax.broadcasted_iota(jnp.int32, (N_PROBES, SUB), 1)
    one = w[0]
    two = w[1]
    arrived = from_left(flags, got_a, got_b)
    cross = inner(one, side[0, 19:20, :] * one + (acc[0] + 2.0 * arrived))
    cross = cross + inner(two, side[1, 19:20, :] * two + acc[1])
    mom[...] = mom_in[...] + jnp.where(lane == 5, cross, 0.0)


def last_kernel(flags, tab, k12, x12, side, halo, got_a, got_b, acc, w, new, tile, v2):
    new[1] = side[1, 19:20, :] * w[1] + acc[1]
    new[0] = side[0, 19:20, :] * w[0] + (acc[0] + from_left(flags, got_a, got_b))
    halo_w = jnp.where(flags[4] == 0, got_a[...], got_b[...])
    halo_product(tab, k12, x12, side, halo, halo_w, tile, v2, new.at[1])


def unsort(rank, fields, store, repeat):
    def block(blk, carry):
        stacked = jnp.concatenate([split2(field[blk]) for field in fields], axis=0)
        place = places()

        def strip(c, carry):
            piece = rank[blk, :, at(c, STRIP)]
            got = None
            for g in range(STRIPS):
                part = nn(stacked[:, g * STRIP : (g + 1) * STRIP], one_hot(marks(piece, g), place))
                got = part if got is None else got + part
            size = 2 * N_PROBES
            store(blk, at(blk * STRIPS + c, STRIP), [halves(got[size * k : size * (k + 1)]) for k in range(len(fields))])
            return carry

        repeat(STRIPS, strip)
        return carry

    repeat(2, block)


def unsort_kernel(rank, wa, wb, wc, out):
    def store(blk, cols, values):
        for k, value in enumerate(values):
            out[16 * k : 16 * (k + 1), cols] = value

    unsort(rank, (wa, wb, wc), store, each)


def steps_kernel(mom, out, sound):
    lane = lax.broadcasted_iota(jnp.int32, (N_PROBES, SUB), 1)
    mu = [jnp.sum(jnp.where(lane == k, mom[...], 0.0), axis=1, keepdims=True) for k in range(6)]
    fine = []

    def form(left, right, shift):
        total, size = None, None
        for i, a in enumerate(left):
            for j, b in enumerate(right):
                part = (a * b) * mu[i + j + shift]
                total = part if total is None else total + part
                size = jnp.abs(part) if size is None else size + jnp.abs(part)
        fine.append(size <= 4000.0 * total)
        return total

    one = jnp.ones((N_PROBES, 1), f32)
    d = [one]
    r = [one]
    s = []
    rr = mu[0]
    for it in range(3):
        step = rr / form(d, d, 1)
        moved = [step * v for v in d]
        s = [a + b for a, b in zip(s + [0.0] * (len(d) - len(s)), moved)]
        r = [r[0]] + [(r[i] if i < len(r) else 0.0) - moved[i - 1] for i in range(1, len(moved) + 1)]
        if it < 2:
            new = form(r, r, 0)
            ratio = new / rr
            d = [r[i] + (ratio * d[i] if i < len(d) else 0.0) for i in range(len(r))]
            rr = new
    norms = [jnp.sqrt(mu[0]), jnp.sqrt(mu[2]), jnp.sqrt(mu[4])]
    norms.append(mu[5] / norms[2])
    size = sum(jnp.abs(a) * b for a, b in zip(r, norms))
    fine.append(size <= 200.0 * jnp.sqrt(rr))
    all_fine = fine[0]
    for other in fine[1:]:
        all_fine = all_fine & other
    sound[0] = jnp.min(jnp.where(all_fine, 1.0, 0.0)).astype(jnp.int32)
    table = jnp.zeros((N_PROBES, SUB), f32)
    for k, value in enumerate(s + r):
        table = jnp.where(lane == k, value, table)
    out[...] = table


def combine_kernel(steps, probes, u, sol, res):
    c = [steps[:, k : k + 1] for k in range(7)]

    def part(b, carry):
        here = at(b, BLK)
        w = [probes[:, here], u[0:16, here], u[16:32, here], u[32:48, here]]
        sol[:, here] = (c[0] * w[0] + c[1] * w[1]) + c[2] * w[2]
        res[:, here] = ((c[3] * w[0] + c[4] * w[1]) + c[5] * w[2]) + c[6] * w[3]
        return carry

    each(2, part)


def plain_product_kernel(flags, side, halo, got_a, got_b, d, acc, back, v, v2):
    acc[...] = jnp.zeros(FIELDS, f32)
    back[...] = jnp.zeros(FIELD, f32)
    v[...] = d[...].astype(bf16)
    v2[...] = jnp.where(flags[4] == 0, got_a[...], got_b[...]).astype(bf16)

    def pair(row_side, col_side, v_row, v_col, acc_row, acc_col):
        def row(i, carry):
            def col(j, carry):
                rows, cols = at(i, SUB), at(j, SUB)
                tile = tile_by_difference(
                    row_side, pl.multiple_of(i * SUB, SUB), col_side, pl.multiple_of(j * SUB, SUB)
                )
                acc_row[:, rows] += nt(v_col[:, cols], tile)
                if acc_col is not None:
                    acc_col[:, cols] += nn(v_row[:, rows], tile)
                return carry

            return lax.fori_loop(0, SUBS, col, carry)

        lax.fori_loop(0, SUBS, row, 0)

    def block(blk, carry):
        @pl.when(flags[2 * blk] > 0)
        def _():
            pair(side.at[blk], side.at[blk], None, v.at[blk], acc.at[blk], None)

        return carry

    lax.fori_loop(0, 2, block, 0)

    @pl.when(flags[1] > 0)
    def _():
        pair(side.at[0], side.at[1], v.at[0], v.at[1], acc.at[0], acc.at[1])

    @pl.when(flags[3] > 0)
    def _():
        pair(side.at[1], halo, v.at[1], v2, acc.at[1], back)


def plain_image_kernel(flags, side, acc, got_a, got_b, d, image, part):
    image[0] = side[0, 19:20, :] * d[0] + (acc[0] + from_left(flags, got_a, got_b))
    image[1] = side[1, 19:20, :] * d[1] + acc[1]
    part[...] = jnp.broadcast_to(inner(d[0], image[0]) + inner(d[1], image[1]), (N_PROBES, SUB))


def plain_step_kernel(norm, curvature, x, r, d, image, x_new, r_new, part):
    step = norm[:, 0:1] / curvature[:, 0:1]
    for b in range(2):
        x_new[b] = x[b] + step * d[b]
        r_new[b] = r[b] - step * image[b]
    part[...] = jnp.broadcast_to(inner(r_new[0], r_new[0]) + inner(r_new[1], r_new[1]), (N_PROBES, SUB))


def plain_turn_kernel(norm, new, r, d, d_new):
    ratio = new[:, 0:1] / norm[:, 0:1]
    for b in range(2):
        d_new[b] = r[b] + ratio * d[b]


def plain_start_kernel(side, x, r, part):
    x[...] = jnp.zeros(FIELDS, f32)
    r[0] = side[0, 0:16, :]
    r[1] = side[1, 0:16, :]
    part[...] = jnp.broadcast_to(inner(r[0], r[0]) + inner(r[1], r[1]), (N_PROBES, SUB))


def plain_end_kernel(rank, x, r, sol, res):
    def store(blk, cols, values):
        sol[:, cols], res[:, cols] = values

    unsort(rank, (x, r), store, looped)


def plain_steps(flags, side, halo, rank, shape):
    fields = jax.ShapeDtypeStruct(FIELDS, f32)
    field = jax.ShapeDtypeStruct(FIELD, f32)
    sums = jax.ShapeDtypeStruct((N_PROBES, SUB), f32)

    def small(body, outs, ins, scratch=()):
        return call(body, outs, ins, (VMEM,) * len(outs), list(scratch), 10**7, "plain")

    x, r, part = small(plain_start_kernel, (fields, fields, sums), [VMEM])(side)

    def step(_, state):
        x, r, d, norm = state
        got = swapped_both(d[0], d[0])
        acc, back = small(
            plain_product_kernel,
            (fields, field),
            [SMEM] + [VMEM] * 5,
            (pltpu.VMEM(FIELDS, bf16), pltpu.VMEM(FIELD, bf16)),
        )(flags, side, halo, *got, d)
        got = swapped_both(back, back)
        image, part = small(plain_image_kernel, (fields, sums), [SMEM] + [VMEM] * 5)(flags, side, acc, *got, d)
        curvature = sum_over(part, "gx")
        x, r, part = small(plain_step_kernel, (fields, fields, sums), [VMEM] * 6)(norm, curvature, x, r, d, image)
        new = sum_over(part, "gx")
        (d,) = small(plain_turn_kernel, (fields,), [VMEM] * 4)(norm, new, r, d)
        return x, r, d, new

    x, r, _, _ = lax.fori_loop(0, 3, step, (x, r, r, sum_over(part, "gx")))
    out = jax.ShapeDtypeStruct(shape, f32)
    return small(plain_end_kernel, (out, out), [VMEM] * 3)(rank, x, r)


def swapped_both(to_a, to_b):
    count = lax.axis_size("gx")
    a = lax.ppermute(to_a, "gx", [(k, k ^ 1) for k in range(count)])
    ends = [(0, 0), (count - 1, count - 1)]
    b = lax.ppermute(to_b, "gx", ends + [(k, ((k + 1) ^ 1) - 1) for k in range(1, count - 1)])
    return a, b


def sum_over(value, axis):
    count = lax.axis_size(axis)
    if count & (count - 1):
        return lax.psum(value, axis)
    step = 1
    while step < count:
        radix = min(4, count // step)
        parts = [value] + [
            lax.ppermute(value, axis, [(k, k ^ (m * step)) for k in range(count)]) for m in range(1, radix)
        ]
        while len(parts) > 1:
            parts = [parts[m] + parts[m + 1] for m in range(0, len(parts), 2)]
        value = parts[0]
        step *= radix
    return value


def on_device(points, noise_var, probes, pair_list, counts):
    noise = noise_var.reshape(1, -1)
    field = pltpu.VMEM(FIELD, f32)
    fields = pltpu.VMEM(FIELDS, f32)
    one_side = pltpu.VMEM((24, BLK), f32)
    right = pltpu.VMEM((N_FEATURES, BLK), bf16)
    table = pltpu.SMEM((STRIPS, SUB), jnp.int32)
    moments = pltpu.VMEM((N_PROBES, SUB), f32)
    off = pltpu.VMEM((STRIPS, STRIP, OFF_W), bf16)
    outside = pltpu.VMEM((STRIPS, STRIP, SUB), bf16)
    far_space = pl.BlockSpec(memory_space=pltpu.HBM)
    shape = probes.shape

    side, first, lhs, rank, probes, flags, tab = call(
        sort_kernel,
        (
            pltpu.VMEM((2, 24, BLK), f32),
            one_side,
            pltpu.VMEM((2, BLK, N_FEATURES), bf16),
            pltpu.VMEM((2, 1, BLK), jnp.int32),
            pltpu.VMEM(shape, f32),
            pltpu.SMEM((6,), jnp.int32),
            pltpu.SMEM((3 * STRIPS, SUB), jnp.int32),
        ),
        [far_space] * 4 + [SMEM],
        (VMEM,) * 5 + (SMEM,) * 2,
        [
            pltpu.VMEM(points.shape, f32),
            pltpu.VMEM(noise.shape, f32),
            pltpu.SMEM(pair_list.shape[::-1], jnp.int32),
            pltpu.VMEM((3 * STRIPS, SUB), jnp.int32),
            pltpu.VMEM((2, 1, BLK), f32),
            pltpu.VMEM((2, STRIPS, STRIP, SUB), f32),
            pltpu.SemaphoreType.DMA((4,)),
        ],
        10**9,
        "sort_blocks",
    )(*[pltpu.with_memory_space_constraint(x, pltpu.HBM) for x in (points, noise, probes, pair_list.T)], counts)

    halos = swapped_both(first, first)
    kd, acc = call(
        diag_build_kernel,
        (pltpu.VMEM((2, STRIPS, STRIP, DIAG_W), bf16), fields),
        [SMEM] + [VMEM] * 2,
        (VMEM,) * 2,
        [TILE, SPLIT, right],
        3 * 10**9,
        "diag_build",
    )(tab, side, lhs)
    k12, x12, tab12, acc, back, halo = call(
        halo_build_kernel,
        (off, outside, table, fields, field, one_side),
        [SMEM] + [VMEM] * 5,
        (VMEM, VMEM, SMEM, VMEM, VMEM, VMEM),
        [pltpu.VMEM((STRIPS, SUB), jnp.int32), TILE, SPLIT, SPLIT, right, pltpu.SemaphoreType.DMA((1,))],
        3 * 10**9,
        "halo_build",
    )(flags, side, lhs, *halos, acc)
    got = swapped_both(back, back)
    k01, x01, acc = call(
        own_build_kernel,
        (off, outside, fields),
        [SMEM] + [VMEM] * 3,
        (VMEM,) * 3,
        [TILE, SPLITS, right],
        5 * 10**9,
        "own_build",
    )(tab, side, lhs, acc)

    w = side
    mom = jnp.zeros((N_PROBES, SUB), f32)
    kept = []
    for level in (1, 2):
        w, send_a, send_b, mom = call(
            functools.partial(finish_kernel, level),
            (fields, field, field, moments),
            [SMEM] * 2 + [VMEM] * 9,
            (VMEM,) * 4,
            [TILE, SPLIT, SPLIT, pltpu.VMEM(FIELD, f32), pltpu.VMEM(FIELD, f32)],
            10**9,
            "finish",
        )(flags, tab12, k12, x12, side, halo, *got, acc, w, mom)
        kept.append(w)
        got = swapped_both(send_a, send_b)
        (acc,) = call(
            own_apply_kernel,
            (fields,),
            [SMEM] + [VMEM] * 5,
            (VMEM,),
            [TILE, SPLITS],
            2 * 10**9,
            "own_apply",
        )(tab, kd, k01, x01, side, w)
    mom = call(moment_kernel, moments, [SMEM] + [VMEM] * 6, VMEM, [], 10**7, "moment")(
        flags, side, acc, *got, w, mom
    )
    total = sum_over(mom, "gx")
    kept.append(
        call(last_kernel, fields, [SMEM] * 2 + [VMEM] * 8, VMEM, [TILE, SPLIT], 10**9, "last")(
            flags, tab12, k12, x12, side, halo, *got, acc, w
        )
    )
    given = call(
        unsort_kernel,
        pltpu.VMEM((3 * N_PROBES, 2 * BLK), f32),
        [VMEM] * 4,
        VMEM,
        [],
        4 * 96 * BLK * BLK,
        "unsort",
    )(rank, *kept)
    steps, sound = call(
        steps_kernel,
        (moments, pltpu.SMEM((1,), jnp.int32)),
        [VMEM],
        (VMEM, SMEM),
        [],
        10**6,
        "steps",
    )(total)

    def from_basis():
        out = jax.ShapeDtypeStruct(shape, f32)
        return tuple(
            call(combine_kernel, (out, out), [VMEM] * 3, (VMEM, VMEM), [], 10**6, "combine")(steps, probes, given)
        )

    def from_start():
        return tuple(plain_steps(flags, side, halo, rank, shape))

    return lax.cond(sound[0] > 0, from_basis, from_start)


def solution(mesh):
    placed = (
        P(None, ("groups", "gx")),
        P(("groups", "gx")),
        P(None, ("groups", "gx")),
        P(("groups", "gx"), None),
        P(("groups", "gx")),
    )
    return jax.shard_map(
        on_device,
        mesh=mesh,
        in_specs=placed,
        out_specs=(P(None, ("groups", "gx")), P(None, ("groups", "gx"))),
        check_vma=False,
    )
```

```python
import functools

import jax
import jax.numpy as jnp
from jax import lax
from jax.experimental import pallas as pl
from jax.experimental.pallas import tpu as pltpu
from jax.sharding import PartitionSpec as P

BLK = 2048
STRIP = 256
STRIPS = BLK // STRIP
SUB = 128
SUBS = BLK // SUB
OFF_W = 768
OFF_SUBS = OFF_W // SUB
EDGE_W = 512
DIAG_W = 512
N_PROBES = 16
N_FEATURES = 64
MIB = 1 << 20

VMEM = pl.BlockSpec(memory_space=pltpu.VMEM)
SMEM = pl.BlockSpec(memory_space=pltpu.SMEM)

f32 = jnp.float32
bf16 = jnp.bfloat16

T_START, T_END, T_EXTRA, T_LIVE, T_NEXT = 0, 1, 2, 3, 4


def nt(left, right):
    return lax.dot_general(left, right, (((1,), (1,)), ((), ())), preferred_element_type=f32)


def nn(left, right):
    return jnp.dot(left, right, preferred_element_type=f32)


def split2(value):
    high = value.astype(bf16)
    low = (value - high.astype(f32)).astype(bf16)
    return jnp.concatenate([high, low], axis=0)


def halves(value):
    n = value.shape[0] // 2
    return value[:n] + value[n:]


def split3(value):
    high = value.astype(bf16).astype(f32)
    rest = value - high
    mid = rest.astype(bf16).astype(f32)
    return high, mid, rest - mid


def multiple(value, size):
    return value if isinstance(value, int) else pl.multiple_of(value, size)


def at(index, size):
    return pl.ds(multiple(index * size, size), size)


def looped(count, body):
    lax.fori_loop(0, count, body, 0)


def each(count, body):
    for index in range(count):
        body(index, 0)


def one_hot(marked, place):
    parts = []
    for h in range(2):
        hit = jnp.broadcast_to(marked[:, h * SUB : (h + 1) * SUB], (STRIP, SUB)) == place
        parts.append(jnp.where(hit, jnp.ones((STRIP, SUB), bf16), jnp.zeros((STRIP, SUB), bf16)))
    return jnp.concatenate(parts, axis=1)


def places():
    return lax.broadcasted_iota(jnp.int32, (STRIP, SUB), 0).astype(f32).astype(bf16)


def marks(rank, g):
    group = lax.shift_right_logical(rank, 8)
    within = jnp.bitwise_and(rank, STRIP - 1)
    return jnp.where(group == g, within, -1).astype(f32).astype(bf16)


def turned(value):
    shape = (STRIP, STRIP)
    same = lax.broadcasted_iota(jnp.int32, shape, 0) == lax.broadcasted_iota(jnp.int32, shape, 1)
    return nt(jnp.where(same, 1.0, 0.0).astype(bf16), value).astype(bf16)


def fill_ranks(y_row, rank_ref, key_ref, before_ref):
    low = jnp.min(y_row, axis=1, keepdims=True)
    high = jnp.max(y_row, axis=1, keepdims=True)
    scale = 255.0 / jnp.maximum(high - low, 1e-6)
    key_ref[...] = jnp.clip(jnp.floor((y_row - low) * scale), 0.0, 255.0)
    shape = (STRIP, STRIP)
    first = lax.broadcasted_iota(jnp.int32, shape, 0)
    second = lax.broadcasted_iota(jnp.int32, shape, 1)
    upper = jnp.where(first < second, 1.0, 0.0).astype(bf16)
    lower = jnp.where(second < first, 1.0, 0.0).astype(bf16)
    ones = jnp.ones((STRIP, SUB), bf16)
    value = places()
    total = None
    for j in range(STRIPS):
        counts = nn(one_hot(key_ref[:, at(j, STRIP)].astype(bf16), value), ones)
        before_ref[j] = counts
        total = counts if total is None else total + counts
    coarse = jnp.floor(total * (1.0 / 16.0)) * 16.0
    before = nn(lower, coarse.astype(bf16)) + nn(lower, (total - coarse).astype(bf16))
    for j in range(STRIPS):
        after = before + before_ref[j]
        before_ref[j] = before
        before = after
    for j in range(STRIPS):
        hit = one_hot(key_ref[:, at(j, STRIP)].astype(bf16), value)
        before = before_ref[j]
        ahead = nn(hit, upper) + jnp.concatenate([before, before], axis=1)
        rank = jnp.sum(hit.astype(f32) * ahead, axis=0, keepdims=True)
        rank_ref[:, at(j, STRIP)] = rank.astype(jnp.int32)


def plan(row_side, col_side, live, diag):
    y_row = row_side[17:18, :]
    y_col = col_side[17:18, :]
    strips = jnp.concatenate([y_row[:, i * STRIP : (i + 1) * STRIP] for i in range(STRIPS)], axis=0)
    low = jnp.min(strips, axis=1, keepdims=True) - 1.0
    high = jnp.max(strips, axis=1, keepdims=True) + 1.0
    groups = jnp.concatenate([y_col[:, j * SUB : (j + 1) * SUB] for j in range(SUBS)], axis=0)
    own = lax.broadcasted_iota(jnp.int32, (SUBS, SUB), 0) == lax.broadcasted_iota(jnp.int32, (SUBS, SUB), 1)

    def across(value):
        return jnp.sum(jnp.where(own, value, 0.0), axis=0, keepdims=True)

    group_low = across(jnp.min(groups, axis=1, keepdims=True))
    group_high = across(jnp.max(groups, axis=1, keepdims=True))
    lane = lax.broadcasted_iota(jnp.int32, (STRIPS, SUB), 1)
    place = lane.astype(f32)
    reached = (group_low < high) & (group_high > low) & (lane < SUBS)
    end = jnp.max(jnp.where(reached, place + 1.0, 0.0), axis=1, keepdims=True)
    strip = lax.broadcasted_iota(jnp.int32, (STRIPS, 1), 0)
    if diag:
        start = strip.astype(f32) * 2.0
        after = start + DIAG_W // SUB
    else:
        first = jnp.min(jnp.where(reached, place, float(SUBS)), axis=1, keepdims=True)
        width = jnp.where((strip == 0) | (strip == STRIPS - 1), float(EDGE_W // SUB), float(OFF_SUBS))
        start = jnp.minimum(first, SUBS - width)
        after = start + width
    extra = jnp.sum(jnp.maximum(end - after, 0.0), axis=0, keepdims=True)
    alive = live.astype(f32)
    table = jnp.where(lane == T_START, start, jnp.where(lane == T_END, end, extra))
    table = jnp.where(lane == T_NEXT, after, table)
    return jnp.where(lane == T_LIVE, alive, table).astype(jnp.int32)


def row_id(width):
    return lax.broadcasted_iota(jnp.int32, (8, width), 0)


def features(offset, left):
    first, second, third = split3(offset)
    norm = jnp.sum(offset * offset, axis=0, keepdims=True)
    n1, n2, n3 = split3(norm)
    ids = row_id(offset.shape[1])
    own, other = (0, 3) if left else (3, 0)
    norms = jnp.where(ids == own, n1, jnp.where(ids == own + 1, n2, jnp.where(ids == own + 2, n3, 0.0)))
    norms = jnp.where((ids >= other) & (ids < other + 3), 1.0, norms)
    if left:
        first, second, third = -2.0 * first, -2.0 * second, -2.0 * third
        parts = [first, first, first, second, second, third]
    else:
        parts = [first, second, third, first, second, first]
    return jnp.concatenate(parts + [norms, jnp.zeros_like(norms)], axis=0), norm


def sort_kernel(
    pts_hbm, nv_hbm, pr_hbm, pair_hbm, count, side, first, lhs, rank, pr_ref, flags, tab,
    pts_ref, nv_ref, pair, plan_ref, key_ref, before_ref, sems
):
    copies = [
        pltpu.make_async_copy(src, dst, sems.at[k])
        for k, (src, dst) in enumerate(
            ((pts_hbm, pts_ref), (nv_hbm, nv_ref), (pr_hbm, pr_ref), (pair_hbm, pair))
        )
    ]
    for copy in copies:
        copy.start()
    copies[0].wait()
    for blk in range(2):
        fill_ranks(pts_ref[1:2, at(blk, BLK)], rank.at[blk], key_ref.at[blk], before_ref.at[blk])
    for copy in copies[1:]:
        copy.wait()
    for local in range(2):
        for ahead in range(2):
            flags[2 * local + ahead] = live_flag(pair, count, local, ahead)
    position = lax.shift_right_logical(pair[0, 0], 1)
    flags[4] = jnp.bitwise_and(position, 1)
    flags[5] = jnp.where(position > 0, 1, 0)
    place = places()
    for blk in range(2):
        cols = at(blk, BLK)
        aux = jnp.concatenate(
            [pts_ref[0:3, cols] * 2.0, nv_ref[:, cols], jnp.zeros((4, BLK), f32)], axis=0
        )
        data = jnp.concatenate(
            [*split3(pr_ref[:, cols]), *split3(aux), jnp.zeros((8, BLK), f32)], axis=0
        ).astype(bf16)
        centre = 0.5 * (jnp.min(aux, axis=1, keepdims=True) + jnp.max(aux, axis=1, keepdims=True))
        centre = jnp.concatenate([jnp.zeros((4, 1), f32), centre[0:3], jnp.zeros((1, 1), f32)], axis=0)
        ranks = rank[blk]
        for g in range(STRIPS):
            marked = marks(ranks, g)
            got = None
            for c in range(STRIPS):
                here = slice(c * STRIP, (c + 1) * STRIP)
                part = nt(data[:, here], one_hot(marked[:, here], place))
                got = part if got is None else got + part
            low = (got[0:16] + got[16:32]) + got[32:48]
            high = ((got[48:56] + got[56:64]) + got[64:72]) + centre
            side[blk, 0:16, at(g, STRIP)] = low
            side[blk, 16:24, at(g, STRIP)] = high
            if blk == 0:
                first[0:16, at(g, STRIP)] = low
                first[16:24, at(g, STRIP)] = high
    plan_ref[0:8, :] = plan(side.at[0], side.at[0], flags[0], True)
    plan_ref[8:16, :] = plan(side.at[0], side.at[1], flags[1], False)
    plan_ref[16:24, :] = plan(side.at[1], side.at[1], flags[2], True)
    copy = pltpu.make_async_copy(plan_ref, tab, sems.at[0])
    copy.start()
    for blk in range(2):
        rows, _ = features(offset_of(side.at[blk], side.at[blk]), True)
        rows = rows.astype(bf16)
        for c in range(STRIPS):
            lhs[blk, at(c, STRIP), :] = turned(rows[:, c * STRIP : (c + 1) * STRIP])
    copy.wait()


def offset_of(side_ref, centre_ref):
    centre = jnp.concatenate([centre_ref[20:23, 0:1], jnp.zeros((5, 1), f32)], axis=0)
    return jnp.where(row_id(BLK) < 3, side_ref[16:24, :] - centre, 0.0)


def live_flag(pair_ref, count_ref, local, ahead):
    flag = jnp.int32(0)
    for s in range(pair_ref.shape[1]):
        owner = pair_ref[0, s]
        match = (
            (jnp.int32(s) < count_ref[0])
            & (jnp.bitwise_and(owner, 1) == local)
            & (pair_ref[1, s] - owner == ahead)
        )
        flag = jnp.where(match, jnp.int32(1), flag)
    return flag


def kernel_values(squared):
    squared = jnp.maximum(squared, 1e-30)
    t = jnp.maximum(1.0 - squared * lax.rsqrt(squared), 0.0)
    t2 = t * t
    return ((t2 * t2) * (1.25 - t)).astype(bf16)


def tile_by_difference(row_side, row_at, col_side, col_at):
    squared = None
    for axis in range(16, 19):
        mine = jnp.broadcast_to(row_side[axis : axis + 1, pl.ds(row_at, SUB)], (SUB, SUB)).T
        diff = mine - col_side[axis : axis + 1, pl.ds(col_at, SUB)]
        part = diff * diff
        squared = part if squared is None else squared + part
    return kernel_values(squared)


def fast_strip(k_ref, i, lhs, rhs, start, width):
    for h in range(width // STRIP):
        right = rhs[:, pl.ds(multiple(start + h * STRIP, SUB), STRIP)]
        for g in range(STRIP // SUB):
            left = lhs[pl.ds(multiple(i * STRIP + g * SUB, SUB), SUB), :]
            k_ref[i, g * SUB : (g + 1) * SUB, h * STRIP : (h + 1) * STRIP] = kernel_values(nn(left, right))


def slow_build(k_ref, row_side, col_side, first_group, groups):
    def strip(i, carry):
        def tile(j, carry):
            for g in range(STRIP // SUB):
                at = pl.multiple_of(i * STRIP + g * SUB, SUB)
                col_at = pl.multiple_of(jnp.minimum(first_group(i) + j, SUBS - 1) * SUB, SUB)
                k_ref[i, g * SUB : (g + 1) * SUB, pl.ds(pl.multiple_of(j * SUB, SUB), SUB)] = (
                    tile_by_difference(row_side, at, col_side, col_at)
                )
            return carry

        return lax.fori_loop(0, groups, tile, carry)

    lax.fori_loop(0, STRIPS, strip, 0)


def right_features(rhs, row_side, col_side):
    offset = offset_of(col_side, row_side)
    rows, norm = features(offset, False)
    rhs[...] = rows.astype(bf16)
    offset = offset_of(row_side, row_side)
    return jnp.maximum(jnp.max(norm), jnp.max(jnp.sum(offset * offset, axis=0, keepdims=True))) <= 100.0


def off_pair(k_ref, tab_ref, base, lhs, rhs, row_side, col_side, v_row, v_col, acc_row, acc_col):
    near = right_features(rhs, row_side, col_side)

    @pl.when(near)
    def _():
        def strip(i, carry):
            start = pl.multiple_of(tab_ref[base + i, T_START] * SUB, SUB)
            fast_strip(k_ref, i, lhs, rhs, start, off_width(i))
            owner_strip(k_ref, i, start, v_col, acc_row)
            partner_strip(k_ref, i, start, v_row, acc_col)
            return carry

        each(STRIPS, strip)

    @pl.when(jnp.logical_not(near))
    def _():
        slow_build(k_ref, row_side, col_side, lambda i: tab_ref[base + i, T_START], OFF_SUBS)
        off_products(k_ref, tab_ref, base, v_row, v_col, acc_row, acc_col, looped)

    return near, lhs, rhs


def diag_pair(k_ref, lhs, rhs, side, v, acc):
    near = right_features(rhs, side, side)

    @pl.when(near)
    def _():
        def strip(i, carry):
            fast_strip(k_ref, i, lhs, rhs, i * STRIP, DIAG_W)
            diag_strip(k_ref, i, v, acc, DIAG_W)
            return carry

        each(STRIPS - 1, strip)
        fast_strip(k_ref, STRIPS - 1, lhs, rhs, (STRIPS - 1) * STRIP, STRIP)
        diag_strip(k_ref, STRIPS - 1, v, acc, STRIP)

    @pl.when(jnp.logical_not(near))
    def _():
        slow_build(k_ref, side, side, lambda i: 2 * i, DIAG_W // SUB)
        diag_products(k_ref, v, acc, looped)


def off_width(i):
    return EDGE_W if isinstance(i, int) and i in (0, STRIPS - 1) else OFF_W


def owner_strip(k_ref, i, start, v_col, acc_row):
    width = off_width(i)
    acc_row[:, at(i, STRIP)] += halves(nt(v_col[:, pl.ds(start, width)], k_ref[i, :, :width]))


def partner_strip(k_ref, i, start, v_row, acc_col):
    width = off_width(i)
    acc_col[:, pl.ds(start, width)] += halves(nn(v_row[:, at(i, STRIP)], k_ref[i, :, :width]))


def off_products(k_ref, tab_ref, base, v_row, v_col, acc_row, acc_col, repeat=each):
    def strip(i, carry):
        start = pl.multiple_of(tab_ref[base + i, T_START] * SUB, SUB)
        if acc_row is not None:
            owner_strip(k_ref, i, start, v_col, acc_row)
        if acc_col is not None:
            partner_strip(k_ref, i, start, v_row, acc_col)
        return carry

    strip(0, 0)
    repeat(STRIPS - 2, lambda i, carry: strip(i + 1, carry))
    strip(STRIPS - 1, 0)


def diag_strip(k_ref, i, v_ref, acc_ref, width):
    start = multiple(i * STRIP, STRIP)
    acc_ref[:, at(i, STRIP)] += halves(nt(v_ref[:, pl.ds(start, width)], k_ref[i, :, :width]))
    if width > STRIP:
        acc_ref[:, at(i + 1, STRIP)] += halves(nn(v_ref[:, at(i, STRIP)], k_ref[i, :, STRIP:width]))


def diag_products(k_ref, v_ref, acc_ref, repeat=each):
    def strip(i, carry):
        diag_strip(k_ref, i, v_ref, acc_ref, DIAG_W)
        return carry

    repeat(STRIPS - 1, strip)
    diag_strip(k_ref, STRIPS - 1, v_ref, acc_ref, STRIP)


def extra_tiles(
    tab_ref, base, row_side, col_side, tile_ref, v_row, v_col, acc_row, acc_col, kept=None, fill=None
):
    @pl.when(tab_ref[base, T_EXTRA] > 0)
    def _():
        def strip(i, carry):
            here = pl.ds(pl.multiple_of(i * STRIP, STRIP), STRIP)
            first = tab_ref[base + i, T_NEXT]

            def tile(j, carry):
                col_at = pl.multiple_of(j * SUB, SUB)
                there = pl.ds(col_at, SUB)

                def by_difference():
                    for g in range(STRIP // SUB):
                        row_at = pl.multiple_of(i * STRIP + g * SUB, SUB)
                        tile_ref[g * SUB : (g + 1) * SUB, :] = tile_by_difference(row_side, row_at, col_side, col_at)

                if kept is None:
                    by_difference()
                elif fill is None:
                    pl.when(j > first)(by_difference)

                    @pl.when(j == first)
                    def _():
                        tile_ref[...] = kept[i]
                else:
                    near, lhs, rhs = fill
                    pl.when(jnp.logical_not(near))(by_difference)

                    @pl.when(near)
                    def _():
                        tile_ref[...] = kernel_values(nn(lhs[here, :], rhs[:, there]))

                    @pl.when(j == first)
                    def _():
                        kept[i] = tile_ref[...]

                if acc_row is not None:
                    acc_row[:, here] += halves(nt(v_col[:, there], tile_ref[...]))
                if acc_col is not None:
                    acc_col[:, there] += halves(nn(v_row[:, here], tile_ref[...]))
                return carry

            return lax.fori_loop(first, tab_ref[base + i, T_END], tile, carry)

        lax.fori_loop(0, STRIPS, strip, 0)


TILE = pltpu.VMEM((STRIP, SUB), bf16)
SPLIT = pltpu.VMEM((2 * N_PROBES, BLK), bf16)
SPLITS = pltpu.VMEM((2, 2 * N_PROBES, BLK), bf16)
FIELD = (N_PROBES, BLK)
FIELDS = (2, N_PROBES, BLK)


def call(body, outs, ins, out_specs, scratch, flops, name, limit=12):
    def run(*args):
        return pl.pallas_call(
            body,
            out_shape=outs,
            in_specs=ins,
            out_specs=out_specs,
            scratch_shapes=scratch,
            compiler_params=pltpu.CompilerParams(vmem_limit_bytes=limit * MIB),
            cost_estimate=pl.CostEstimate(flops=flops, bytes_accessed=MIB, transcendentals=0),
            name=name,
        )(*args)

    return run


def diag_build_kernel(tab, side, lhs, kd, acc, tile, v, rhs):
    def block(blk, carry):
        acc[blk] = jnp.zeros(FIELD, f32)
        base = 2 * STRIPS * blk

        @pl.when(tab[base, T_LIVE] > 0)
        def _():
            v[...] = split2(side[blk, 0:16, :])
            diag_pair(kd.at[blk], lhs.at[blk], rhs, side.at[blk], v, acc.at[blk])
            extra_tiles(tab, base, side.at[blk], side.at[blk], tile, v, v, acc.at[blk], acc.at[blk])

        return carry

    each(2, block)


def halo_build_kernel(
    flags, side, lhs, got_a, got_b, acc_in, k12, x12, tab, acc, back, halo, plan_ref, tile, v1, v2, rhs, sem
):
    halo[...] = jnp.where(flags[4] == 0, got_a[...], got_b[...])
    plan_ref[...] = plan(side.at[1], halo, flags[3], False)
    copy = pltpu.make_async_copy(plan_ref, tab, sem.at[0])
    copy.start()
    acc[...] = acc_in[...]
    back[...] = jnp.zeros(FIELD, f32)
    copy.wait()

    @pl.when(flags[3] > 0)
    def _():
        v1[...] = split2(side[1, 0:16, :])
        v2[...] = split2(halo[0:16, :])
        fill = off_pair(k12, tab, 0, lhs.at[1], rhs, side.at[1], halo, v1, v2, acc.at[1], back)
        extra_tiles(tab, 0, side.at[1], halo, tile, v1, v2, acc.at[1], back, x12, fill)


def own_build_kernel(tab, side, lhs, acc_in, k01, x01, acc, tile, v, rhs):
    acc[...] = acc_in[...]

    @pl.when(tab[STRIPS, T_LIVE] > 0)
    def _():
        v[0] = split2(side[0, 0:16, :])
        v[1] = split2(side[1, 0:16, :])
        args = side.at[0], side.at[1]
        ends = v.at[0], v.at[1], acc.at[0], acc.at[1]
        fill = off_pair(k01, tab, STRIPS, lhs.at[0], rhs, *args, *ends)
        extra_tiles(tab, STRIPS, *args, tile, *ends, x01, fill)


def own_apply_kernel(tab, kd, k01, x01, side, w, acc, tile, v):
    def block(blk, carry):
        acc[blk] = jnp.zeros(FIELD, f32)
        v[blk] = split2(w[blk])
        base = 2 * STRIPS * blk

        @pl.when(tab[base, T_LIVE] > 0)
        def _():
            diag_products(kd.at[blk], v.at[blk], acc.at[blk])
            extra_tiles(
                tab, base, side.at[blk], side.at[blk], tile, v.at[blk], v.at[blk], acc.at[blk], acc.at[blk]
            )

        return carry

    each(2, block)

    @pl.when(tab[STRIPS, T_LIVE] > 0)
    def _():
        ends = v.at[0], v.at[1], acc.at[0], acc.at[1]
        off_products(k01, tab, STRIPS, *ends)
        extra_tiles(tab, STRIPS, side.at[0], side.at[1], tile, *ends, x01)


def from_left(flags, got_a, got_b):
    arrived = jnp.where(flags[4] == 0, got_b[...], got_a[...])
    return jnp.where(flags[5] > 0, arrived, 0.0)


def inner(left, right):
    return jnp.sum(left * right, axis=1, keepdims=True)


def halo_product(tab, k12, x12, side, halo, halo_w, tile, v2, acc):
    @pl.when(tab[0, T_LIVE] > 0)
    def _():
        v2[...] = split2(halo_w)
        off_products(k12, tab, 0, None, v2, acc, None)
        extra_tiles(tab, 0, side.at[1], halo, tile, None, v2, acc, None, x12)


def finish_kernel(
    level, flags, tab, k12, x12, side, halo, got_a, got_b, acc_in, w, mom_in, new, send_a, send_b, mom,
    tile, v1, v2, acc, back
):
    acc[...] = acc_in[1]
    if level > 1:
        halo_w = jnp.where(flags[4] == 0, got_a[...], got_b[...])
        halo_product(tab, k12, x12, side, halo, halo_w, tile, v2, acc)
    before0 = w[0, 0:16, :]
    before1 = w[1, 0:16, :]
    next1 = side[1, 19:20, :] * before1 + acc[...]
    new[1] = next1
    back[...] = jnp.zeros(FIELD, f32)

    @pl.when(tab[0, T_LIVE] > 0)
    def _():
        v1[...] = split2(next1)
        off_products(k12, tab, 0, v1, None, None, back)
        extra_tiles(tab, 0, side.at[1], halo, tile, v1, None, None, back, x12)

    next0 = side[0, 19:20, :] * before0 + (acc_in[0] + from_left(flags, got_a, got_b))
    new[0] = next0
    send_a[...] = jnp.where(flags[4] == 0, back[...], next0)
    send_b[...] = jnp.where(flags[4] == 0, next0, back[...])
    lane = lax.broadcasted_iota(jnp.int32, (N_PROBES, SUB), 1)
    cross = inner(before0, next0) + inner(before1, next1)
    own = inner(next0, next0) + inner(next1, next1)
    total = jnp.where(lane == 2 * level - 1, cross, jnp.where(lane == 2 * level, own, 0.0))
    if level == 1:
        total = jnp.where(lane == 0, inner(before0, before0) + inner(before1, before1), total)
    else:
        total = total + mom_in[...]
    mom[...] = total


def moment_kernel(flags, side, acc, got_a, got_b, w, mom_in, mom):
    lane = lax.broadcasted_iota(jnp.int32, (N_PROBES, SUB), 1)
    one = w[0]
    two = w[1]
    arrived = from_left(flags, got_a, got_b)
    cross = inner(one, side[0, 19:20, :] * one + (acc[0] + 2.0 * arrived))
    cross = cross + inner(two, side[1, 19:20, :] * two + acc[1])
    mom[...] = mom_in[...] + jnp.where(lane == 5, cross, 0.0)


def last_kernel(flags, tab, k12, x12, side, halo, got_a, got_b, acc, w, new, tile, v2):
    new[1] = side[1, 19:20, :] * w[1] + acc[1]
    new[0] = side[0, 19:20, :] * w[0] + (acc[0] + from_left(flags, got_a, got_b))
    halo_w = jnp.where(flags[4] == 0, got_a[...], got_b[...])
    halo_product(tab, k12, x12, side, halo, halo_w, tile, v2, new.at[1])


def unsort(rank, fields, store, repeat, only=None):
    def block(blk, carry):
        stacked = jnp.concatenate([split2(field[blk]) for field in fields], axis=0)
        place = places()

        def strip(c, carry):
            piece = rank[blk, :, at(c, STRIP)]
            got = None
            for g in range(STRIPS):
                part = nn(stacked[:, g * STRIP : (g + 1) * STRIP], one_hot(marks(piece, g), place))
                got = part if got is None else got + part
            size = 2 * N_PROBES
            store(blk, at(c if only is not None else blk * STRIPS + c, STRIP), [halves(got[size * k : size * (k + 1)]) for k in range(len(fields))])
            return carry

        repeat(STRIPS, strip)
        return carry

    if only is None:
        repeat(2, block)
    else:
        block(only, 0)


def unsort_kernel(only, rank, wa, wb, wc, out):
    def store(blk, cols, values):
        for k, value in enumerate(values):
            out[16 * k : 16 * (k + 1), cols] = value

    unsort(rank, (wa, wb, wc), store, each, only)


def steps_kernel(mom, out, sound):
    lane = lax.broadcasted_iota(jnp.int32, (N_PROBES, SUB), 1)
    mu = [jnp.sum(jnp.where(lane == k, mom[...], 0.0), axis=1, keepdims=True) for k in range(6)]
    fine = []

    def form(left, right, shift):
        total, size = None, None
        for i, a in enumerate(left):
            for j, b in enumerate(right):
                part = (a * b) * mu[i + j + shift]
                total = part if total is None else total + part
                size = jnp.abs(part) if size is None else size + jnp.abs(part)
        fine.append(size <= 4000.0 * total)
        return total

    one = jnp.ones((N_PROBES, 1), f32)
    d = [one]
    r = [one]
    s = []
    rr = mu[0]
    for it in range(3):
        step = rr / form(d, d, 1)
        moved = [step * v for v in d]
        s = [a + b for a, b in zip(s + [0.0] * (len(d) - len(s)), moved)]
        r = [r[0]] + [(r[i] if i < len(r) else 0.0) - moved[i - 1] for i in range(1, len(moved) + 1)]
        if it < 2:
            new = form(r, r, 0)
            ratio = new / rr
            d = [r[i] + (ratio * d[i] if i < len(d) else 0.0) for i in range(len(r))]
            rr = new
    norms = [jnp.sqrt(mu[0]), jnp.sqrt(mu[2]), jnp.sqrt(mu[4])]
    norms.append(mu[5] / norms[2])
    size = sum(jnp.abs(a) * b for a, b in zip(r, norms))
    fine.append(size <= 200.0 * jnp.sqrt(rr))
    all_fine = fine[0]
    for other in fine[1:]:
        all_fine = all_fine & other
    sound[0] = jnp.min(jnp.where(all_fine, 1.0, 0.0)).astype(jnp.int32)
    table = jnp.zeros((N_PROBES, SUB), f32)
    for k, value in enumerate(s + r):
        table = jnp.where(lane == k, value, table)
    out[...] = table


def combine_kernel(steps, probes, u0, u1, sol, res):
    c = [steps[:, k : k + 1] for k in range(7)]

    def part(b, carry):
        here = at(b, BLK)
        u = (u0, u1)[b]
        w = [probes[:, here], u[0:16, :], u[16:32, :], u[32:48, :]]
        sol[:, here] = (c[0] * w[0] + c[1] * w[1]) + c[2] * w[2]
        res[:, here] = ((c[3] * w[0] + c[4] * w[1]) + c[5] * w[2]) + c[6] * w[3]
        return carry

    each(2, part)


def plain_product_kernel(flags, side, halo, got_a, got_b, d, acc, back, v, v2):
    acc[...] = jnp.zeros(FIELDS, f32)
    back[...] = jnp.zeros(FIELD, f32)
    v[...] = d[...].astype(bf16)
    v2[...] = jnp.where(flags[4] == 0, got_a[...], got_b[...]).astype(bf16)

    def pair(row_side, col_side, v_row, v_col, acc_row, acc_col):
        def row(i, carry):
            def col(j, carry):
                rows, cols = at(i, SUB), at(j, SUB)
                tile = tile_by_difference(
                    row_side, pl.multiple_of(i * SUB, SUB), col_side, pl.multiple_of(j * SUB, SUB)
                )
                acc_row[:, rows] += nt(v_col[:, cols], tile)
                if acc_col is not None:
                    acc_col[:, cols] += nn(v_row[:, rows], tile)
                return carry

            return lax.fori_loop(0, SUBS, col, carry)

        lax.fori_loop(0, SUBS, row, 0)

    def block(blk, carry):
        @pl.when(flags[2 * blk] > 0)
        def _():
            pair(side.at[blk], side.at[blk], None, v.at[blk], acc.at[blk], None)

        return carry

    lax.fori_loop(0, 2, block, 0)

    @pl.when(flags[1] > 0)
    def _():
        pair(side.at[0], side.at[1], v.at[0], v.at[1], acc.at[0], acc.at[1])

    @pl.when(flags[3] > 0)
    def _():
        pair(side.at[1], halo, v.at[1], v2, acc.at[1], back)


def plain_image_kernel(flags, side, acc, got_a, got_b, d, image, part):
    image[0] = side[0, 19:20, :] * d[0] + (acc[0] + from_left(flags, got_a, got_b))
    image[1] = side[1, 19:20, :] * d[1] + acc[1]
    part[...] = jnp.broadcast_to(inner(d[0], image[0]) + inner(d[1], image[1]), (N_PROBES, SUB))


def plain_step_kernel(norm, curvature, x, r, d, image, x_new, r_new, part):
    step = norm[:, 0:1] / curvature[:, 0:1]
    for b in range(2):
        x_new[b] = x[b] + step * d[b]
        r_new[b] = r[b] - step * image[b]
    part[...] = jnp.broadcast_to(inner(r_new[0], r_new[0]) + inner(r_new[1], r_new[1]), (N_PROBES, SUB))


def plain_turn_kernel(norm, new, r, d, d_new):
    ratio = new[:, 0:1] / norm[:, 0:1]
    for b in range(2):
        d_new[b] = r[b] + ratio * d[b]


def plain_start_kernel(side, x, r, part):
    x[...] = jnp.zeros(FIELDS, f32)
    r[0] = side[0, 0:16, :]
    r[1] = side[1, 0:16, :]
    part[...] = jnp.broadcast_to(inner(r[0], r[0]) + inner(r[1], r[1]), (N_PROBES, SUB))


def plain_end_kernel(rank, x, r, sol, res):
    def store(blk, cols, values):
        sol[:, cols], res[:, cols] = values

    unsort(rank, (x, r), store, looped)


def plain_steps(flags, side, halo, rank, shape):
    fields = jax.ShapeDtypeStruct(FIELDS, f32)
    field = jax.ShapeDtypeStruct(FIELD, f32)
    sums = jax.ShapeDtypeStruct((N_PROBES, SUB), f32)

    def small(body, outs, ins, scratch=()):
        return call(body, outs, ins, (VMEM,) * len(outs), list(scratch), 10**7, "plain")

    x, r, part = small(plain_start_kernel, (fields, fields, sums), [VMEM])(side)

    def step(_, state):
        x, r, d, norm = state
        got = swapped_both(d[0], d[0])
        acc, back = small(
            plain_product_kernel,
            (fields, field),
            [SMEM] + [VMEM] * 5,
            (pltpu.VMEM(FIELDS, bf16), pltpu.VMEM(FIELD, bf16)),
        )(flags, side, halo, *got, d)
        got = swapped_both(back, back)
        image, part = small(plain_image_kernel, (fields, sums), [SMEM] + [VMEM] * 5)(flags, side, acc, *got, d)
        curvature = sum_over(part, "gx")
        x, r, part = small(plain_step_kernel, (fields, fields, sums), [VMEM] * 6)(norm, curvature, x, r, d, image)
        new = sum_over(part, "gx")
        (d,) = small(plain_turn_kernel, (fields,), [VMEM] * 4)(norm, new, r, d)
        return x, r, d, new

    x, r, _, _ = lax.fori_loop(0, 3, step, (x, r, r, sum_over(part, "gx")))
    out = jax.ShapeDtypeStruct(shape, f32)
    return small(plain_end_kernel, (out, out), [VMEM] * 3)(rank, x, r)


def swapped_both(to_a, to_b):
    count = lax.axis_size("gx")
    a = lax.ppermute(to_a, "gx", [(k, k ^ 1) for k in range(count)])
    ends = [(0, 0), (count - 1, count - 1)]
    b = lax.ppermute(to_b, "gx", ends + [(k, ((k + 1) ^ 1) - 1) for k in range(1, count - 1)])
    return a, b


def sum_over(value, axis):
    count = lax.axis_size(axis)
    if count & (count - 1):
        return lax.psum(value, axis)
    step = 1
    while step < count:
        radix = min(4, count // step)
        parts = [value] + [
            lax.ppermute(value, axis, [(k, k ^ (m * step)) for k in range(count)]) for m in range(1, radix)
        ]
        while len(parts) > 1:
            parts = [parts[m] + parts[m + 1] for m in range(0, len(parts), 2)]
        value = parts[0]
        step *= radix
    return value


def on_device(points, noise_var, probes, pair_list, counts):
    noise = noise_var.reshape(1, -1)
    field = pltpu.VMEM(FIELD, f32)
    fields = pltpu.VMEM(FIELDS, f32)
    one_side = pltpu.VMEM((24, BLK), f32)
    right = pltpu.VMEM((N_FEATURES, BLK), bf16)
    table = pltpu.SMEM((STRIPS, SUB), jnp.int32)
    moments = pltpu.VMEM((N_PROBES, SUB), f32)
    off = pltpu.VMEM((STRIPS, STRIP, OFF_W), bf16)
    outside = pltpu.VMEM((STRIPS, STRIP, SUB), bf16)
    far_space = pl.BlockSpec(memory_space=pltpu.HBM)
    shape = probes.shape

    side, first, lhs, rank, probes, flags, tab = call(
        sort_kernel,
        (
            pltpu.VMEM((2, 24, BLK), f32),
            one_side,
            pltpu.VMEM((2, BLK, N_FEATURES), bf16),
            pltpu.VMEM((2, 1, BLK), jnp.int32),
            pltpu.VMEM(shape, f32),
            pltpu.SMEM((6,), jnp.int32),
            pltpu.SMEM((3 * STRIPS, SUB), jnp.int32),
        ),
        [far_space] * 4 + [SMEM],
        (VMEM,) * 5 + (SMEM,) * 2,
        [
            pltpu.VMEM(points.shape, f32),
            pltpu.VMEM(noise.shape, f32),
            pltpu.SMEM(pair_list.shape[::-1], jnp.int32),
            pltpu.VMEM((3 * STRIPS, SUB), jnp.int32),
            pltpu.VMEM((2, 1, BLK), f32),
            pltpu.VMEM((2, STRIPS, STRIP, SUB), f32),
            pltpu.SemaphoreType.DMA((4,)),
        ],
        10**9,
        "sort_blocks",
    )(*[pltpu.with_memory_space_constraint(x, pltpu.HBM) for x in (points, noise, probes, pair_list.T)], counts)

    halos = swapped_both(first, first)
    kd, acc = call(
        diag_build_kernel,
        (pltpu.VMEM((2, STRIPS, STRIP, DIAG_W), bf16), fields),
        [SMEM] + [VMEM] * 2,
        (VMEM,) * 2,
        [TILE, SPLIT, right],
        3 * 10**9,
        "diag_build",
    )(tab, side, lhs)
    k12, x12, tab12, acc, back, halo = call(
        halo_build_kernel,
        (off, outside, table, fields, field, one_side),
        [SMEM] + [VMEM] * 5,
        (VMEM, VMEM, SMEM, VMEM, VMEM, VMEM),
        [pltpu.VMEM((STRIPS, SUB), jnp.int32), TILE, SPLIT, SPLIT, right, pltpu.SemaphoreType.DMA((1,))],
        3 * 10**9,
        "halo_build",
    )(flags, side, lhs, *halos, acc)
    got = swapped_both(back, back)
    k01, x01, acc = call(
        own_build_kernel,
        (off, outside, fields),
        [SMEM] + [VMEM] * 3,
        (VMEM,) * 3,
        [TILE, SPLITS, right],
        5 * 10**9,
        "own_build",
    )(tab, side, lhs, acc)

    w = side
    mom = jnp.zeros((N_PROBES, SUB), f32)
    kept = []
    for level in (1, 2):
        w, send_a, send_b, mom = call(
            functools.partial(finish_kernel, level),
            (fields, field, field, moments),
            [SMEM] * 2 + [VMEM] * 9,
            (VMEM,) * 4,
            [TILE, SPLIT, SPLIT, pltpu.VMEM(FIELD, f32), pltpu.VMEM(FIELD, f32)],
            10**9,
            "finish",
        )(flags, tab12, k12, x12, side, halo, *got, acc, w, mom)
        kept.append(w)
        got = swapped_both(send_a, send_b)
        (acc,) = call(
            own_apply_kernel,
            (fields,),
            [SMEM] + [VMEM] * 5,
            (VMEM,),
            [TILE, SPLITS],
            2 * 10**9,
            "own_apply",
        )(tab, kd, k01, x01, side, w)
    mom = call(moment_kernel, moments, [SMEM] + [VMEM] * 6, VMEM, [], 10**7, "moment")(
        flags, side, acc, *got, w, mom
    )
    total = sum_over(mom, "gx")
    kept.append(
        call(last_kernel, fields, [SMEM] * 2 + [VMEM] * 8, VMEM, [TILE, SPLIT], 10**9, "last")(
            flags, tab12, k12, x12, side, halo, *got, acc, w
        )
    )
    given = [
        call(
            functools.partial(unsort_kernel, b),
            pltpu.VMEM((3 * N_PROBES, BLK), f32),
            [VMEM] * 4,
            VMEM,
            [],
            2 * 96 * BLK * BLK,
            "unsort",
        )(rank, *kept)
        for b in range(2)
    ]
    steps, sound = call(
        steps_kernel,
        (moments, pltpu.SMEM((1,), jnp.int32)),
        [VMEM],
        (VMEM, SMEM),
        [],
        10**6,
        "steps",
    )(total)

    def from_basis():
        out = jax.ShapeDtypeStruct(shape, f32)
        return tuple(
            call(combine_kernel, (out, out), [VMEM] * 4, (VMEM, VMEM), [], 10**6, "combine")(steps, probes, *given)
        )

    def from_start():
        return tuple(plain_steps(flags, side, halo, rank, shape))

    return lax.cond(sound[0] > 0, from_basis, from_start)


def solution(mesh):
    placed = (
        P(None, ("groups", "gx")),
        P(("groups", "gx")),
        P(None, ("groups", "gx")),
        P(("groups", "gx"), None),
        P(("groups", "gx")),
    )
    return jax.shard_map(
        on_device,
        mesh=mesh,
        in_specs=placed,
        out_specs=(P(None, ("groups", "gx")), P(None, ("groups", "gx"))),
        check_vma=False,
    )
```
